32 devices in a mesh: section: 2 (over x), ctx: 4 (over z), fsdp: 4 (over y, core).
Axes of the slice: x: 2, y: 2, z: 4, core: 2. Of those that a mesh axis runs over, the one named last changes fastest.
Arguments:
- inputs: bfloat16 [2, 1024, 1536], P(None, ('ctx', 'fsdp')), may hold values from -6 to 6
- cotangent: bfloat16 [2, 1024, 1536], P(None, ('ctx', 'fsdp')), may hold values from -6 to 6
- attention_gain: bfloat16 [2, 1536], P('section', 'fsdp'), may hold values from 0.5 to 1.5
- query_key_value: bfloat16 [2, 1536, 3072], P('section', 'fsdp'), may hold values from -0.15625 to 0.15625
- output_weight: bfloat16 [2, 1536, 1536], P('section', 'fsdp'), may hold values from -1.25 to 1.25
- feed_gain: bfloat16 [2, 1536], P('section', 'fsdp'), may hold values from 0.5 to 1.5
- gate_up: bfloat16 [2, 1536, 8192], P('section', 'fsdp'), may hold values from -0.15625 to 0.15625
- down_weight: bfloat16 [2, 4096, 1536], P('section', 'fsdp'), may hold values from -0.09375 to 0.09375
- block_order: int32 [2, 16], replicated, may hold values from 0 to 15, each once within a row
Outputs:
- section_outputs: bfloat16 [2, 2, 1024, 1536], P('section', None, ('ctx', 'fsdp'))
- section_input_grads: float32 [2, 2, 1024, 1536], P('section', None, ('ctx', 'fsdp'))
- attention_gain_grad: float32 [2, 1536], P('section', 'fsdp')
- query_key_value_grad: float32 [2, 1536, 3072], P('section', 'fsdp')
- output_weight_grad: float32 [2, 1536, 1536], P('section', 'fsdp')
- feed_gain_grad: float32 [2, 1536], P('section', 'fsdp')
- gate_up_grad: float32 [2, 1536, 8192], P('section', 'fsdp')
- down_weight_grad: float32 [2, 4096, 1536], P('section', 'fsdp')
The draws below stay inside these ranges and needn't reach their ends.
Inputs may be any that keep to these rules, and one draw needn't show every extreme that they name: `block_order`: each row holds every block place once.
All inputs are finite; a program needn't handle non-finite values.
Results may differ from the reference program's by a relative error of at most 0.035.
Values may be sent and summed in bfloat16 or wider, within the bound.
A program may use at most 320 MiB of HBM per device.

```python
import jax
import jax.numpy as jnp
from jax import lax

D = 1536
HEADS = 16
KV_HEADS = 8
HEAD = 96
FF = 4096
TOK_DEV = 64
MB = 2
NBLK = 16
LENGTH = 1024
N_SECTION = 2


def levels(rng, dims, cuts, smallest, top_value):
    loudness = 1.0
    for axis_at, parts in cuts:
        heights = jax.random.uniform(jax.random.fold_in(jax.random.fold_in(rng, 6), axis_at), (parts,), jnp.float32, smallest / len(cuts), top_value / len(cuts))
        loudness = loudness * jnp.repeat(jnp.exp(heights), dims[axis_at] // parts).reshape((-1,) + (1,) * (len(dims) - 1 - axis_at))
    return loudness


def normal_values(stream_key, extent, scale, most, split=(), kind=jnp.bfloat16):
    result = jax.random.normal(stream_key, extent, jnp.float32) * scale
    if len(split) > 0:
        result = levels(stream_key, extent, split, -0.22, 0.18) * result
    return jnp.clip(result, min=-most, max=most).astype(kind)


def setup_inputs(seed: int = 0) -> dict:
    key_of = jax.random.split(jax.random.key(seed), 10)
    inputs = normal_values(key_of[0], (MB, LENGTH, D), 1.0, 6.0, ((1, 16),))
    cotangent = normal_values(key_of[1], (MB, LENGTH, D), 1.0, 6.0, ((1, 16),))
    attention_gain = jnp.clip(1.0 + 0.1 * jax.random.normal(key_of[2], (N_SECTION, D), jnp.float32), 0.5, 1.5).astype(jnp.bfloat16)
    query_key_value = normal_values(key_of[3], (N_SECTION, D, D + 2 * KV_HEADS * HEAD), D ** -0.5, 0.15625, ((0, 2), (1, 4)))
    output_weight = normal_values(key_of[4], (N_SECTION, D, D), (D // 64) ** -0.5, 1.25, ((0, 2), (1, 4)))
    feed_gain = jnp.clip(1.0 + 0.1 * jax.random.normal(key_of[5], (N_SECTION, D), jnp.float32), 0.5, 1.5).astype(jnp.bfloat16)
    gate_up = normal_values(key_of[6], (N_SECTION, D, 2 * FF), D ** -0.5, 0.15625, ((0, 2), (1, 4)))
    down_weight = normal_values(key_of[7], (N_SECTION, FF, D), FF ** -0.5, 0.09375, ((0, 2), (1, 4)))
    block_order = jax.vmap(lambda own: jax.random.permutation(own, NBLK))(jax.random.split(key_of[8], MB)).reshape((MB, NBLK)).astype(jnp.int32)
    return dict(inputs=inputs, cotangent=cotangent, attention_gain=attention_gain, query_key_value=query_key_value, output_weight=output_weight, feed_gain=feed_gain, gate_up=gate_up, down_weight=down_weight, block_order=block_order)


norm_eps = 1e-05
rope_base = 100000.0
masked_value = -1e+30

@jax.custom_vjp
def low(v):
    return lax.optimization_barrier(v.astype(jnp.bfloat16)).astype(jnp.float32)

@jax.custom_vjp
def low_back(v):
    return v

def low_keep(v):
    return (low(v), None)

def low_pass(kept, grad):
    return (grad,)

def back_keep(v):
    return (v, None)

def back_low(kept, grad):
    return (low(grad),)
low.defvjp(low_keep, low_pass)
low_back.defvjp(back_keep, back_low)

def highdot(left, right):
    return jnp.dot(left, right, precision=lax.Precision.HIGHEST)

def rms_scale(values, gain):
    return values * lax.rsqrt(lax.optimization_barrier(jnp.mean(values * values, axis=-1, keepdims=True)) + norm_eps) * gain

def angle_tables(positions, head_size):
    frequency = rope_base ** (-(jnp.arange(head_size // 2, dtype=jnp.float32) * 2.0 / head_size))
    angles = positions.astype(jnp.float32)[:, None] * frequency[None, :]
    return (jnp.cos(angles)[:, None, :], jnp.sin(angles)[:, None, :])

def rotate(values, cosine, sine):
    half = values.shape[-1] // 2
    first = values[..., :half]
    second = values[..., half:]
    return jnp.concatenate([first * cosine - second * sine, second * cosine + first * sine], axis=-1)

def attention(queries, keys, values, positions):
    length = queries.shape[0]
    ratio = HEADS // KV_HEADS
    block = 8 * TOK_DEV
    scale = HEAD ** (-0.5)

    def one_block(index):
        start = index * block
        query_block = lax.dynamic_slice_in_dim(queries, start, block, 0).reshape(block, KV_HEADS, ratio, HEAD)
        query_places = lax.dynamic_slice_in_dim(positions, start, block, 0)
        raw = jnp.einsum('qgrd,kgd->grqk', query_block, keys, precision=lax.Precision.HIGHEST)
        scores = low_back(raw * scale)
        allowed = positions[None, :] <= query_places[:, None]
        scores = jnp.where(allowed[None, None], scores, masked_value)
        top = lax.optimization_barrier(jnp.max(scores, axis=-1, keepdims=True))
        weights = jnp.exp(scores - top)
        weights = weights / lax.optimization_barrier(jnp.sum(weights, axis=-1, keepdims=True))
        mixed = jnp.einsum('grqk,kgd->qgrd', low(weights), values, precision=lax.Precision.HIGHEST)
        return mixed.reshape(block, HEADS * HEAD)
    results = lax.map(jax.checkpoint(one_block), jnp.arange(length // block, dtype=jnp.int32))
    return results.reshape(length, HEADS * HEAD)

def layer(hidden_rows, positions, attention_gain, query_key_value, output_weight, feed_gain, gate_up, down_weight):
    length = hidden_rows.shape[0]
    kv_width = KV_HEADS * HEAD
    cosine, sine = angle_tables(positions, HEAD)
    normed = low(rms_scale(hidden_rows, attention_gain))
    mixed = highdot(normed, query_key_value)
    queries = low(rotate(low_back(mixed[:, :D]).reshape(length, HEADS, HEAD), cosine, sine))
    keys = low(rotate(low_back(mixed[:, D:D + kv_width]).reshape(length, KV_HEADS, HEAD), cosine, sine))
    values = low_back(low(mixed[:, D + kv_width:])).reshape(length, KV_HEADS, HEAD)
    context = low_back(low(attention(queries, keys, values, positions)))
    middle = hidden_rows + low_back(highdot(context, output_weight))
    normed_two = low(rms_scale(middle, feed_gain))
    both = low_back(highdot(normed_two, gate_up))
    hidden = low(jax.nn.silu(both[:, :FF]) * both[:, FF:])
    return middle + low_back(highdot(hidden, down_weight))

def reference(inputs, cotangent, attention_gain, query_key_value, output_weight, feed_gain, gate_up, down_weight, block_order):
    length = inputs.shape[1]
    local = jnp.arange(length, dtype=jnp.int32)
    positions = jnp.take(block_order, local // TOK_DEV, axis=1) * TOK_DEV + local % TOK_DEV
    weights_all = tuple((array.astype(jnp.float32) for array in (attention_gain, query_key_value, output_weight, feed_gain, gate_up, down_weight)))
    first_rows = inputs.astype(jnp.float32)
    probes = jnp.zeros((N_SECTION, MB, length, D), jnp.float32)

    def forward(first_rows, weights_all, probes):

        def run(carry, item):
            sequence, position_row, probe_row = item
            hidden_rows = sequence
            results = []
            for section in range(N_SECTION):
                hidden_rows = layer(hidden_rows + probe_row[section], position_row, *[array[section] for array in weights_all])
                if section + 1 < N_SECTION:
                    hidden_rows = low_back(low(hidden_rows))
                results.append(hidden_rows)
            return (carry, jnp.stack(results))
        _, results = lax.scan(run, jnp.zeros((), jnp.float32), (first_rows, positions, jnp.swapaxes(probes, 0, 1)))
        return results
    results, pullback = jax.vjp(forward, first_rows, weights_all, probes)
    output_grads = jnp.zeros_like(results).at[:, N_SECTION - 1].set(cotangent.astype(jnp.float32))
    _, weight_grads, probe_grads = pullback(output_grads)
    section_outputs = jnp.swapaxes(results, 0, 1).astype(jnp.bfloat16)
    return (section_outputs, probe_grads, weight_grads[0], weight_grads[1], weight_grads[2], weight_grads[3], weight_grads[4], weight_grads[5])
```

```python
import jax
import jax.numpy as jnp
from jax import lax
from jax.experimental import pallas as pl
from jax.experimental.pallas import tpu as pltpu
from jax.sharding import PartitionSpec as P

MESH = pl.DeviceIdType.MESH


def greet():
    c = lax.axis_index("ctx")
    f = lax.axis_index("fsdp")
    barrier = pltpu.get_barrier_semaphore()
    inner = jnp.logical_and(c > 0, c < 3)
    for peer in (f + 2 - 4 * (f // 2), f + 1 - 2 * lax.rem(f, 2)):
        pl.semaphore_signal(barrier, inc=1, device_id={"fsdp": peer}, device_id_type=MESH)

    @pl.when(c < 3)
    def _():
        pl.semaphore_signal(barrier, inc=1, device_id={"ctx": c + 1}, device_id_type=MESH)

    @pl.when(c > 0)
    def _():
        pl.semaphore_signal(barrier, inc=1, device_id={"ctx": c - 1}, device_id_type=MESH)

    @pl.when(inner)
    def _():
        pl.semaphore_wait(barrier, 4)

    @pl.when(jnp.logical_not(inner))
    def _():
        pl.semaphore_wait(barrier, 3)


def near_order(c):
    low = c < 2
    return [c, c + 1 - 2 * lax.rem(c, 2), jnp.where(low, 2, 1), jnp.where(low, 3, 0)]


def gather_rows(own, whole, send, recv):
    c = lax.axis_index("ctx")
    f = lax.axis_index("fsdp")
    across = f + 2 - 4 * (f // 2)
    twin = f + 1 - 2 * lax.rem(f, 2)
    cross = across + 1 - 2 * lax.rem(f, 2)
    inner = jnp.logical_and(c > 0, c < 3)
    rows = own.shape[0]
    order = near_order(c)

    def at(cc, ff):
        return whole.at[pl.ds(pl.multiple_of((cc * 4 + ff) * rows, rows), rows)]

    def copy(src, dst, slot, arrival, peer):
        return pltpu.make_async_remote_copy(
            src, dst, send.at[slot], recv.at[arrival], device_id=peer, device_id_type=MESH
        )

    up = copy(own, at(c, f), 0, c, {"ctx": jnp.minimum(c + 1, 3)})
    down = copy(own, at(c, f), 1, c, {"ctx": jnp.maximum(c - 1, 0)})
    pl.when(c < 3)(up.start)
    pl.when(c > 0)(down.start)
    sent = []
    forwards = []
    first = copy(own, at(c, f), 2, 4 + c, {"fsdp": across})
    first.start()
    second = copy(own, at(c, f), 6, 8 + c, {"fsdp": twin})
    second.start()
    sent += [first, second]
    whole[pl.ds(pl.multiple_of((c * 4 + f) * rows, rows), rows), :] = own[...]

    def spread_across(step):
        d = order[step]
        block = at(d, across)
        copy(block, block, 0, 4 + d, {"fsdp": across}).wait_recv()
        one = copy(block, block, 10 + step, 12 + d, {"fsdp": twin})
        one.start()
        sent.append(one)

    for step in range(1, 4):
        d = order[step]
        block = at(d, f)
        copy(block, block, 0, d, {"fsdp": twin}).wait_recv()
        onward = jnp.where(d < c, jnp.minimum(c + 1, 3), jnp.maximum(c - 1, 0))
        forward = copy(block, block, 13 + step, d, {"ctx": onward})
        pl.when(inner)(forward.start)
        forwards.append(forward)
        one = copy(block, block, 2 + step, 4 + d, {"fsdp": across})
        one.start()
        two = copy(block, block, 6 + step, 8 + d, {"fsdp": twin})
        two.start()
        sent += [one, two]
        spread_across(step - 1)
    spread_across(3)
    for step in range(4):
        d = order[step]
        copy(at(d, twin), at(d, twin), 0, 8 + d, {"fsdp": twin}).wait_recv()
        copy(at(d, cross), at(d, cross), 0, 12 + d, {"fsdp": twin}).wait_recv()
    pl.when(c < 3)(up.wait_send)
    pl.when(c > 0)(down.wait_send)
    for forward in forwards:
        pl.when(inner)(forward.wait_send)
    for one in sent:
        one.wait_send()


GATHER_SENDS = 17
GATHER_RECVS = 16


def scatter_sum(part, total, land, send, recv):
    c = lax.axis_index("ctx")
    f = lax.axis_index("fsdp")
    across = f + 2 - 4 * (f // 2)
    twin = f + 1 - 2 * lax.rem(f, 2)
    cross = across + 1 - 2 * lax.rem(f, 2)
    inner = jnp.logical_and(c > 0, c < 3)
    rows = total.shape[0]
    order = near_order(c)[::-1]

    def rows_at(cc, ff):
        return pl.ds(pl.multiple_of((cc * 4 + ff) * rows, rows), rows)

    def at(cc, ff):
        return part.at[rows_at(cc, ff)]

    def copy(src, dst, slot, arrival, peer):
        return pltpu.make_async_remote_copy(
            src, dst, send.at[slot], recv.at[arrival], device_id=peer, device_id_type=MESH
        )

    def landed(slot):
        copy(land.at[slot], land.at[slot], 0, slot, {"fsdp": twin}).wait_recv()
        return land[slot].astype(jnp.float32)

    sent = []
    for step in range(4):
        d = order[step]
        one = copy(at(d, cross), land.at[step], step, step, {"fsdp": twin})
        one.start()
        two = copy(at(d, twin), land.at[4 + step], 4 + step, 4 + step, {"fsdp": twin})
        two.start()
        sent += [one, two]

    def over(step):
        d = order[step]
        mine = rows_at(d, across)
        part[mine, :] = (part[mine, :].astype(jnp.float32) + landed(step)).astype(part.dtype)
        one = copy(at(d, across), land.at[8 + step], 8 + step, 8 + step, {"fsdp": across})
        one.start()
        sent.append(one)

    over(0)
    lines = []
    for step in range(4):
        d = order[step]
        mine = rows_at(d, f)
        if step < 3:
            over(step + 1)
        value = part[mine, :].astype(jnp.float32) + landed(4 + step) + landed(8 + step)
        if step < 3:
            part[mine, :] = value.astype(part.dtype)

            @pl.when(inner)
            def _():
                part[mine, :] = (value + landed(12 + d)).astype(part.dtype)

            onward = jnp.where(d > c, c + 1, c - 1)
            slot = jnp.where(jnp.logical_and(d < c, d == c - 1), 16, 12 + d)
            line = copy(at(d, f), land.at[slot], 12 + step, slot, {"ctx": onward})
            line.start()
            sent.append(line)
        else:
            total[...] = value

            @pl.when(c > 0)
            def _():
                total[...] += landed(12 + c)

            @pl.when(c < 3)
            def _():
                total[...] += landed(16)
    for one in sent:
        one.wait_send()


SCATTER_SENDS = 15
SCATTER_RECVS = 17


def gather_kernel(own, whole, send, recv):
    greet()
    gather_rows(own, whole, send, recv)


def scatter_kernel(part, total, work, land, send, recv):
    greet()
    work[...] = part[...]
    scatter_sum(work, total, land, send, recv)


def gather_call(own):
    rows, w = own.shape
    return pl.pallas_call(
        gather_kernel,
        out_shape=jax.ShapeDtypeStruct((16 * rows, w), own.dtype),
        in_specs=[pl.BlockSpec(memory_space=pltpu.VMEM)],
        out_specs=pl.BlockSpec(memory_space=pltpu.VMEM),
        scratch_shapes=[pltpu.SemaphoreType.DMA((GATHER_SENDS,)), pltpu.SemaphoreType.DMA((GATHER_RECVS,))],
        compiler_params=pltpu.CompilerParams(collective_id=0, has_side_effects=True, vmem_limit_bytes=48 << 20),
    )(own)


def scatter_call(part):
    w = part.shape[1]
    rows = part.shape[0] // 16
    return pl.pallas_call(
        scatter_kernel,
        out_shape=jax.ShapeDtypeStruct((rows, w), jnp.float32),
        in_specs=[pl.BlockSpec(memory_space=pltpu.VMEM)],
        out_specs=pl.BlockSpec(memory_space=pltpu.VMEM),
        scratch_shapes=[
            pltpu.VMEM(part.shape, part.dtype),
            pltpu.VMEM((17, rows, w), part.dtype),
            pltpu.SemaphoreType.DMA((SCATTER_SENDS,)), pltpu.SemaphoreType.DMA((SCATTER_RECVS,))],
        compiler_params=pltpu.CompilerParams(collective_id=1, has_side_effects=True, vmem_limit_bytes=48 << 20),
    )(part)


KV_HEADS = 8
HEAD = 96
LANES = 128
SPAN = 64
norm_eps = 1e-05
rope_base = 100000.0
masked_value = -1e30
BF = jnp.bfloat16
F32 = jnp.float32


def on_line():
    return lax.axis_size("ctx") == 4 and lax.axis_size("fsdp") == 4


def gather(own):
    if on_line():
        return gather_call(own)
    return lax.all_gather(own, ("ctx", "fsdp"), axis=0, tiled=True)


def scatter(part):
    if on_line():
        return scatter_call(part.astype(BF))
    return lax.psum_scatter(part, ("ctx", "fsdp"), scatter_dimension=0, tiled=True)


def spread_halves(columns):
    halves = columns.reshape(columns.shape[:-1] + (2, HEAD // 2))
    halves = jnp.pad(halves, [(0, 0)] * (halves.ndim - 1) + [(0, SPAN - HEAD // 2)])
    return halves.reshape(columns.shape[:-1] + (LANES,))


def join_halves(columns):
    halves = columns.reshape(columns.shape[:-1] + (2, SPAN))[..., : HEAD // 2]
    return halves.reshape(columns.shape[:-1] + (HEAD,))


def angle_tables(positions):
    frequency = rope_base ** (-(jnp.arange(HEAD // 2, dtype=F32) * 2.0 / HEAD))
    frequency = jnp.pad(frequency, (0, SPAN - HEAD // 2))
    angles = positions.astype(F32)[:, None] * frequency[None, :]
    cosine = jnp.cos(angles)
    sine = jnp.sin(angles)
    return jnp.concatenate([cosine, cosine], axis=1), jnp.concatenate([-sine, sine], axis=1)


def rotate(values, cosine, sine):
    return values * cosine + jnp.roll(values, SPAN, axis=1) * sine


def rotate_back(grads, cosine, sine):
    return grads * cosine - jnp.roll(grads, SPAN, axis=1) * sine


def norm_rows(values):
    return lax.rsqrt(jnp.mean(values * values, axis=-1, keepdims=True) + norm_eps)


def norm_back(grad_out, values, factor, gain):
    shaped = grad_out * gain
    common = jnp.mean(shaped * values, axis=-1, keepdims=True)
    grad_in = factor * shaped - values * (factor * factor * factor) * common
    return grad_in, jnp.sum(grad_out * values * factor, axis=0)


def dot(left, right):
    return jnp.dot(left, right, preferred_element_type=F32)


def dot_nt(left, right):
    return lax.dot_general(left, right, (((1,), (1,)), ((), ())), preferred_element_type=F32)


def dot_tn(left, right):
    return lax.dot_general(left, right, (((0,), (0,)), ((), ())), preferred_element_type=F32)


class Plan:
    def __init__(self, width, hidden_units):
        self.c = lax.axis_index("ctx")
        self.f = lax.axis_index("fsdp")
        self.C = lax.axis_size("ctx")
        self.F = lax.axis_size("fsdp")
        self.heads = width // HEAD
        self.ratio = self.heads // KV_HEADS
        self.heads_f = self.heads // self.F
        self.groups_f = KV_HEADS // self.F
        self.share = self.C // self.heads_f
        self.units = hidden_units // (self.F * self.C)
        self.local_head = self.c // self.share
        self.part = self.c % self.share


def pick(array, index, axis):
    return lax.dynamic_index_in_dim(array, index, axis, keepdims=False)


def pack_weights(plan, mix, gate_up):
    depth = mix.shape[0]
    width = plan.heads * HEAD
    kv_width = KV_HEADS * HEAD
    F = plan.F
    queries = pick(mix[:, :width].reshape(depth, F, plan.heads_f, HEAD), plan.local_head, 2)
    group = plan.local_head // plan.ratio
    keys = pick(mix[:, width : width + kv_width].reshape(depth, F, plan.groups_f, HEAD), group, 2)
    values = pick(mix[:, width + kv_width :].reshape(depth, F, plan.groups_f, HEAD), group, 2)
    values = jnp.pad(values, ((0, 0), (0, 0), (0, LANES - HEAD)))
    half = gate_up.shape[1] // 2
    gate = pick(gate_up[:, :half].reshape(depth, F, plan.C, plan.units), plan.c, 2)
    up = pick(gate_up[:, half:].reshape(depth, F, plan.C, plan.units), plan.c, 2)
    packed = jnp.concatenate([spread_halves(queries), spread_halves(keys), values, gate, up], axis=2)
    return jnp.swapaxes(packed, 0, 1)


def attend(plan, q_part, k, v, positions, part_positions):
    scores = dot_nt(q_part, k) * HEAD ** (-0.5)
    allowed = positions[None, :] <= part_positions[:, None]
    scores = jnp.where(allowed, scores, masked_value)
    top = jnp.max(scores, axis=-1, keepdims=True)
    weights = jnp.exp(scores - top)
    total = jnp.sum(weights, axis=-1, keepdims=True)
    context = dot((weights / total).astype(BF), v)
    return context.astype(BF), top + jnp.log(total)


def attend_back(q_part, k, v, context_grad, context, log_total, positions, part_positions):
    scale = HEAD ** (-0.5)
    common = jnp.sum(context_grad.astype(F32) * context.astype(F32), axis=-1, keepdims=True)
    allowed = positions[None, :] <= part_positions[:, None]
    scores = dot_nt(q_part, k) * scale
    weights = jnp.exp(jnp.where(allowed, scores, masked_value) - log_total)
    weight_grad = dot_nt(context_grad, v)
    score_grad = (weights * (weight_grad - common)).astype(BF)
    value_grad = dot_tn(weights.astype(BF), context_grad)
    key_grad = dot_tn(score_grad, q_part) * scale
    query_grad = dot(score_grad, k) * scale
    return query_grad, key_grad, value_grad


def forward_layer(plan, x_own, weights, gains, positions, part_positions, tables):
    cut, out, down = weights
    cosine, sine = tables
    length = positions.shape[0]
    x_all = gather(x_own)
    x32 = x_all.astype(F32)
    factor = norm_rows(x32)
    normed = (x32 * factor * gains[0]).astype(BF)
    mixed = dot(normed, cut[:, : 3 * LANES])
    q = rotate(mixed[:, :LANES], cosine, sine).astype(BF)
    k = rotate(mixed[:, LANES : 2 * LANES], cosine, sine).astype(BF)
    v = mixed[:, 2 * LANES :].astype(BF)
    rows = length // plan.share
    start = plan.part * rows
    q_part = lax.dynamic_slice_in_dim(q, start, rows, 0)
    context, log_total = attend(plan, q_part, k, v, positions, part_positions)
    partial = dot(context[:, :HEAD], out).astype(BF)
    if plan.share > 1:
        partial = lax.dynamic_update_slice_in_dim(
            jnp.zeros((length, partial.shape[1]), BF), partial, start, 0
        )
    middle = x_own.astype(F32) + scatter(partial)
    factor_two = norm_rows(middle)
    normed_two = gather((middle * factor_two * gains[1]).astype(BF))
    both = dot(normed_two, cut[:, 3 * LANES :])
    hidden = (jax.nn.silu(both[:, : plan.units]) * both[:, plan.units :]).astype(BF)
    result = middle + scatter(dot(hidden, down).astype(BF))
    kept = (x_own, normed, q_part, k, v, context, log_total, middle, normed_two, both, hidden)
    return result.astype(BF), kept


def backward_layer(plan, grad_own, weights, gains, kept, positions, part_positions, tables, part_tables):
    cut, out, down = weights
    x_own, normed, q_part, k, v, context, log_total, middle, normed_two, both, hidden = kept
    length = positions.shape[0]
    rows = length // plan.share
    start = plan.part * rows
    grad_all = gather(grad_own)
    hidden_grad = dot_nt(grad_all, down)
    gate = both[:, : plan.units]
    up = both[:, plan.units :]
    sig = jax.nn.sigmoid(gate)
    gate_grad = hidden_grad * up * sig * (1.0 + gate * (1.0 - sig))
    up_grad = hidden_grad * gate * sig
    both_grad = jnp.concatenate([gate_grad, up_grad], axis=1).astype(BF)
    normed_two_grad = scatter(dot_nt(both_grad, cut[:, 3 * LANES :]).astype(BF))
    middle_grad, feed_gain_grad = norm_back(normed_two_grad, middle, norm_rows(middle), gains[1])
    middle_grad = middle_grad + grad_own.astype(F32)
    middle_low = gather(middle_grad.astype(BF))
    middle_part = lax.dynamic_slice_in_dim(middle_low, start, rows, 0)
    context_grad = jnp.pad(dot_nt(middle_part, out), ((0, 0), (0, LANES - HEAD))).astype(BF)
    query_grad, key_grad, value_grad = attend_back(
        q_part, k, v, context_grad, context, log_total, positions, part_positions
    )
    query_grad = rotate_back(query_grad, *part_tables).astype(BF)
    if plan.share > 1:
        query_grad = lax.dynamic_update_slice_in_dim(
            jnp.zeros((length, LANES), BF), query_grad, start, 0
        )
    key_grad = rotate_back(key_grad, *tables).astype(BF)
    mixed_grad = jnp.concatenate([query_grad, key_grad, value_grad.astype(BF)], axis=1)
    normed_grad = scatter(dot_nt(mixed_grad, cut[:, : 3 * LANES]).astype(BF))
    x32 = x_own.astype(F32)
    start_grad, attention_gain_grad = norm_back(normed_grad, x32, norm_rows(x32), gains[0])
    start_grad = start_grad + middle_grad
    cut_grad = jnp.concatenate(
        [dot_tn(normed, mixed_grad).astype(BF), dot_tn(normed_two, both_grad).astype(BF)], axis=1
    )
    out_grad = dot_tn(context, middle_part).astype(BF)[:HEAD]
    down_grad = dot_tn(hidden, grad_all).astype(BF)
    return start_grad, (cut_grad, out_grad, down_grad), (attention_gain_grad, feed_gain_grad)


def swap_sections(array):
    return lax.ppermute(array, "section", [(0, 1), (1, 0)])


def on_device(
    inputs, cotangent, attention_gain, query_key_value, output_weight, feed_gain, gate_up, down_weight, block_order
):
    section = lax.axis_index("section")
    width = inputs.shape[2]
    hidden_units = down_weight.shape[1] * lax.axis_size("fsdp")
    plan = Plan(width, hidden_units)
    rows = inputs.shape[1]
    C, F = plan.C, plan.F
    length = rows * C * F
    depth = query_key_value.shape[1]

    def by_layer(own, other):
        first = section == 0
        return jnp.where(first, own, other), jnp.where(first, other, own)

    order = pick(block_order, section, 0)
    positions = (order[:, None] * rows + jnp.arange(rows, dtype=jnp.int32)[None, :]).reshape(length)
    part_rows = length // plan.share
    part_positions = lax.dynamic_slice_in_dim(positions, plan.part * part_rows, part_rows, 0)
    tables = angle_tables(positions)
    part_tables = angle_tables(part_positions)

    gains = lax.all_gather(
        jnp.stack([attention_gain[0], feed_gain[0]]), ("section", "fsdp"), axis=0, tiled=False
    )
    gains = gains.reshape(2, F, 2, depth)
    gains = jnp.swapaxes(gains, 1, 2).reshape(2, 2, width).astype(F32)

    packed = pack_weights(plan, query_key_value[0], gate_up[0])
    own_cut = lax.all_to_all(packed, "fsdp", 0, 0).reshape(width, -1)
    own_out = lax.dynamic_slice_in_dim(output_weight[0], plan.local_head * HEAD, HEAD, 0)
    own_down = lax.dynamic_slice_in_dim(down_weight[0], plan.c * plan.units, plan.units, 0)
    cuts = by_layer(own_cut, swap_sections(own_cut))
    outs = by_layer(own_out, swap_sections(own_out))
    downs = by_layer(own_down, swap_sections(own_down))
    weights = [(cuts[s], outs[s], downs[s]) for s in range(2)]

    x = pick(inputs, section, 0)
    kept = []
    results = []
    for s in range(2):
        x, keep = forward_layer(plan, x, weights[s], gains[s], positions, part_positions, tables)
        kept.append(keep)
        results.append(x)
    grad = pick(cotangent, section, 0)
    input_grads = [None, None]
    weight_grads = [None, None]
    gain_grads = [None, None]
    for s in (1, 0):
        start_grad, weight_grads[s], gain_grads[s] = backward_layer(
            plan, grad, weights[s], gains[s], kept[s], positions, part_positions, tables, part_tables
        )
        input_grads[s] = start_grad
        grad = start_grad.astype(BF)

    def mine_and_theirs(first, second):
        return jnp.where(section == 0, first, second), jnp.where(section == 0, second, first)

    def by_batch(first, second):
        own, away = mine_and_theirs(first, second)
        return jnp.stack(by_layer(own, swap_sections(away)))

    section_outputs = by_batch(*results)
    section_input_grads = by_batch(*input_grads)

    def collected(index):
        own, away = mine_and_theirs(weight_grads[0][index], weight_grads[1][index])
        return (own.astype(F32) + swap_sections(away).astype(F32)).astype(BF)

    cut_grad = collected(0)
    cut_grad = lax.all_to_all(cut_grad.reshape(F, depth, -1), "fsdp", 0, 0)
    cut_grad = lax.all_gather(cut_grad, "ctx", axis=0, tiled=False)
    out_grad = lax.all_gather(collected(1), "ctx", axis=0, tiled=False)
    down_grad = lax.all_gather(collected(2), "ctx", axis=0, tiled=True).astype(F32)

    def heads_of(columns, count):
        folded = columns.astype(F32).reshape(count, C // count, F, depth, columns.shape[-1]).sum(axis=1)
        return jnp.transpose(folded, (2, 1, 0, 3))

    q_grad = join_halves(heads_of(cut_grad[..., :LANES], plan.heads_f)).reshape(depth, -1)
    k_grad = join_halves(heads_of(cut_grad[..., LANES : 2 * LANES], plan.groups_f)).reshape(depth, -1)
    v_grad = heads_of(cut_grad[..., 2 * LANES : 3 * LANES], plan.groups_f)[..., :HEAD].reshape(depth, -1)
    mix_grad = jnp.concatenate([q_grad, k_grad, v_grad], axis=1)
    both = jnp.transpose(cut_grad[..., 3 * LANES :], (2, 1, 0, 3)).astype(F32)
    gate_up_grad = jnp.concatenate(
        [both[..., : plan.units].reshape(depth, -1), both[..., plan.units :].reshape(depth, -1)], axis=1
    )
    out_grad = out_grad.astype(F32).reshape(plan.heads_f, plan.share, HEAD, width).sum(axis=1).reshape(-1, width)

    gain_sum = jnp.stack([jnp.stack(gain_grads[0]), jnp.stack(gain_grads[1])])
    gain_sum = lax.psum(gain_sum, ("section", "ctx", "fsdp"))
    gain_sum = lax.dynamic_slice_in_dim(pick(gain_sum, section, 0), plan.f * depth, depth, 1)
    return (
        section_outputs[None],
        section_input_grads[None],
        gain_sum[0][None],
        mix_grad[None],
        out_grad[None],
        gain_sum[1][None],
        gate_up_grad[None],
        down_grad[None],
    )


def solution(mesh):
    placed = (
        P(None, ("ctx", "fsdp"), None),
        P(None, ("ctx", "fsdp"), None),
        P("section", "fsdp"),
        P("section", "fsdp", None),
        P("section", "fsdp", None),
        P("section", "fsdp"),
        P("section", "fsdp", None),
        P("section", "fsdp", None),
        P(),
    )
    return jax.shard_map(
        on_device,
        mesh=mesh,
        in_specs=placed,
        out_specs=(
            P("section", None, ("ctx", "fsdp"), None),
            P("section", None, ("ctx", "fsdp"), None),
            P("section", "fsdp"),
            P("section", "fsdp", None),
            P("section", "fsdp", None),
            P("section", "fsdp"),
            P("section", "fsdp", None),
            P("section", "fsdp", None),
        ),
        check_vma=False,
    )
```

```python
import functools

import jax
import jax.numpy as jnp
from jax import lax
from jax.experimental import pallas as pl
from jax.experimental.pallas import tpu as pltpu
from jax.sharding import PartitionSpec as P

KV_HEADS = 8
HEAD = 96
LANES = 128
SPAN = 64
norm_eps = 1e-05
rope_base = 100000.0
masked_value = -1e30
BF = jnp.bfloat16
F32 = jnp.float32

MESH = pl.DeviceIdType.MESH


def greet():
    c = lax.axis_index("ctx")
    f = lax.axis_index("fsdp")
    barrier = pltpu.get_barrier_semaphore()
    inner = jnp.logical_and(c > 0, c < 3)
    for peer in (f + 2 - 4 * (f // 2), f + 1 - 2 * lax.rem(f, 2)):
        pl.semaphore_signal(barrier, inc=1, device_id={"fsdp": peer}, device_id_type=MESH)

    @pl.when(c < 3)
    def _():
        pl.semaphore_signal(barrier, inc=1, device_id={"ctx": c + 1}, device_id_type=MESH)

    @pl.when(c > 0)
    def _():
        pl.semaphore_signal(barrier, inc=1, device_id={"ctx": c - 1}, device_id_type=MESH)

    @pl.when(inner)
    def _():
        pl.semaphore_wait(barrier, 4)

    @pl.when(jnp.logical_not(inner))
    def _():
        pl.semaphore_wait(barrier, 3)


def near_order(c):
    low = c < 2
    return [c, c + 1 - 2 * lax.rem(c, 2), jnp.where(low, 2, 1), jnp.where(low, 3, 0)]


def gather_rows(whole, rows, send, recv, ready=None):
    c = lax.axis_index("ctx")
    f = lax.axis_index("fsdp")
    across = f + 2 - 4 * (f // 2)
    twin = f + 1 - 2 * lax.rem(f, 2)
    cross = across + 1 - 2 * lax.rem(f, 2)
    inner = jnp.logical_and(c > 0, c < 3)
    outer = jnp.logical_not(inner)
    order = near_order(c)
    pair = order[1]
    half = rows // 2
    sent = []

    def at(cc, ff, h):
        return whole.at[pl.ds(pl.multiple_of((cc * 4 + ff) * rows + h * half, half), half)]

    def copy(src, slot, arrival, peer):
        return pltpu.make_async_remote_copy(
            src, src, send.at[slot], recv.at[arrival], device_id=peer, device_id_type=MESH
        )

    def go(src, slot, arrival, peer, when=None):
        one = copy(src, slot, arrival, peer)
        if when is None:
            one.start()
        else:
            pl.when(when)(one.start)
        sent.append((one, when))

    def arrived(ref, arrival):
        copy(ref, 0, arrival, {"fsdp": twin}).wait_recv()

    up_to = {"ctx": jnp.minimum(c + 1, 3)}
    down_to = {"ctx": jnp.maximum(c - 1, 0)}
    for h in range(2):
        go(at(c, f, h), h, 2 * c + h, up_to, c < 3)
        go(at(c, f, h), 2 + h, 2 * c + h, down_to, c > 0)
        go(at(c, f, h), 4 + h, 8 + 2 * c + h, {"fsdp": across})
    for h in range(2):
        go(at(c, f, h), 12 + h, 16 + 2 * c + h, {"fsdp": twin})

    def along(step, h):
        d = order[step]
        block = at(d, f, h)
        arrived(block, 2 * d + h)
        go(block, 28 + 2 * step + h, 2 * d + h, {"ctx": jnp.where(d < c, jnp.minimum(c + 1, 3), jnp.maximum(c - 1, 0))}, inner)
        if (step, h) != (1, 0):
            go(block, 4 + 2 * step + h, 8 + 2 * d + h, {"fsdp": across})
        go(block, 12 + 2 * step + h, 16 + 2 * d + h, {"fsdp": twin})

    def over(step, h):
        d = order[step]
        block = at(d, across, h)
        arrived(block, 32 if (step, h) == (1, 0) else 8 + 2 * d + h)
        go(block, 20 + 2 * step + h, 24 + 2 * d + h, {"fsdp": twin})

    def complete(step):
        d = order[step]
        for h in range(2):
            arrived(at(d, twin, h), 16 + 2 * d + h)
            arrived(at(d, cross, h), 24 + 2 * d + h)
        if ready is not None:
            ready(d)

    along(1, 0)
    over(0, 0)
    go(at(c, across, 0), 36, 32, {"ctx": pair}, outer)
    along(1, 1)
    over(0, 1)
    along(2, 0)
    along(2, 1)
    complete(0)
    over(1, 1)
    along(3, 0)
    over(2, 0)
    along(3, 1)
    go(at(c, across, 0), 37, 32, {"ctx": pair}, inner)
    over(2, 1)
    complete(2)
    over(3, 0)
    over(1, 0)
    complete(1)
    over(3, 1)
    complete(3)
    for one, when in sent:
        if when is None:
            one.wait_send()
        else:
            pl.when(when)(one.wait_send)


GATHER_SENDS = 38
GATHER_RECVS = 33


def scatter_sum(part, total, land, send, recv, produce=None, meanwhile=None):
    c = lax.axis_index("ctx")
    f = lax.axis_index("fsdp")
    across = f + 2 - 4 * (f // 2)
    twin = f + 1 - 2 * lax.rem(f, 2)
    cross = across + 1 - 2 * lax.rem(f, 2)
    inner = jnp.logical_and(c > 0, c < 3)
    rows = total.shape[0]
    half = rows // 2
    order = near_order(c)[::-1]
    pair = order[2]
    sent = []

    def rows_at(cc, ff, h=None):
        start = (cc * 4 + ff) * rows
        if h is None:
            return pl.ds(pl.multiple_of(start, rows), rows)
        return pl.ds(pl.multiple_of(start + h * half, half), half)

    def copy(src, dst, slot, arrival, peer):
        return pltpu.make_async_remote_copy(
            src, dst, send.at[slot], recv.at[arrival], device_id=peer, device_id_type=MESH
        )

    def go(src, dst, slot, arrival, peer):
        one = copy(src, dst, slot, arrival, peer)
        one.start()
        sent.append(one)

    def piece(slot, h):
        return land.at[slot, pl.ds(h * half, half)]

    def landed(ref, arrival):
        copy(ref, ref, 0, arrival, {"fsdp": twin}).wait_recv()
        return ref[...].astype(F32)

    def begin(step):
        d = order[step]
        if produce is not None:
            produce(d)
        go(part.at[rows_at(d, cross)], land.at[step], step, step, {"fsdp": twin})
        go(part.at[rows_at(d, twin)], land.at[4 + step], 4 + step, 4 + step, {"fsdp": twin})

    def over(step, h):
        d = order[step]
        mine = rows_at(d, across, h)
        if h == 0:
            copy(land.at[step], land.at[step], 0, step, {"fsdp": twin}).wait_recv()
        value = part[mine, :].astype(F32) + land[step, h * half : (h + 1) * half, :].astype(F32)
        if (step, h) == (3, 0):
            value = value + landed(piece(17, 0), 26)
        part[mine, :] = value.astype(BF)
        if (step, h) == (2, 0):
            go(part.at[mine], piece(17, 0), 16, 26, {"ctx": pair})
        else:
            go(part.at[mine], piece(8 + step, h), 8 + 2 * step + h, 8 + 2 * step + h, {"fsdp": across})

    def onward(step, h):
        d = order[step]
        mine = rows_at(d, f, h)
        if h == 0:
            copy(land.at[4 + step], land.at[4 + step], 0, 4 + step, {"fsdp": twin}).wait_recv()
        value = part[mine, :].astype(F32) + land[4 + step, h * half : (h + 1) * half, :].astype(F32)
        if (step, h) != (2, 0):
            value = value + landed(piece(8 + step, h), 8 + 2 * step + h)
        if step == 3:
            total[h * half : (h + 1) * half, :] = value
            return
        part[mine, :] = value.astype(BF)

        @pl.when(inner)
        def _():
            part[mine, :] = (part[mine, :].astype(F32) + landed(piece(12 + d, h), 16 + 2 * d + h)).astype(BF)

        target = jnp.where(d > c, c + 1, c - 1)
        here = jnp.logical_and(d < c, d == c - 1)
        go(part.at[mine], piece(jnp.where(here, 16, 12 + d), h), 17 + 2 * step + h,
           jnp.where(here, 24, 16 + 2 * d) + h, {"ctx": target})

    begin(0)
    over(0, 0)
    over(0, 1)
    begin(1)
    begin(2)
    over(2, 0)
    over(1, 0)
    onward(0, 0)
    over(1, 1)
    onward(0, 1)
    begin(3)
    over(2, 1)
    onward(1, 0)
    over(3, 0)
    onward(1, 1)
    over(3, 1)
    onward(2, 0)
    onward(2, 1)
    if meanwhile is not None:
        meanwhile()
    for h in range(2):
        onward(3, h)

        @pl.when(c > 0)
        def _():
            total[h * half : (h + 1) * half, :] += landed(piece(12 + c, h), 16 + 2 * c + h)

        @pl.when(c < 3)
        def _():
            total[h * half : (h + 1) * half, :] += landed(piece(16, h), 24 + h)

    for one in sent:
        one.wait_send()


SCATTER_SENDS = 23
SCATTER_RECVS = 27


def kernel_dot(left, right):
    return jnp.dot(left, right, preferred_element_type=F32)


def kernel_dot_nt(left, right):
    return lax.dot_general(left, right, (((1,), (1,)), ((), ())), preferred_element_type=F32)


def kernel_dot_tn(left, right):
    return lax.dot_general(left, right, (((0,), (0,)), ((), ())), preferred_element_type=F32)


def turn(values):
    return pltpu.roll(values, SPAN, axis=1)


def mean_square(values):
    return lax.rsqrt(jnp.mean(values * values, axis=-1, keepdims=True) + norm_eps)


class Loads:
    def __init__(self, sems):
        self.sems = sems
        self.copies = []

    def start(self, src, dst):
        one = pltpu.make_async_copy(src, dst, self.sems.at[len(self.copies)])
        one.start()
        self.copies.append(one)
        return one


def plane_rows(d, rows):
    return pl.ds(pl.multiple_of(d * 4 * rows, 4 * rows), 4 * rows)


def forward_kernel(layer, x_own, w_mix, w_gate, w_out, w_down, w_gains, cosine, sine, place_col, place_row,
                   normed_o, q_o, k_o, v_o, context_o, log_o, middle_o, normed_two_o, both_o, result_o,
                   x_v, normed_v, q_v, k_v, v_v, context_v, log_v, middle_v, two_v, both_v, hidden_v, result_v,
                   mix_v, gate_v, out_v, down_v, gains_v, part_v, land_a, land_b, total_v, local, save,
                   send_a, recv_a, send_b, recv_b, send_c, recv_c, send_d, recv_d):
    c = lax.axis_index("ctx")
    f = lax.axis_index("fsdp")
    rows = x_own.shape[0]
    units = down_v.shape[0]
    own_rows = pl.ds(pl.multiple_of((c * 4 + f) * rows, rows), rows)
    loads = Loads(local)
    saves = Loads(save)
    load_x = loads.start(x_own, x_v.at[own_rows])
    load_gains = loads.start(w_gains.at[layer], gains_v)
    load_mix = loads.start(w_mix.at[layer], mix_v)
    out_v[...] = jnp.zeros_like(out_v)
    greet()
    load_x.wait()
    load_gains.wait()
    load_mix.wait()
    load_out = loads.start(w_out.at[layer], out_v.at[pl.ds(0, HEAD)])
    load_gate = loads.start(w_gate.at[layer], gate_v)
    load_down = loads.start(w_down.at[layer], down_v)

    def project(d):
        here = plane_rows(d, rows)
        x = x_v[here, :].astype(F32)
        normed = (x * mean_square(x) * gains_v[0:1, :].astype(F32)).astype(BF)
        normed_v[here, :] = normed
        mixed = kernel_dot(normed, mix_v[...])
        cos = cosine[here, :]
        sin = sine[here, :]
        q = mixed[:, :LANES]
        k = mixed[:, LANES : 2 * LANES]
        q_v[here, :] = (q * cos + turn(q) * sin).astype(BF)
        k_v[here, :] = (k * cos + turn(k) * sin).astype(BF)
        v_v[here, :] = mixed[:, 2 * LANES :].astype(BF)

    gather_rows(x_v, rows, send_a, recv_a, project)
    for src, dst in ((normed_v, normed_o), (q_v, q_o), (k_v, k_o), (v_v, v_o)):
        saves.start(src, dst)
    load_out.wait()
    scale = HEAD ** (-0.5)

    def attention(d):
        here = plane_rows(d, rows)
        scores = kernel_dot_nt(q_v[here, :], k_v[...]) * scale
        allowed = place_row[...] <= place_col[here, :]
        scores = jnp.where(allowed, scores, masked_value)
        top = jnp.max(scores, axis=-1, keepdims=True)
        weights = jnp.exp(scores - top)
        amount = jnp.sum(weights, axis=-1, keepdims=True)
        context = (kernel_dot(weights.astype(BF), v_v[...]) / amount).astype(BF)
        context_v[here, :] = context
        log_v[here, :] = jnp.broadcast_to(top + jnp.log(amount), (4 * rows, LANES))
        part_v[here, :] = kernel_dot(context, out_v[...]).astype(BF)

    scatter_sum(part_v, total_v, land_a, send_b, recv_b, attention)
    saves.start(context_v, context_o)
    saves.start(log_v, log_o)
    middle = x_v[own_rows, :].astype(F32) + total_v[...]
    middle_v[...] = middle
    saves.start(middle_v, middle_o)
    two_v[own_rows, :] = (middle * mean_square(middle) * gains_v[1:2, :].astype(F32)).astype(BF)
    load_gate.wait()

    def feed(d):
        here = plane_rows(d, rows)
        both = kernel_dot(two_v[here, :], gate_v[...])
        both_v[here, :] = both
        gate = both[:, :units]
        hidden_v[here, :] = (gate * jax.nn.sigmoid(gate) * both[:, units:]).astype(BF)

    gather_rows(two_v, rows, send_c, recv_c, feed)
    saves.start(two_v, normed_two_o)
    saves.start(both_v, both_o)
    load_down.wait()

    def lower(d):
        here = plane_rows(d, rows)
        part_v[here, :] = kernel_dot(hidden_v[here, :], down_v[...]).astype(BF)

    scatter_sum(part_v, total_v, land_b, send_d, recv_d, lower)
    result_v[...] = (middle_v[...] + total_v[...]).astype(BF)
    saves.start(result_v, result_o)
    for one in saves.copies:
        one.wait()


def backward_kernel(layer, grad_own, w_mix, w_gate, w_out, w_down, w_gains, cosine, sine, place_col, place_row,
                    x_own, normed, q, k, v, context, log, middle, normed_two, both,
                    start_o, low_o, mix_grad_o, gate_grad_o, out_grad_o, down_grad_o, gain_grad_o,
                    grad_v, x_v, normed_v, q_v, k_v, v_v, context_v, log_v, middle_v, two_v, both_v, both_grad_v, hidden_v,
                    low_v, mixed_v, key_grad_v, value_grad_v, start_v, start_low_v,
                    mix_grad_v, gate_grad_v, out_grad_v, down_grad_v, gain_grad_v,
                    mix_v, gate_v, out_v, down_v, gains_v, part_v, land_a, land_b, total_v, local, save,
                    send_a, recv_a, send_b, recv_b, send_c, recv_c, send_d, recv_d):
    c = lax.axis_index("ctx")
    f = lax.axis_index("fsdp")
    rows = grad_own.shape[0]
    length, width = grad_v.shape
    units = down_v.shape[0]
    own_rows = pl.ds(pl.multiple_of((c * 4 + f) * rows, rows), rows)
    loads = Loads(local)
    saves = Loads(save)
    load_grad = loads.start(grad_own, grad_v.at[own_rows])
    load_down = loads.start(w_down.at[layer], down_v)
    load_both = loads.start(both, both_v)
    load_gate = loads.start(w_gate.at[layer], gate_v)
    out_v[...] = jnp.zeros_like(out_v)
    key_grad_v[...] = jnp.zeros_like(key_grad_v)
    value_grad_v[...] = jnp.zeros_like(value_grad_v)
    greet()
    load_grad.wait()
    later = [
        loads.start(src, dst)
        for src, dst in (
            (normed_two, two_v), (middle, middle_v), (w_gains.at[layer], gains_v),
            (w_out.at[layer], out_v.at[pl.ds(0, HEAD)]), (q, q_v), (k, k_v), (v, v_v),
            (context, context_v), (log, log_v), (w_mix.at[layer], mix_v), (normed, normed_v), (x_own, x_v),
        )
    ]
    load_down.wait()
    load_both.wait()

    def feed(d):
        here = plane_rows(d, rows)
        hidden_grad = kernel_dot_nt(grad_v[here, :], down_v[...])
        gate = both_v[here, :units]
        up = both_v[here, units:]
        sig = jax.nn.sigmoid(gate)
        silu = gate * sig
        hidden_v[here, :] = (silu * up).astype(BF)
        both_grad_v[here, :units] = (hidden_grad * up * sig * (1.0 + gate * (1.0 - sig))).astype(BF)
        both_grad_v[here, units:] = (hidden_grad * silu).astype(BF)

    gather_rows(grad_v, rows, send_a, recv_a, feed)
    load_gate.wait()

    def spread(d):
        here = plane_rows(d, rows)
        part_v[here, :] = kernel_dot_nt(both_grad_v[here, :], gate_v[...]).astype(BF)

    def feed_weights():
        later[0].wait()
        down_grad_v[...] = kernel_dot_tn(hidden_v[...], grad_v[...]).astype(BF)
        for part in range(2):
            gate_grad_v[part] = kernel_dot_tn(
                two_v[...], both_grad_v[:, part * units : (part + 1) * units]
            ).astype(BF)
        saves.start(down_grad_v, down_grad_o)
        saves.start(gate_grad_v, gate_grad_o)

    scatter_sum(part_v, total_v, land_a, send_b, recv_b, spread, feed_weights)
    for one in later[1:]:
        one.wait()

    def norm_grads(error, value, gain, row):
        factor = mean_square(value)
        shaped = error * gain
        common = jnp.mean(shaped * value, axis=-1, keepdims=True)
        gain_grad_v[row : row + 1, :] = jnp.sum(error * value * factor, axis=0, keepdims=True)
        return factor * shaped - value * (factor * factor * factor) * common

    gain_grad_v[...] = jnp.zeros_like(gain_grad_v)
    middle_grad = norm_grads(total_v[...], middle_v[...], gains_v[1:2, :].astype(F32), 1)
    middle_grad = middle_grad + grad_v[own_rows, :].astype(F32)
    middle_v[...] = middle_grad
    low_v[own_rows, :] = middle_grad.astype(BF)
    scale = HEAD ** (-0.5)

    def attention(d):
        here = plane_rows(d, rows)
        context_grad = kernel_dot_nt(low_v[here, :], out_v[...])
        common = jnp.sum(context_grad * context_v[here, :].astype(F32), axis=-1, keepdims=True)
        context_grad = context_grad.astype(BF)
        queries = q_v[here, :]
        scores = kernel_dot_nt(queries, k_v[...]) * scale
        allowed = place_row[...] <= place_col[here, :]
        weights = jnp.exp(jnp.where(allowed, scores, masked_value) - log_v[here, 0:1])
        weight_grad = kernel_dot_nt(context_grad, v_v[...])
        score_grad = (weights * (weight_grad - common)).astype(BF)
        value_grad_v[...] += kernel_dot_tn(weights.astype(BF), context_grad)
        key_grad_v[...] += kernel_dot_tn(score_grad, queries)
        query_grad = kernel_dot(score_grad, k_v[...]) * scale
        mixed_v[here, :LANES] = (query_grad * cosine[here, :] - turn(query_grad) * sine[here, :]).astype(BF)

    gather_rows(low_v, rows, send_c, recv_c, attention)
    key_grad = key_grad_v[...] * scale
    mixed_v[:, LANES : 2 * LANES] = (key_grad * cosine[...] - turn(key_grad) * sine[...]).astype(BF)
    mixed_v[:, 2 * LANES :] = value_grad_v[...].astype(BF)

    def spread_two(d):
        here = plane_rows(d, rows)
        part_v[here, :] = kernel_dot_nt(mixed_v[here, :], mix_v[...]).astype(BF)

    def mix_weights():
        out_grad_v[...] = kernel_dot_tn(context_v[...], low_v[...])[:HEAD].astype(BF)
        for part in range(3):
            mix_grad_v[part] = kernel_dot_tn(
                normed_v[...], mixed_v[:, part * LANES : (part + 1) * LANES]
            ).astype(BF)
        saves.start(out_grad_v, out_grad_o)
        saves.start(mix_grad_v, mix_grad_o)

    scatter_sum(part_v, total_v, land_b, send_d, recv_d, spread_two, mix_weights)
    start_grad = norm_grads(total_v[...], x_v[...].astype(F32), gains_v[0:1, :].astype(F32), 0) + middle_v[...]
    start_v[...] = start_grad
    start_low_v[...] = start_grad.astype(BF)
    saves.start(start_v, start_o)
    saves.start(start_low_v, low_o)
    saves.start(gain_grad_v, gain_grad_o)
    for one in saves.copies:
        one.wait()


def link_sems():
    dma = pltpu.SemaphoreType.DMA
    return [dma((GATHER_SENDS,)), dma((GATHER_RECVS,)), dma((SCATTER_SENDS,)), dma((SCATTER_RECVS,))] * 2


def forward_call(layer, x_own, shared, tables, places):
    rows, width = x_own.shape
    length = 16 * rows
    units = shared[3].shape[1]
    anywhere = pl.BlockSpec(memory_space=pl.ANY)
    inside = pl.BlockSpec(memory_space=pltpu.VMEM)

    def low(*shape):
        return (shape, BF)

    def full(*shape):
        return (shape, F32)

    kept = [low(length, width)] + [low(length, LANES)] * 4 + [
        full(length, LANES), full(rows, width), low(length, width), full(length, 2 * units), low(rows, width)]
    inner = [low(length, width), low(length, width)] + [low(length, LANES)] * 4 + [
        full(length, LANES), full(rows, width), low(length, width), full(length, 2 * units), low(length, units),
        low(rows, width), low(width, 3 * LANES), low(width, 2 * units), low(LANES, width), low(units, width),
        low(16, width), low(length, width), low(18, rows, width), low(18, rows, width), full(rows, width)]
    return pl.pallas_call(
        functools.partial(forward_kernel, layer),
        out_shape=[jax.ShapeDtypeStruct(*one) for one in kept],
        in_specs=[anywhere] * 6 + [inside] * 4,
        out_specs=[anywhere] * len(kept),
        scratch_shapes=[pltpu.VMEM(*one) for one in inner]
        + [pltpu.SemaphoreType.DMA((6,)), pltpu.SemaphoreType.DMA((10,))] + link_sems(),
        compiler_params=pltpu.CompilerParams(
            collective_id=4 + layer, has_side_effects=True, vmem_limit_bytes=60 << 20),
    )(x_own, *shared, *tables, *places)


def backward_call(layer, grad_own, shared, tables, places, x_own, kept):
    rows, width = grad_own.shape
    length = 16 * rows
    units = shared[3].shape[1]
    anywhere = pl.BlockSpec(memory_space=pl.ANY)
    inside = pl.BlockSpec(memory_space=pltpu.VMEM)

    def low(*shape):
        return (shape, BF)

    def full(*shape):
        return (shape, F32)

    grads = [low(3, width, LANES), low(2, width, units), low(HEAD, width), low(units, width), full(2, width)]
    outs = [full(rows, width), low(rows, width)] + grads
    inner = [low(length, width), low(rows, width), low(length, width)] + [low(length, LANES)] * 4 + [
        full(length, LANES), full(rows, width), low(length, width), full(length, 2 * units), low(length, 2 * units),
        low(length, units), low(length, width), low(length, 3 * LANES), full(length, LANES), full(length, LANES),
        full(rows, width), low(rows, width)] + grads + [
        low(width, 3 * LANES), low(width, 2 * units), low(LANES, width), low(units, width),
        low(16, width), low(length, width), low(18, rows, width), low(18, rows, width), full(rows, width)]
    return pl.pallas_call(
        functools.partial(backward_kernel, layer),
        out_shape=[jax.ShapeDtypeStruct(*one) for one in outs],
        in_specs=[anywhere] * 6 + [inside] * 4 + [anywhere] * 10,
        out_specs=[anywhere] * len(outs),
        scratch_shapes=[pltpu.VMEM(*one) for one in inner]
        + [pltpu.SemaphoreType.DMA((16,)), pltpu.SemaphoreType.DMA((7,))] + link_sems(),
        compiler_params=pltpu.CompilerParams(
            collective_id=6 + layer, has_side_effects=True, vmem_limit_bytes=60 << 20),
    )(grad_own, *shared, *tables, *places, x_own, *kept)


def greet_all(peers):
    barrier = pltpu.get_barrier_semaphore()
    for peer in peers:
        pl.semaphore_signal(barrier, inc=1, device_id=peer, device_id_type=MESH)
    pl.semaphore_wait(barrier, len(peers))


def head_choice(value_part):
    source = lax.broadcasted_iota(jnp.int32, (4 * HEAD, 4 * LANES), 0)
    lane = lax.broadcasted_iota(jnp.int32, (4 * HEAD, 4 * LANES), 1)
    head = lane // LANES
    inside = lane - head * LANES
    if value_part:
        wanted = jnp.where(inside < HEAD, head * HEAD + inside, -1)
    else:
        half = inside // SPAN
        place = inside - half * SPAN
        wanted = jnp.where(place < HEAD // 2, head * HEAD + half * (HEAD // 2) + place, -1)
    return jnp.where(source == wanted, 1.0, 0.0).astype(BF)


def share_kernel(mix, out, gate_up, down, gains, w_mix, w_gate, w_out, w_down, w_gains,
                 mix_v, heads_v, local, send, recv):
    s = lax.axis_index("section")
    c = lax.axis_index("ctx")
    f = lax.axis_index("fsdp")
    depth = mix.shape[1]
    units = w_down.shape[1]
    hidden_units = gate_up.shape[2] // 2
    other = 1 - s
    peers = [lax.rem(f + k, 4) for k in range(1, 4)]
    greet_all([{"fsdp": peer} for peer in peers] + [{"section": other}]
              + [{"section": other, "fsdp": peer} for peer in peers])
    load = pltpu.make_async_copy(mix.at[0], mix_v, local.at[0])
    load.start()
    rows = pl.ds(pl.multiple_of(f * depth, depth), depth)
    pending = []

    def copy(src, dst, slot, arrival, peer):
        return pltpu.make_async_remote_copy(
            src, dst, send.at[slot], recv.at[arrival], device_id=peer, device_id_type=MESH
        )

    def go(src, dst, slot, arrival, peer):
        one = copy(src, dst, slot, arrival, peer)
        one.start()
        pending.append(one)

    mine = w_gains.at[s, :, pl.ds(pl.multiple_of(f * depth, depth), depth)]
    for k, peer in enumerate(peers):
        go(gains, mine, 20 + k, 16 + 4 * s + f, {"fsdp": peer})
        go(gains, mine, 23 + k, 16 + 4 * s + f, {"section": other, "fsdp": peer})
    go(gains, mine, 26, 16 + 4 * s + f, {"section": other})
    keep_gains = pltpu.make_async_copy(gains, mine, local.at[1])
    keep_gains.start()

    load.wait()
    for g in range(8):
        choice = head_choice(g >= 6)
        heads_v[:, g * 512 : (g + 1) * 512] = jnp.dot(
            mix_v[:, g * 384 : (g + 1) * 384], choice, preferred_element_type=F32
        ).astype(BF)

    def lanes(peer, part):
        head = peer * 4 + c
        start = head * LANES if part == 0 else (16 + 8 * (part - 1) + head // 2) * LANES
        return heads_v.at[:, pl.ds(pl.multiple_of(start, LANES), LANES)]

    def put(peer, part):
        return w_mix.at[s, rows, pl.ds(part * LANES, LANES)]

    for k, peer in enumerate(peers):
        for part in range(3):
            copy(lanes(peer, part), put(peer, part), k, f, {"fsdp": peer}).start()
    own_mix = [pltpu.make_async_copy(lanes(f, part), put(f, part), local.at[2 + part]) for part in range(3)]
    for one in own_mix:
        one.start()

    def gate_piece(peer, part):
        start = pl.multiple_of(part * hidden_units + (peer * 4 + c) * units, units)
        return gate_up.at[0, :, pl.ds(start, units)]

    def gate_put(part):
        return w_gate.at[s, rows, pl.ds(part * units, units)]

    for k, peer in enumerate(peers):
        for part in range(2):
            copy(gate_piece(peer, part), gate_put(part), 3 + k, 4 + f, {"fsdp": peer}).start()
    own_gate = [pltpu.make_async_copy(gate_piece(f, part), gate_put(part), local.at[5 + part]) for part in range(2)]
    for one in own_gate:
        one.start()
    out_rows = out.at[0, pl.ds(pl.multiple_of(c * HEAD, HEAD), HEAD)]
    down_rows = down.at[0, pl.ds(pl.multiple_of(c * units, units), units)]
    own_out = pltpu.make_async_copy(out_rows, w_out.at[s], local.at[7])
    own_out.start()
    own_down = pltpu.make_async_copy(down_rows, w_down.at[s], local.at[8])
    own_down.start()

    def slab(ref, origin):
        return ref.at[s, pl.ds(pl.multiple_of(origin * depth, depth), depth)]

    for one in own_mix:
        one.wait()
    go(slab(w_mix, f), slab(w_mix, f), 6, 8 + f, {"section": other})
    for k in range(3):
        origin = lax.rem(f + 3 - k, 4)
        copy(slab(w_mix, origin), slab(w_mix, origin), 0, origin, {"fsdp": origin}).wait_recv()
        go(slab(w_mix, origin), slab(w_mix, origin), 7 + k, 8 + origin, {"section": other})
    go(out_rows, w_out.at[s], 10, 24, {"section": other})
    for one in own_gate:
        one.wait()
    go(slab(w_gate, f), slab(w_gate, f), 11, 12 + f, {"section": other})
    for k in range(3):
        origin = lax.rem(f + 3 - k, 4)
        copy(slab(w_gate, origin), slab(w_gate, origin), 0, 4 + origin, {"fsdp": origin}).wait_recv()
        go(slab(w_gate, origin), slab(w_gate, origin), 12 + k, 12 + origin, {"section": other})
    go(down_rows, w_down.at[s], 15, 25, {"section": other})

    def from_there(ref, arrival):
        copy(ref, ref, 0, arrival, {"section": other}).wait_recv()

    for origin in range(4):
        theirs = pl.ds(origin * depth, depth)
        from_there(w_mix.at[other, theirs], 8 + origin)
        from_there(w_gate.at[other, theirs], 12 + origin)
    from_there(w_out.at[other], 24)
    from_there(w_down.at[other], 25)
    for origin in range(4):
        from_there(w_gains.at[other, :, pl.ds(origin * depth, depth)], 16 + 4 * other + origin)
    for k in range(3):
        origin = lax.rem(f + 3 - k, 4)
        from_there(w_gains.at[s, :, pl.ds(pl.multiple_of(origin * depth, depth), depth)], 16 + 4 * s + origin)
    keep_gains.wait()
    own_out.wait()
    own_down.wait()
    for k, peer in enumerate(peers):
        copy(slab(w_mix, f), slab(w_mix, f), k, 0, {"fsdp": peer}).wait_send()
        copy(slab(w_gate, f), slab(w_gate, f), 3 + k, 0, {"fsdp": peer}).wait_send()
    for one in pending:
        one.wait_send()


def share_call(mix, out, gate_up, down, gains):
    depth = mix.shape[1]
    width = 4 * depth
    units = gate_up.shape[2] // 32
    anywhere = pl.BlockSpec(memory_space=pl.ANY)
    return pl.pallas_call(
        share_kernel,
        out_shape=(
            jax.ShapeDtypeStruct((2, width, 3 * LANES), BF),
            jax.ShapeDtypeStruct((2, width, 2 * units), BF),
            jax.ShapeDtypeStruct((2, HEAD, width), BF),
            jax.ShapeDtypeStruct((2, units, width), BF),
            jax.ShapeDtypeStruct((2, 16, width), BF),
        ),
        in_specs=[anywhere] * 5,
        out_specs=(anywhere,) * 5,
        scratch_shapes=[
            pltpu.VMEM((depth, mix.shape[2]), BF),
            pltpu.VMEM((depth, 32 * LANES), BF),
            pltpu.SemaphoreType.DMA((9,)),
            pltpu.SemaphoreType.DMA((27,)),
            pltpu.SemaphoreType.DMA((26,)),
        ],
        compiler_params=pltpu.CompilerParams(collective_id=2, has_side_effects=True, vmem_limit_bytes=48 << 20),
    )(mix, out, gate_up, down, gains)


def return_kernel(mix_0, mix_1, gate_0, gate_1, out_0, out_1, down_0, down_1, gains,
                  mix_out, gate_out, out_out, down_out, gain_out,
                  mix_v, gate_v, out_v, down_v, mix_x, gate_x, out_x, down_x, gain_v, gain_x,
                  local, send, recv, line_send, line_recv):
    s = lax.axis_index("section")
    c = lax.axis_index("ctx")
    f = lax.axis_index("fsdp")
    other = 1 - s
    units = down_0.shape[0]
    depth = mix_out.shape[1]
    inner = jnp.logical_and(c > 0, c < 3)
    peers = [lax.rem(f + k, 4) for k in range(1, 4)]
    pair = c + 1 - 2 * lax.rem(c, 2)
    far = lax.rem(c + 2, 4)
    barrier = pltpu.get_barrier_semaphore()
    for peer in [{"fsdp": peer} for peer in peers] + [{"section": other}, {"ctx": pair}, {"ctx": far}]:
        pl.semaphore_signal(barrier, inc=1, device_id=peer, device_id_type=MESH)

    @pl.when(inner)
    def _():
        pl.semaphore_signal(barrier, inc=1, device_id={"ctx": 3 - c}, device_id_type=MESH)
        pl.semaphore_wait(barrier, 7)

    @pl.when(jnp.logical_not(inner))
    def _():
        pl.semaphore_wait(barrier, 6)

    def copy(src, dst, slot, arrival, peer):
        return pltpu.make_async_remote_copy(
            src, dst, send.at[slot], recv.at[arrival], device_id=peer, device_id_type=MESH
        )

    def rows_of(k):
        return pl.ds(k * depth, depth)

    def away(mix, gate, out, down):
        copy(down, down_x, 8, 8, {"section": other}).start()
        for k in range(4):
            copy(gate.at[:, rows_of(k)], gate_x.at[:, rows_of(k)], k, k, {"section": other}).start()
        copy(out, out_x, 9, 9, {"section": other}).start()
        for k in range(4):
            copy(mix.at[:, rows_of(k)], mix_x.at[:, rows_of(k)], 4 + k, 4 + k, {"section": other}).start()

    def home(mix, gate, out, down):
        for k, (src, dst) in enumerate(((down, down_v), (gate, gate_v), (out, out_v), (mix, mix_v))):
            pltpu.make_async_copy(src, dst, local.at[k]).start()

    @pl.when(s == 0)
    def _():
        away(mix_1, gate_1, out_1, down_1)
        home(mix_0, gate_0, out_0, down_0)

    @pl.when(s == 1)
    def _():
        away(mix_0, gate_0, out_0, down_0)
        home(mix_1, gate_1, out_1, down_1)

    def home_wait(k, dst):
        pltpu.make_async_copy(dst, dst, local.at[k]).wait()

    def arrived(ref, arrival):
        copy(ref, ref, 0, arrival, {"section": other}).wait_recv()

    def gate_at(cc, ff):
        return gate_out.at[:, :, pl.ds(pl.multiple_of((ff * 4 + cc) * units, units), units)]

    def mix_at(cc, ff):
        return mix_out.at[:, :, pl.ds(pl.multiple_of((ff * 4 + cc) * LANES, LANES), LANES)]

    def out_at(cc, ff):
        return out_out.at[pl.ds(pl.multiple_of(cc * HEAD, HEAD), HEAD)]

    def down_at(cc, ff):
        return down_out.at[pl.ds(pl.multiple_of(cc * units, units), units)]

    items = [(down_at, f)] + [(gate_at, lax.rem(f + k, 4)) for k in (0, 3, 2, 1)] + [(out_at, f)] + [
        (mix_at, lax.rem(f + k, 4)) for k in (0, 3, 2, 1)
    ]

    def line(place, origin, index, cc, slot, target):
        key = cc * 10 + index
        return pltpu.make_async_remote_copy(
            place(cc, origin), place(cc, origin), line_send.at[slot], line_recv.at[key],
            device_id={"ctx": target}, device_id_type=MESH,
        )

    above = jnp.minimum(c + 1, 3)
    below = jnp.maximum(c - 1, 0)

    def start_line(index):
        place, origin = items[index]
        pl.when(c < 3)(line(place, origin, index, c, index, above).start)
        pl.when(c > 0)(line(place, origin, index, c, 10 + index, below).start)

    def fold(mine, theirs, arrival):
        arrived(theirs, arrival)
        mine[...] = (mine[...].astype(F32) + theirs[...].astype(F32)).astype(BF)

    def keep(src, dst, k):
        one = pltpu.make_async_copy(src, dst, local.at[k])
        one.start()
        one.wait()

    home_wait(0, down_v)
    fold(down_v, down_x, 8)
    keep(down_v, down_at(c, f), 4)
    start_line(0)

    def to_owners(mine, theirs, place, arrival_x, arrival_y, slot):
        for k in (1, 2, 3, 0):
            owner = lax.rem(f + k, 4)
            rows = pl.ds(pl.multiple_of(owner * depth, depth), depth)
            fold(mine.at[:, rows], theirs.at[:, rows], arrival_x + owner)
            if k:
                copy(mine.at[:, rows], place(c, f), slot + k, arrival_y + f, {"fsdp": owner}).start()
            else:
                keep(mine.at[:, rows], place(c, f), 4)

    home_wait(1, gate_v)
    to_owners(gate_v, gate_x, gate_at, 0, 10, 10)
    start_line(1)
    home_wait(2, out_v)
    fold(out_v, out_x, 9)
    keep(out_v, out_at(c, f), 4)
    start_line(5)
    for k in range(3):
        origin = items[2 + k][1]
        arrived(gate_at(c, origin), 10 + origin)
        start_line(2 + k)
    home_wait(3, mix_v)
    to_owners(mix_v, mix_x, mix_at, 4, 14, 14)
    start_line(6)
    for k in range(3):
        origin = items[7 + k][1]
        arrived(mix_at(c, origin), 14 + origin)
        start_line(7 + k)

    gain_v[0] = gains[...]
    twin = f + 1 - 2 * lax.rem(f, 2)
    across = f + 2 - 4 * (f // 2)
    targets = [{"section": other}, {"fsdp": twin}, {"fsdp": across}, {"ctx": pair}, {"ctx": far}]
    gain_copies = []
    for k, target in enumerate(targets):
        one = copy(gain_v.at[k], gain_x.at[k], 18 + k, 18 + k, target)
        one.start()
        one.wait_recv()
        gain_copies.append(one)
        if k < 4:
            gain_v[k + 1] = gain_v[k] + gain_x[k]
        else:
            gain_out[...] = gain_v[k] + gain_x[k]

    order = near_order(c)
    forwards = []
    for step in range(1, 4):
        d = order[step]
        onward = jnp.where(d < c, above, below)
        for index, (place, origin) in enumerate(items):
            one = line(place, origin, index, d, 20 + (step - 1) * 10 + index, onward)
            one.wait_recv()
            pl.when(inner)(one.start)
            forwards.append(one)
    for index, (place, origin) in enumerate(items):
        pl.when(c < 3)(line(place, origin, index, c, index, above).wait_send)
        pl.when(c > 0)(line(place, origin, index, c, 10 + index, below).wait_send)
    for one in forwards:
        pl.when(inner)(one.wait_send)
    for one in gain_copies:
        one.wait_send()
    for k in range(4):
        copy(gate_x.at[:, rows_of(k)], gate_x.at[:, rows_of(k)], k, 0, {"section": other}).wait_send()
        copy(mix_x.at[:, rows_of(k)], mix_x.at[:, rows_of(k)], 4 + k, 0, {"section": other}).wait_send()
        if k:
            copy(gate_x.at[:, rows_of(k)], gate_x.at[:, rows_of(k)], 10 + k, 0, {"section": other}).wait_send()
            copy(mix_x.at[:, rows_of(k)], mix_x.at[:, rows_of(k)], 14 + k, 0, {"section": other}).wait_send()
    copy(down_x, down_x, 8, 0, {"section": other}).wait_send()
    copy(out_x, out_x, 9, 0, {"section": other}).wait_send()


def return_call(first, second, gains):
    mix, gate, out, down = first
    units, width = down.shape
    depth = width // 4
    anywhere = pl.BlockSpec(memory_space=pl.ANY)
    inside = pl.BlockSpec(memory_space=pltpu.VMEM)
    return pl.pallas_call(
        return_kernel,
        out_shape=(
            jax.ShapeDtypeStruct((3, depth, 16 * LANES), BF),
            jax.ShapeDtypeStruct((2, depth, 16 * units), BF),
            jax.ShapeDtypeStruct((4 * HEAD, width), BF),
            jax.ShapeDtypeStruct((4 * units, width), BF),
            jax.ShapeDtypeStruct(gains.shape, F32),
        ),
        in_specs=[anywhere] * 8 + [inside],
        out_specs=(anywhere,) * 4 + (inside,),
        scratch_shapes=[
            pltpu.VMEM(mix.shape, BF), pltpu.VMEM(gate.shape, BF), pltpu.VMEM(out.shape, BF), pltpu.VMEM(down.shape, BF),
            pltpu.VMEM(mix.shape, BF), pltpu.VMEM(gate.shape, BF), pltpu.VMEM(out.shape, BF), pltpu.VMEM(down.shape, BF),
            pltpu.VMEM((5,) + gains.shape, F32), pltpu.VMEM((5,) + gains.shape, F32),
            pltpu.SemaphoreType.DMA((5,)),
            pltpu.SemaphoreType.DMA((23,)),
            pltpu.SemaphoreType.DMA((23,)),
            pltpu.SemaphoreType.DMA((50,)),
            pltpu.SemaphoreType.DMA((40,)),
        ],
        compiler_params=pltpu.CompilerParams(collective_id=3, has_side_effects=True, vmem_limit_bytes=56 << 20),
    )(mix, second[0], gate, second[1], out, second[2], down, second[3], gains)


def on_line():
    return lax.axis_size("ctx") == 4 and lax.axis_size("fsdp") == 4


def gather(own):
    return lax.all_gather(own, ("ctx", "fsdp"), axis=0, tiled=True)


def scatter(part):
    return lax.psum_scatter(part, ("ctx", "fsdp"), scatter_dimension=0, tiled=True)


def spread_halves(columns):
    halves = columns.reshape(columns.shape[:-1] + (2, HEAD // 2))
    halves = jnp.pad(halves, [(0, 0)] * (halves.ndim - 1) + [(0, SPAN - HEAD // 2)])
    return halves.reshape(columns.shape[:-1] + (LANES,))


def join_halves(columns):
    halves = columns.reshape(columns.shape[:-1] + (2, SPAN))[..., : HEAD // 2]
    return halves.reshape(columns.shape[:-1] + (HEAD,))


def angle_tables(positions):
    frequency = rope_base ** (-(jnp.arange(HEAD // 2, dtype=F32) * 2.0 / HEAD))
    frequency = jnp.pad(frequency, (0, SPAN - HEAD // 2))
    angles = positions.astype(F32)[:, None] * frequency[None, :]
    cosine = jnp.cos(angles)
    sine = jnp.sin(angles)
    return jnp.concatenate([cosine, cosine], axis=1), jnp.concatenate([-sine, sine], axis=1)


def rotate(values, cosine, sine):
    return values * cosine + jnp.roll(values, SPAN, axis=1) * sine


def rotate_back(grads, cosine, sine):
    return grads * cosine - jnp.roll(grads, SPAN, axis=1) * sine


def norm_rows(values):
    return lax.rsqrt(jnp.mean(values * values, axis=-1, keepdims=True) + norm_eps)


def norm_back(grad_out, values, factor, gain):
    shaped = grad_out * gain
    common = jnp.mean(shaped * values, axis=-1, keepdims=True)
    grad_in = factor * shaped - values * (factor * factor * factor) * common
    return grad_in, jnp.sum(grad_out * values * factor, axis=0)


def dot(left, right):
    return jnp.dot(left, right, preferred_element_type=F32)


def dot_nt(left, right):
    return lax.dot_general(left, right, (((1,), (1,)), ((), ())), preferred_element_type=F32)


def dot_tn(left, right):
    return lax.dot_general(left, right, (((0,), (0,)), ((), ())), preferred_element_type=F32)


class Plan:
    def __init__(self, width, hidden_units):
        self.c = lax.axis_index("ctx")
        self.f = lax.axis_index("fsdp")
        self.C = lax.axis_size("ctx")
        self.F = lax.axis_size("fsdp")
        self.heads = width // HEAD
        self.ratio = self.heads // KV_HEADS
        self.heads_f = self.heads // self.F
        self.groups_f = KV_HEADS // self.F
        self.share = self.C // self.heads_f
        self.units = hidden_units // (self.F * self.C)
        self.local_head = self.c // self.share
        self.part = self.c % self.share


def pick(array, index, axis):
    return lax.dynamic_index_in_dim(array, index, axis, keepdims=False)


def pack_weights(plan, mix, gate_up):
    depth = mix.shape[0]
    width = plan.heads * HEAD
    kv_width = KV_HEADS * HEAD
    F = plan.F
    queries = pick(mix[:, :width].reshape(depth, F, plan.heads_f, HEAD), plan.local_head, 2)
    group = plan.local_head // plan.ratio
    keys = pick(mix[:, width : width + kv_width].reshape(depth, F, plan.groups_f, HEAD), group, 2)
    values = pick(mix[:, width + kv_width :].reshape(depth, F, plan.groups_f, HEAD), group, 2)
    values = jnp.pad(values, ((0, 0), (0, 0), (0, LANES - HEAD)))
    half = gate_up.shape[1] // 2
    gate = pick(gate_up[:, :half].reshape(depth, F, plan.C, plan.units), plan.c, 2)
    up = pick(gate_up[:, half:].reshape(depth, F, plan.C, plan.units), plan.c, 2)
    packed = jnp.concatenate([spread_halves(queries), spread_halves(keys), values, gate, up], axis=2)
    return jnp.swapaxes(packed, 0, 1)


def attend(plan, q_part, k, v, positions, part_positions):
    scores = dot_nt(q_part, k) * HEAD ** (-0.5)
    allowed = positions[None, :] <= part_positions[:, None]
    scores = jnp.where(allowed, scores, masked_value)
    top = jnp.max(scores, axis=-1, keepdims=True)
    weights = jnp.exp(scores - top)
    total = jnp.sum(weights, axis=-1, keepdims=True)
    context = dot((weights / total).astype(BF), v)
    return context.astype(BF), top + jnp.log(total)


def attend_back(q_part, k, v, context_grad, context, log_total, positions, part_positions):
    scale = HEAD ** (-0.5)
    common = jnp.sum(context_grad.astype(F32) * context.astype(F32), axis=-1, keepdims=True)
    allowed = positions[None, :] <= part_positions[:, None]
    scores = dot_nt(q_part, k) * scale
    weights = jnp.exp(jnp.where(allowed, scores, masked_value) - log_total)
    weight_grad = dot_nt(context_grad, v)
    score_grad = (weights * (weight_grad - common)).astype(BF)
    value_grad = dot_tn(weights.astype(BF), context_grad)
    key_grad = dot_tn(score_grad, q_part) * scale
    query_grad = dot(score_grad, k) * scale
    return query_grad, key_grad, value_grad


def forward_layer(plan, x_own, weights, gains, positions, part_positions, tables):
    mix_cut, gate_cut, out, down = weights
    cosine, sine = tables
    length = positions.shape[0]
    x_all = gather(x_own)
    x32 = x_all.astype(F32)
    factor = norm_rows(x32)
    normed = (x32 * factor * gains[0]).astype(BF)
    mixed = dot(normed, mix_cut)
    q = rotate(mixed[:, :LANES], cosine, sine).astype(BF)
    k = rotate(mixed[:, LANES : 2 * LANES], cosine, sine).astype(BF)
    v = mixed[:, 2 * LANES :].astype(BF)
    rows = length // plan.share
    start = plan.part * rows
    q_part = lax.dynamic_slice_in_dim(q, start, rows, 0)
    context, log_total = attend(plan, q_part, k, v, positions, part_positions)
    partial = dot(context[:, :HEAD], out).astype(BF)
    if plan.share > 1:
        partial = lax.dynamic_update_slice_in_dim(
            jnp.zeros((length, partial.shape[1]), BF), partial, start, 0
        )
    middle = x_own.astype(F32) + scatter(partial)
    factor_two = norm_rows(middle)
    normed_two = gather((middle * factor_two * gains[1]).astype(BF))
    both = dot(normed_two, gate_cut)
    hidden = (jax.nn.silu(both[:, : plan.units]) * both[:, plan.units :]).astype(BF)
    result = middle + scatter(dot(hidden, down).astype(BF))
    kept = (x_own, normed, q_part, k, v, context, log_total, middle, normed_two, both, hidden)
    return result.astype(BF), kept


def backward_layer(plan, grad_own, weights, gains, kept, positions, part_positions, tables, part_tables):
    mix_cut, gate_cut, out, down = weights
    x_own, normed, q_part, k, v, context, log_total, middle, normed_two, both, hidden = kept
    length = positions.shape[0]
    rows = length // plan.share
    start = plan.part * rows
    grad_all = gather(grad_own)
    hidden_grad = dot_nt(grad_all, down)
    gate = both[:, : plan.units]
    up = both[:, plan.units :]
    sig = jax.nn.sigmoid(gate)
    gate_grad = hidden_grad * up * sig * (1.0 + gate * (1.0 - sig))
    up_grad = hidden_grad * gate * sig
    both_grad = jnp.concatenate([gate_grad, up_grad], axis=1).astype(BF)
    normed_two_grad = scatter(dot_nt(both_grad, gate_cut).astype(BF))
    middle_grad, feed_gain_grad = norm_back(normed_two_grad, middle, norm_rows(middle), gains[1])
    middle_grad = middle_grad + grad_own.astype(F32)
    middle_low = gather(middle_grad.astype(BF))
    middle_part = lax.dynamic_slice_in_dim(middle_low, start, rows, 0)
    context_grad = jnp.pad(dot_nt(middle_part, out), ((0, 0), (0, LANES - HEAD))).astype(BF)
    query_grad, key_grad, value_grad = attend_back(
        q_part, k, v, context_grad, context, log_total, positions, part_positions
    )
    query_grad = rotate_back(query_grad, *part_tables).astype(BF)
    if plan.share > 1:
        query_grad = lax.dynamic_update_slice_in_dim(
            jnp.zeros((length, LANES), BF), query_grad, start, 0
        )
    key_grad = rotate_back(key_grad, *tables).astype(BF)
    mixed_grad = jnp.concatenate([query_grad, key_grad, value_grad.astype(BF)], axis=1)
    normed_grad = scatter(dot_nt(mixed_grad, mix_cut).astype(BF))
    x32 = x_own.astype(F32)
    start_grad, attention_gain_grad = norm_back(normed_grad, x32, norm_rows(x32), gains[0])
    start_grad = start_grad + middle_grad
    mix_grad = jnp.stack(
        [dot_tn(normed, part).astype(BF) for part in (query_grad, key_grad, value_grad.astype(BF))]
    )
    gate_cut_grad = jnp.stack(
        [dot_tn(normed_two, part.astype(BF)).astype(BF) for part in (gate_grad, up_grad)]
    )
    out_grad = dot_tn(context, middle_part).astype(BF)[:HEAD]
    down_grad = dot_tn(hidden, grad_all).astype(BF)
    return start_grad, (mix_grad, gate_cut_grad, out_grad, down_grad), jnp.stack([attention_gain_grad, feed_gain_grad])


def swap_sections(array):
    return lax.ppermute(array, "section", [(0, 1), (1, 0)])


def by_layer_of(section, own, other):
    first = section == 0
    return jnp.where(first, own, other), jnp.where(first, other, own)


def shared_weights(plan, section, attention_gain, query_key_value, output_weight, feed_gain, gate_up, down_weight):
    depth = query_key_value.shape[1]
    width = depth * plan.F
    gains = lax.all_gather(
        jnp.stack([attention_gain[0], feed_gain[0]]), ("section", "fsdp"), axis=0, tiled=False
    )
    gains = gains.reshape(2, plan.F, 2, depth)
    gains = jnp.swapaxes(gains, 1, 2).reshape(2, 2, width).astype(F32)
    packed = pack_weights(plan, query_key_value[0], gate_up[0])
    own_cut = lax.all_to_all(packed, "fsdp", 0, 0).reshape(width, -1)
    own_out = lax.dynamic_slice_in_dim(output_weight[0], plan.local_head * HEAD, HEAD, 0)
    own_down = lax.dynamic_slice_in_dim(down_weight[0], plan.c * plan.units, plan.units, 0)
    cuts = by_layer_of(section, own_cut, swap_sections(own_cut))
    outs = by_layer_of(section, own_out, swap_sections(own_out))
    downs = by_layer_of(section, own_down, swap_sections(own_down))
    weights = [(cuts[s][:, : 3 * LANES], cuts[s][:, 3 * LANES :], outs[s], downs[s]) for s in range(2)]
    return weights, gains


def returned_grads(plan, section, weight_grads, gain_grads, depth):
    C, F = plan.C, plan.F
    gain_sum = jnp.concatenate([gain_grads[0], gain_grads[1]])
    if on_line():
        mixes, both, out_grad, down_grad, gain_sum = return_call(
            weight_grads[0], weight_grads[1], jnp.pad(gain_sum, ((0, 4), (0, 0)))
        )
        slots = mixes.astype(F32).reshape(3, depth, 16, LANES)
        q_grad = join_halves(slots[0]).reshape(depth, -1)
        pairs = slots[1:].reshape(2, depth, KV_HEADS, 2, LANES).sum(axis=3)
        k_grad = join_halves(pairs[0]).reshape(depth, -1)
        v_grad = pairs[1][..., :HEAD].reshape(depth, -1)
        mix_grad = jnp.concatenate([q_grad, k_grad, v_grad], axis=1)
        gate_up_grad = jnp.concatenate([both[0], both[1]], axis=1).astype(F32)
        out_grad = out_grad.astype(F32)
        down_grad = down_grad.astype(F32)
        gain_sum = gain_sum[:4]
    else:
        def collected(index):
            first, second = weight_grads[0][index], weight_grads[1][index]
            own = jnp.where(section == 0, first, second)
            away = jnp.where(section == 0, second, first)
            return (own.astype(F32) + swap_sections(away).astype(F32)).astype(BF)

        cut_grad = jnp.concatenate(list(collected(0)) + list(collected(1)), axis=1)
        cut_grad = lax.all_to_all(cut_grad.reshape(F, depth, -1), "fsdp", 0, 0)
        cut_grad = lax.all_gather(cut_grad, "ctx", axis=0, tiled=False)
        out_grad = lax.all_gather(collected(2), "ctx", axis=0, tiled=False)
        down_grad = lax.all_gather(collected(3), "ctx", axis=0, tiled=True).astype(F32)

        def heads_of(columns, count):
            folded = columns.astype(F32).reshape(count, C // count, F, depth, columns.shape[-1]).sum(axis=1)
            return jnp.transpose(folded, (2, 1, 0, 3))

        q_grad = join_halves(heads_of(cut_grad[..., :LANES], plan.heads_f)).reshape(depth, -1)
        k_grad = join_halves(heads_of(cut_grad[..., LANES : 2 * LANES], plan.groups_f)).reshape(depth, -1)
        v_grad = heads_of(cut_grad[..., 2 * LANES : 3 * LANES], plan.groups_f)[..., :HEAD].reshape(depth, -1)
        mix_grad = jnp.concatenate([q_grad, k_grad, v_grad], axis=1)
        both = jnp.transpose(cut_grad[..., 3 * LANES :], (2, 1, 0, 3)).astype(F32)
        gate_up_grad = jnp.concatenate(
            [both[..., : plan.units].reshape(depth, -1), both[..., plan.units :].reshape(depth, -1)], axis=1
        )
        out_grad = out_grad.astype(F32).reshape(plan.heads_f, plan.share, HEAD, depth * F).sum(axis=1).reshape(-1, depth * F)

        gain_sum = lax.psum(gain_sum, ("section", "ctx", "fsdp"))
    gain_sum = lax.dynamic_slice_in_dim(gain_sum, 2 * section, 2, 0)
    gain_sum = lax.dynamic_slice_in_dim(gain_sum, plan.f * depth, depth, 1)
    return mix_grad, gate_up_grad, out_grad, down_grad, gain_sum


def on_device(
    inputs, cotangent, attention_gain, query_key_value, output_weight, feed_gain, gate_up, down_weight, block_order
):
    section = lax.axis_index("section")
    width = inputs.shape[2]
    hidden_units = down_weight.shape[1] * lax.axis_size("fsdp")
    plan = Plan(width, hidden_units)
    rows = inputs.shape[1]
    C, F = plan.C, plan.F
    length = rows * C * F
    depth = query_key_value.shape[1]

    def by_layer(own, other):
        first = section == 0
        return jnp.where(first, own, other), jnp.where(first, other, own)

    order = pick(block_order, section, 0)
    positions = (order[:, None] * rows + jnp.arange(rows, dtype=jnp.int32)[None, :]).reshape(length)
    part_rows = length // plan.share
    part_positions = lax.dynamic_slice_in_dim(positions, plan.part * part_rows, part_rows, 0)
    tables = angle_tables(positions)
    part_tables = angle_tables(part_positions)

    x = pick(inputs, section, 0)
    grad = pick(cotangent, section, 0)
    results = []
    input_grads = [None, None]
    weight_grads = [None, None]
    gain_grads = [None, None]
    kept = []
    if on_line():
        own_gains = jnp.pad(jnp.concatenate([attention_gain, feed_gain]), ((0, 14), (0, 0)))
        shared = share_call(query_key_value, output_weight, gate_up, down_weight, own_gains)
        places = (positions[:, None], positions[None, :])
        for s in range(2):
            *keep, result = forward_call(s, x, shared, tables, places)
            kept.append((x, keep))
            results.append(result)
            x = result
        for s in (1, 0):
            input_grads[s], grad, *weight_grads[s], gain_grads[s] = backward_call(
                s, grad, shared, tables, places, *kept[s]
            )
    else:
        weights, gains = shared_weights(
            plan, section, attention_gain, query_key_value, output_weight, feed_gain, gate_up, down_weight
        )
        for s in range(2):
            x, keep = forward_layer(plan, x, weights[s], gains[s], positions, part_positions, tables)
            kept.append(keep)
            results.append(x)
        for s in (1, 0):
            input_grads[s], weight_grads[s], gain_grads[s] = backward_layer(
                plan, grad, weights[s], gains[s], kept[s], positions, part_positions, tables, part_tables
            )
            grad = input_grads[s].astype(BF)

    def mine_and_theirs(first, second):
        return jnp.where(section == 0, first, second), jnp.where(section == 0, second, first)

    def by_batch(first, second):
        own, away = mine_and_theirs(first, second)
        return jnp.stack(by_layer(own, swap_sections(away)))

    section_outputs = by_batch(*results)
    section_input_grads = by_batch(*input_grads)

    shard_grads = returned_grads(plan, section, weight_grads, gain_grads, depth)
    mix_grad, gate_up_grad, out_grad, down_grad, gain_sum = shard_grads
    return (
        section_outputs[None],
        section_input_grads[None],
        gain_sum[0][None],
        mix_grad[None],
        out_grad[None],
        gain_sum[1][None],
        gate_up_grad[None],
        down_grad[None],
    )


def solution(mesh):
    placed = (
        P(None, ("ctx", "fsdp"), None),
        P(None, ("ctx", "fsdp"), None),
        P("section", "fsdp"),
        P("section", "fsdp", None),
        P("section", "fsdp", None),
        P("section", "fsdp"),
        P("section", "fsdp", None),
        P("section", "fsdp", None),
        P(),
    )
    return jax.shard_map(
        on_device,
        mesh=mesh,
        in_specs=placed,
        out_specs=(
            P("section", None, ("ctx", "fsdp"), None),
            P("section", None, ("ctx", "fsdp"), None),
            P("section", "fsdp"),
            P("section", "fsdp", None),
            P("section", "fsdp", None),
            P("section", "fsdp"),
            P("section", "fsdp", None),
            P("section", "fsdp", None),
        ),
        check_vma=False,
    )
```

```python
import functools

import jax
import jax.numpy as jnp
from jax import lax
from jax.experimental import pallas as pl
from jax.experimental.pallas import tpu as pltpu
from jax.sharding import PartitionSpec as P

KV_HEADS = 8
HEAD = 96
LANES = 128
SPAN = 64
norm_eps = 1e-05
rope_base = 100000.0
masked_value = -1e30
BF = jnp.bfloat16
F32 = jnp.float32

MESH = pl.DeviceIdType.MESH


def greet():
    c = lax.axis_index("ctx")
    f = lax.axis_index("fsdp")
    barrier = pltpu.get_barrier_semaphore()
    inner = jnp.logical_and(c > 0, c < 3)
    for peer in (f + 2 - 4 * (f // 2), f + 1 - 2 * lax.rem(f, 2)):
        pl.semaphore_signal(barrier, inc=1, device_id={"fsdp": peer}, device_id_type=MESH)

    @pl.when(c < 3)
    def _():
        pl.semaphore_signal(barrier, inc=1, device_id={"ctx": c + 1}, device_id_type=MESH)

    @pl.when(c > 0)
    def _():
        pl.semaphore_signal(barrier, inc=1, device_id={"ctx": c - 1}, device_id_type=MESH)

    @pl.when(inner)
    def _():
        pl.semaphore_wait(barrier, 4)

    @pl.when(jnp.logical_not(inner))
    def _():
        pl.semaphore_wait(barrier, 3)


def near_order(c):
    low = c < 2
    return [c, c + 1 - 2 * lax.rem(c, 2), jnp.where(low, 2, 1), jnp.where(low, 3, 0)]


def gather_rows(whole, rows, send, recv, ready=None, started=None):
    c = lax.axis_index("ctx")
    f = lax.axis_index("fsdp")
    across = f + 2 - 4 * (f // 2)
    twin = f + 1 - 2 * lax.rem(f, 2)
    cross = across + 1 - 2 * lax.rem(f, 2)
    inner = jnp.logical_and(c > 0, c < 3)
    outer = jnp.logical_not(inner)
    order = near_order(c)
    pair = order[1]
    half = rows // 2
    sent = []

    def at(cc, ff, h):
        return whole.at[pl.ds(pl.multiple_of((cc * 4 + ff) * rows + h * half, half), half)]

    def copy(src, slot, arrival, peer):
        return pltpu.make_async_remote_copy(
            src, src, send.at[slot], recv.at[arrival], device_id=peer, device_id_type=MESH
        )

    def go(src, slot, arrival, peer, when=None):
        one = copy(src, slot, arrival, peer)
        if when is None:
            one.start()
        else:
            pl.when(when)(one.start)
        sent.append((one, when))

    def arrived(ref, arrival):
        copy(ref, 0, arrival, {"fsdp": twin}).wait_recv()

    up_to = {"ctx": jnp.minimum(c + 1, 3)}
    down_to = {"ctx": jnp.maximum(c - 1, 0)}
    for h in range(2):
        go(at(c, f, h), h, 2 * c + h, up_to, c < 3)
        go(at(c, f, h), 2 + h, 2 * c + h, down_to, c > 0)
        go(at(c, f, h), 4 + h, 8 + 2 * c + h, {"fsdp": across})
    for h in range(2):
        go(at(c, f, h), 12 + h, 16 + 2 * c + h, {"fsdp": twin})
    if started is not None:
        started()

    def along(step, h):
        d = order[step]
        block = at(d, f, h)
        arrived(block, 2 * d + h)
        go(block, 28 + 2 * step + h, 2 * d + h, {"ctx": jnp.where(d < c, jnp.minimum(c + 1, 3), jnp.maximum(c - 1, 0))}, inner)
        if (step, h) != (1, 0):
            go(block, 4 + 2 * step + h, 8 + 2 * d + h, {"fsdp": across})
        go(block, 12 + 2 * step + h, 16 + 2 * d + h, {"fsdp": twin})

    def over(step, h):
        d = order[step]
        block = at(d, across, h)
        arrived(block, 32 if (step, h) == (1, 0) else 8 + 2 * d + h)
        go(block, 20 + 2 * step + h, 24 + 2 * d + h, {"fsdp": twin})

    def complete(step):
        d = order[step]
        for h in range(2):
            arrived(at(d, twin, h), 16 + 2 * d + h)
            arrived(at(d, cross, h), 24 + 2 * d + h)
        if ready is not None:
            ready(d)

    along(1, 0)
    over(0, 0)
    go(at(c, across, 0), 36, 32, {"ctx": pair}, outer)
    along(1, 1)
    over(0, 1)
    along(2, 0)
    along(2, 1)
    complete(0)
    over(1, 1)
    along(3, 0)
    over(2, 0)
    along(3, 1)
    go(at(c, across, 0), 37, 32, {"ctx": pair}, inner)
    over(2, 1)
    complete(2)
    over(3, 0)
    over(1, 0)
    complete(1)
    over(3, 1)
    complete(3)
    for one, when in sent:
        if when is None:
            one.wait_send()
        else:
            pl.when(when)(one.wait_send)


GATHER_SENDS = 38
GATHER_RECVS = 33


def scatter_sum(part, total, land, send, recv, produce=None, meanwhile=None, tick=None):
    c = lax.axis_index("ctx")
    f = lax.axis_index("fsdp")
    across = f + 2 - 4 * (f // 2)
    twin = f + 1 - 2 * lax.rem(f, 2)
    cross = across + 1 - 2 * lax.rem(f, 2)
    inner = jnp.logical_and(c > 0, c < 3)
    rows = total.shape[0]
    half = rows // 2
    order = near_order(c)[::-1]
    pair = order[2]
    sent = []

    def rows_at(cc, ff, h=None):
        start = (cc * 4 + ff) * rows
        if h is None:
            return pl.ds(pl.multiple_of(start, rows), rows)
        return pl.ds(pl.multiple_of(start + h * half, half), half)

    def copy(src, dst, slot, arrival, peer):
        return pltpu.make_async_remote_copy(
            src, dst, send.at[slot], recv.at[arrival], device_id=peer, device_id_type=MESH
        )

    def go(src, dst, slot, arrival, peer):
        one = copy(src, dst, slot, arrival, peer)
        one.start()
        sent.append(one)

    def piece(slot, h):
        return land.at[slot, pl.ds(h * half, half)]

    def landed(ref, arrival):
        copy(ref, ref, 0, arrival, {"fsdp": twin}).wait_recv()
        return ref[...].astype(F32)

    def begin(step):
        d = order[step]
        if produce is not None:
            produce(d)
        go(part.at[rows_at(d, cross)], land.at[step], step, step, {"fsdp": twin})
        go(part.at[rows_at(d, twin)], land.at[4 + step], 4 + step, 4 + step, {"fsdp": twin})

    def over(step, h):
        d = order[step]
        mine = rows_at(d, across, h)
        if h == 0:
            copy(land.at[step], land.at[step], 0, step, {"fsdp": twin}).wait_recv()
        value = part[mine, :].astype(F32) + land[step, h * half : (h + 1) * half, :].astype(F32)
        if (step, h) == (3, 0):
            value = value + landed(piece(17, 0), 26)
        part[mine, :] = value.astype(BF)
        if (step, h) == (2, 0):
            go(part.at[mine], piece(17, 0), 16, 26, {"ctx": pair})
        else:
            go(part.at[mine], piece(8 + step, h), 8 + 2 * step + h, 8 + 2 * step + h, {"fsdp": across})

    def onward(step, h):
        d = order[step]
        mine = rows_at(d, f, h)
        if h == 0:
            copy(land.at[4 + step], land.at[4 + step], 0, 4 + step, {"fsdp": twin}).wait_recv()
        value = part[mine, :].astype(F32) + land[4 + step, h * half : (h + 1) * half, :].astype(F32)
        if (step, h) != (2, 0):
            value = value + landed(piece(8 + step, h), 8 + 2 * step + h)
        if step == 3:
            total[h * half : (h + 1) * half, :] = value
            return
        part[mine, :] = value.astype(BF)

        @pl.when(inner)
        def _():
            part[mine, :] = (part[mine, :].astype(F32) + landed(piece(12 + d, h), 16 + 2 * d + h)).astype(BF)

        target = jnp.where(d > c, c + 1, c - 1)
        here = jnp.logical_and(d < c, d == c - 1)
        go(part.at[mine], piece(jnp.where(here, 16, 12 + d), h), 17 + 2 * step + h,
           jnp.where(here, 24, 16 + 2 * d) + h, {"ctx": target})

    begin(0)
    over(0, 0)
    over(0, 1)
    begin(1)
    begin(2)
    over(2, 0)
    over(1, 0)
    onward(0, 0)
    over(1, 1)
    onward(0, 1)
    begin(3)
    over(2, 1)
    onward(1, 0)
    if tick is not None:
        tick()
    over(3, 0)
    onward(1, 1)
    over(3, 1)
    if tick is not None:
        tick()
    onward(2, 0)
    onward(2, 1)
    if meanwhile is not None:
        meanwhile()
    for h in range(2):
        onward(3, h)

        @pl.when(c > 0)
        def _():
            total[h * half : (h + 1) * half, :] += landed(piece(12 + c, h), 16 + 2 * c + h)

        @pl.when(c < 3)
        def _():
            total[h * half : (h + 1) * half, :] += landed(piece(16, h), 24 + h)

    for one in sent:
        one.wait_send()


SCATTER_SENDS = 23
SCATTER_RECVS = 27


def kernel_dot(left, right):
    return jnp.dot(left, right, preferred_element_type=F32)


def kernel_dot_nt(left, right):
    return lax.dot_general(left, right, (((1,), (1,)), ((), ())), preferred_element_type=F32)


def kernel_dot_tn(left, right):
    return lax.dot_general(left, right, (((0,), (0,)), ((), ())), preferred_element_type=F32)


def turn(values):
    return pltpu.roll(values, SPAN, axis=1)


def mean_square(values):
    return lax.rsqrt(jnp.mean(values * values, axis=-1, keepdims=True) + norm_eps)


def greet_all(peers):
    barrier = pltpu.get_barrier_semaphore()
    for peer in peers:
        pl.semaphore_signal(barrier, inc=1, device_id=peer, device_id_type=MESH)
    return len(peers)


def greet_more(peers):
    c = lax.axis_index("ctx")
    barrier = pltpu.get_barrier_semaphore()
    count = greet_all(peers)
    inner = jnp.logical_and(c > 0, c < 3)

    @pl.when(c < 3)
    def _():
        pl.semaphore_signal(barrier, inc=1, device_id={"ctx": c + 1}, device_id_type=MESH)

    @pl.when(c > 0)
    def _():
        pl.semaphore_signal(barrier, inc=1, device_id={"ctx": c - 1}, device_id_type=MESH)

    @pl.when(inner)
    def _():
        pl.semaphore_wait(barrier, count + 2)

    @pl.when(jnp.logical_not(inner))
    def _():
        pl.semaphore_wait(barrier, count + 1)


def head_choice(value_part):
    source = lax.broadcasted_iota(jnp.int32, (4 * HEAD, 4 * LANES), 0)
    lane = lax.broadcasted_iota(jnp.int32, (4 * HEAD, 4 * LANES), 1)
    head = lane // LANES
    inside = lane - head * LANES
    if value_part:
        wanted = jnp.where(inside < HEAD, head * HEAD + inside, -1)
    else:
        half = inside // SPAN
        place = inside - half * SPAN
        wanted = jnp.where(place < HEAD // 2, head * HEAD + half * (HEAD // 2) + place, -1)
    return jnp.where(source == wanted, 1.0, 0.0).astype(BF)


class Share:
    def __init__(self, sources, targets, scratch, sems):
        self.mix, self.out, self.gate_up, self.down, self.gains = sources
        self.w_mix, self.w_gate, self.w_out, self.w_down, self.w_gains = targets
        self.mix_v, self.heads_v = scratch
        self.local, self.send, self.recv = sems
        self.s = lax.axis_index("section")
        self.c = lax.axis_index("ctx")
        self.f = lax.axis_index("fsdp")
        self.other = 1 - self.s
        self.depth = self.mix.shape[1]
        self.units = self.w_down.shape[1]
        self.peers = [lax.rem(self.f + k, 4) for k in range(1, 4)]
        self.rows = pl.ds(pl.multiple_of(self.f * self.depth, self.depth), self.depth)
        self.pending = []

    def greeted(self):
        return (
            [{"fsdp": peer} for peer in self.peers]
            + [{"section": self.other}]
            + [{"section": self.other, "fsdp": peer} for peer in self.peers]
        )

    def copy(self, src, dst, slot, arrival, peer):
        return pltpu.make_async_remote_copy(
            src, dst, self.send.at[slot], self.recv.at[arrival], device_id=peer, device_id_type=MESH
        )

    def go(self, src, dst, slot, arrival, peer):
        one = self.copy(src, dst, slot, arrival, peer)
        one.start()
        self.pending.append(one)

    def keep(self, src, dst, slot):
        one = pltpu.make_async_copy(src, dst, self.local.at[slot])
        one.start()
        return one

    def load(self):
        self.loaded = self.keep(self.mix.at[0], self.mix_v, 0)

    def lanes(self, peer, part):
        head = peer * 4 + self.c
        start = head * LANES if part == 0 else (16 + 8 * (part - 1) + head // 2) * LANES
        return self.heads_v.at[:, pl.ds(pl.multiple_of(start, LANES), LANES)]

    def put(self, part):
        return self.w_mix.at[self.s, self.rows, pl.ds(part * LANES, LANES)]

    def send_mix(self):
        self.loaded.wait()
        for g in range(8):
            self.heads_v[:, g * 4 * LANES : (g + 1) * 4 * LANES] = kernel_dot(
                self.mix_v[:, g * 4 * HEAD : (g + 1) * 4 * HEAD], head_choice(g >= 6)
            ).astype(BF)
        for k, peer in enumerate(self.peers):
            for part in range(3):
                self.copy(self.lanes(peer, part), self.put(part), k, self.f, {"fsdp": peer}).start()
        self.own_mix = [self.keep(self.lanes(self.f, part), self.put(part), 2 + part) for part in range(3)]
        out_rows = self.out.at[0, pl.ds(pl.multiple_of(self.c * HEAD, HEAD), HEAD)]
        down_rows = self.down.at[0, pl.ds(pl.multiple_of(self.c * self.units, self.units), self.units)]
        self.own_out = self.keep(out_rows, self.w_out.at[self.s], 7)
        self.own_down = self.keep(down_rows, self.w_down.at[self.s], 8)
        mine = self.w_gains.at[self.s, :, pl.ds(pl.multiple_of(self.f * self.depth, self.depth), self.depth)]
        for k, peer in enumerate(self.peers):
            self.go(self.gains, mine, 20 + k, 16 + 4 * self.s + self.f, {"fsdp": peer})
            self.go(self.gains, mine, 23 + k, 16 + 4 * self.s + self.f, {"section": self.other, "fsdp": peer})
        self.go(self.gains, mine, 26, 16 + 4 * self.s + self.f, {"section": self.other})
        self.own_gains = self.keep(self.gains, mine, 1)

    def gate_piece(self, peer, part):
        hidden_units = self.gate_up.shape[2] // 2
        start = pl.multiple_of(part * hidden_units + (peer * 4 + self.c) * self.units, self.units)
        return self.gate_up.at[0, :, pl.ds(start, self.units)]

    def gate_put(self, part):
        return self.w_gate.at[self.s, self.rows, pl.ds(part * self.units, self.units)]

    def send_gate(self):
        for k, peer in enumerate(self.peers):
            for part in range(2):
                self.copy(self.gate_piece(peer, part), self.gate_put(part), 3 + k, 4 + self.f, {"fsdp": peer}).start()

    def keep_gate(self):
        self.own_gate = [self.keep(self.gate_piece(self.f, part), self.gate_put(part), 5 + part) for part in range(2)]

    def slab(self, ref, origin):
        return ref.at[self.s, pl.ds(pl.multiple_of(origin * self.depth, self.depth), self.depth)]

    def cross_own(self, ref, copies, slot, base):
        for one in copies:
            one.wait()
        self.go(self.slab(ref, self.f), self.slab(ref, self.f), slot, base + self.f, {"section": self.other})

    def cross_slab(self, ref, k, slot, arrival, base):
        origin = lax.rem(self.f + 3 - k, 4)
        block = self.slab(ref, origin)
        self.copy(block, block, 0, arrival + origin, {"fsdp": origin}).wait_recv()
        self.go(block, block, slot + k, base + origin, {"section": self.other})

    def cross_mix(self):
        self.cross_own(self.w_mix, self.own_mix, 6, 8)
        for k in range(3):
            self.cross_slab(self.w_mix, k, 7, 0, 8)
        self.own_out.wait()
        self.go(self.w_out.at[self.s], self.w_out.at[self.s], 10, 24, {"section": self.other})
        self.cross_own(self.w_gate, self.own_gate, 11, 12)

    def cross_gate(self):
        for k in range(3):
            self.cross_slab(self.w_gate, k, 12, 4, 12)
        self.own_down.wait()
        self.go(self.w_down.at[self.s], self.w_down.at[self.s], 15, 25, {"section": self.other})

    def there(self, ref, arrival):
        self.copy(ref, ref, 0, arrival, {"section": self.other}).wait_recv()

    def mix_there(self):
        self.own_gains.wait()
        for origin in range(4):
            rows = pl.ds(origin * self.depth, self.depth)
            self.there(self.w_mix.at[self.other, rows], 8 + origin)
            self.there(self.w_gains.at[self.other, :, rows], 16 + 4 * self.other + origin)
        for k in range(3):
            origin = lax.rem(self.f + 3 - k, 4)
            columns = pl.ds(pl.multiple_of(origin * self.depth, self.depth), self.depth)
            self.there(self.w_gains.at[self.s, :, columns], 16 + 4 * self.s + origin)
        self.there(self.w_out.at[self.other], 24)

    def gate_there(self):
        for origin in range(4):
            self.there(self.w_gate.at[self.other, pl.ds(origin * self.depth, self.depth)], 12 + origin)

    def down_there(self):
        self.there(self.w_down.at[self.other], 25)

    def finish(self):
        for k, peer in enumerate(self.peers):
            block = self.slab(self.w_mix, self.f)
            self.copy(block, block, k, 0, {"fsdp": peer}).wait_send()
            block = self.slab(self.w_gate, self.f)
            self.copy(block, block, 3 + k, 0, {"fsdp": peer}).wait_send()
        for one in self.pending:
            one.wait_send()


class Loads:
    def __init__(self, sems):
        self.sems = sems
        self.copies = []

    def start(self, src, dst):
        one = pltpu.make_async_copy(src, dst, self.sems.at[len(self.copies)])
        one.start()
        self.copies.append(one)
        return one


def plane_rows(d, rows):
    return pl.ds(pl.multiple_of(d * 4 * rows, 4 * rows), 4 * rows)


def forward_body(layer, share, x_own, weights, tables, kept, scratch, sems):
    w_mix, w_gate, w_out, w_down, w_gains = weights
    cosine, sine, place_col, place_row = tables
    normed_o, q_o, k_o, v_o, context_o, log_o, middle_o, normed_two_o, both_o, result_o = kept
    (x_v, normed_v, q_v, k_v, v_v, context_v, log_v, middle_v, two_v, both_v, hidden_v, result_v,
     mix_v, gate_v, out_v, down_v, gains_v, part_v, land_a, land_b, total_v) = scratch
    local, save, send_a, recv_a, send_b, recv_b, send_c, recv_c, send_d, recv_d = sems
    c = lax.axis_index("ctx")
    f = lax.axis_index("fsdp")
    rows = x_own.shape[0]
    units = down_v.shape[0]
    own_rows = pl.ds(pl.multiple_of((c * 4 + f) * rows, rows), rows)
    loads = Loads(local)
    saves = Loads(save)
    load_x = loads.start(x_own, x_v.at[own_rows])
    out_v[...] = jnp.zeros_like(out_v)

    def load_first():
        return [
            loads.start(w_gains.at[layer], gains_v),
            loads.start(w_mix.at[layer], mix_v),
            loads.start(w_out.at[layer], out_v.at[pl.ds(0, HEAD)]),
        ]

    def project(d):
        here = plane_rows(d, rows)
        x = x_v[here, :].astype(F32)
        normed = (x * mean_square(x) * gains_v[0:1, :].astype(F32)).astype(BF)
        normed_v[here, :] = normed
        mixed = kernel_dot(normed, mix_v[...])
        cos = cosine[here, :]
        sin = sine[here, :]
        q = mixed[:, :LANES]
        k = mixed[:, LANES : 2 * LANES]
        q_v[here, :] = (q * cos + turn(q) * sin).astype(BF)
        k_v[here, :] = (k * cos + turn(k) * sin).astype(BF)
        v_v[here, :] = mixed[:, 2 * LANES :].astype(BF)

    if share is None:
        first = load_first()
        load_gate = loads.start(w_gate.at[layer], gate_v)
        load_down = loads.start(w_down.at[layer], down_v)
        greet()
        load_x.wait()
        for one in first:
            one.wait()
        gather_rows(x_v, rows, send_a, recv_a, project)
    else:
        share.load()
        share.keep_gate()
        greet_more(share.greeted())
        load_x.wait()
        share.send_mix()
        gather_rows(x_v, rows, send_a, recv_a, started=share.cross_mix)
        share.send_gate()
        share.mix_there()
        first = load_first()
        for one in first:
            one.wait()
        for d in range(4):
            project(d)
        share.cross_gate()
    for src, dst in ((normed_v, normed_o), (q_v, q_o), (k_v, k_o), (v_v, v_o)):
        saves.start(src, dst)
    scale = HEAD ** (-0.5)

    def attention(d):
        here = plane_rows(d, rows)
        scores = kernel_dot_nt(q_v[here, :], k_v[...]) * scale
        allowed = place_row[...] <= place_col[here, :]
        scores = jnp.where(allowed, scores, masked_value)
        top = jnp.max(scores, axis=-1, keepdims=True)
        weights = jnp.exp(scores - top)
        amount = jnp.sum(weights, axis=-1, keepdims=True)
        context = (kernel_dot(weights.astype(BF), v_v[...]) / amount).astype(BF)
        context_v[here, :] = context
        log_v[here, :] = jnp.broadcast_to(top + jnp.log(amount), (4 * rows, LANES))
        part_v[here, :] = kernel_dot(context, out_v[...]).astype(BF)

    scatter_sum(part_v, total_v, land_a, send_b, recv_b, attention)
    saves.start(context_v, context_o)
    saves.start(log_v, log_o)
    middle = x_v[own_rows, :].astype(F32) + total_v[...]
    middle_v[...] = middle
    saves.start(middle_v, middle_o)
    two_v[own_rows, :] = (middle * mean_square(middle) * gains_v[1:2, :].astype(F32)).astype(BF)

    def gate_ready():
        if share is None:
            load_gate.wait()
        else:
            share.gate_there()
            loads.start(w_gate.at[layer], gate_v).wait()

    def feed(d):
        here = plane_rows(d, rows)
        both = kernel_dot(two_v[here, :], gate_v[...])
        both_v[here, :] = both
        gate = both[:, :units]
        hidden_v[here, :] = (gate * jax.nn.sigmoid(gate) * both[:, units:]).astype(BF)

    gather_rows(two_v, rows, send_c, recv_c, feed, gate_ready)
    saves.start(two_v, normed_two_o)
    saves.start(both_v, both_o)
    if share is None:
        load_down.wait()
    else:
        share.down_there()
        loads.start(w_down.at[layer], down_v).wait()

    def lower(d):
        here = plane_rows(d, rows)
        part_v[here, :] = kernel_dot(hidden_v[here, :], down_v[...]).astype(BF)

    scatter_sum(part_v, total_v, land_b, send_d, recv_d, lower)
    result_v[...] = (middle_v[...] + total_v[...]).astype(BF)
    saves.start(result_v, result_o)
    for one in saves.copies:
        one.wait()
    if share is not None:
        share.finish()


def forward_kernel(layer, *refs):
    x_own, *refs = refs
    weights, refs = refs[:5], refs[5:]
    tables, refs = refs[:4], refs[4:]
    kept, refs = refs[:10], refs[10:]
    scratch, sems = refs[:21], refs[21:]
    forward_body(layer, None, x_own, weights, tables, kept, scratch, sems)


def forward_share_kernel(*refs):
    x_own, *refs = refs
    sources, refs = refs[:5], refs[5:]
    tables, refs = refs[:4], refs[4:]
    kept, refs = refs[:10], refs[10:]
    weights, refs = refs[:5], refs[5:]
    scratch, refs = refs[:21], refs[21:]
    packing, refs = refs[:2], refs[2:]
    sems, share_sems = refs[:10], refs[10:]
    share = Share(sources, weights, packing, share_sems)
    forward_body(0, share, x_own, weights, tables, kept, scratch, sems)


def backward_body(layer, grad_own, weights, tables, saved, outs, scratch, sems, returning):
    w_mix, w_gate, w_out, w_down, w_gains = weights
    cosine, sine, place_col, place_row = tables
    x_own, normed, q, k, v, context, log, middle, normed_two, both = saved
    (grad_v, x_v, normed_v, q_v, k_v, v_v, context_v, log_v, middle_v, two_v, both_v, both_grad_v, hidden_v,
     low_v, mixed_v, kv_land, kv_v, key_grad_v, value_grad_v, start_v, start_low_v,
     mix_grad_v, gate_grad_v, out_grad_v, down_grad_v, gain_grad_v,
     mix_v, gate_v, out_v, down_v, gains_v, part_v, land_a, land_b, total_v) = scratch
    local, save, pair_sems, send_a, recv_a, send_b, recv_b, send_c, recv_c, send_d, recv_d = sems
    c = lax.axis_index("ctx")
    f = lax.axis_index("fsdp")
    odd = lax.rem(c, 2)
    rows = grad_own.shape[0]
    units = down_v.shape[0]
    own_rows = pl.ds(pl.multiple_of((c * 4 + f) * rows, rows), rows)
    loads = Loads(local)
    saves = Loads(save)
    load_grad = loads.start(grad_own, grad_v.at[own_rows])
    load_down = loads.start(w_down.at[layer], down_v)
    load_both = loads.start(both, both_v)
    load_gate = loads.start(w_gate.at[layer], gate_v)
    out_v[...] = jnp.zeros_like(out_v)
    key_grad_v[...] = jnp.zeros_like(key_grad_v)
    value_grad_v[...] = jnp.zeros_like(value_grad_v)
    gain_grad_v[...] = jnp.zeros_like(gain_grad_v)
    if returning is None:
        greet()
    else:
        peers = [{"fsdp": lax.rem(f + k, 4)} for k in range(1, 4)]
        greet_more(peers + [{"section": 1 - lax.axis_index("section")}, {"ctx": lax.rem(c + 2, 4)}])
    load_grad.wait()
    later = [
        loads.start(src, dst)
        for src, dst in (
            (normed_two, two_v), (middle, middle_v), (w_gains.at[layer], gains_v),
            (w_out.at[layer], out_v.at[pl.ds(0, HEAD)]), (q, q_v), (k, k_v), (v, v_v),
            (context, context_v), (log, log_v), (w_mix.at[layer], mix_v), (normed, normed_v), (x_own, x_v),
        )
    ]
    load_down.wait()
    load_both.wait()
    if returning is not None:
        begin_feed, begin_mix, feed_steps, mix_steps, sum_gains, along_line = returning
        steps = feed_steps()

    def feed(d):
        here = plane_rows(d, rows)
        hidden_grad = kernel_dot_nt(grad_v[here, :], down_v[...])
        gate = both_v[here, :units]
        up = both_v[here, units:]
        sig = jax.nn.sigmoid(gate)
        silu = gate * sig
        hidden_v[here, :] = (silu * up).astype(BF)
        both_grad_v[here, :units] = (hidden_grad * up * sig * (1.0 + gate * (1.0 - sig))).astype(BF)
        both_grad_v[here, units:] = (hidden_grad * silu).astype(BF)

    gather_rows(grad_v, rows, send_a, recv_a, feed)
    load_gate.wait()

    def spread(d):
        here = plane_rows(d, rows)
        part_v[here, :] = kernel_dot_nt(both_grad_v[here, :], gate_v[...]).astype(BF)

    def feed_weights():
        later[0].wait()
        down_grad_v[...] = kernel_dot_tn(hidden_v[...], grad_v[...]).astype(BF)
        for part in range(2):
            gate_grad_v[part] = kernel_dot_tn(
                two_v[...], both_grad_v[:, part * units : (part + 1) * units]
            ).astype(BF)
        if returning is None:
            saves.start(down_grad_v, outs[4])
            saves.start(gate_grad_v, outs[2])
        else:
            begin_feed()

    scatter_sum(part_v, total_v, land_a, send_b, recv_b, spread, feed_weights)
    for one in later[1:]:
        one.wait()

    def norm_grads(error, value, gain, row):
        factor = mean_square(value)
        shaped = error * gain
        common = jnp.mean(shaped * value, axis=-1, keepdims=True)
        gain_grad_v[row : row + 1, :] = jnp.sum(error * value * factor, axis=0, keepdims=True)
        return factor * shaped - value * (factor * factor * factor) * common

    middle_grad = norm_grads(total_v[...], middle_v[...], gains_v[1:2, :].astype(F32), 1)
    middle_grad = middle_grad + grad_v[own_rows, :].astype(F32)
    middle_v[...] = middle_grad
    low_v[own_rows, :] = middle_grad.astype(BF)
    scale = HEAD ** (-0.5)

    def attention(d):
        here = plane_rows(d, rows)
        context_grad = kernel_dot_nt(low_v[here, :], out_v[...])
        common = jnp.sum(context_grad * context_v[here, :].astype(F32), axis=-1, keepdims=True)
        context_grad = context_grad.astype(BF)
        queries = q_v[here, :]
        scores = kernel_dot_nt(queries, k_v[...]) * scale
        allowed = place_row[...] <= place_col[here, :]
        weights = jnp.exp(jnp.where(allowed, scores, masked_value) - log_v[here, 0:1])
        weight_grad = kernel_dot_nt(context_grad, v_v[...])
        score_grad = (weights * (weight_grad - common)).astype(BF)
        value_grad_v[...] += kernel_dot_tn(weights.astype(BF), context_grad)
        key_grad_v[...] += kernel_dot_tn(score_grad, queries)
        query_grad = kernel_dot(score_grad, k_v[...]) * scale
        mixed_v[here, :LANES] = (query_grad * cosine[here, :] - turn(query_grad) * sine[here, :]).astype(BF)

    gather_rows(low_v, rows, send_c, recv_c, attention)
    key_grad = key_grad_v[...] * scale
    mixed_v[:, LANES : 2 * LANES] = (key_grad * cosine[...] - turn(key_grad) * sine[...]).astype(BF)
    mixed_v[:, 2 * LANES :] = value_grad_v[...].astype(BF)
    pair = {"ctx": c + 1 - 2 * odd}

    def pair_copy(part):
        return pltpu.make_async_remote_copy(
            mixed_v.at[:, pl.ds(part * LANES, LANES)], kv_land, pair_sems.at[0], pair_sems.at[1],
            device_id=pair, device_id_type=MESH,
        )

    pl.when(odd == 0)(pair_copy(2).start)
    pl.when(odd == 1)(pair_copy(1).start)

    def spread_two(d):
        here = plane_rows(d, rows)
        part_v[here, :] = kernel_dot_nt(mixed_v[here, :], mix_v[...]).astype(BF)

    def mix_weights():
        out_grad_v[...] = kernel_dot_tn(context_v[...], low_v[...])[:HEAD].astype(BF)
        mix_grad_v[0] = kernel_dot_tn(normed_v[...], mixed_v[:, :LANES]).astype(BF)
        pair_copy(1).wait_recv()
        mine = jnp.where(odd == 0, mixed_v[:, LANES : 2 * LANES].astype(F32), mixed_v[:, 2 * LANES :].astype(F32))
        kv_v[...] = (mine + kv_land[...].astype(F32)).astype(BF)
        mix_grad_v[1] = kernel_dot_tn(normed_v[...], kv_v[...]).astype(BF)
        if returning is None:
            saves.start(out_grad_v, outs[3])
            saves.start(mix_grad_v, outs[1])
        else:
            begin_mix()

    def next_step():
        if returning is not None:
            next(steps)()

    scatter_sum(part_v, total_v, land_b, send_d, recv_d, spread_two, mix_weights, next_step)
    start_grad = norm_grads(total_v[...], x_v[...].astype(F32), gains_v[0:1, :].astype(F32), 0) + middle_v[...]
    start_v[...] = start_grad
    saves.start(start_v, outs[0])
    if returning is None:
        start_low_v[...] = start_grad.astype(BF)
        saves.start(start_low_v, outs[6])
        saves.start(gain_grad_v, outs[5])
    else:
        for step in steps:
            step()
        for step in mix_steps():
            step()
        sum_gains(gain_grad_v)
        along_line()
    pair_copy(1).wait_send()
    for one in saves.copies:
        one.wait()


SAVED = 10
BACK_SCRATCH = 35


def backward_kernel(layer, *refs):
    grad_own, *refs = refs
    weights, refs = refs[:5], refs[5:]
    tables, refs = refs[:4], refs[4:]
    saved, refs = refs[:SAVED], refs[SAVED:]
    outs, refs = refs[:7], refs[7:]
    scratch, sems = refs[:BACK_SCRATCH], refs[BACK_SCRATCH:]
    backward_body(layer, grad_own, weights, tables, saved, outs, scratch, sems, None)


def backward_return_kernel(*refs):
    grad_own, *refs = refs
    weights, refs = refs[:5], refs[5:]
    tables, refs = refs[:4], refs[4:]
    saved, refs = refs[:SAVED], refs[SAVED:]
    (mix_old, gate_old, out_old, down_old, gain_old), refs = refs[:5], refs[5:]
    outs, refs = refs[:1], refs[1:]
    finals, refs = refs[:5], refs[5:]
    scratch, refs = refs[:BACK_SCRATCH], refs[BACK_SCRATCH:]
    own, refs = refs[:10], refs[10:]
    sems, return_sems = refs[:11], refs[11:]
    mix_new, gate_new, out_new, down_new, gain_new = scratch[21:26]
    gain_v = own[8]
    *steps, sum_gains, along_line = returner(
        tuple(finals) + tuple(own), return_sems,
        gate_new, down_new, mix_new, out_new, gate_old, down_old, mix_old, out_old,
    )

    def all_gains(gain_grad_v):
        gain_v[0] = jnp.zeros(gain_v.shape[1:], F32)
        gain_v[0, 0:2, :] = gain_grad_v[...]
        gain_v[0, 2:4, :] = gain_old[...]
        sum_gains()

    backward_body(
        0, grad_own, weights, tables, saved, outs, scratch, sems, tuple(steps) + (all_gains, along_line)
    )


def link_sems():
    dma = pltpu.SemaphoreType.DMA
    return [dma((GATHER_SENDS,)), dma((GATHER_RECVS,)), dma((SCATTER_SENDS,)), dma((SCATTER_RECVS,))] * 2


def low(*shape):
    return (shape, BF)


def full(*shape):
    return (shape, F32)


def shapes(specs):
    return [jax.ShapeDtypeStruct(*one) for one in specs]


def rooms(specs):
    return [pltpu.VMEM(*one) for one in specs]


def signals(*counts):
    return [pltpu.SemaphoreType.DMA((count,)) for count in counts]


def forward_call(layer, x_own, weights, tables):
    rows, width = x_own.shape
    length = 16 * rows
    sharing = layer == 0
    if sharing:
        depth = weights[0].shape[1]
        units = weights[2].shape[2] // 32
        packing = [low(depth, weights[0].shape[2]), low(depth, 32 * LANES)]
    else:
        units = weights[3].shape[1]
        packing = []
    anywhere = pl.BlockSpec(memory_space=pl.ANY)
    inside = pl.BlockSpec(memory_space=pltpu.VMEM)
    kept = [low(length, width)] + [low(length, LANES)] * 4 + [
        full(length, LANES), full(rows, width), low(length, width), full(length, 2 * units), low(rows, width)]
    shared = [low(2, width, 3 * LANES), low(2, width, 2 * units), low(2, HEAD, width), low(2, units, width), low(2, 16, width)]
    scratch = [low(length, width), low(length, width)] + [low(length, LANES)] * 4 + [
        full(length, LANES), full(rows, width), low(length, width), full(length, 2 * units), low(length, units),
        low(rows, width), low(width, 3 * LANES), low(width, 2 * units), low(LANES, width), low(units, width),
        low(16, width), low(length, width), low(18, rows, width), low(18, rows, width), full(rows, width)]
    outs = kept + shared if sharing else kept
    return pl.pallas_call(
        forward_share_kernel if sharing else functools.partial(forward_kernel, layer),
        out_shape=shapes(outs),
        in_specs=[anywhere] * 6 + [inside] * 4,
        out_specs=[anywhere] * len(outs),
        scratch_shapes=rooms(scratch + packing) + signals(6, 10) + link_sems() + (signals(9, 27, 26) if sharing else []),
        compiler_params=pltpu.CompilerParams(
            collective_id=layer, has_side_effects=True, vmem_limit_bytes=60 << 20),
    )(x_own, *weights, *tables)


def backward_call(layer, grad_own, weights, tables, saved, old=()):
    rows, width = grad_own.shape
    length = 16 * rows
    units = weights[3].shape[1]
    depth = width // 4
    returning = layer == 0
    anywhere = pl.BlockSpec(memory_space=pl.ANY)
    inside = pl.BlockSpec(memory_space=pltpu.VMEM)
    grads = [low(2, width, LANES), low(2, width, units), low(HEAD, width), low(units, width), full(2, width)]
    scratch = [low(length, width), low(rows, width), low(length, width)] + [low(length, LANES)] * 4 + [
        full(length, LANES), full(rows, width), low(length, width), full(length, 2 * units), low(length, 2 * units),
        low(length, units), low(length, width), low(length, 3 * LANES), low(length, LANES), low(length, LANES),
        full(length, LANES), full(length, LANES),
        full(rows, width), low(rows, width)] + grads + [
        low(width, 3 * LANES), low(width, 2 * units), low(LANES, width), low(units, width),
        low(16, width), low(length, width), low(18, rows, width), low(18, rows, width), full(rows, width)]
    sems = signals(16, 7, 2) + link_sems()
    if returning:
        outs = [full(rows, width), low(2, depth, 16 * LANES), low(2, depth, 16 * units), low(4 * HEAD, width),
                low(4 * units, width), full(8, width)]
        out_specs = [anywhere] * 5 + [inside]
        scratch += grads[:4] + grads[:4] + [full(5, 8, width), full(5, 8, width)]
        sems += signals(5, 23, 23, 50, 40)
    else:
        outs = [full(rows, width)] + grads + [low(rows, width)]
        out_specs = [anywhere] * len(outs)
    return pl.pallas_call(
        backward_return_kernel if returning else functools.partial(backward_kernel, layer),
        out_shape=shapes(outs),
        in_specs=[anywhere] * 6 + [inside] * 4 + [anywhere] * SAVED + ([anywhere] * 4 + [inside] if returning else []),
        out_specs=out_specs,
        scratch_shapes=rooms(scratch) + sems,
        compiler_params=pltpu.CompilerParams(
            collective_id=2 + layer, has_side_effects=True, vmem_limit_bytes=60 << 20),
    )(grad_own, *weights, *tables, *saved, *old)


def returner(refs, sems, gate_new, down_new, mix_new, out_new, gate_old, down_old, mix_old, out_old):
    (mix_out, gate_out, out_out, down_out, gain_out,
     mix_v, gate_v, out_v, down_v, mix_x, gate_x, out_x, down_x, gain_v, gain_x) = refs
    local, send, recv, line_send, line_recv = sems
    s = lax.axis_index("section")
    c = lax.axis_index("ctx")
    f = lax.axis_index("fsdp")
    other = {"section": 1 - s}
    units = down_v.shape[0]
    depth = mix_out.shape[1]
    inner = jnp.logical_and(c > 0, c < 3)
    above = jnp.minimum(c + 1, 3)
    below = jnp.maximum(c - 1, 0)

    def copy(src, dst, slot, arrival, peer):
        return pltpu.make_async_remote_copy(
            src, dst, send.at[slot], recv.at[arrival], device_id=peer, device_id_type=MESH
        )

    def rows_of(k):
        return pl.ds(k * depth, depth)

    def cross_feed(gate_away, down_away, gate_home, down_home):
        copy(down_away, down_x, 8, 8, other).start()
        for k in range(4):
            copy(gate_away.at[:, rows_of(k)], gate_x.at[:, rows_of(k)], k, k, other).start()
        pltpu.make_async_copy(down_home, down_v, local.at[0]).start()
        pltpu.make_async_copy(gate_home, gate_v, local.at[1]).start()

    def cross_mix(mix_away, out_away, mix_home, out_home):
        copy(out_away, out_x, 9, 9, other).start()
        for k in range(4):
            copy(mix_away.at[:, rows_of(k)], mix_x.at[:, rows_of(k)], 4 + k, 4 + k, other).start()
        pltpu.make_async_copy(out_home, out_v, local.at[2]).start()
        pltpu.make_async_copy(mix_home, mix_v, local.at[3]).start()

    def begin_feed():
        pl.when(s == 0)(lambda: cross_feed(gate_old, down_old, gate_new, down_new))
        pl.when(s == 1)(lambda: cross_feed(gate_new, down_new, gate_old, down_old))

    def begin_mix():
        pl.when(s == 0)(lambda: cross_mix(mix_old, out_old, mix_new, out_new))
        pl.when(s == 1)(lambda: cross_mix(mix_new, out_new, mix_old, out_old))

    def home_wait(k, dst):
        pltpu.make_async_copy(dst, dst, local.at[k]).wait()

    def arrived(ref, arrival):
        copy(ref, ref, 0, arrival, other).wait_recv()

    def gate_at(cc, ff):
        return gate_out.at[:, :, pl.ds(pl.multiple_of((ff * 4 + cc) * units, units), units)]

    def mix_at(cc, ff):
        return mix_out.at[:, :, pl.ds(pl.multiple_of((ff * 4 + cc) * LANES, LANES), LANES)]

    def out_at(cc, ff):
        return out_out.at[pl.ds(pl.multiple_of(cc * HEAD, HEAD), HEAD)]

    def down_at(cc, ff):
        return down_out.at[pl.ds(pl.multiple_of(cc * units, units), units)]

    origins = [lax.rem(f + k, 4) for k in (0, 3, 2, 1)]
    items = [(down_at, f)] + [(gate_at, one) for one in origins] + [(out_at, f)] + [(mix_at, one) for one in origins]

    def line(index, cc, slot, target):
        place, origin = items[index]
        return pltpu.make_async_remote_copy(
            place(cc, origin), place(cc, origin), line_send.at[slot], line_recv.at[cc * 10 + index],
            device_id={"ctx": target}, device_id_type=MESH,
        )

    def start_line(index):
        pl.when(c < 3)(line(index, c, index, above).start)
        pl.when(c > 0)(line(index, c, 10 + index, below).start)

    def fold(mine, theirs, arrival):
        arrived(theirs, arrival)
        mine[...] = (mine[...].astype(F32) + theirs[...].astype(F32)).astype(BF)

    def keep(src, dst):
        one = pltpu.make_async_copy(src, dst, local.at[4])
        one.start()
        one.wait()

    def whole_item(k, mine, theirs, arrival, place, index):
        home_wait(k, mine)
        fold(mine, theirs, arrival)
        keep(mine, place(c, f))
        start_line(index)

    def to_owner(k, mine, theirs, place, arrival_x, arrival_y, slot, index):
        owner = lax.rem(f + k, 4)
        rows = pl.ds(pl.multiple_of(owner * depth, depth), depth)
        fold(mine.at[:, rows], theirs.at[:, rows], arrival_x + owner)
        if k:
            copy(mine.at[:, rows], place(c, f), slot + k, arrival_y + f, {"fsdp": owner}).start()
        else:
            keep(mine.at[:, rows], place(c, f))
            start_line(index)

    def from_owner(k, place, arrival, index):
        arrived(place(c, origins[k]), arrival + origins[k])
        start_line(index)

    def feed_steps():
        yield lambda: whole_item(0, down_v, down_x, 8, down_at, 0)

        def first():
            home_wait(1, gate_v)
            to_owner(1, gate_v, gate_x, gate_at, 0, 10, 10, 1)

        yield first
        for k in (2, 3, 0):
            yield functools.partial(to_owner, k, gate_v, gate_x, gate_at, 0, 10, 10, 1)
        for k in range(1, 4):
            yield functools.partial(from_owner, k, gate_at, 10, 1 + k)

    def mix_steps():
        yield lambda: whole_item(2, out_v, out_x, 9, out_at, 5)

        def first():
            home_wait(3, mix_v)
            to_owner(1, mix_v, mix_x, mix_at, 4, 14, 14, 6)

        yield first
        for k in (2, 3, 0):
            yield functools.partial(to_owner, k, mix_v, mix_x, mix_at, 4, 14, 14, 6)
        for k in range(1, 4):
            yield functools.partial(from_owner, k, mix_at, 14, 6 + k)

    def sum_gains():
        targets = [other, {"fsdp": f + 1 - 2 * lax.rem(f, 2)}, {"fsdp": f + 2 - 4 * (f // 2)},
                   {"ctx": c + 1 - 2 * lax.rem(c, 2)}, {"ctx": lax.rem(c + 2, 4)}]
        copies = []
        for k, target in enumerate(targets):
            one = copy(gain_v.at[k], gain_x.at[k], 18 + k, 18 + k, target)
            one.start()
            one.wait_recv()
            copies.append(one)
            if k < 4:
                gain_v[k + 1] = gain_v[k] + gain_x[k]
            else:
                gain_out[...] = gain_v[k] + gain_x[k]
        for one in copies:
            one.wait_send()

    def along_line():
        order = near_order(c)
        forwards = []
        for step in range(1, 4):
            d = order[step]
            for index in range(10):
                one = line(index, d, 20 + (step - 1) * 10 + index, jnp.where(d < c, above, below))
                one.wait_recv()
                pl.when(inner)(one.start)
                forwards.append(one)
        for index in range(10):
            pl.when(c < 3)(line(index, c, index, above).wait_send)
            pl.when(c > 0)(line(index, c, 10 + index, below).wait_send)
        for one in forwards:
            pl.when(inner)(one.wait_send)
        for k in range(4):
            gate_rows = gate_x.at[:, rows_of(k)]
            mix_rows = mix_x.at[:, rows_of(k)]
            copy(gate_rows, gate_rows, k, 0, other).wait_send()
            copy(mix_rows, mix_rows, 4 + k, 0, other).wait_send()
            if k:
                copy(gate_rows, gate_rows, 10 + k, 0, other).wait_send()
                copy(mix_rows, mix_rows, 14 + k, 0, other).wait_send()
        copy(down_x, down_x, 8, 0, other).wait_send()
        copy(out_x, out_x, 9, 0, other).wait_send()

    return begin_feed, begin_mix, feed_steps, mix_steps, sum_gains, along_line


def widen_kernel(mix, gate, out, down, mix_f, gate_f, out_f, down_f):
    rows = mix.shape[1]

    def choice(count, wanted):
        lane = lax.broadcasted_iota(jnp.int32, (count, 4 * HEAD), 0)
        column = lax.broadcasted_iota(jnp.int32, (count, 4 * HEAD), 1)
        return jnp.where(lane == wanted(column // HEAD, lax.rem(column, HEAD)), 1.0, 0.0).astype(BF)

    def halves(place):
        half = place // (HEAD // 2)
        return half * SPAN + place - half * (HEAD // 2)

    queries = choice(4 * LANES, lambda head, place: head * LANES + halves(place))
    keys = choice(8 * LANES, lambda head, place: 2 * head * LANES + halves(place))
    values = choice(8 * LANES, lambda head, place: (2 * head + 1) * LANES + place)
    width = 4 * 4 * HEAD
    for g in range(4):
        mix_f[:, g * 4 * HEAD : (g + 1) * 4 * HEAD] = kernel_dot(mix[0, :, g * 4 * LANES : (g + 1) * 4 * LANES], queries)
    for g in range(2):
        slots = mix[1, :, g * 8 * LANES : (g + 1) * 8 * LANES]
        at = width + g * 4 * HEAD
        mix_f[:, at : at + 4 * HEAD] = kernel_dot(slots, keys)
        at = width + (g + 2) * 4 * HEAD
        mix_f[:, at : at + 4 * HEAD] = kernel_dot(slots, values)
    half = gate.shape[2]
    gate_f[:, :half] = gate[0].astype(F32)
    gate_f[:, half:] = gate[1].astype(F32)
    out_f[...] = out[...].astype(F32)
    down_f[...] = down[...].astype(F32)


def widen_call(mix, gate, out, down):
    steps = 8
    depth = mix.shape[1]
    width = out.shape[1]
    rows = depth // steps
    down_rows = down.shape[0] // steps
    return pl.pallas_call(
        widen_kernel,
        grid=(steps,),
        out_shape=(
            jax.ShapeDtypeStruct((depth, 2 * width), F32),
            jax.ShapeDtypeStruct((depth, 2 * gate.shape[2]), F32),
            jax.ShapeDtypeStruct(out.shape, F32),
            jax.ShapeDtypeStruct(down.shape, F32),
        ),
        in_specs=[
            pl.BlockSpec((2, rows, mix.shape[2]), lambda i: (0, i, 0)),
            pl.BlockSpec((2, rows, gate.shape[2]), lambda i: (0, i, 0)),
            pl.BlockSpec((rows, width), lambda i: (i, 0)),
            pl.BlockSpec((down_rows, width), lambda i: (i, 0)),
        ],
        out_specs=(
            pl.BlockSpec((rows, 2 * width), lambda i: (i, 0)),
            pl.BlockSpec((rows, 2 * gate.shape[2]), lambda i: (i, 0)),
            pl.BlockSpec((rows, width), lambda i: (i, 0)),
            pl.BlockSpec((down_rows, width), lambda i: (i, 0)),
        ),
        compiler_params=pltpu.CompilerParams(vmem_limit_bytes=48 << 20),
    )(mix, gate, out, down)


def on_line():
    return lax.axis_size("ctx") == 4 and lax.axis_size("fsdp") == 4


def gather(own):
    return lax.all_gather(own, ("ctx", "fsdp"), axis=0, tiled=True)


def scatter(part):
    return lax.psum_scatter(part, ("ctx", "fsdp"), scatter_dimension=0, tiled=True)


def spread_halves(columns):
    halves = columns.reshape(columns.shape[:-1] + (2, HEAD // 2))
    halves = jnp.pad(halves, [(0, 0)] * (halves.ndim - 1) + [(0, SPAN - HEAD // 2)])
    return halves.reshape(columns.shape[:-1] + (LANES,))


def join_halves(columns):
    halves = columns.reshape(columns.shape[:-1] + (2, SPAN))[..., : HEAD // 2]
    return halves.reshape(columns.shape[:-1] + (HEAD,))


def angle_tables(positions):
    frequency = rope_base ** (-(jnp.arange(HEAD // 2, dtype=F32) * 2.0 / HEAD))
    frequency = jnp.pad(frequency, (0, SPAN - HEAD // 2))
    angles = positions.astype(F32)[:, None] * frequency[None, :]
    cosine = jnp.cos(angles)
    sine = jnp.sin(angles)
    return jnp.concatenate([cosine, cosine], axis=1), jnp.concatenate([-sine, sine], axis=1)


def rotate(values, cosine, sine):
    return values * cosine + jnp.roll(values, SPAN, axis=1) * sine


def rotate_back(grads, cosine, sine):
    return grads * cosine - jnp.roll(grads, SPAN, axis=1) * sine


def norm_rows(values):
    return lax.rsqrt(jnp.mean(values * values, axis=-1, keepdims=True) + norm_eps)


def norm_back(grad_out, values, factor, gain):
    shaped = grad_out * gain
    common = jnp.mean(shaped * values, axis=-1, keepdims=True)
    grad_in = factor * shaped - values * (factor * factor * factor) * common
    return grad_in, jnp.sum(grad_out * values * factor, axis=0)


def dot(left, right):
    return jnp.dot(left, right, preferred_element_type=F32)


def dot_nt(left, right):
    return lax.dot_general(left, right, (((1,), (1,)), ((), ())), preferred_element_type=F32)


def dot_tn(left, right):
    return lax.dot_general(left, right, (((0,), (0,)), ((), ())), preferred_element_type=F32)


class Plan:
    def __init__(self, width, hidden_units):
        self.c = lax.axis_index("ctx")
        self.f = lax.axis_index("fsdp")
        self.C = lax.axis_size("ctx")
        self.F = lax.axis_size("fsdp")
        self.heads = width // HEAD
        self.ratio = self.heads // KV_HEADS
        self.heads_f = self.heads // self.F
        self.groups_f = KV_HEADS // self.F
        self.share = self.C // self.heads_f
        self.units = hidden_units // (self.F * self.C)
        self.local_head = self.c // self.share
        self.part = self.c % self.share


def pick(array, index, axis):
    return lax.dynamic_index_in_dim(array, index, axis, keepdims=False)


def pack_weights(plan, mix, gate_up):
    depth = mix.shape[0]
    width = plan.heads * HEAD
    kv_width = KV_HEADS * HEAD
    F = plan.F
    queries = pick(mix[:, :width].reshape(depth, F, plan.heads_f, HEAD), plan.local_head, 2)
    group = plan.local_head // plan.ratio
    keys = pick(mix[:, width : width + kv_width].reshape(depth, F, plan.groups_f, HEAD), group, 2)
    values = pick(mix[:, width + kv_width :].reshape(depth, F, plan.groups_f, HEAD), group, 2)
    values = jnp.pad(values, ((0, 0), (0, 0), (0, LANES - HEAD)))
    half = gate_up.shape[1] // 2
    gate = pick(gate_up[:, :half].reshape(depth, F, plan.C, plan.units), plan.c, 2)
    up = pick(gate_up[:, half:].reshape(depth, F, plan.C, plan.units), plan.c, 2)
    packed = jnp.concatenate([spread_halves(queries), spread_halves(keys), values, gate, up], axis=2)
    return jnp.swapaxes(packed, 0, 1)


def attend(plan, q_part, k, v, positions, part_positions):
    scores = dot_nt(q_part, k) * HEAD ** (-0.5)
    allowed = positions[None, :] <= part_positions[:, None]
    scores = jnp.where(allowed, scores, masked_value)
    top = jnp.max(scores, axis=-1, keepdims=True)
    weights = jnp.exp(scores - top)
    total = jnp.sum(weights, axis=-1, keepdims=True)
    context = dot((weights / total).astype(BF), v)
    return context.astype(BF), top + jnp.log(total)


def attend_back(q_part, k, v, context_grad, context, log_total, positions, part_positions):
    scale = HEAD ** (-0.5)
    common = jnp.sum(context_grad.astype(F32) * context.astype(F32), axis=-1, keepdims=True)
    allowed = positions[None, :] <= part_positions[:, None]
    scores = dot_nt(q_part, k) * scale
    weights = jnp.exp(jnp.where(allowed, scores, masked_value) - log_total)
    weight_grad = dot_nt(context_grad, v)
    score_grad = (weights * (weight_grad - common)).astype(BF)
    value_grad = dot_tn(weights.astype(BF), context_grad)
    key_grad = dot_tn(score_grad, q_part) * scale
    query_grad = dot(score_grad, k) * scale
    return query_grad, key_grad, value_grad


def forward_layer(plan, x_own, weights, gains, positions, part_positions, tables):
    mix_cut, gate_cut, out, down = weights
    cosine, sine = tables
    length = positions.shape[0]
    x_all = gather(x_own)
    x32 = x_all.astype(F32)
    factor = norm_rows(x32)
    normed = (x32 * factor * gains[0]).astype(BF)
    mixed = dot(normed, mix_cut)
    q = rotate(mixed[:, :LANES], cosine, sine).astype(BF)
    k = rotate(mixed[:, LANES : 2 * LANES], cosine, sine).astype(BF)
    v = mixed[:, 2 * LANES :].astype(BF)
    rows = length // plan.share
    start = plan.part * rows
    q_part = lax.dynamic_slice_in_dim(q, start, rows, 0)
    context, log_total = attend(plan, q_part, k, v, positions, part_positions)
    partial = dot(context[:, :HEAD], out).astype(BF)
    if plan.share > 1:
        partial = lax.dynamic_update_slice_in_dim(
            jnp.zeros((length, partial.shape[1]), BF), partial, start, 0
        )
    middle = x_own.astype(F32) + scatter(partial)
    factor_two = norm_rows(middle)
    normed_two = gather((middle * factor_two * gains[1]).astype(BF))
    both = dot(normed_two, gate_cut)
    hidden = (jax.nn.silu(both[:, : plan.units]) * both[:, plan.units :]).astype(BF)
    result = middle + scatter(dot(hidden, down).astype(BF))
    kept = (x_own, normed, q_part, k, v, context, log_total, middle, normed_two, both, hidden)
    return result.astype(BF), kept


def backward_layer(plan, grad_own, weights, gains, kept, positions, part_positions, tables, part_tables):
    mix_cut, gate_cut, out, down = weights
    x_own, normed, q_part, k, v, context, log_total, middle, normed_two, both, hidden = kept
    length = positions.shape[0]
    rows = length // plan.share
    start = plan.part * rows
    grad_all = gather(grad_own)
    hidden_grad = dot_nt(grad_all, down)
    gate = both[:, : plan.units]
    up = both[:, plan.units :]
    sig = jax.nn.sigmoid(gate)
    gate_grad = hidden_grad * up * sig * (1.0 + gate * (1.0 - sig))
    up_grad = hidden_grad * gate * sig
    both_grad = jnp.concatenate([gate_grad, up_grad], axis=1).astype(BF)
    normed_two_grad = scatter(dot_nt(both_grad, gate_cut).astype(BF))
    middle_grad, feed_gain_grad = norm_back(normed_two_grad, middle, norm_rows(middle), gains[1])
    middle_grad = middle_grad + grad_own.astype(F32)
    middle_low = gather(middle_grad.astype(BF))
    middle_part = lax.dynamic_slice_in_dim(middle_low, start, rows, 0)
    context_grad = jnp.pad(dot_nt(middle_part, out), ((0, 0), (0, LANES - HEAD))).astype(BF)
    query_grad, key_grad, value_grad = attend_back(
        q_part, k, v, context_grad, context, log_total, positions, part_positions
    )
    query_grad = rotate_back(query_grad, *part_tables).astype(BF)
    if plan.share > 1:
        query_grad = lax.dynamic_update_slice_in_dim(
            jnp.zeros((length, LANES), BF), query_grad, start, 0
        )
    key_grad = rotate_back(key_grad, *tables).astype(BF)
    mixed_grad = jnp.concatenate([query_grad, key_grad, value_grad.astype(BF)], axis=1)
    normed_grad = scatter(dot_nt(mixed_grad, mix_cut).astype(BF))
    x32 = x_own.astype(F32)
    start_grad, attention_gain_grad = norm_back(normed_grad, x32, norm_rows(x32), gains[0])
    start_grad = start_grad + middle_grad
    mix_grad = jnp.stack(
        [dot_tn(normed, part).astype(BF) for part in (query_grad, key_grad, value_grad.astype(BF))]
    )
    gate_cut_grad = jnp.stack(
        [dot_tn(normed_two, part.astype(BF)).astype(BF) for part in (gate_grad, up_grad)]
    )
    out_grad = dot_tn(context, middle_part).astype(BF)[:HEAD]
    down_grad = dot_tn(hidden, grad_all).astype(BF)
    return start_grad, (mix_grad, gate_cut_grad, out_grad, down_grad), jnp.stack([attention_gain_grad, feed_gain_grad])


def swap_sections(array):
    return lax.ppermute(array, "section", [(0, 1), (1, 0)])


def by_layer_of(section, own, other):
    first = section == 0
    return jnp.where(first, own, other), jnp.where(first, other, own)


def shared_weights(plan, section, attention_gain, query_key_value, output_weight, feed_gain, gate_up, down_weight):
    depth = query_key_value.shape[1]
    width = depth * plan.F
    gains = lax.all_gather(
        jnp.stack([attention_gain[0], feed_gain[0]]), ("section", "fsdp"), axis=0, tiled=False
    )
    gains = gains.reshape(2, plan.F, 2, depth)
    gains = jnp.swapaxes(gains, 1, 2).reshape(2, 2, width).astype(F32)
    packed = pack_weights(plan, query_key_value[0], gate_up[0])
    own_cut = lax.all_to_all(packed, "fsdp", 0, 0).reshape(width, -1)
    own_out = lax.dynamic_slice_in_dim(output_weight[0], plan.local_head * HEAD, HEAD, 0)
    own_down = lax.dynamic_slice_in_dim(down_weight[0], plan.c * plan.units, plan.units, 0)
    cuts = by_layer_of(section, own_cut, swap_sections(own_cut))
    outs = by_layer_of(section, own_out, swap_sections(own_out))
    downs = by_layer_of(section, own_down, swap_sections(own_down))
    weights = [(cuts[s][:, : 3 * LANES], cuts[s][:, 3 * LANES :], outs[s], downs[s]) for s in range(2)]
    return weights, gains


def own_gain_sums(plan, section, gain_sum, depth):
    gain_sum = lax.dynamic_slice_in_dim(gain_sum, 2 * section, 2, 0)
    return lax.dynamic_slice_in_dim(gain_sum, plan.f * depth, depth, 1)


def returned_grads(plan, section, weight_grads, gain_grads, depth):
    C, F = plan.C, plan.F
    gain_sum = jnp.concatenate([gain_grads[0], gain_grads[1]])

    def collected(index):
        first, second = weight_grads[0][index], weight_grads[1][index]
        own = jnp.where(section == 0, first, second)
        away = jnp.where(section == 0, second, first)
        return (own.astype(F32) + swap_sections(away).astype(F32)).astype(BF)

    cut_grad = jnp.concatenate(list(collected(0)) + list(collected(1)), axis=1)
    cut_grad = lax.all_to_all(cut_grad.reshape(F, depth, -1), "fsdp", 0, 0)
    cut_grad = lax.all_gather(cut_grad, "ctx", axis=0, tiled=False)
    out_grad = lax.all_gather(collected(2), "ctx", axis=0, tiled=False)
    down_grad = lax.all_gather(collected(3), "ctx", axis=0, tiled=True).astype(F32)

    def heads_of(columns, count):
        folded = columns.astype(F32).reshape(count, C // count, F, depth, columns.shape[-1]).sum(axis=1)
        return jnp.transpose(folded, (2, 1, 0, 3))

    q_grad = join_halves(heads_of(cut_grad[..., :LANES], plan.heads_f)).reshape(depth, -1)
    k_grad = join_halves(heads_of(cut_grad[..., LANES : 2 * LANES], plan.groups_f)).reshape(depth, -1)
    v_grad = heads_of(cut_grad[..., 2 * LANES : 3 * LANES], plan.groups_f)[..., :HEAD].reshape(depth, -1)
    mix_grad = jnp.concatenate([q_grad, k_grad, v_grad], axis=1)
    both = jnp.transpose(cut_grad[..., 3 * LANES :], (2, 1, 0, 3)).astype(F32)
    gate_up_grad = jnp.concatenate(
        [both[..., : plan.units].reshape(depth, -1), both[..., plan.units :].reshape(depth, -1)], axis=1
    )
    out_grad = out_grad.astype(F32).reshape(plan.heads_f, plan.share, HEAD, depth * F).sum(axis=1).reshape(-1, depth * F)

    gain_sum = lax.psum(gain_sum, ("section", "ctx", "fsdp"))
    return mix_grad, gate_up_grad, out_grad, down_grad, own_gain_sums(plan, section, gain_sum, depth)


def on_device(
    inputs, cotangent, attention_gain, query_key_value, output_weight, feed_gain, gate_up, down_weight, block_order
):
    section = lax.axis_index("section")
    width = inputs.shape[2]
    hidden_units = down_weight.shape[1] * lax.axis_size("fsdp")
    plan = Plan(width, hidden_units)
    rows = inputs.shape[1]
    C, F = plan.C, plan.F
    length = rows * C * F
    depth = query_key_value.shape[1]

    def by_layer(own, other):
        first = section == 0
        return jnp.where(first, own, other), jnp.where(first, other, own)

    order = pick(block_order, section, 0)
    positions = (order[:, None] * rows + jnp.arange(rows, dtype=jnp.int32)[None, :]).reshape(length)
    part_rows = length // plan.share
    part_positions = lax.dynamic_slice_in_dim(positions, plan.part * part_rows, part_rows, 0)
    tables = angle_tables(positions)
    part_tables = angle_tables(part_positions)

    x = pick(inputs, section, 0)
    grad = pick(cotangent, section, 0)
    results = []
    input_grads = [None, None]
    weight_grads = [None, None]
    gain_grads = [None, None]
    kept = []
    if on_line():
        own_gains = jnp.pad(jnp.concatenate([attention_gain, feed_gain]), ((0, 14), (0, 0)))
        shards = (query_key_value, output_weight, gate_up, down_weight, own_gains)
        common = tuple(tables) + (positions[:, None], positions[None, :])
        first = forward_call(0, x, shards, common)
        weights = first[10:]
        results.append(first[9])
        second = forward_call(1, first[9], weights, common)
        results.append(second[9])
        input_grads[1], *old, grad = backward_call(1, grad, weights, common, [first[9], *second[:9]])
        input_grads[0], *wide, gain_sum = backward_call(0, grad, weights, common, [x, *first[:9]], old)
        mix_grad, gate_up_grad, out_grad, down_grad = widen_call(*wide)
        gain_sum = own_gain_sums(plan, section, gain_sum, depth)
    else:
        weights, gains = shared_weights(
            plan, section, attention_gain, query_key_value, output_weight, feed_gain, gate_up, down_weight
        )
        for s in range(2):
            x, keep = forward_layer(plan, x, weights[s], gains[s], positions, part_positions, tables)
            kept.append(keep)
            results.append(x)
        for s in (1, 0):
            input_grads[s], weight_grads[s], gain_grads[s] = backward_layer(
                plan, grad, weights[s], gains[s], kept[s], positions, part_positions, tables, part_tables
            )
            grad = input_grads[s].astype(BF)
        shard_grads = returned_grads(plan, section, weight_grads, gain_grads, depth)
        mix_grad, gate_up_grad, out_grad, down_grad, gain_sum = shard_grads

    def mine_and_theirs(first, second):
        return jnp.where(section == 0, first, second), jnp.where(section == 0, second, first)

    def by_batch(first, second):
        own, away = mine_and_theirs(first, second)
        return jnp.stack(by_layer(own, swap_sections(away)))

    section_outputs = by_batch(*results)
    section_input_grads = by_batch(*input_grads)

    return (
        section_outputs[None],
        section_input_grads[None],
        gain_sum[0][None],
        mix_grad[None],
        out_grad[None],
        gain_sum[1][None],
        gate_up_grad[None],
        down_grad[None],
    )


def solution(mesh):
    placed = (
        P(None, ("ctx", "fsdp"), None),
        P(None, ("ctx", "fsdp"), None),
        P("section", "fsdp"),
        P("section", "fsdp", None),
        P("section", "fsdp", None),
        P("section", "fsdp"),
        P("section", "fsdp", None),
        P("section", "fsdp", None),
        P(),
    )
    return jax.shard_map(
        on_device,
        mesh=mesh,
        in_specs=placed,
        out_specs=(
            P("section", None, ("ctx", "fsdp"), None),
            P("section", None, ("ctx", "fsdp"), None),
            P("section", "fsdp"),
            P("section", "fsdp", None),
            P("section", "fsdp", None),
            P("section", "fsdp"),
            P("section", "fsdp", None),
            P("section", "fsdp", None),
        ),
        check_vma=False,
    )
```

```python
import functools

import jax
import jax.numpy as jnp
from jax import lax
from jax.experimental import pallas as pl
from jax.experimental.pallas import tpu as pltpu
from jax.sharding import PartitionSpec as P

KV_HEADS = 8
HEAD = 96
LANES = 128
SPAN = 64
norm_eps = 1e-05
rope_base = 100000.0
masked_value = -1e30
BF = jnp.bfloat16
F32 = jnp.float32

MESH = pl.DeviceIdType.MESH


def greet():
    c = lax.axis_index("ctx")
    f = lax.axis_index("fsdp")
    barrier = pltpu.get_barrier_semaphore()
    inner = jnp.logical_and(c > 0, c < 3)
    for peer in (f + 2 - 4 * (f // 2), f + 1 - 2 * lax.rem(f, 2)):
        pl.semaphore_signal(barrier, inc=1, device_id={"fsdp": peer}, device_id_type=MESH)
    pl.semaphore_signal(barrier, inc=1, device_id={"ctx": lax.rem(c + 2, 4)}, device_id_type=MESH)

    @pl.when(c < 3)
    def _():
        pl.semaphore_signal(barrier, inc=1, device_id={"ctx": c + 1}, device_id_type=MESH)

    @pl.when(c > 0)
    def _():
        pl.semaphore_signal(barrier, inc=1, device_id={"ctx": c - 1}, device_id_type=MESH)

    @pl.when(inner)
    def _():
        pl.semaphore_wait(barrier, 5)

    @pl.when(jnp.logical_not(inner))
    def _():
        pl.semaphore_wait(barrier, 4)


def near_order(c):
    low = c < 2
    return [c, c + 1 - 2 * lax.rem(c, 2), jnp.where(low, 2, 1), jnp.where(low, 3, 0)]


def own_block(c, f):
    return c * 4 + lax.rem(f, 2) * 2 + f // 2


def gather_rows(whole, rows, send, recv, ready=None, started=None):
    c = lax.axis_index("ctx")
    f = lax.axis_index("fsdp")
    y = f // 2
    lane = lax.rem(f, 2)
    inner = jnp.logical_and(c > 0, c < 3)
    outer = jnp.logical_not(inner)
    order = near_order(c)
    pair = order[1]
    half = rows // 2
    to_across = {"fsdp": f + 2 - 4 * y}
    to_twin = {"fsdp": f + 1 - 2 * lane}
    to_pair = {"ctx": pair}

    def at(d, k, yy, h):
        return whole.at[pl.ds(pl.multiple_of((d * 4 + k * 2 + yy) * rows + h * half, half), half)]

    def block(d, k, yy):
        return whole.at[pl.ds(pl.multiple_of((d * 4 + k * 2 + yy) * rows, rows), rows)]

    def two(d, k):
        return whole.at[pl.ds(pl.multiple_of((d * 4 + k * 2) * rows, rows), 2 * rows)]

    def copy(src, slot, arrival, peer):
        return pltpu.make_async_remote_copy(
            src, src, send.at[slot], recv.at[arrival], device_id=peer, device_id_type=MESH
        )

    def go(src, slot, arrival, peer, when=None):
        one = copy(src, slot, arrival, peer)
        if when is None:
            one.start()
        else:
            pl.when(when)(one.start)

    def arrived(ref, arrival):
        copy(ref, 0, arrival, to_twin).wait_recv()

    def gone(count, slot):
        copy(whole.at[pl.ds(0, count * half)], slot, 0, to_twin).wait_send()

    for h in range(2):
        go(at(c, lane, y, h), 0, 2 * c + h, {"ctx": jnp.minimum(c + 1, 3)}, c < 3)
        go(at(c, lane, y, h), 1, 2 * c + h, {"ctx": jnp.maximum(c - 1, 0)}, c > 0)
        go(at(c, lane, y, h), 3, 8 + c, to_across)
    if started is not None:
        started()

    events = [
        (pair, 0),
        (jnp.where(inner, order[2], pair), jnp.where(inner, 0, 1)),
        (jnp.where(inner, pair, order[2]), jnp.where(inner, 1, 0)),
        (order[2], 1),
        (order[3], 0),
        (order[3], 1),
    ]

    def along(index):
        d, h = events[index]
        piece = at(d, lane, y, h)
        arrived(piece, 2 * d + h)
        go(piece, 2, 2 * d + h, {"ctx": jnp.where(d < c, c + 1, c - 1)}, inner)
        go(piece, 3, 8 + d, to_across, jnp.logical_or(d != pair, h == 0) if index in (1, 2) else None)

    def complete(d):
        arrived(two(d, 1 - lane), 13 + d)
        if ready is not None:
            ready(d)

    def pair_half(when):
        go(at(c, lane, 1 - y, 1), 4, 12, to_pair, when)

    along(0)
    along(1)
    along(2)
    arrived(block(c, lane, 1 - y), 8 + c)
    pair_half(outer)
    go(two(c, lane), 5, 13 + c, to_twin)
    along(3)
    complete(c)
    along(4)
    along(5)
    pair_half(inner)
    arrived(block(order[2], lane, 1 - y), 8 + order[2])
    go(two(order[2], lane), 5, 13 + order[2], to_twin)
    go(block(order[3], lane, y), 5, 13 + order[3], to_twin)
    complete(order[2])
    arrived(at(pair, lane, 1 - y, 0), 8 + pair)
    arrived(at(pair, lane, 1 - y, 1), 12)
    go(two(pair, lane), 5, 13 + pair, to_twin)
    arrived(block(order[3], lane, 1 - y), 8 + order[3])
    go(block(order[3], lane, 1 - y), 5, 17, to_twin)
    complete(pair)
    arrived(block(order[3], 1 - lane, y), 13 + order[3])
    arrived(block(order[3], 1 - lane, 1 - y), 17)
    if ready is not None:
        ready(order[3])
    pl.when(c < 3)(lambda: gone(2, 0))
    pl.when(c > 0)(lambda: gone(2, 1))
    pl.when(inner)(lambda: gone(6, 2))
    gone(7, 3)
    gone(1, 4)
    gone(16, 5)


GATHER_SENDS = 6
GATHER_RECVS = 18


def scatter_sum(part, total, land, send, recv, produce=None, meanwhile=None):
    c = lax.axis_index("ctx")
    f = lax.axis_index("fsdp")
    y = f // 2
    lane = lax.rem(f, 2)
    inner = jnp.logical_and(c > 0, c < 3)
    rows = total.shape[0]
    half = rows // 2
    order = near_order(c)[::-1]
    to_across = {"fsdp": f + 2 - 4 * y}
    to_twin = {"fsdp": f + 1 - 2 * lane}
    to_pair = {"ctx": order[2]}

    def rows_at(d, yy, h):
        return pl.ds(pl.multiple_of((d * 4 + lane * 2 + yy) * rows + h * half, half), half)

    def copy(src, dst, slot, arrival, peer):
        return pltpu.make_async_remote_copy(
            src, dst, send.at[slot], recv.at[arrival], device_id=peer, device_id_type=MESH
        )

    def go(src, dst, slot, arrival, peer):
        copy(src, dst, slot, arrival, peer).start()

    def gone(count, slot):
        ref = part.at[pl.ds(0, count * half)]
        copy(ref, ref, slot, 0, to_twin).wait_send()

    def piece(slot, h):
        return land.at[slot, pl.ds(h * half, half)]

    def landed(ref, arrival):
        copy(ref, ref, 0, arrival, to_twin).wait_recv()
        return ref[...].astype(F32)

    def begin(step):
        d = order[step]
        if produce is not None:
            produce(d)
        for yy, slot in ((1 - y, step), (y, 27 + step)):
            other = pl.ds(pl.multiple_of((d * 4 + 2 - lane * 2 + yy) * rows, rows), rows)
            go(part.at[other], land.at[2 * step + yy], 0, slot, to_twin)

    def twin_there(step, yy, slot):
        ref = land.at[2 * step + yy]
        copy(ref, ref, 0, slot, to_twin).wait_recv()

    def over(step, h, first=False):
        d = order[step]
        if first:
            twin_there(step, 1 - y, step)
        mine = rows_at(d, 1 - y, h)
        value = part[mine, :].astype(F32) + piece(2 * step + 1 - y, h)[...].astype(F32)
        if (step, h) == (3, 1):
            value = value + landed(piece(17, 0), 26)
        part[mine, :] = value.astype(BF)
        if (step, h) == (2, 1):
            go(part.at[mine], piece(17, 0), 3, 26, to_pair)
        else:
            go(part.at[mine], piece(8 + step, h), 1, 8 + 2 * step + h, to_across)

    def onward(step, h, first=False):
        d = order[step]
        mine = rows_at(d, y, h)
        if first:
            twin_there(step, y, 27 + step)
        value = part[mine, :].astype(F32) + piece(2 * step + y, h)[...].astype(F32)
        if (step, h) != (2, 1):
            value = value + landed(piece(8 + step, h), 8 + 2 * step + h)
        if step == 3:
            total[h * half : (h + 1) * half, :] = value
            return
        part[mine, :] = value.astype(BF)

        if step < 2:

            @pl.when(inner)
            def _():
                part[mine, :] = (part[mine, :].astype(F32) + landed(piece(12 + d, h), 16 + 2 * d + h)).astype(BF)

        here = jnp.logical_and(d < c, d == c - 1)
        target = jnp.where(d > c, c + 1, c - 1)
        slot = jnp.where(here, 16, 12 + d)
        arrival = jnp.where(here, 24, 16 + 2 * d) + h
        if step == 0:
            target = jnp.where(inner, d, target)
            slot = jnp.where(inner, 18, slot)
            arrival = jnp.where(inner, 31 + h, arrival)
        go(part.at[mine], piece(slot, h), 2, arrival, {"ctx": target})

    begin(0)
    over(0, 0, True)
    over(0, 1)
    begin(1)
    begin(2)
    over(2, 1, True)
    over(1, 0, True)
    onward(0, 0, True)
    over(1, 1)
    onward(0, 1)
    if meanwhile is not None:
        meanwhile()
    begin(3)
    over(2, 0)
    onward(1, 0, True)
    over(3, 0, True)
    onward(1, 1)
    over(3, 1)
    onward(2, 1, True)
    onward(2, 0)
    for h in range(2):
        onward(3, h, h == 0)

        @pl.when(c > 0)
        def _():
            total[h * half : (h + 1) * half, :] += landed(piece(12 + c, h), 16 + 2 * c + h)

        @pl.when(c < 3)
        def _():
            total[h * half : (h + 1) * half, :] += landed(piece(16, h), 24 + h)

        @pl.when(jnp.logical_not(inner))
        def _():
            total[h * half : (h + 1) * half, :] += landed(piece(18, h), 31 + h)

    gone(16, 0)
    gone(7, 1)
    gone(6, 2)
    gone(1, 3)


SCATTER_SENDS = 4
SCATTER_RECVS = 33


def kernel_dot(left, right):
    return jnp.dot(left, right, preferred_element_type=F32)


def kernel_dot_nt(left, right):
    return lax.dot_general(left, right, (((1,), (1,)), ((), ())), preferred_element_type=F32)


def kernel_dot_tn(left, right):
    return lax.dot_general(left, right, (((0,), (0,)), ((), ())), preferred_element_type=F32)


def turn(values):
    return pltpu.roll(values, SPAN, axis=1)


def mean_square(values):
    return lax.rsqrt(jnp.mean(values * values, axis=-1, keepdims=True) + norm_eps)


def greet_all(peers):
    barrier = pltpu.get_barrier_semaphore()
    for peer in peers:
        pl.semaphore_signal(barrier, inc=1, device_id=peer, device_id_type=MESH)
    return len(peers)


def greet_more(peers):
    c = lax.axis_index("ctx")
    barrier = pltpu.get_barrier_semaphore()
    count = greet_all(peers)
    inner = jnp.logical_and(c > 0, c < 3)

    @pl.when(c < 3)
    def _():
        pl.semaphore_signal(barrier, inc=1, device_id={"ctx": c + 1}, device_id_type=MESH)

    @pl.when(c > 0)
    def _():
        pl.semaphore_signal(barrier, inc=1, device_id={"ctx": c - 1}, device_id_type=MESH)

    @pl.when(inner)
    def _():
        pl.semaphore_wait(barrier, count + 2)

    @pl.when(jnp.logical_not(inner))
    def _():
        pl.semaphore_wait(barrier, count + 1)


def head_choice(value_part):
    source = lax.broadcasted_iota(jnp.int32, (4 * HEAD, 4 * LANES), 0)
    lane = lax.broadcasted_iota(jnp.int32, (4 * HEAD, 4 * LANES), 1)
    head = lane // LANES
    inside = lane - head * LANES
    if value_part:
        wanted = jnp.where(inside < HEAD, head * HEAD + inside, -1)
    else:
        half = inside // SPAN
        place = inside - half * SPAN
        wanted = jnp.where(place < HEAD // 2, head * HEAD + half * (HEAD // 2) + place, -1)
    return jnp.where(source == wanted, 1.0, 0.0).astype(BF)


class Share:
    def __init__(self, sources, targets, scratch, sems):
        self.mix, self.out, self.gate_up, self.down, self.gains = sources
        self.w_mix, self.w_gate, self.w_out, self.w_down, self.w_gains = targets
        self.mix_v, self.heads_v, self.gate_s, self.out_s, self.down_s = scratch
        self.local, self.send, self.recv = sems
        self.s = lax.axis_index("section")
        self.c = lax.axis_index("ctx")
        self.f = lax.axis_index("fsdp")
        self.other = 1 - self.s
        self.depth = self.mix.shape[1]
        self.units = self.w_down.shape[1]
        self.peers = [lax.rem(self.f + k, 4) for k in range(1, 4)]
        self.rows = pl.ds(pl.multiple_of(self.f * self.depth, self.depth), self.depth)
        self.pending = []

    def greeted(self):
        return (
            [{"fsdp": peer} for peer in self.peers]
            + [{"section": self.other}, {"ctx": lax.rem(self.c + 2, 4)}]
            + [{"section": self.other, "fsdp": peer} for peer in self.peers]
        )

    def copy(self, src, dst, slot, arrival, peer):
        return pltpu.make_async_remote_copy(
            src, dst, self.send.at[slot], self.recv.at[arrival], device_id=peer, device_id_type=MESH
        )

    def go(self, src, dst, slot, arrival, peer):
        one = self.copy(src, dst, slot, arrival, peer)
        one.start()
        self.pending.append(one)

    def keep(self, src, dst, slot):
        one = pltpu.make_async_copy(src, dst, self.local.at[slot])
        one.start()
        return one

    def load(self):
        self.loaded = self.keep(self.mix.at[0], self.mix_v, 0)
        out_rows = self.out.at[0, pl.ds(pl.multiple_of(self.c * HEAD, HEAD), HEAD)]
        down_rows = self.down.at[0, pl.ds(pl.multiple_of(self.c * self.units, self.units), self.units)]
        self.staged = [
            self.keep(self.gate_piece(self.f, part), self.gate_s.at[:, pl.ds(part * self.units, self.units)], 5 + part)
            for part in range(2)
        ]
        self.staged.append(self.keep(out_rows, self.out_s, 7))
        self.staged.append(self.keep(down_rows, self.down_s, 8))

    def lanes(self, peer, part):
        head = peer * 4 + self.c
        start = head * LANES if part == 0 else (16 + 8 * (part - 1) + head // 2) * LANES
        return self.heads_v.at[:, pl.ds(pl.multiple_of(start, LANES), LANES)]

    def put(self, part):
        return self.w_mix.at[self.s, self.rows, pl.ds(part * LANES, LANES)]

    def send_mix(self):
        self.loaded.wait()
        for g in range(8):
            self.heads_v[:, g * 4 * LANES : (g + 1) * 4 * LANES] = kernel_dot(
                self.mix_v[:, g * 4 * HEAD : (g + 1) * 4 * HEAD], head_choice(g >= 6)
            ).astype(BF)
        for k, peer in enumerate(self.peers):
            for part in range(3):
                self.copy(self.lanes(peer, part), self.put(part), k, self.f, {"fsdp": peer}).start()
        self.own_mix = [self.keep(self.lanes(self.f, part), self.put(part), 2 + part) for part in range(3)]
        for one in self.staged:
            one.wait()
        self.own_gate = self.keep(self.gate_s, self.slab(self.w_gate, self.f), 5)
        self.own_out = self.keep(self.out_s, self.w_out.at[self.s], 7)
        self.own_down = self.keep(self.down_s, self.w_down.at[self.s], 8)
        mine = self.w_gains.at[self.s, :, pl.ds(pl.multiple_of(self.f * self.depth, self.depth), self.depth)]
        for k, peer in enumerate(self.peers):
            self.go(self.gains, mine, 20 + k, 16 + 4 * self.s + self.f, {"fsdp": peer})
            self.go(self.gains, mine, 23 + k, 16 + 4 * self.s + self.f, {"section": self.other, "fsdp": peer})
        self.go(self.gains, mine, 26, 16 + 4 * self.s + self.f, {"section": self.other})
        self.own_gains = self.keep(self.gains, mine, 1)

    def gate_piece(self, peer, part):
        hidden_units = self.gate_up.shape[2] // 2
        start = pl.multiple_of(part * hidden_units + (peer * 4 + self.c) * self.units, self.units)
        return self.gate_up.at[0, :, pl.ds(start, self.units)]

    def gate_put(self, part):
        return self.w_gate.at[self.s, self.rows, pl.ds(part * self.units, self.units)]

    def send_gate(self):
        for k, peer in enumerate(self.peers):
            for part in range(2):
                self.copy(self.gate_piece(peer, part), self.gate_put(part), 3 + k, 4 + self.f, {"fsdp": peer}).start()

    def slab(self, ref, origin):
        return ref.at[self.s, pl.ds(pl.multiple_of(origin * self.depth, self.depth), self.depth)]

    def cross_slab(self, ref, k, slot, arrival, base):
        origin = lax.rem(self.f + 3 - k, 4)
        block = self.slab(ref, origin)
        self.copy(block, block, 0, arrival + origin, {"fsdp": origin}).wait_recv()
        self.go(block, block, slot + k, base + origin, {"section": self.other})

    def cross_mix(self):
        for one in self.own_mix:
            one.wait()
        self.go(self.slab(self.w_mix, self.f), self.slab(self.w_mix, self.f), 6, 8 + self.f, {"section": self.other})
        for k in range(3):
            self.cross_slab(self.w_mix, k, 7, 0, 8)
        self.send_gate()
        self.go(self.out_s, self.w_out.at[self.s], 10, 24, {"section": self.other})
        self.go(self.gate_s, self.slab(self.w_gate, self.f), 11, 12 + self.f, {"section": self.other})

    def cross_gate(self):
        for k in range(3):
            self.cross_slab(self.w_gate, k, 12, 4, 12)
        self.go(self.down_s, self.w_down.at[self.s], 15, 25, {"section": self.other})

    def there(self, ref, arrival):
        self.copy(ref, ref, 0, arrival, {"section": self.other}).wait_recv()

    def mix_there(self):
        for one in (self.own_gains, self.own_gate, self.own_out, self.own_down):
            one.wait()
        for origin in range(4):
            rows = pl.ds(origin * self.depth, self.depth)
            self.there(self.w_mix.at[self.other, rows], 8 + origin)
            self.there(self.w_gains.at[self.other, :, rows], 16 + 4 * self.other + origin)
        for k in range(3):
            origin = lax.rem(self.f + 3 - k, 4)
            columns = pl.ds(pl.multiple_of(origin * self.depth, self.depth), self.depth)
            self.there(self.w_gains.at[self.s, :, columns], 16 + 4 * self.s + origin)
        self.there(self.w_out.at[self.other], 24)

    def gate_there(self):
        for origin in range(4):
            self.there(self.w_gate.at[self.other, pl.ds(origin * self.depth, self.depth)], 12 + origin)

    def down_there(self):
        self.there(self.w_down.at[self.other], 25)

    def finish(self):
        for k, peer in enumerate(self.peers):
            block = self.slab(self.w_mix, self.f)
            self.copy(block, block, k, 0, {"fsdp": peer}).wait_send()
            block = self.slab(self.w_gate, self.f)
            self.copy(block, block, 3 + k, 0, {"fsdp": peer}).wait_send()
        for one in self.pending:
            one.wait_send()


class Loads:
    def __init__(self, sems):
        self.sems = sems
        self.copies = []

    def start(self, src, dst):
        one = pltpu.make_async_copy(src, dst, self.sems.at[len(self.copies)])
        one.start()
        self.copies.append(one)
        return one


def plane_rows(d, rows):
    return pl.ds(pl.multiple_of(d * 4 * rows, 4 * rows), 4 * rows)


def forward_body(layer, share, x_own, weights, tables, kept, scratch, sems):
    w_mix, w_gate, w_out, w_down, w_gains = weights
    cosine, sine, place_col, place_row = tables
    normed_o, q_o, k_o, v_o, context_o, log_o, middle_o, normed_two_o, both_o, result_o = kept
    (x_v, normed_v, q_v, k_v, v_v, context_v, log_v, middle_v, two_v, both_v, hidden_v, result_v,
     mix_v, gate_v, out_v, down_v, gains_v, part_v, land_a, land_b, total_v) = scratch
    local, save, send_a, recv_a, send_b, recv_b, send_c, recv_c, send_d, recv_d = sems
    c = lax.axis_index("ctx")
    f = lax.axis_index("fsdp")
    rows = x_own.shape[0]
    units = down_v.shape[0]
    own_rows = pl.ds(pl.multiple_of(own_block(c, f) * rows, rows), rows)
    loads = Loads(local)
    saves = Loads(save)
    load_x = loads.start(x_own, x_v.at[own_rows])
    out_v[...] = jnp.zeros_like(out_v)

    def load_first():
        return [
            loads.start(w_gains.at[layer], gains_v),
            loads.start(w_mix.at[layer], mix_v),
            loads.start(w_out.at[layer], out_v.at[pl.ds(0, HEAD)]),
        ]

    def project(d):
        here = plane_rows(d, rows)
        x = x_v[here, :].astype(F32)
        normed = (x * mean_square(x) * gains_v[0:1, :].astype(F32)).astype(BF)
        normed_v[here, :] = normed
        mixed = kernel_dot(normed, mix_v[...])
        cos = cosine[here, :]
        sin = sine[here, :]
        q = mixed[:, :LANES]
        k = mixed[:, LANES : 2 * LANES]
        q_v[here, :] = (q * cos + turn(q) * sin).astype(BF)
        k_v[here, :] = (k * cos + turn(k) * sin).astype(BF)
        v_v[here, :] = mixed[:, 2 * LANES :].astype(BF)

    if share is None:
        first = load_first()
        load_gate = loads.start(w_gate.at[layer], gate_v)
        load_down = loads.start(w_down.at[layer], down_v)
        greet()
        load_x.wait()
        for one in first:
            one.wait()
        gather_rows(x_v, rows, send_a, recv_a, project)
    else:
        share.load()
        greet_more(share.greeted())
        load_x.wait()
        share.send_mix()
        gather_rows(x_v, rows, send_a, recv_a, started=share.cross_mix)
        share.mix_there()
        first = load_first()
        for one in first:
            one.wait()
        for d in range(4):
            project(d)
        share.cross_gate()
    for src, dst in ((normed_v, normed_o), (q_v, q_o), (k_v, k_o), (v_v, v_o)):
        saves.start(src, dst)
    scale = HEAD ** (-0.5)

    def attention(d):
        here = plane_rows(d, rows)
        scores = kernel_dot_nt(q_v[here, :], k_v[...]) * scale
        allowed = place_row[...] <= place_col[here, :]
        scores = jnp.where(allowed, scores, masked_value)
        top = jnp.max(scores, axis=-1, keepdims=True)
        weights = jnp.exp(scores - top)
        amount = jnp.sum(weights, axis=-1, keepdims=True)
        context = (kernel_dot(weights.astype(BF), v_v[...]) / amount).astype(BF)
        context_v[here, :] = context
        log_v[here, :] = jnp.broadcast_to(top + jnp.log(amount), (4 * rows, LANES))
        part_v[here, :] = kernel_dot(context, out_v[...]).astype(BF)

    scatter_sum(part_v, total_v, land_a, send_b, recv_b, attention)
    saves.start(context_v, context_o)
    saves.start(log_v, log_o)
    middle = x_v[own_rows, :].astype(F32) + total_v[...]
    middle_v[...] = middle
    saves.start(middle_v, middle_o)
    two_v[own_rows, :] = (middle * mean_square(middle) * gains_v[1:2, :].astype(F32)).astype(BF)

    def gate_ready():
        if share is None:
            load_gate.wait()
        else:
            share.gate_there()
            loads.start(w_gate.at[layer], gate_v).wait()

    def feed(d):
        here = plane_rows(d, rows)
        both = kernel_dot(two_v[here, :], gate_v[...])
        both_v[here, :] = both
        gate = both[:, :units]
        hidden_v[here, :] = (gate * jax.nn.sigmoid(gate) * both[:, units:]).astype(BF)

    gather_rows(two_v, rows, send_c, recv_c, feed, gate_ready)
    saves.start(two_v, normed_two_o)
    saves.start(both_v, both_o)
    if share is None:
        load_down.wait()
    else:
        share.down_there()
        loads.start(w_down.at[layer], down_v).wait()

    def lower(d):
        here = plane_rows(d, rows)
        part_v[here, :] = kernel_dot(hidden_v[here, :], down_v[...]).astype(BF)

    scatter_sum(part_v, total_v, land_b, send_d, recv_d, lower)
    result_v[...] = (middle_v[...] + total_v[...]).astype(BF)
    saves.start(result_v, result_o)
    for one in saves.copies:
        one.wait()
    if share is not None:
        share.finish()


def forward_kernel(layer, *refs):
    x_own, *refs = refs
    weights, refs = refs[:5], refs[5:]
    tables, refs = refs[:4], refs[4:]
    kept, refs = refs[:10], refs[10:]
    scratch, sems = refs[:21], refs[21:]
    forward_body(layer, None, x_own, weights, tables, kept, scratch, sems)


def forward_share_kernel(*refs):
    x_own, *refs = refs
    sources, refs = refs[:5], refs[5:]
    tables, refs = refs[:4], refs[4:]
    kept, refs = refs[:10], refs[10:]
    weights, refs = refs[:5], refs[5:]
    scratch, refs = refs[:21], refs[21:]
    packing, refs = refs[:5], refs[5:]
    sems, share_sems = refs[:10], refs[10:]
    share = Share(sources, weights, packing, share_sems)
    forward_body(0, share, x_own, weights, tables, kept, scratch, sems)


def backward_body(layer, grad_own, weights, tables, saved, outs, scratch, sems, returning):
    w_mix, w_gate, w_out, w_down, w_gains = weights
    cosine, sine, place_col, place_row = tables
    x_own, normed, q, k, v, context, log, middle, normed_two, both = saved
    (grad_v, x_v, normed_v, q_v, k_v, v_v, context_v, log_v, middle_v, two_v, both_v, both_grad_v, hidden_v,
     low_v, mixed_v, kv_land, kv_v, key_grad_v, value_grad_v, start_v, start_low_v,
     mix_grad_v, gate_grad_v, out_grad_v, down_grad_v, gain_grad_v,
     mix_v, gate_v, out_v, down_v, gains_v, part_v, land_a, land_b, total_v) = scratch
    local, save, pair_sems, send_a, recv_a, send_b, recv_b, send_c, recv_c, send_d, recv_d = sems
    c = lax.axis_index("ctx")
    f = lax.axis_index("fsdp")
    odd = lax.rem(c, 2)
    rows = grad_own.shape[0]
    units = down_v.shape[0]
    own_rows = pl.ds(pl.multiple_of(own_block(c, f) * rows, rows), rows)
    loads = Loads(local)
    saves = Loads(save)
    load_grad = loads.start(grad_own, grad_v.at[own_rows])
    load_down = loads.start(w_down.at[layer], down_v)
    load_both = loads.start(both, both_v)
    load_gate = loads.start(w_gate.at[layer], gate_v)
    out_v[...] = jnp.zeros_like(out_v)
    key_grad_v[...] = jnp.zeros_like(key_grad_v)
    value_grad_v[...] = jnp.zeros_like(value_grad_v)
    gain_grad_v[...] = jnp.zeros_like(gain_grad_v)
    if returning is None:
        greet()
    else:
        peers = [{"fsdp": lax.rem(f + k, 4)} for k in range(1, 4)]
        greet_more(peers + [{"section": 1 - lax.axis_index("section")}, {"ctx": lax.rem(c + 2, 4)}])
    load_grad.wait()
    later = [
        loads.start(src, dst)
        for src, dst in (
            (normed_two, two_v), (middle, middle_v), (w_gains.at[layer], gains_v),
            (w_out.at[layer], out_v.at[pl.ds(0, HEAD)]), (q, q_v), (k, k_v), (v, v_v),
            (context, context_v), (log, log_v), (w_mix.at[layer], mix_v), (normed, normed_v), (x_own, x_v),
        )
    ]
    load_down.wait()
    load_both.wait()
    if returning is not None:
        begin_old, begin_feed, begin_mix, finish = returning
        begin_old()

    def feed(d):
        here = plane_rows(d, rows)
        hidden_grad = kernel_dot_nt(grad_v[here, :], down_v[...])
        gate = both_v[here, :units]
        up = both_v[here, units:]
        sig = jax.nn.sigmoid(gate)
        silu = gate * sig
        hidden_v[here, :] = (silu * up).astype(BF)
        both_grad_v[here, :units] = (hidden_grad * up * sig * (1.0 + gate * (1.0 - sig))).astype(BF)
        both_grad_v[here, units:] = (hidden_grad * silu).astype(BF)

    gather_rows(grad_v, rows, send_a, recv_a, feed)
    load_gate.wait()

    def spread(d):
        here = plane_rows(d, rows)
        part_v[here, :] = kernel_dot_nt(both_grad_v[here, :], gate_v[...]).astype(BF)

    def feed_weights():
        later[0].wait()
        down_grad_v[...] = kernel_dot_tn(hidden_v[...], grad_v[...]).astype(BF)
        for part in range(2):
            gate_grad_v[part] = kernel_dot_tn(
                two_v[...], both_grad_v[:, part * units : (part + 1) * units]
            ).astype(BF)
        if returning is None:
            saves.start(down_grad_v, outs[4])
            saves.start(gate_grad_v, outs[2])
        else:
            begin_feed()

    scatter_sum(part_v, total_v, land_a, send_b, recv_b, spread, feed_weights)
    for one in later[1:]:
        one.wait()

    def norm_grads(error, value, gain, row):
        factor = mean_square(value)
        shaped = error * gain
        common = jnp.mean(shaped * value, axis=-1, keepdims=True)
        gain_grad_v[row : row + 1, :] = jnp.sum(error * value * factor, axis=0, keepdims=True)
        return factor * shaped - value * (factor * factor * factor) * common

    middle_grad = norm_grads(total_v[...], middle_v[...], gains_v[1:2, :].astype(F32), 1)
    middle_grad = middle_grad + grad_v[own_rows, :].astype(F32)
    middle_v[...] = middle_grad
    low_v[own_rows, :] = middle_grad.astype(BF)
    scale = HEAD ** (-0.5)

    def attention(d):
        here = plane_rows(d, rows)
        context_grad = kernel_dot_nt(low_v[here, :], out_v[...])
        common = jnp.sum(context_grad * context_v[here, :].astype(F32), axis=-1, keepdims=True)
        context_grad = context_grad.astype(BF)
        queries = q_v[here, :]
        scores = kernel_dot_nt(queries, k_v[...]) * scale
        allowed = place_row[...] <= place_col[here, :]
        weights = jnp.exp(jnp.where(allowed, scores, masked_value) - log_v[here, 0:1])
        weight_grad = kernel_dot_nt(context_grad, v_v[...])
        score_grad = (weights * (weight_grad - common)).astype(BF)
        value_grad_v[...] += kernel_dot_tn(weights.astype(BF), context_grad)
        key_grad_v[...] += kernel_dot_tn(score_grad, queries)
        query_grad = kernel_dot(score_grad, k_v[...]) * scale
        mixed_v[here, :LANES] = (query_grad * cosine[here, :] - turn(query_grad) * sine[here, :]).astype(BF)

    gather_rows(low_v, rows, send_c, recv_c, attention)
    key_grad = key_grad_v[...] * scale
    mixed_v[:, LANES : 2 * LANES] = (key_grad * cosine[...] - turn(key_grad) * sine[...]).astype(BF)
    mixed_v[:, 2 * LANES :] = value_grad_v[...].astype(BF)
    pair = {"ctx": c + 1 - 2 * odd}

    def pair_copy(part):
        return pltpu.make_async_remote_copy(
            mixed_v.at[:, pl.ds(part * LANES, LANES)], kv_land, pair_sems.at[0], pair_sems.at[1],
            device_id=pair, device_id_type=MESH,
        )

    pl.when(odd == 0)(pair_copy(2).start)
    pl.when(odd == 1)(pair_copy(1).start)

    def spread_two(d):
        here = plane_rows(d, rows)
        part_v[here, :] = kernel_dot_nt(mixed_v[here, :], mix_v[...]).astype(BF)

    def mix_weights():
        out_grad_v[...] = kernel_dot_tn(context_v[...], low_v[...])[:HEAD].astype(BF)
        half = HEAD // 2
        columns = kernel_dot_tn(mixed_v[:, :LANES], normed_v[...])
        mix_grad_v[:half, :] = columns[:half].astype(BF)
        mix_grad_v[half:HEAD, :] = columns[SPAN : SPAN + half].astype(BF)
        pair_copy(1).wait_recv()
        mine = jnp.where(odd == 0, mixed_v[:, LANES : 2 * LANES].astype(F32), mixed_v[:, 2 * LANES :].astype(F32))
        kv_v[...] = (mine + kv_land[...].astype(F32)).astype(BF)
        columns = kernel_dot_tn(kv_v[...], normed_v[...])
        mix_grad_v[HEAD : HEAD + half, :] = columns[:half].astype(BF)
        mix_grad_v[HEAD + half :, :] = jnp.where(
            odd == 0, columns[SPAN : SPAN + half], columns[half:HEAD]
        ).astype(BF)
        if returning is None:
            saves.start(out_grad_v, outs[3])
            saves.start(mix_grad_v, outs[1])
        else:
            begin_mix()

    scatter_sum(part_v, total_v, land_b, send_d, recv_d, spread_two, mix_weights)
    start_grad = norm_grads(total_v[...], x_v[...].astype(F32), gains_v[0:1, :].astype(F32), 0) + middle_v[...]
    start_v[...] = start_grad
    if returning is None:
        saves.start(start_v, outs[0])
        start_low_v[...] = start_grad.astype(BF)
        saves.start(start_low_v, outs[6])
        saves.start(gain_grad_v, outs[5])
    else:
        finish(gain_grad_v)
    pair_copy(1).wait_send()
    for one in saves.copies:
        one.wait()


SAVED = 10
BACK_SCRATCH = 35


def backward_kernel(layer, *refs):
    grad_own, *refs = refs
    weights, refs = refs[:5], refs[5:]
    tables, refs = refs[:4], refs[4:]
    saved, refs = refs[:SAVED], refs[SAVED:]
    outs, refs = refs[:7], refs[7:]
    scratch, sems = refs[:BACK_SCRATCH], refs[BACK_SCRATCH:]
    backward_body(layer, grad_own, weights, tables, saved, outs, scratch, sems, None)


def backward_return_kernel(*refs):
    grad_own, *refs = refs
    weights, refs = refs[:5], refs[5:]
    tables, refs = refs[:4], refs[4:]
    saved, refs = refs[:SAVED], refs[SAVED:]
    (start_old, mix_old, gate_old, out_old, down_old, gain_old), refs = refs[:6], refs[6:]
    (result_new, result_old), refs = refs[:2], refs[2:]
    (results_o, starts_o), refs = refs[:2], refs[2:]
    finals, refs = refs[:5], refs[5:]
    scratch, refs = refs[:BACK_SCRATCH], refs[BACK_SCRATCH:]
    own, refs = refs[:10], refs[10:]
    sems, return_sems, swap_sems = refs[:11], refs[11:16], refs[16]
    start_new = scratch[19]
    mix_new, gate_new, out_new, down_new, gain_new = scratch[21:26]
    gain_v = own[8]
    s = lax.axis_index("section")
    begin_old, begin_feed, begin_mix, steps_after, wait_all = returner(
        tuple(finals) + tuple(own), return_sems,
        gate_new, down_new, mix_new, out_new, gate_old, down_old, mix_old, out_old,
    )

    def swap_copy(src, dst, slot):
        return pltpu.make_async_remote_copy(
            src, dst, swap_sems.at[slot], swap_sems.at[2 + slot], device_id={"section": 1 - s}, device_id_type=MESH
        )

    def swap_rows(away, home, out, slot):
        swap_copy(away, out.at[s], slot).start()
        pltpu.make_async_copy(home, out.at[s], swap_sems.at[4 + slot]).start()

    def finish(gain_grad_v):
        @pl.when(s == 0)
        def _():
            swap_rows(result_old, result_new, results_o, 0)
            swap_rows(start_old, start_new, starts_o, 1)

        @pl.when(s == 1)
        def _():
            swap_rows(result_new, result_old, results_o, 0)
            swap_rows(start_new, start_old, starts_o, 1)

        gain_v[0] = jnp.zeros(gain_v.shape[1:], F32)
        gain_v[0, 0:2, :] = gain_grad_v[...]
        gain_v[0, 2:4, :] = gain_old[...]
        steps_after()
        wait_all()
        for slot, out in enumerate((results_o, starts_o)):
            pltpu.make_async_copy(out.at[s], out.at[s], swap_sems.at[4 + slot]).wait()
            swap_copy(out.at[s], out.at[1 - s], slot).wait()

    backward_body(0, grad_own, weights, tables, saved, None, scratch, sems, (begin_old, begin_feed, begin_mix, finish))


def link_sems():
    dma = pltpu.SemaphoreType.DMA
    return [dma((GATHER_SENDS,)), dma((GATHER_RECVS,)), dma((SCATTER_SENDS,)), dma((SCATTER_RECVS,))] * 2


def low(*shape):
    return (shape, BF)


def full(*shape):
    return (shape, F32)


def shapes(specs):
    return [jax.ShapeDtypeStruct(*one) for one in specs]


def rooms(specs):
    return [pltpu.VMEM(*one) for one in specs]


def signals(*counts):
    return [pltpu.SemaphoreType.DMA((count,)) for count in counts]


def forward_call(layer, x_own, weights, tables):
    rows, width = x_own.shape
    length = 16 * rows
    sharing = layer == 0
    if sharing:
        depth = weights[0].shape[1]
        units = weights[2].shape[2] // 32
        packing = [low(depth, weights[0].shape[2]), low(depth, 32 * LANES), low(depth, 2 * units), low(HEAD, width),
                   low(units, width)]
    else:
        units = weights[3].shape[1]
        packing = []
    anywhere = pl.BlockSpec(memory_space=pl.ANY)
    inside = pl.BlockSpec(memory_space=pltpu.VMEM)
    kept = [low(length, width)] + [low(length, LANES)] * 4 + [
        full(length, LANES), full(rows, width), low(length, width), full(length, 2 * units), low(rows, width)]
    shared = [low(2, width, 3 * LANES), low(2, width, 2 * units), low(2, HEAD, width), low(2, units, width), low(2, 16, width)]
    scratch = [low(length, width), low(length, width)] + [low(length, LANES)] * 4 + [
        full(length, LANES), full(rows, width), low(length, width), full(length, 2 * units), low(length, units),
        low(rows, width), low(width, 3 * LANES), low(width, 2 * units), low(LANES, width), low(units, width),
        low(16, width), low(length, width), low(19, rows, width), low(19, rows, width), full(rows, width)]
    outs = kept + shared if sharing else kept
    return pl.pallas_call(
        forward_share_kernel if sharing else functools.partial(forward_kernel, layer),
        out_shape=shapes(outs),
        in_specs=[anywhere] * 6 + [inside] * 4,
        out_specs=[anywhere] * len(outs),
        scratch_shapes=rooms(scratch + packing) + signals(6, 10) + link_sems() + (signals(9, 27, 26) if sharing else []),
        compiler_params=pltpu.CompilerParams(
            collective_id=layer, has_side_effects=True, vmem_limit_bytes=60 << 20),
    )(x_own, *weights, *tables)


def backward_call(layer, grad_own, weights, tables, saved, old=(), results=()):
    rows, width = grad_own.shape
    length = 16 * rows
    units = weights[3].shape[1]
    depth = width // 4
    returning = layer == 0
    anywhere = pl.BlockSpec(memory_space=pl.ANY)
    inside = pl.BlockSpec(memory_space=pltpu.VMEM)
    grads = [low(2 * HEAD, width), low(2, width, units), low(HEAD, width), low(units, width), full(2, width)]
    scratch = [low(length, width), low(rows, width), low(length, width)] + [low(length, LANES)] * 4 + [
        full(length, LANES), full(rows, width), low(length, width), full(length, 2 * units), low(length, 2 * units),
        low(length, units), low(length, width), low(length, 3 * LANES), low(length, LANES), low(length, LANES),
        full(length, LANES), full(length, LANES),
        full(rows, width), low(rows, width)] + grads + [
        low(width, 3 * LANES), low(width, 2 * units), low(LANES, width), low(units, width),
        low(16, width), low(length, width), low(19, rows, width), low(19, rows, width), full(rows, width)]
    sems = signals(16, 7, 2) + link_sems()
    if returning:
        outs = [low(2, rows, width), full(2, rows, width), low(16 * 2 * HEAD, depth), low(2, depth, 16 * units),
                low(4 * HEAD, width), low(4 * units, width), full(8, width)]
        out_specs = [anywhere] * 6 + [inside]
        scratch += grads[:4] + grads[:4] + [full(5, 8, width), full(5, 8, width)]
        sems += signals(5, 23, 23, 50, 40, 6)
    else:
        outs = [full(rows, width)] + grads + [low(rows, width)]
        out_specs = [anywhere] * len(outs)
    return pl.pallas_call(
        backward_return_kernel if returning else functools.partial(backward_kernel, layer),
        out_shape=shapes(outs),
        in_specs=[anywhere] * 6 + [inside] * 4 + [anywhere] * SAVED
        + ([anywhere] * 5 + [inside] + [anywhere] * 2 if returning else []),
        out_specs=out_specs,
        scratch_shapes=rooms(scratch) + sems,
        compiler_params=pltpu.CompilerParams(
            collective_id=2 + layer, has_side_effects=True, vmem_limit_bytes=60 << 20),
    )(grad_own, *weights, *tables, *saved, *old, *results)


def returner(refs, sems, gate_new, down_new, mix_new, out_new, gate_old, down_old, mix_old, out_old):
    (mix_out, gate_out, out_out, down_out, gain_out,
     mix_v, gate_v, out_v, down_v, mix_x, gate_x, out_x, down_x, gain_v, gain_x) = refs
    local, send, recv, line_send, line_recv = sems
    s = lax.axis_index("section")
    c = lax.axis_index("ctx")
    f = lax.axis_index("fsdp")
    other = {"section": 1 - s}
    units = down_v.shape[0]
    depth = gate_out.shape[1]
    inner = jnp.logical_and(c > 0, c < 3)
    above = jnp.minimum(c + 1, 3)
    below = jnp.maximum(c - 1, 0)

    def copy(src, dst, slot, arrival, peer):
        return pltpu.make_async_remote_copy(
            src, dst, send.at[slot], recv.at[arrival], device_id=peer, device_id_type=MESH
        )

    def owner_part(owner):
        return pl.ds(pl.multiple_of(owner * depth, depth), depth)

    def cross_parts(away, theirs, first):
        for k in range(4):
            owner = lax.rem(f + k, 4)
            part = owner_part(owner)
            copy(away.at[:, part], theirs.at[:, part], first + k, first + owner, other).start()

    def cross_whole(away, theirs, slot):
        copy(away, theirs, slot, slot, other).start()

    def home(src, dst, k):
        pltpu.make_async_copy(src, dst, local.at[k]).start()

    def begin_old():
        @pl.when(s == 0)
        def _():
            cross_whole(down_old, down_x, 8)
            cross_parts(gate_old, gate_x, 0)
            cross_whole(out_old, out_x, 9)
            cross_parts(mix_old, mix_x, 4)

        @pl.when(s == 1)
        def _():
            home(down_old, down_v, 0)
            home(gate_old, gate_v, 1)
            home(out_old, out_v, 2)
            home(mix_old, mix_v, 3)

    def begin_feed():
        @pl.when(s == 0)
        def _():
            home(down_new, down_v, 0)
            home(gate_new, gate_v, 1)

        @pl.when(s == 1)
        def _():
            cross_whole(down_new, down_x, 8)
            cross_parts(gate_new, gate_x, 0)

    def begin_mix():
        @pl.when(s == 0)
        def _():
            home(out_new, out_v, 2)
            home(mix_new, mix_v, 3)

        @pl.when(s == 1)
        def _():
            cross_whole(out_new, out_x, 9)
            cross_parts(mix_new, mix_x, 4)

    def home_wait(k, dst):
        pltpu.make_async_copy(dst, dst, local.at[k]).wait()

    def arrived(ref, arrival):
        copy(ref, ref, 0, arrival, other).wait_recv()

    def gate_at(cc, ff):
        return gate_out.at[:, :, pl.ds(pl.multiple_of((ff * 4 + cc) * units, units), units)]

    def mix_at(cc, ff):
        return mix_out.at[pl.ds(pl.multiple_of((ff * 4 + cc) * 2 * HEAD, 2 * HEAD), 2 * HEAD)]

    def rows_at(ref, cc, count):
        return ref.at[pl.ds(pl.multiple_of(cc * count, count), count)]

    def out_at(cc, ff):
        return rows_at(out_out, cc, HEAD)

    def down_at(cc, ff):
        return rows_at(down_out, cc, units)

    origins = [lax.rem(f + k, 4) for k in (0, 3, 2, 1)]
    items = [(down_at, f)] + [(gate_at, one) for one in origins] + [(out_at, f)] + [(mix_at, one) for one in origins]

    def line(index, cc, slot, target):
        place, origin = items[index]
        return pltpu.make_async_remote_copy(
            place(cc, origin), place(cc, origin), line_send.at[slot], line_recv.at[cc * 10 + index],
            device_id={"ctx": target}, device_id_type=MESH,
        )

    def start_line(index):
        pl.when(c < 3)(line(index, c, index, above).start)
        pl.when(c > 0)(line(index, c, 10 + index, below).start)

    def fold(mine, theirs, arrival):
        arrived(theirs, arrival)
        mine[...] = (mine[...].astype(F32) + theirs[...].astype(F32)).astype(BF)

    def keep(src, dst):
        one = pltpu.make_async_copy(src, dst, local.at[4])
        one.start()
        one.wait()

    def whole_item(k, mine, theirs, arrival, place, index):
        home_wait(k, mine)
        fold(mine, theirs, arrival)
        keep(mine, place(c, f))
        start_line(index)

    def to_owner(k, mine, theirs, place, arrival_x, arrival_y, slot, index):
        owner = lax.rem(f + k, 4)
        rows = owner_part(owner)
        fold(mine.at[:, rows], theirs.at[:, rows], arrival_x + owner)
        if k:
            copy(mine.at[:, rows], place(c, f), slot + k, arrival_y + f, {"fsdp": owner}).start()
        else:
            keep(mine.at[:, rows], place(c, f))
            start_line(index)

    def from_owner(k, place, arrival, index):
        arrived(place(c, origins[k]), arrival + origins[k])
        start_line(index)

    gain_targets = [other, {"fsdp": f + 1 - 2 * lax.rem(f, 2)}, {"fsdp": f + 2 - 4 * (f // 2)},
                    {"ctx": c + 1 - 2 * lax.rem(c, 2)}, {"ctx": lax.rem(c + 2, 4)}]

    def gain_copy(k):
        return copy(gain_v.at[k], gain_x.at[k], 18 + k, 18 + k, gain_targets[k])

    def gain_sum(k):
        gain_copy(k).wait_recv()
        if k < 4:
            gain_v[k + 1] = gain_v[k] + gain_x[k]
            gain_copy(k + 1).start()
        else:
            gain_out[...] = gain_v[k] + gain_x[k]

    order = near_order(c)

    def onward(index, step):
        d = order[step]
        return line(index, d, 20 + (step - 1) * 10 + index, jnp.where(d < c, above, below))

    def pass_on(index, step):
        one = onward(index, step)
        one.wait_recv()
        pl.when(inner)(one.start)

    def near(index):
        pass_on(index, 1)
        pl.when(inner)(lambda: pass_on(index, 2))

    def far(index):
        pl.when(jnp.logical_not(inner))(lambda: pass_on(index, 2))
        pass_on(index, 3)

    def gate_first():
        home_wait(1, gate_v)
        to_owner(0, gate_v, gate_x, gate_at, 0, 10, 10, 1)

    def gate_rest(k):
        return lambda: to_owner(k, gate_v, gate_x, gate_at, 0, 10, 10, 1)

    def gate_from(k):
        return lambda: from_owner(k, gate_at, 10, 1 + k)

    def mix_first():
        home_wait(3, mix_v)
        to_owner(0, mix_v, mix_x, mix_at, 4, 14, 14, 6)

    def mix_rest(k):
        return lambda: to_owner(k, mix_v, mix_x, mix_at, 4, 14, 14, 6)

    def mix_from(k):
        return lambda: from_owner(k, mix_at, 14, 6 + k)

    def down_first():
        whole_item(0, down_v, down_x, 8, down_at, 0)

    def out_first():
        whole_item(2, out_v, out_x, 9, out_at, 5)

    def passing(*steps):
        return [functools.partial(near if sign > 0 else far, abs(sign) - 1) for sign in steps]

    after = [
        [down_first, gate_first, gate_rest(1), gate_rest(2), gate_rest(3)],
        passing(1) + [gate_from(1), gate_from(2), gate_from(3), out_first, mix_first, mix_rest(1), mix_rest(2), mix_rest(3)],
        passing(2, -1, 3, -2, 4) + [mix_from(1), mix_from(2), mix_from(3)],
        passing(-3, 5, -4, 6, -5, 7),
        passing(-6, 8, -7, 9, -8, 10, -9, -10),
    ]
    def steps_after():
        gain_copy(0).start()
        for k, steps in enumerate(after):
            for step in steps:
                step()
            gain_sum(k)

    def wait_all():
        for index in range(10):
            pl.when(c < 3)(line(index, c, index, above).wait_send)
            pl.when(c > 0)(line(index, c, 10 + index, below).wait_send)
            for step in range(1, 4):
                pl.when(inner)(onward(index, step).wait_send)
        for k in range(5):
            gain_copy(k).wait_send()
        for k in range(4):
            gate_part = gate_x.at[:, pl.ds(k * depth, depth)]
            mix_part = mix_x.at[:, pl.ds(k * depth, depth)]
            for slot in (k, 10 + k) if k else (k,):
                copy(gate_part, gate_part, slot, 0, other).wait_send()
                copy(mix_part, mix_part, 4 + slot, 0, other).wait_send()
        copy(down_x, down_x, 8, 0, other).wait_send()
        copy(out_x, out_x, 9, 0, other).wait_send()

    return begin_old, begin_feed, begin_mix, steps_after, wait_all


def widen_kernel(mix, gate, out, down, mix_f, gate_f, out_f, down_f, places, turned):
    step = pl.program_id(0)
    rows = gate.shape[1]
    four = 4 * HEAD
    width = 4 * four

    @pl.when(step == 0)
    def _():
        source = lax.broadcasted_iota(jnp.int32, (2 * four, 2 * four), 0)
        column = lax.broadcasted_iota(jnp.int32, (2 * four, 2 * four), 1)
        query = (column // HEAD) * 2 * HEAD + lax.rem(column, HEAD)
        rest = column - four
        kind = rest // (2 * HEAD)
        rest = rest - kind * 2 * HEAD
        other = (2 * (rest // HEAD) + kind) * 2 * HEAD + HEAD + lax.rem(rest, HEAD)
        places[...] = jnp.where(source == jnp.where(column < four, query, other), 1.0, 0.0).astype(BF)
        groups = [kernel_dot_tn(mix[g * 2 * four : (g + 1) * 2 * four, :], places[...]) for g in range(4)]
        for g in range(4):
            turned[:, g * four : (g + 1) * four] = groups[g][:, :four]
        for g in range(2):
            for kind in range(2):
                at = width + kind * 2 * four + g * four
                low_part = four + kind * 2 * HEAD
                turned[:, at : at + four] = jnp.concatenate(
                    [groups[2 * g + k][:, low_part : low_part + 2 * HEAD] for k in range(2)], axis=1
                )

    mix_f[...] = turned[pl.ds(pl.multiple_of(step * rows, rows), rows), :]
    half = gate.shape[2]
    gate_f[:, :half] = gate[0].astype(F32)
    gate_f[:, half:] = gate[1].astype(F32)
    out_f[...] = out[...].astype(F32)
    down_f[...] = down[...].astype(F32)


def widen_call(mix, gate, out, down):
    steps = 8
    depth = gate.shape[1]
    width = out.shape[1]
    rows = depth // steps
    down_rows = down.shape[0] // steps
    return pl.pallas_call(
        widen_kernel,
        grid=(steps,),
        out_shape=shapes([
            full(depth, 2 * width), full(depth, 2 * gate.shape[2]), full(*out.shape), full(*down.shape)
        ]),
        in_specs=[
            pl.BlockSpec(mix.shape, lambda i: (0, 0)),
            pl.BlockSpec((2, rows, gate.shape[2]), lambda i: (0, i, 0)),
            pl.BlockSpec((rows, width), lambda i: (i, 0)),
            pl.BlockSpec((down_rows, width), lambda i: (i, 0)),
        ],
        out_specs=[
            pl.BlockSpec((rows, 2 * width), lambda i: (i, 0)),
            pl.BlockSpec((rows, 2 * gate.shape[2]), lambda i: (i, 0)),
            pl.BlockSpec((rows, width), lambda i: (i, 0)),
            pl.BlockSpec((down_rows, width), lambda i: (i, 0)),
        ],
        scratch_shapes=rooms([low(8 * HEAD, 8 * HEAD), full(depth, 2 * width)]),
        compiler_params=pltpu.CompilerParams(vmem_limit_bytes=48 << 20),
    )(mix, gate, out, down)


def on_line():
    return lax.axis_size("ctx") == 4 and lax.axis_size("fsdp") == 4


def gather(own):
    return lax.all_gather(own, ("ctx", "fsdp"), axis=0, tiled=True)


def scatter(part):
    return lax.psum_scatter(part, ("ctx", "fsdp"), scatter_dimension=0, tiled=True)


def spread_halves(columns):
    halves = columns.reshape(columns.shape[:-1] + (2, HEAD // 2))
    halves = jnp.pad(halves, [(0, 0)] * (halves.ndim - 1) + [(0, SPAN - HEAD // 2)])
    return halves.reshape(columns.shape[:-1] + (LANES,))


def join_halves(columns):
    halves = columns.reshape(columns.shape[:-1] + (2, SPAN))[..., : HEAD // 2]
    return halves.reshape(columns.shape[:-1] + (HEAD,))


def angle_tables(positions):
    frequency = rope_base ** (-(jnp.arange(HEAD // 2, dtype=F32) * 2.0 / HEAD))
    frequency = jnp.pad(frequency, (0, SPAN - HEAD // 2))
    angles = positions.astype(F32)[:, None] * frequency[None, :]
    cosine = jnp.cos(angles)
    sine = jnp.sin(angles)
    return jnp.concatenate([cosine, cosine], axis=1), jnp.concatenate([-sine, sine], axis=1)


def rotate(values, cosine, sine):
    return values * cosine + jnp.roll(values, SPAN, axis=1) * sine


def rotate_back(grads, cosine, sine):
    return grads * cosine - jnp.roll(grads, SPAN, axis=1) * sine


def norm_rows(values):
    return lax.rsqrt(jnp.mean(values * values, axis=-1, keepdims=True) + norm_eps)


def norm_back(grad_out, values, factor, gain):
    shaped = grad_out * gain
    common = jnp.mean(shaped * values, axis=-1, keepdims=True)
    grad_in = factor * shaped - values * (factor * factor * factor) * common
    return grad_in, jnp.sum(grad_out * values * factor, axis=0)


def dot(left, right):
    return jnp.dot(left, right, preferred_element_type=F32)


def dot_nt(left, right):
    return lax.dot_general(left, right, (((1,), (1,)), ((), ())), preferred_element_type=F32)


def dot_tn(left, right):
    return lax.dot_general(left, right, (((0,), (0,)), ((), ())), preferred_element_type=F32)


class Plan:
    def __init__(self, width, hidden_units):
        self.c = lax.axis_index("ctx")
        self.f = lax.axis_index("fsdp")
        self.C = lax.axis_size("ctx")
        self.F = lax.axis_size("fsdp")
        self.heads = width // HEAD
        self.ratio = self.heads // KV_HEADS
        self.heads_f = self.heads // self.F
        self.groups_f = KV_HEADS // self.F
        self.share = self.C // self.heads_f
        self.units = hidden_units // (self.F * self.C)
        self.local_head = self.c // self.share
        self.part = self.c % self.share


def pick(array, index, axis):
    return lax.dynamic_index_in_dim(array, index, axis, keepdims=False)


def pack_weights(plan, mix, gate_up):
    depth = mix.shape[0]
    width = plan.heads * HEAD
    kv_width = KV_HEADS * HEAD
    F = plan.F
    queries = pick(mix[:, :width].reshape(depth, F, plan.heads_f, HEAD), plan.local_head, 2)
    group = plan.local_head // plan.ratio
    keys = pick(mix[:, width : width + kv_width].reshape(depth, F, plan.groups_f, HEAD), group, 2)
    values = pick(mix[:, width + kv_width :].reshape(depth, F, plan.groups_f, HEAD), group, 2)
    values = jnp.pad(values, ((0, 0), (0, 0), (0, LANES - HEAD)))
    half = gate_up.shape[1] // 2
    gate = pick(gate_up[:, :half].reshape(depth, F, plan.C, plan.units), plan.c, 2)
    up = pick(gate_up[:, half:].reshape(depth, F, plan.C, plan.units), plan.c, 2)
    packed = jnp.concatenate([spread_halves(queries), spread_halves(keys), values, gate, up], axis=2)
    return jnp.swapaxes(packed, 0, 1)


def attend(plan, q_part, k, v, positions, part_positions):
    scores = dot_nt(q_part, k) * HEAD ** (-0.5)
    allowed = positions[None, :] <= part_positions[:, None]
    scores = jnp.where(allowed, scores, masked_value)
    top = jnp.max(scores, axis=-1, keepdims=True)
    weights = jnp.exp(scores - top)
    total = jnp.sum(weights, axis=-1, keepdims=True)
    context = dot((weights / total).astype(BF), v)
    return context.astype(BF), top + jnp.log(total)


def attend_back(q_part, k, v, context_grad, context, log_total, positions, part_positions):
    scale = HEAD ** (-0.5)
    common = jnp.sum(context_grad.astype(F32) * context.astype(F32), axis=-1, keepdims=True)
    allowed = positions[None, :] <= part_positions[:, None]
    scores = dot_nt(q_part, k) * scale
    weights = jnp.exp(jnp.where(allowed, scores, masked_value) - log_total)
    weight_grad = dot_nt(context_grad, v)
    score_grad = (weights * (weight_grad - common)).astype(BF)
    value_grad = dot_tn(weights.astype(BF), context_grad)
    key_grad = dot_tn(score_grad, q_part) * scale
    query_grad = dot(score_grad, k) * scale
    return query_grad, key_grad, value_grad


def forward_layer(plan, x_own, weights, gains, positions, part_positions, tables):
    mix_cut, gate_cut, out, down = weights
    cosine, sine = tables
    length = positions.shape[0]
    x_all = gather(x_own)
    x32 = x_all.astype(F32)
    factor = norm_rows(x32)
    normed = (x32 * factor * gains[0]).astype(BF)
    mixed = dot(normed, mix_cut)
    q = rotate(mixed[:, :LANES], cosine, sine).astype(BF)
    k = rotate(mixed[:, LANES : 2 * LANES], cosine, sine).astype(BF)
    v = mixed[:, 2 * LANES :].astype(BF)
    rows = length // plan.share
    start = plan.part * rows
    q_part = lax.dynamic_slice_in_dim(q, start, rows, 0)
    context, log_total = attend(plan, q_part, k, v, positions, part_positions)
    partial = dot(context[:, :HEAD], out).astype(BF)
    if plan.share > 1:
        partial = lax.dynamic_update_slice_in_dim(
            jnp.zeros((length, partial.shape[1]), BF), partial, start, 0
        )
    middle = x_own.astype(F32) + scatter(partial)
    factor_two = norm_rows(middle)
    normed_two = gather((middle * factor_two * gains[1]).astype(BF))
    both = dot(normed_two, gate_cut)
    hidden = (jax.nn.silu(both[:, : plan.units]) * both[:, plan.units :]).astype(BF)
    result = middle + scatter(dot(hidden, down).astype(BF))
    kept = (x_own, normed, q_part, k, v, context, log_total, middle, normed_two, both, hidden)
    return result.astype(BF), kept


def backward_layer(plan, grad_own, weights, gains, kept, positions, part_positions, tables, part_tables):
    mix_cut, gate_cut, out, down = weights
    x_own, normed, q_part, k, v, context, log_total, middle, normed_two, both, hidden = kept
    length = positions.shape[0]
    rows = length // plan.share
    start = plan.part * rows
    grad_all = gather(grad_own)
    hidden_grad = dot_nt(grad_all, down)
    gate = both[:, : plan.units]
    up = both[:, plan.units :]
    sig = jax.nn.sigmoid(gate)
    gate_grad = hidden_grad * up * sig * (1.0 + gate * (1.0 - sig))
    up_grad = hidden_grad * gate * sig
    both_grad = jnp.concatenate([gate_grad, up_grad], axis=1).astype(BF)
    normed_two_grad = scatter(dot_nt(both_grad, gate_cut).astype(BF))
    middle_grad, feed_gain_grad = norm_back(normed_two_grad, middle, norm_rows(middle), gains[1])
    middle_grad = middle_grad + grad_own.astype(F32)
    middle_low = gather(middle_grad.astype(BF))
    middle_part = lax.dynamic_slice_in_dim(middle_low, start, rows, 0)
    context_grad = jnp.pad(dot_nt(middle_part, out), ((0, 0), (0, LANES - HEAD))).astype(BF)
    query_grad, key_grad, value_grad = attend_back(
        q_part, k, v, context_grad, context, log_total, positions, part_positions
    )
    query_grad = rotate_back(query_grad, *part_tables).astype(BF)
    if plan.share > 1:
        query_grad = lax.dynamic_update_slice_in_dim(
            jnp.zeros((length, LANES), BF), query_grad, start, 0
        )
    key_grad = rotate_back(key_grad, *tables).astype(BF)
    mixed_grad = jnp.concatenate([query_grad, key_grad, value_grad.astype(BF)], axis=1)
    normed_grad = scatter(dot_nt(mixed_grad, mix_cut).astype(BF))
    x32 = x_own.astype(F32)
    start_grad, attention_gain_grad = norm_back(normed_grad, x32, norm_rows(x32), gains[0])
    start_grad = start_grad + middle_grad
    mix_grad = jnp.stack(
        [dot_tn(normed, part).astype(BF) for part in (query_grad, key_grad, value_grad.astype(BF))]
    )
    gate_cut_grad = jnp.stack(
        [dot_tn(normed_two, part.astype(BF)).astype(BF) for part in (gate_grad, up_grad)]
    )
    out_grad = dot_tn(context, middle_part).astype(BF)[:HEAD]
    down_grad = dot_tn(hidden, grad_all).astype(BF)
    return start_grad, (mix_grad, gate_cut_grad, out_grad, down_grad), jnp.stack([attention_gain_grad, feed_gain_grad])


def swap_sections(array):
    return lax.ppermute(array, "section", [(0, 1), (1, 0)])


def by_layer_of(section, own, other):
    first = section == 0
    return jnp.where(first, own, other), jnp.where(first, other, own)


def shared_weights(plan, section, attention_gain, query_key_value, output_weight, feed_gain, gate_up, down_weight):
    depth = query_key_value.shape[1]
    width = depth * plan.F
    gains = lax.all_gather(
        jnp.stack([attention_gain[0], feed_gain[0]]), ("section", "fsdp"), axis=0, tiled=False
    )
    gains = gains.reshape(2, plan.F, 2, depth)
    gains = jnp.swapaxes(gains, 1, 2).reshape(2, 2, width).astype(F32)
    packed = pack_weights(plan, query_key_value[0], gate_up[0])
    own_cut = lax.all_to_all(packed, "fsdp", 0, 0).reshape(width, -1)
    own_out = lax.dynamic_slice_in_dim(output_weight[0], plan.local_head * HEAD, HEAD, 0)
    own_down = lax.dynamic_slice_in_dim(down_weight[0], plan.c * plan.units, plan.units, 0)
    cuts = by_layer_of(section, own_cut, swap_sections(own_cut))
    outs = by_layer_of(section, own_out, swap_sections(own_out))
    downs = by_layer_of(section, own_down, swap_sections(own_down))
    weights = [(cuts[s][:, : 3 * LANES], cuts[s][:, 3 * LANES :], outs[s], downs[s]) for s in range(2)]
    return weights, gains


def own_gain_sums(plan, section, gain_sum, depth):
    gain_sum = lax.dynamic_slice_in_dim(gain_sum, 2 * section, 2, 0)
    return lax.dynamic_slice_in_dim(gain_sum, plan.f * depth, depth, 1)


def returned_grads(plan, section, weight_grads, gain_grads, depth):
    C, F = plan.C, plan.F
    gain_sum = jnp.concatenate([gain_grads[0], gain_grads[1]])

    def collected(index):
        first, second = weight_grads[0][index], weight_grads[1][index]
        own = jnp.where(section == 0, first, second)
        away = jnp.where(section == 0, second, first)
        return (own.astype(F32) + swap_sections(away).astype(F32)).astype(BF)

    cut_grad = jnp.concatenate(list(collected(0)) + list(collected(1)), axis=1)
    cut_grad = lax.all_to_all(cut_grad.reshape(F, depth, -1), "fsdp", 0, 0)
    cut_grad = lax.all_gather(cut_grad, "ctx", axis=0, tiled=False)
    out_grad = lax.all_gather(collected(2), "ctx", axis=0, tiled=False)
    down_grad = lax.all_gather(collected(3), "ctx", axis=0, tiled=True).astype(F32)

    def heads_of(columns, count):
        folded = columns.astype(F32).reshape(count, C // count, F, depth, columns.shape[-1]).sum(axis=1)
        return jnp.transpose(folded, (2, 1, 0, 3))

    q_grad = join_halves(heads_of(cut_grad[..., :LANES], plan.heads_f)).reshape(depth, -1)
    k_grad = join_halves(heads_of(cut_grad[..., LANES : 2 * LANES], plan.groups_f)).reshape(depth, -1)
    v_grad = heads_of(cut_grad[..., 2 * LANES : 3 * LANES], plan.groups_f)[..., :HEAD].reshape(depth, -1)
    mix_grad = jnp.concatenate([q_grad, k_grad, v_grad], axis=1)
    both = jnp.transpose(cut_grad[..., 3 * LANES :], (2, 1, 0, 3)).astype(F32)
    gate_up_grad = jnp.concatenate(
        [both[..., : plan.units].reshape(depth, -1), both[..., plan.units :].reshape(depth, -1)], axis=1
    )
    out_grad = out_grad.astype(F32).reshape(plan.heads_f, plan.share, HEAD, depth * F).sum(axis=1).reshape(-1, depth * F)

    gain_sum = lax.psum(gain_sum, ("section", "ctx", "fsdp"))
    return mix_grad, gate_up_grad, out_grad, down_grad, own_gain_sums(plan, section, gain_sum, depth)


def on_device(
    inputs, cotangent, attention_gain, query_key_value, output_weight, feed_gain, gate_up, down_weight, block_order
):
    section = lax.axis_index("section")
    width = inputs.shape[2]
    hidden_units = down_weight.shape[1] * lax.axis_size("fsdp")
    plan = Plan(width, hidden_units)
    rows = inputs.shape[1]
    C, F = plan.C, plan.F
    length = rows * C * F
    depth = query_key_value.shape[1]

    def by_layer(own, other):
        first = section == 0
        return jnp.where(first, own, other), jnp.where(first, other, own)

    order = pick(block_order, section, 0)
    if on_line():
        order = jnp.swapaxes(order.reshape(C, F // 2, 2), 1, 2).reshape(C * F)
    positions = (order[:, None] * rows + jnp.arange(rows, dtype=jnp.int32)[None, :]).reshape(length)
    part_rows = length // plan.share
    part_positions = lax.dynamic_slice_in_dim(positions, plan.part * part_rows, part_rows, 0)
    tables = angle_tables(positions)
    part_tables = angle_tables(part_positions)

    x = pick(inputs, section, 0)
    grad = pick(cotangent, section, 0)
    results = []
    input_grads = [None, None]
    weight_grads = [None, None]
    gain_grads = [None, None]
    kept = []
    if on_line():
        own_gains = jnp.pad(jnp.concatenate([attention_gain, feed_gain]), ((0, 14), (0, 0)))
        shards = (query_key_value, output_weight, gate_up, down_weight, own_gains)
        common = tuple(tables) + (positions[:, None], positions[None, :])
        first = forward_call(0, x, shards, common)
        weights = first[10:]
        results.append(first[9])
        second = forward_call(1, first[9], weights, common)
        results.append(second[9])
        input_grads[1], *old, grad = backward_call(1, grad, weights, common, [first[9], *second[:9]])
        section_outputs, section_input_grads, *wide, gain_sum = backward_call(
            0, grad, weights, common, [x, *first[:9]], [input_grads[1], *old], results
        )
        mix_grad, gate_up_grad, out_grad, down_grad = widen_call(*wide)
        gain_sum = own_gain_sums(plan, section, gain_sum, depth)
    else:
        weights, gains = shared_weights(
            plan, section, attention_gain, query_key_value, output_weight, feed_gain, gate_up, down_weight
        )
        for s in range(2):
            x, keep = forward_layer(plan, x, weights[s], gains[s], positions, part_positions, tables)
            kept.append(keep)
            results.append(x)
        for s in (1, 0):
            input_grads[s], weight_grads[s], gain_grads[s] = backward_layer(
                plan, grad, weights[s], gains[s], kept[s], positions, part_positions, tables, part_tables
            )
            grad = input_grads[s].astype(BF)
        def mine_and_theirs(first, second):
            return jnp.where(section == 0, first, second), jnp.where(section == 0, second, first)

        def by_batch(first, second):
            own, away = mine_and_theirs(first, second)
            return jnp.stack(by_layer(own, swap_sections(away)))

        section_outputs = by_batch(*results)
        section_input_grads = by_batch(*input_grads)

        shard_grads = returned_grads(plan, section, weight_grads, gain_grads, depth)
        mix_grad, gate_up_grad, out_grad, down_grad, gain_sum = shard_grads

    return (
        section_outputs[None],
        section_input_grads[None],
        gain_sum[0][None],
        mix_grad[None],
        out_grad[None],
        gain_sum[1][None],
        gate_up_grad[None],
        down_grad[None],
    )


def solution(mesh):
    placed = (
        P(None, ("ctx", "fsdp"), None),
        P(None, ("ctx", "fsdp"), None),
        P("section", "fsdp"),
        P("section", "fsdp", None),
        P("section", "fsdp", None),
        P("section", "fsdp"),
        P("section", "fsdp", None),
        P("section", "fsdp", None),
        P(),
    )
    return jax.shard_map(
        on_device,
        mesh=mesh,
        in_specs=placed,
        out_specs=(
            P("section", None, ("ctx", "fsdp"), None),
            P("section", None, ("ctx", "fsdp"), None),
            P("section", "fsdp"),
            P("section", "fsdp", None),
            P("section", "fsdp", None),
            P("section", "fsdp"),
            P("section", "fsdp", None),
            P("section", "fsdp", None),
        ),
        check_vma=False,
    )
```

```python
import functools

import jax
import jax.numpy as jnp
import numpy as np
from jax import lax
from jax.experimental import pallas as pl
from jax.experimental.pallas import tpu as pltpu
from jax.sharding import PartitionSpec as P

KV_HEADS = 8
HEAD = 96
LANES = 128
SPAN = 64
norm_eps = 1e-05
rope_base = 100000.0
masked_value = -1e30
BF = jnp.bfloat16
F32 = jnp.float32

MESH = pl.DeviceIdType.MESH


def greet():
    c = lax.axis_index("ctx")
    f = lax.axis_index("fsdp")
    barrier = pltpu.get_barrier_semaphore()
    inner = jnp.logical_and(c > 0, c < 3)
    for peer in (f + 2 - 4 * (f // 2), f + 1 - 2 * lax.rem(f, 2)):
        pl.semaphore_signal(barrier, inc=1, device_id={"fsdp": peer}, device_id_type=MESH)
    pl.semaphore_signal(barrier, inc=1, device_id={"ctx": lax.rem(c + 2, 4)}, device_id_type=MESH)

    @pl.when(c < 3)
    def _():
        pl.semaphore_signal(barrier, inc=1, device_id={"ctx": c + 1}, device_id_type=MESH)

    @pl.when(c > 0)
    def _():
        pl.semaphore_signal(barrier, inc=1, device_id={"ctx": c - 1}, device_id_type=MESH)

    @pl.when(inner)
    def _():
        pl.semaphore_wait(barrier, 5)

    @pl.when(jnp.logical_not(inner))
    def _():
        pl.semaphore_wait(barrier, 4)


def near_order(c):
    low = c < 2
    return [c, c + 1 - 2 * lax.rem(c, 2), jnp.where(low, 2, 1), jnp.where(low, 3, 0)]


def own_block(c, f):
    return c * 4 + lax.rem(f, 2) * 2 + f // 2


def gather_rows(whole, rows, send, recv, ready=None, started=None):
    c = lax.axis_index("ctx")
    f = lax.axis_index("fsdp")
    y = f // 2
    lane = lax.rem(f, 2)
    inner = jnp.logical_and(c > 0, c < 3)
    outer = jnp.logical_not(inner)
    order = near_order(c)
    pair = order[1]
    half = rows // 2
    to_across = {"fsdp": f + 2 - 4 * y}
    to_twin = {"fsdp": f + 1 - 2 * lane}
    to_pair = {"ctx": pair}

    def at(d, k, yy, h):
        return whole.at[pl.ds(pl.multiple_of((d * 4 + k * 2 + yy) * rows + h * half, half), half)]

    def block(d, k, yy):
        return whole.at[pl.ds(pl.multiple_of((d * 4 + k * 2 + yy) * rows, rows), rows)]

    def two(d, k):
        return whole.at[pl.ds(pl.multiple_of((d * 4 + k * 2) * rows, rows), 2 * rows)]

    def copy(src, slot, arrival, peer):
        return pltpu.make_async_remote_copy(
            src, src, send.at[slot], recv.at[arrival], device_id=peer, device_id_type=MESH
        )

    def go(src, slot, arrival, peer, when=None):
        one = copy(src, slot, arrival, peer)
        if when is None:
            one.start()
        else:
            pl.when(when)(one.start)

    def arrived(ref, arrival):
        copy(ref, 0, arrival, to_twin).wait_recv()

    def gone(count, slot):
        copy(whole.at[pl.ds(0, count * half)], slot, 0, to_twin).wait_send()

    for h in range(2):
        go(at(c, lane, y, h), 0, 2 * c + h, {"ctx": jnp.minimum(c + 1, 3)}, c < 3)
        go(at(c, lane, y, h), 1, 2 * c + h, {"ctx": jnp.maximum(c - 1, 0)}, c > 0)
        go(at(c, lane, y, h), 3, 8 + c, to_across)
    if started is not None:
        started()

    events = [
        (pair, 0),
        (jnp.where(inner, order[2], pair), jnp.where(inner, 0, 1)),
        (jnp.where(inner, pair, order[2]), jnp.where(inner, 1, 0)),
        (order[2], 1),
        (order[3], 0),
        (order[3], 1),
    ]

    def along(index):
        d, h = events[index]
        piece = at(d, lane, y, h)
        arrived(piece, 2 * d + h)
        go(piece, 2, 2 * d + h, {"ctx": jnp.where(d < c, c + 1, c - 1)}, inner)
        go(piece, 3, 8 + d, to_across, jnp.logical_or(d != pair, h == 0) if index in (1, 2) else None)

    def complete(d):
        arrived(two(d, 1 - lane), 13 + d)
        if ready is not None:
            ready(d)

    def pair_half(when):
        go(at(c, lane, 1 - y, 1), 4, 12, to_pair, when)

    along(0)
    along(1)
    along(2)
    arrived(block(c, lane, 1 - y), 8 + c)
    pair_half(outer)
    go(two(c, lane), 5, 13 + c, to_twin)
    along(3)
    complete(c)
    along(4)
    along(5)
    pair_half(inner)
    arrived(block(order[2], lane, 1 - y), 8 + order[2])
    go(two(order[2], lane), 5, 13 + order[2], to_twin)
    go(block(order[3], lane, y), 5, 13 + order[3], to_twin)
    complete(order[2])
    arrived(at(pair, lane, 1 - y, 0), 8 + pair)
    arrived(at(pair, lane, 1 - y, 1), 12)
    go(two(pair, lane), 5, 13 + pair, to_twin)
    arrived(block(order[3], lane, 1 - y), 8 + order[3])
    go(block(order[3], lane, 1 - y), 5, 17, to_twin)
    complete(pair)
    arrived(block(order[3], 1 - lane, y), 13 + order[3])
    arrived(block(order[3], 1 - lane, 1 - y), 17)
    if ready is not None:
        ready(order[3])
    pl.when(c < 3)(lambda: gone(2, 0))
    pl.when(c > 0)(lambda: gone(2, 1))
    pl.when(inner)(lambda: gone(6, 2))
    gone(7, 3)
    gone(1, 4)
    gone(16, 5)


GATHER_SENDS = 6
GATHER_RECVS = 18


def scatter_sum(part, total, land, send, recv, produce=None, meanwhile=None, ending=None):
    c = lax.axis_index("ctx")
    f = lax.axis_index("fsdp")
    y = f // 2
    lane = lax.rem(f, 2)
    inner = jnp.logical_and(c > 0, c < 3)
    rows = total.shape[0]
    half = rows // 2
    order = near_order(c)[::-1]
    to_across = {"fsdp": f + 2 - 4 * y}
    to_twin = {"fsdp": f + 1 - 2 * lane}
    to_pair = {"ctx": order[2]}

    def rows_at(d, yy, h):
        return pl.ds(pl.multiple_of((d * 4 + lane * 2 + yy) * rows + h * half, half), half)

    def copy(src, dst, slot, arrival, peer):
        return pltpu.make_async_remote_copy(
            src, dst, send.at[slot], recv.at[arrival], device_id=peer, device_id_type=MESH
        )

    def go(src, dst, slot, arrival, peer):
        copy(src, dst, slot, arrival, peer).start()

    def gone(count, slot):
        ref = part.at[pl.ds(0, count * half)]
        copy(ref, ref, slot, 0, to_twin).wait_send()

    def piece(slot, h):
        return land.at[slot, pl.ds(h * half, half)]

    def landed(ref, arrival):
        copy(ref, ref, 0, arrival, to_twin).wait_recv()
        return ref[...].astype(F32)

    def begin(step):
        d = order[step]
        if produce is not None:
            produce(d)
        for yy, slot in ((1 - y, step), (y, 27 + step)):
            other = pl.ds(pl.multiple_of((d * 4 + 2 - lane * 2 + yy) * rows, rows), rows)
            go(part.at[other], land.at[2 * step + yy], 0, slot, to_twin)

    def twin_there(step, yy, slot):
        ref = land.at[2 * step + yy]
        copy(ref, ref, 0, slot, to_twin).wait_recv()

    def over(step, h, first=False):
        d = order[step]
        if first:
            twin_there(step, 1 - y, step)
        mine = rows_at(d, 1 - y, h)
        value = part[mine, :].astype(F32) + piece(2 * step + 1 - y, h)[...].astype(F32)
        if (step, h) == (3, 1):
            value = value + landed(piece(17, 0), 26)
        part[mine, :] = value.astype(BF)
        if (step, h) == (2, 1):
            go(part.at[mine], piece(17, 0), 3, 26, to_pair)
        else:
            go(part.at[mine], piece(8 + step, h), 1, 8 + 2 * step + h, to_across)

    def onward(step, h, first=False):
        d = order[step]
        mine = rows_at(d, y, h)
        if first:
            twin_there(step, y, 27 + step)
        value = part[mine, :].astype(F32) + piece(2 * step + y, h)[...].astype(F32)
        if (step, h) != (2, 1):
            value = value + landed(piece(8 + step, h), 8 + 2 * step + h)
        if step == 3:
            total[h * half : (h + 1) * half, :] = value
            return
        part[mine, :] = value.astype(BF)

        if step < 2:

            @pl.when(inner)
            def _():
                part[mine, :] = (part[mine, :].astype(F32) + landed(piece(12 + d, h), 16 + 2 * d + h)).astype(BF)

        here = jnp.logical_and(d < c, d == c - 1)
        target = jnp.where(d > c, c + 1, c - 1)
        slot = jnp.where(here, 16, 12 + d)
        arrival = jnp.where(here, 24, 16 + 2 * d) + h
        if step == 0:
            target = jnp.where(inner, d, target)
            slot = jnp.where(inner, 18, slot)
            arrival = jnp.where(inner, 31 + h, arrival)
        go(part.at[mine], piece(slot, h), 2, arrival, {"ctx": target})

    begin(0)
    over(0, 0, True)
    over(0, 1)
    begin(1)
    begin(2)
    over(2, 1, True)
    over(1, 0, True)
    onward(0, 0, True)
    over(1, 1)
    onward(0, 1)
    if meanwhile is not None:
        meanwhile()
    begin(3)
    over(2, 0)
    onward(1, 0, True)
    over(3, 0, True)
    onward(1, 1)
    over(3, 1)
    onward(2, 1, True)
    onward(2, 0)
    if ending is not None:
        ending()
    for h in range(2):
        onward(3, h, h == 0)

        @pl.when(c > 0)
        def _():
            total[h * half : (h + 1) * half, :] += landed(piece(12 + c, h), 16 + 2 * c + h)

        @pl.when(c < 3)
        def _():
            total[h * half : (h + 1) * half, :] += landed(piece(16, h), 24 + h)

        @pl.when(jnp.logical_not(inner))
        def _():
            total[h * half : (h + 1) * half, :] += landed(piece(18, h), 31 + h)

    gone(16, 0)
    gone(7, 1)
    gone(6, 2)
    gone(1, 3)


SCATTER_SENDS = 4
SCATTER_RECVS = 33


def kernel_dot(left, right):
    return jnp.dot(left, right, preferred_element_type=F32)


def kernel_dot_nt(left, right):
    return lax.dot_general(left, right, (((1,), (1,)), ((), ())), preferred_element_type=F32)


def kernel_dot_tn(left, right):
    return lax.dot_general(left, right, (((0,), (0,)), ((), ())), preferred_element_type=F32)


def turn(values):
    return pltpu.roll(values, SPAN, axis=1)


def mean_square(values):
    return lax.rsqrt(jnp.mean(values * values, axis=-1, keepdims=True) + norm_eps)


def greet_all(peers):
    barrier = pltpu.get_barrier_semaphore()
    for peer in peers:
        pl.semaphore_signal(barrier, inc=1, device_id=peer, device_id_type=MESH)
    return len(peers)


def greet_more(peers):
    c = lax.axis_index("ctx")
    barrier = pltpu.get_barrier_semaphore()
    count = greet_all(peers)
    inner = jnp.logical_and(c > 0, c < 3)

    @pl.when(c < 3)
    def _():
        pl.semaphore_signal(barrier, inc=1, device_id={"ctx": c + 1}, device_id_type=MESH)

    @pl.when(c > 0)
    def _():
        pl.semaphore_signal(barrier, inc=1, device_id={"ctx": c - 1}, device_id_type=MESH)

    @pl.when(inner)
    def _():
        pl.semaphore_wait(barrier, count + 2)

    @pl.when(jnp.logical_not(inner))
    def _():
        pl.semaphore_wait(barrier, count + 1)


def head_choice(value_part):
    source = lax.broadcasted_iota(jnp.int32, (4 * HEAD, 4 * LANES), 0)
    lane = lax.broadcasted_iota(jnp.int32, (4 * HEAD, 4 * LANES), 1)
    head = lane // LANES
    inside = lane - head * LANES
    if value_part:
        wanted = jnp.where(inside < HEAD, head * HEAD + inside, -1)
    else:
        half = inside // SPAN
        place = inside - half * SPAN
        wanted = jnp.where(place < HEAD // 2, head * HEAD + half * (HEAD // 2) + place, -1)
    return jnp.where(source == wanted, 1.0, 0.0).astype(BF)


class Share:
    def __init__(self, sources, targets, scratch, sems):
        self.mix, self.out, self.gate_up, self.down, self.attention_gain, self.feed_gain = sources
        self.w_mix, self.w_gate, self.w_out, self.w_down, self.w_gains = targets
        self.mix_v, self.heads_v, self.gate_s, self.out_s, self.down_s, self.gains = scratch
        self.local, self.send, self.recv = sems
        self.s = lax.axis_index("section")
        self.c = lax.axis_index("ctx")
        self.f = lax.axis_index("fsdp")
        self.other = 1 - self.s
        self.depth = self.mix.shape[1]
        self.units = self.w_down.shape[1]
        self.peers = [lax.rem(self.f + k, 4) for k in range(1, 4)]
        self.rows = pl.ds(pl.multiple_of(self.f * self.depth, self.depth), self.depth)
        self.pending = []

    def greeted(self):
        return (
            [{"fsdp": peer} for peer in self.peers]
            + [{"section": self.other}, {"ctx": lax.rem(self.c + 2, 4)}]
            + [{"section": self.other, "fsdp": peer} for peer in self.peers]
        )

    def copy(self, src, dst, slot, arrival, peer):
        return pltpu.make_async_remote_copy(
            src, dst, self.send.at[slot], self.recv.at[arrival], device_id=peer, device_id_type=MESH
        )

    def go(self, src, dst, slot, arrival, peer):
        one = self.copy(src, dst, slot, arrival, peer)
        one.start()
        self.pending.append(one)

    def keep(self, src, dst, slot):
        one = pltpu.make_async_copy(src, dst, self.local.at[slot])
        one.start()
        return one

    def load(self):
        self.gains[...] = jnp.zeros_like(self.gains)
        self.gains[0:1, :] = self.attention_gain[...]
        self.gains[1:2, :] = self.feed_gain[...]
        self.loaded = self.keep(self.mix.at[0], self.mix_v, 0)
        out_rows = self.out.at[0, pl.ds(pl.multiple_of(self.c * HEAD, HEAD), HEAD)]
        down_rows = self.down.at[0, pl.ds(pl.multiple_of(self.c * self.units, self.units), self.units)]
        self.staged = [
            self.keep(self.gate_piece(self.f, part), self.gate_s.at[:, pl.ds(part * self.units, self.units)], 5 + part)
            for part in range(2)
        ]
        self.staged.append(self.keep(out_rows, self.out_s, 7))
        self.staged.append(self.keep(down_rows, self.down_s, 8))

    def lanes(self, peer, part):
        head = peer * 4 + self.c
        start = head * LANES if part == 0 else (16 + 8 * (part - 1) + head // 2) * LANES
        return self.heads_v.at[:, pl.ds(pl.multiple_of(start, LANES), LANES)]

    def put(self, part):
        return self.w_mix.at[self.s, self.rows, pl.ds(part * LANES, LANES)]

    def send_mix(self):
        self.loaded.wait()
        for g in range(8):
            self.heads_v[:, g * 4 * LANES : (g + 1) * 4 * LANES] = kernel_dot(
                self.mix_v[:, g * 4 * HEAD : (g + 1) * 4 * HEAD], head_choice(g >= 6)
            ).astype(BF)
        for k, peer in enumerate(self.peers):
            for part in range(3):
                self.copy(self.lanes(peer, part), self.put(part), k, self.f, {"fsdp": peer}).start()
        self.own_mix = [self.keep(self.lanes(self.f, part), self.put(part), 2 + part) for part in range(3)]
        for one in self.staged:
            one.wait()
        self.own_gate = self.keep(self.gate_s, self.slab(self.w_gate, self.f), 5)
        self.own_out = self.keep(self.out_s, self.w_out.at[self.s], 7)
        self.own_down = self.keep(self.down_s, self.w_down.at[self.s], 8)
        mine = self.w_gains.at[self.s, :, pl.ds(pl.multiple_of(self.f * self.depth, self.depth), self.depth)]
        for k, peer in enumerate(self.peers):
            self.go(self.gains, mine, 20 + k, 16 + 4 * self.s + self.f, {"fsdp": peer})
            self.go(self.gains, mine, 23 + k, 16 + 4 * self.s + self.f, {"section": self.other, "fsdp": peer})
        self.go(self.gains, mine, 26, 16 + 4 * self.s + self.f, {"section": self.other})
        self.own_gains = self.keep(self.gains, mine, 1)

    def gate_piece(self, peer, part):
        hidden_units = self.gate_up.shape[2] // 2
        start = pl.multiple_of(part * hidden_units + (peer * 4 + self.c) * self.units, self.units)
        return self.gate_up.at[0, :, pl.ds(start, self.units)]

    def gate_put(self, part):
        return self.w_gate.at[self.s, self.rows, pl.ds(part * self.units, self.units)]

    def send_gate(self):
        for k, peer in enumerate(self.peers):
            for part in range(2):
                self.copy(self.gate_piece(peer, part), self.gate_put(part), 3 + k, 4 + self.f, {"fsdp": peer}).start()

    def slab(self, ref, origin):
        return ref.at[self.s, pl.ds(pl.multiple_of(origin * self.depth, self.depth), self.depth)]

    def cross_slab(self, ref, k, slot, arrival, base):
        origin = lax.rem(self.f + 3 - k, 4)
        block = self.slab(ref, origin)
        self.copy(block, block, 0, arrival + origin, {"fsdp": origin}).wait_recv()
        self.go(block, block, slot + k, base + origin, {"section": self.other})

    def cross_mix(self, between):
        for one in self.own_mix:
            one.wait()
        self.go(self.slab(self.w_mix, self.f), self.slab(self.w_mix, self.f), 6, 8 + self.f, {"section": self.other})
        between()
        for k in range(3):
            self.cross_slab(self.w_mix, k, 7, 0, 8)
        self.send_gate()
        self.go(self.out_s, self.w_out.at[self.s], 10, 24, {"section": self.other})
        self.go(self.gate_s, self.slab(self.w_gate, self.f), 11, 12 + self.f, {"section": self.other})

    def cross_gate(self):
        for k in range(3):
            self.cross_slab(self.w_gate, k, 12, 4, 12)
        self.go(self.down_s, self.w_down.at[self.s], 15, 25, {"section": self.other})

    def there(self, ref, arrival):
        self.copy(ref, ref, 0, arrival, {"section": self.other}).wait_recv()

    def mix_there(self):
        for one in (self.own_gains, self.own_gate, self.own_out, self.own_down):
            one.wait()
        for origin in range(4):
            rows = pl.ds(origin * self.depth, self.depth)
            self.there(self.w_mix.at[self.other, rows], 8 + origin)
            self.there(self.w_gains.at[self.other, :, rows], 16 + 4 * self.other + origin)
        for k in range(3):
            origin = lax.rem(self.f + 3 - k, 4)
            columns = pl.ds(pl.multiple_of(origin * self.depth, self.depth), self.depth)
            self.there(self.w_gains.at[self.s, :, columns], 16 + 4 * self.s + origin)
        self.there(self.w_out.at[self.other], 24)

    def gate_there(self):
        for origin in range(4):
            self.there(self.w_gate.at[self.other, pl.ds(origin * self.depth, self.depth)], 12 + origin)

    def down_there(self):
        self.there(self.w_down.at[self.other], 25)

    def finish(self):
        for k, peer in enumerate(self.peers):
            block = self.slab(self.w_mix, self.f)
            self.copy(block, block, k, 0, {"fsdp": peer}).wait_send()
            block = self.slab(self.w_gate, self.f)
            self.copy(block, block, 3 + k, 0, {"fsdp": peer}).wait_send()
        for one in self.pending:
            one.wait_send()


class Loads:
    def __init__(self, sems):
        self.sems = sems
        self.copies = []

    def start(self, src, dst):
        one = pltpu.make_async_copy(src, dst, self.sems.at[len(self.copies)])
        one.start()
        self.copies.append(one)
        return one


def plane_rows(d, rows):
    return pl.ds(pl.multiple_of(d * 4 * rows, 4 * rows), 4 * rows)


def make_tables(block_order, frequency, cosine, sine, place_col, place_row):
    s = lax.axis_index("section")
    blocks = block_order.shape[1]
    rows = place_col.shape[0] // blocks
    order = jnp.where(s == 0, block_order[0:1, :], block_order[1:2, :])
    inside_col = lax.broadcasted_iota(jnp.int32, (rows, 1), 0)
    inside_row = lax.broadcasted_iota(jnp.int32, (1, 2 * rows), 1)
    firsts = []
    for b in range(blocks):
        source = b - b % 4 + (b % 2) * 2 + (b % 4) // 2
        firsts.append(order[:, source : source + 1] * rows)
        place_col[b * rows : (b + 1) * rows, :] = firsts[b] + inside_col
    for b in range(0, blocks, 2):
        place_row[:, b * rows : (b + 2) * rows] = jnp.where(
            inside_row < rows, firsts[b] + inside_row, firsts[b + 1] + inside_row - rows
        )
    lane = lax.broadcasted_iota(jnp.int32, (4 * rows, LANES), 1)
    for part in range(blocks // 4):
        here = pl.ds(part * 4 * rows, 4 * rows)
        angles = place_col[here, :].astype(F32) * frequency[...]
        wave = jnp.sin(angles)
        cosine[here, :] = jnp.cos(angles)
        sine[here, :] = jnp.where(lane < SPAN, -wave, wave)


def forward_body(layer, share, x_own, weights, tables, kept, scratch, sems, prepare=None):
    w_mix, w_gate, w_out, w_down, w_gains = weights
    cosine, sine, place_col, place_row = tables
    normed_o, q_o, k_o, v_o, context_o, log_o, middle_o, normed_two_o, both_o, result_o = kept
    (x_v, normed_v, q_v, k_v, v_v, context_v, log_v, middle_v, two_v, both_v, hidden_v, result_v,
     mix_v, gate_v, out_v, down_v, gains_v, part_v, land_a, land_b, total_v) = scratch
    local, save, send_a, recv_a, send_b, recv_b, send_c, recv_c, send_d, recv_d = sems
    c = lax.axis_index("ctx")
    f = lax.axis_index("fsdp")
    rows = x_own.shape[0]
    units = down_v.shape[0]
    own_rows = pl.ds(pl.multiple_of(own_block(c, f) * rows, rows), rows)
    loads = Loads(local)
    saves = Loads(save)
    load_x = loads.start(x_own, x_v.at[own_rows])
    out_v[...] = jnp.zeros_like(out_v)

    def load_first():
        return [
            loads.start(w_gains.at[layer], gains_v),
            loads.start(w_mix.at[layer], mix_v),
            loads.start(w_out.at[layer], out_v.at[pl.ds(0, HEAD)]),
        ]

    def project(d):
        here = plane_rows(d, rows)
        x = x_v[here, :].astype(F32)
        normed = (x * mean_square(x) * gains_v[0:1, :].astype(F32)).astype(BF)
        normed_v[here, :] = normed
        mixed = kernel_dot(normed, mix_v[...])
        cos = cosine[here, :]
        sin = sine[here, :]
        q = mixed[:, :LANES]
        k = mixed[:, LANES : 2 * LANES]
        q_v[here, :] = (q * cos + turn(q) * sin).astype(BF)
        k_v[here, :] = (k * cos + turn(k) * sin).astype(BF)
        v_v[here, :] = mixed[:, 2 * LANES :].astype(BF)

    if share is None:
        first = load_first()
        load_gate = loads.start(w_gate.at[layer], gate_v)
        load_down = loads.start(w_down.at[layer], down_v)
        greet()
        load_x.wait()
        for one in first:
            one.wait()
        gather_rows(x_v, rows, send_a, recv_a, project)
    else:
        share.load()
        greet_more(share.greeted())
        load_x.wait()
        share.send_mix()
        gather_rows(x_v, rows, send_a, recv_a, started=lambda: share.cross_mix(prepare))
        share.mix_there()
        first = load_first()
        for one in first:
            one.wait()
        for d in range(4):
            project(d)
        share.cross_gate()
    for src, dst in ((normed_v, normed_o), (q_v, q_o), (k_v, k_o), (v_v, v_o)):
        saves.start(src, dst)
    scale = HEAD ** (-0.5)

    def attention(d):
        here = plane_rows(d, rows)
        scores = kernel_dot_nt(q_v[here, :], k_v[...]) * scale
        allowed = place_row[...] <= place_col[here, :]
        scores = jnp.where(allowed, scores, masked_value)
        top = jnp.max(scores, axis=-1, keepdims=True)
        weights = jnp.exp(scores - top)
        amount = jnp.sum(weights, axis=-1, keepdims=True)
        context = (kernel_dot(weights.astype(BF), v_v[...]) / amount).astype(BF)
        context_v[here, :] = context
        log_v[here, :] = jnp.broadcast_to(top + jnp.log(amount), (4 * rows, LANES))
        part_v[here, :] = kernel_dot(context, out_v[...]).astype(BF)

    scatter_sum(part_v, total_v, land_a, send_b, recv_b, attention)
    saves.start(context_v, context_o)
    saves.start(log_v, log_o)
    middle = x_v[own_rows, :].astype(F32) + total_v[...]
    middle_v[...] = middle
    saves.start(middle_v, middle_o)
    two_v[own_rows, :] = (middle * mean_square(middle) * gains_v[1:2, :].astype(F32)).astype(BF)

    def gate_ready():
        if share is None:
            load_gate.wait()
        else:
            share.gate_there()
            loads.start(w_gate.at[layer], gate_v).wait()

    def feed(d):
        here = plane_rows(d, rows)
        both = kernel_dot(two_v[here, :], gate_v[...])
        both_v[here, :] = both
        gate = both[:, :units]
        hidden_v[here, :] = (gate * jax.nn.sigmoid(gate) * both[:, units:]).astype(BF)

    gather_rows(two_v, rows, send_c, recv_c, feed, gate_ready)
    saves.start(two_v, normed_two_o)
    saves.start(both_v, both_o)
    if share is None:
        load_down.wait()
    else:
        share.down_there()
        loads.start(w_down.at[layer], down_v).wait()

    def lower(d):
        here = plane_rows(d, rows)
        part_v[here, :] = kernel_dot(hidden_v[here, :], down_v[...]).astype(BF)

    scatter_sum(part_v, total_v, land_b, send_d, recv_d, lower)
    result_v[...] = (middle_v[...] + total_v[...]).astype(BF)
    saves.start(result_v, result_o)
    for one in saves.copies:
        one.wait()
    if share is not None:
        share.finish()


def forward_kernel(layer, *refs):
    x_own, *refs = refs
    weights, refs = refs[:5], refs[5:]
    tables, refs = refs[:4], refs[4:]
    kept, refs = refs[:10], refs[10:]
    scratch, sems = refs[:21], refs[21:]
    forward_body(layer, None, x_own, weights, tables, kept, scratch, sems)


def forward_share_kernel(*refs):
    inputs, *refs = refs
    sources, refs = refs[:6], refs[6:]
    (block_order, frequency), refs = refs[:2], refs[2:]
    kept, refs = refs[:10], refs[10:]
    weights, refs = refs[:5], refs[5:]
    tables, refs = refs[:4], refs[4:]
    scratch, refs = refs[:21], refs[21:]
    packing, refs = refs[:6], refs[6:]
    sems, share_sems = refs[:10], refs[10:]
    share = Share(sources, weights, packing, share_sems)
    forward_body(
        0, share, inputs.at[lax.axis_index("section")], weights, tables, kept, scratch, sems,
        lambda: make_tables(block_order, frequency, *tables),
    )


def backward_body(layer, grad_own, weights, tables, saved, outs, scratch, sems, returning):
    w_mix, w_gate, w_out, w_down, w_gains = weights
    cosine, sine, place_col, place_row = tables
    x_own, normed, q, k, v, context, log, middle, normed_two, both = saved
    (grad_v, x_v, normed_v, q_v, k_v, v_v, context_v, log_v, middle_v, two_v, both_v, both_grad_v, hidden_v,
     low_v, mixed_v, kv_land, kv_v, key_grad_v, value_grad_v, start_v, start_low_v,
     mix_grad_v, gate_grad_v, out_grad_v, down_grad_v, gain_grad_v,
     mix_v, gate_v, out_v, down_v, gains_v, part_v, land_a, land_b, total_v) = scratch
    local, save, pair_sems, send_a, recv_a, send_b, recv_b, send_c, recv_c, send_d, recv_d = sems
    c = lax.axis_index("ctx")
    f = lax.axis_index("fsdp")
    odd = lax.rem(c, 2)
    rows = x_own.shape[0]
    units = down_v.shape[0]
    own_rows = pl.ds(pl.multiple_of(own_block(c, f) * rows, rows), rows)
    loads = Loads(local)
    saves = Loads(save)
    load_grad = loads.start(grad_own, grad_v.at[own_rows])
    load_down = loads.start(w_down.at[layer], down_v)
    load_both = loads.start(both, both_v)
    load_gate = loads.start(w_gate.at[layer], gate_v)
    out_v[...] = jnp.zeros_like(out_v)
    key_grad_v[...] = jnp.zeros_like(key_grad_v)
    value_grad_v[...] = jnp.zeros_like(value_grad_v)
    gain_grad_v[...] = jnp.zeros_like(gain_grad_v)
    if returning is None:
        greet()
    else:
        peers = [{"fsdp": lax.rem(f + k, 4)} for k in range(1, 4)]
        greet_more(peers + [{"section": 1 - lax.axis_index("section")}, {"ctx": lax.rem(c + 2, 4)}])
    load_grad.wait()
    later = [
        loads.start(src, dst)
        for src, dst in (
            (normed_two, two_v), (middle, middle_v), (w_gains.at[layer], gains_v),
            (w_out.at[layer], out_v.at[pl.ds(0, HEAD)]), (q, q_v), (k, k_v), (v, v_v),
            (context, context_v), (log, log_v), (w_mix.at[layer], mix_v), (normed, normed_v), (x_own, x_v),
        )
    ]
    load_down.wait()
    load_both.wait()
    if returning is not None:
        begin_old, begin_feed, begin_mix, begin_return, finish = returning
        begin_old()

    def feed(d):
        here = plane_rows(d, rows)
        hidden_grad = kernel_dot_nt(grad_v[here, :], down_v[...])
        gate = both_v[here, :units]
        up = both_v[here, units:]
        sig = jax.nn.sigmoid(gate)
        silu = gate * sig
        hidden_v[here, :] = (silu * up).astype(BF)
        both_grad_v[here, :units] = (hidden_grad * up * sig * (1.0 + gate * (1.0 - sig))).astype(BF)
        both_grad_v[here, units:] = (hidden_grad * silu).astype(BF)

    gather_rows(grad_v, rows, send_a, recv_a, feed)
    load_gate.wait()

    def spread(d):
        here = plane_rows(d, rows)
        part_v[here, :] = kernel_dot_nt(both_grad_v[here, :], gate_v[...]).astype(BF)

    def feed_weights():
        later[0].wait()
        down_grad_v[...] = kernel_dot_tn(hidden_v[...], grad_v[...]).astype(BF)
        for part in range(2):
            gate_grad_v[part] = kernel_dot_tn(
                two_v[...], both_grad_v[:, part * units : (part + 1) * units]
            ).astype(BF)
        if returning is None:
            saves.start(down_grad_v, outs[4])
            saves.start(gate_grad_v, outs[2])
        else:
            begin_feed()

    scatter_sum(part_v, total_v, land_a, send_b, recv_b, spread, feed_weights)
    for one in later[1:]:
        one.wait()

    def norm_grads(error, value, gain, row):
        factor = mean_square(value)
        shaped = error * gain
        common = jnp.mean(shaped * value, axis=-1, keepdims=True)
        gain_grad_v[row : row + 1, :] = jnp.sum(error * value * factor, axis=0, keepdims=True)
        return factor * shaped - value * (factor * factor * factor) * common

    middle_grad = norm_grads(total_v[...], middle_v[...], gains_v[1:2, :].astype(F32), 1)
    middle_grad = middle_grad + grad_v[own_rows, :].astype(F32)
    middle_v[...] = middle_grad
    low_v[own_rows, :] = middle_grad.astype(BF)
    scale = HEAD ** (-0.5)

    def attention(d):
        here = plane_rows(d, rows)
        context_grad = kernel_dot_nt(low_v[here, :], out_v[...])
        common = jnp.sum(context_grad * context_v[here, :].astype(F32), axis=-1, keepdims=True)
        context_grad = context_grad.astype(BF)
        queries = q_v[here, :]
        scores = kernel_dot_nt(queries, k_v[...]) * scale
        allowed = place_row[...] <= place_col[here, :]
        weights = jnp.exp(jnp.where(allowed, scores, masked_value) - log_v[here, 0:1])
        weight_grad = kernel_dot_nt(context_grad, v_v[...])
        score_grad = (weights * (weight_grad - common)).astype(BF)
        value_grad_v[...] += kernel_dot_tn(weights.astype(BF), context_grad)
        key_grad_v[...] += kernel_dot_tn(score_grad, queries)
        query_grad = kernel_dot(score_grad, k_v[...]) * scale
        mixed_v[here, :LANES] = (query_grad * cosine[here, :] - turn(query_grad) * sine[here, :]).astype(BF)

    gather_rows(low_v, rows, send_c, recv_c, attention)
    key_grad = key_grad_v[...] * scale
    mixed_v[:, LANES : 2 * LANES] = (key_grad * cosine[...] - turn(key_grad) * sine[...]).astype(BF)
    mixed_v[:, 2 * LANES :] = value_grad_v[...].astype(BF)
    pair = {"ctx": c + 1 - 2 * odd}

    def pair_copy(part):
        return pltpu.make_async_remote_copy(
            mixed_v.at[:, pl.ds(part * LANES, LANES)], kv_land, pair_sems.at[0], pair_sems.at[1],
            device_id=pair, device_id_type=MESH,
        )

    pl.when(odd == 0)(pair_copy(2).start)
    pl.when(odd == 1)(pair_copy(1).start)

    def spread_two(d):
        here = plane_rows(d, rows)
        part_v[here, :] = kernel_dot_nt(mixed_v[here, :], mix_v[...]).astype(BF)

    def mix_weights():
        out_grad_v[...] = kernel_dot_tn(context_v[...], low_v[...])[:HEAD].astype(BF)
        half = HEAD // 2
        columns = kernel_dot_tn(mixed_v[:, :LANES], normed_v[...])
        mix_grad_v[:half, :] = columns[:half].astype(BF)
        mix_grad_v[half:HEAD, :] = columns[SPAN : SPAN + half].astype(BF)
        pair_copy(1).wait_recv()
        mine = jnp.where(odd == 0, mixed_v[:, LANES : 2 * LANES].astype(F32), mixed_v[:, 2 * LANES :].astype(F32))
        kv_v[...] = (mine + kv_land[...].astype(F32)).astype(BF)
        columns = kernel_dot_tn(kv_v[...], normed_v[...])
        mix_grad_v[HEAD : HEAD + half, :] = columns[:half].astype(BF)
        mix_grad_v[HEAD + half :, :] = jnp.where(
            odd == 0, columns[SPAN : SPAN + half], columns[half:HEAD]
        ).astype(BF)
        if returning is None:
            saves.start(out_grad_v, outs[3])
            saves.start(mix_grad_v, outs[1])
        else:
            begin_mix()

    scatter_sum(part_v, total_v, land_b, send_d, recv_d, spread_two, mix_weights,
                None if returning is None else begin_return)
    start_grad = norm_grads(total_v[...], x_v[...].astype(F32), gains_v[0:1, :].astype(F32), 0) + middle_v[...]
    start_v[...] = start_grad
    if returning is None:
        saves.start(start_v, outs[0])
        start_low_v[...] = start_grad.astype(BF)
        saves.start(start_low_v, outs[6])
        saves.start(gain_grad_v, outs[5])
    else:
        finish(gain_grad_v)
    pair_copy(1).wait_send()
    for one in saves.copies:
        one.wait()


SAVED = 10
BACK_SCRATCH = 35


def backward_kernel(layer, *refs):
    grad_own, *refs = refs
    weights, refs = refs[:5], refs[5:]
    tables, refs = refs[:4], refs[4:]
    saved, refs = refs[:SAVED], refs[SAVED:]
    outs, refs = refs[:7], refs[7:]
    scratch, sems = refs[:BACK_SCRATCH], refs[BACK_SCRATCH:]
    backward_body(layer, grad_own.at[lax.axis_index("section")], weights, tables, saved, outs, scratch, sems, None)


def backward_return_kernel(*refs):
    grad_own, *refs = refs
    weights, refs = refs[:5], refs[5:]
    tables, refs = refs[:4], refs[4:]
    saved, refs = refs[:SAVED], refs[SAVED:]
    (start_old, mix_old, gate_old, out_old, down_old, gain_old), refs = refs[:6], refs[6:]
    (result_new, result_old), refs = refs[:2], refs[2:]
    (results_o, starts_o), refs = refs[:2], refs[2:]
    finals, refs = refs[:5], refs[5:]
    scratch, refs = refs[:BACK_SCRATCH], refs[BACK_SCRATCH:]
    own, refs = refs[:10], refs[10:]
    sems, return_sems, swap_sems = refs[:11], refs[11:16], refs[16]
    start_new = scratch[19]
    mix_new, gate_new, out_new, down_new, gain_new = scratch[21:26]
    gain_v = own[8]
    s = lax.axis_index("section")
    begin_old, begin_feed, begin_mix, begin_return, steps_after, wait_all = returner(
        tuple(finals) + tuple(own), return_sems,
        gate_new, down_new, mix_new, out_new, gate_old, down_old, mix_old, out_old,
    )

    def swap_copy(src, dst, slot):
        return pltpu.make_async_remote_copy(
            src, dst, swap_sems.at[slot], swap_sems.at[2 + slot], device_id={"section": 1 - s}, device_id_type=MESH
        )

    def swap_rows(away, home, out, slot):
        swap_copy(away, out.at[s], slot).start()
        pltpu.make_async_copy(home, out.at[s], swap_sems.at[4 + slot]).start()

    def finish(gain_grad_v):
        @pl.when(s == 0)
        def _():
            swap_rows(result_old, result_new, results_o, 0)
            swap_rows(start_old, start_new, starts_o, 1)

        @pl.when(s == 1)
        def _():
            swap_rows(result_new, result_old, results_o, 0)
            swap_rows(start_new, start_old, starts_o, 1)

        gain_v[0] = jnp.zeros(gain_v.shape[1:], F32)
        gain_v[0, 0:2, :] = gain_grad_v[...]
        gain_v[0, 2:4, :] = gain_old[...]
        steps_after()
        wait_all()
        for slot, out in enumerate((results_o, starts_o)):
            pltpu.make_async_copy(out.at[s], out.at[s], swap_sems.at[4 + slot]).wait()
            swap_copy(out.at[s], out.at[1 - s], slot).wait()

    saved = [saved[0].at[s], *saved[1:]]
    backward_body(0, grad_own, weights, tables, saved, None, scratch, sems, (begin_old, begin_feed, begin_mix, begin_return, finish))


def link_sems():
    dma = pltpu.SemaphoreType.DMA
    return [dma((GATHER_SENDS,)), dma((GATHER_RECVS,)), dma((SCATTER_SENDS,)), dma((SCATTER_RECVS,))] * 2


def low(*shape):
    return (shape, BF)


def full(*shape):
    return (shape, F32)


def shapes(specs):
    return [jax.ShapeDtypeStruct(*one) for one in specs]


def rooms(specs):
    return [pltpu.VMEM(*one) for one in specs]


def signals(*counts):
    return [pltpu.SemaphoreType.DMA((count,)) for count in counts]


def forward_scratch(rows, width, units):
    length = 16 * rows
    return [low(length, width), low(length, width)] + [low(length, LANES)] * 4 + [
        full(length, LANES), full(rows, width), low(length, width), full(length, 2 * units), low(length, units),
        low(rows, width), low(width, 3 * LANES), low(width, 2 * units), low(LANES, width), low(units, width),
        low(16, width), low(length, width), low(19, rows, width), low(19, rows, width), full(rows, width)]


def forward_kept(rows, width, units):
    length = 16 * rows
    return [low(length, width)] + [low(length, LANES)] * 4 + [
        full(length, LANES), full(rows, width), low(length, width), full(length, 2 * units), low(rows, width)]


ANYWHERE = pl.BlockSpec(memory_space=pl.ANY)
INSIDE = pl.BlockSpec(memory_space=pltpu.VMEM)


def forward_share_call(inputs, shards, gains, block_order):
    rows, width = inputs.shape[1:]
    length = 16 * rows
    depth = shards[0].shape[1]
    units = shards[2].shape[2] // 32
    frequency = np.zeros((2, SPAN), np.float32)
    frequency[:, : HEAD // 2] = np.float32(rope_base) ** (-(np.arange(HEAD // 2, dtype=np.float32) * 2.0 / HEAD))
    packing = [low(depth, shards[0].shape[2]), low(depth, 32 * LANES), low(depth, 2 * units), low(HEAD, width),
               low(units, width), low(16, depth)]
    kept = forward_kept(rows, width, units)
    weights = [low(2, width, 3 * LANES), low(2, width, 2 * units), low(2, HEAD, width), low(2, units, width), low(2, 16, width)]
    tables = [full(length, LANES), full(length, LANES), ((length, 1), jnp.int32), ((1, length), jnp.int32)]
    return pl.pallas_call(
        forward_share_kernel,
        out_shape=shapes(kept + weights + tables),
        in_specs=[ANYWHERE] * 5 + [INSIDE] * 4,
        out_specs=[ANYWHERE] * 15 + [INSIDE] * 4,
        scratch_shapes=rooms(forward_scratch(rows, width, units) + packing) + signals(6, 10) + link_sems()
        + signals(9, 27, 26),
        compiler_params=pltpu.CompilerParams(collective_id=0, has_side_effects=True, vmem_limit_bytes=60 << 20),
    )(inputs, *shards, *gains, block_order, jnp.asarray(frequency.reshape(1, LANES)))


def forward_call(layer, x_own, weights, tables):
    rows, width = x_own.shape
    units = weights[3].shape[1]
    kept = forward_kept(rows, width, units)
    return pl.pallas_call(
        functools.partial(forward_kernel, layer),
        out_shape=shapes(kept),
        in_specs=[ANYWHERE] * 6 + [INSIDE] * 4,
        out_specs=[ANYWHERE] * len(kept),
        scratch_shapes=rooms(forward_scratch(rows, width, units)) + signals(6, 10) + link_sems(),
        compiler_params=pltpu.CompilerParams(collective_id=layer, has_side_effects=True, vmem_limit_bytes=60 << 20),
    )(x_own, *weights, *tables)


def backward_call(layer, grad_own, weights, tables, saved, old=(), results=()):
    rows, width = grad_own.shape[-2:]
    length = 16 * rows
    units = weights[3].shape[1]
    depth = width // 4
    returning = layer == 0
    anywhere = pl.BlockSpec(memory_space=pl.ANY)
    inside = pl.BlockSpec(memory_space=pltpu.VMEM)
    grads = [low(2 * HEAD, width), low(2, width, units), low(HEAD, width), low(units, width), full(2, width)]
    scratch = [low(length, width), low(rows, width), low(length, width)] + [low(length, LANES)] * 4 + [
        full(length, LANES), full(rows, width), low(length, width), full(length, 2 * units), low(length, 2 * units),
        low(length, units), low(length, width), low(length, 3 * LANES), low(length, LANES), low(length, LANES),
        full(length, LANES), full(length, LANES),
        full(rows, width), low(rows, width)] + grads + [
        low(width, 3 * LANES), low(width, 2 * units), low(LANES, width), low(units, width),
        low(16, width), low(length, width), low(19, rows, width), low(19, rows, width), full(rows, width)]
    sems = signals(16, 7, 2) + link_sems()
    if returning:
        outs = [low(2, rows, width), full(2, rows, width), low(16 * 2 * HEAD, depth), low(2, depth, 16 * units),
                low(4 * HEAD, width), low(4 * units, width), full(8, width)]
        out_specs = [anywhere] * 6 + [inside]
        scratch += grads[:4] + grads[:4] + [full(5, 8, width), full(5, 8, width)]
        sems += signals(5, 23, 23, 50, 40, 6)
    else:
        outs = [full(rows, width)] + grads + [low(rows, width)]
        out_specs = [anywhere] * len(outs)
    return pl.pallas_call(
        backward_return_kernel if returning else functools.partial(backward_kernel, layer),
        out_shape=shapes(outs),
        in_specs=[anywhere] * 6 + [inside] * 4 + [anywhere] * SAVED
        + ([anywhere] * 5 + [inside] + [anywhere] * 2 if returning else []),
        out_specs=out_specs,
        scratch_shapes=rooms(scratch) + sems,
        compiler_params=pltpu.CompilerParams(
            collective_id=2 + layer, has_side_effects=True, vmem_limit_bytes=60 << 20),
    )(grad_own, *weights, *tables, *saved, *old, *results)


def returner(refs, sems, gate_new, down_new, mix_new, out_new, gate_old, down_old, mix_old, out_old):
    (mix_out, gate_out, out_out, down_out, gain_out,
     mix_v, gate_v, out_v, down_v, mix_x, gate_x, out_x, down_x, gain_v, gain_x) = refs
    local, send, recv, line_send, line_recv = sems
    s = lax.axis_index("section")
    c = lax.axis_index("ctx")
    f = lax.axis_index("fsdp")
    other = {"section": 1 - s}
    units = down_v.shape[0]
    depth = gate_out.shape[1]
    inner = jnp.logical_and(c > 0, c < 3)
    above = jnp.minimum(c + 1, 3)
    below = jnp.maximum(c - 1, 0)

    def copy(src, dst, slot, arrival, peer):
        return pltpu.make_async_remote_copy(
            src, dst, send.at[slot], recv.at[arrival], device_id=peer, device_id_type=MESH
        )

    def owner_part(owner):
        return pl.ds(pl.multiple_of(owner * depth, depth), depth)

    def cross_parts(away, theirs, first):
        for k in range(4):
            owner = lax.rem(f + k, 4)
            part = owner_part(owner)
            copy(away.at[:, part], theirs.at[:, part], first + k, first + owner, other).start()

    def cross_whole(away, theirs, slot):
        copy(away, theirs, slot, slot, other).start()

    def home(src, dst, k):
        pltpu.make_async_copy(src, dst, local.at[k]).start()

    def begin_old():
        @pl.when(s == 0)
        def _():
            cross_whole(down_old, down_x, 8)
            cross_parts(gate_old, gate_x, 0)
            cross_whole(out_old, out_x, 9)
            cross_parts(mix_old, mix_x, 4)

        @pl.when(s == 1)
        def _():
            home(down_old, down_v, 0)
            home(gate_old, gate_v, 1)
            home(out_old, out_v, 2)
            home(mix_old, mix_v, 3)

    def begin_feed():
        @pl.when(s == 0)
        def _():
            home(down_new, down_v, 0)
            home(gate_new, gate_v, 1)

        @pl.when(s == 1)
        def _():
            cross_whole(down_new, down_x, 8)
            cross_parts(gate_new, gate_x, 0)

    def begin_mix():
        @pl.when(s == 0)
        def _():
            home(out_new, out_v, 2)
            home(mix_new, mix_v, 3)

        @pl.when(s == 1)
        def _():
            cross_whole(out_new, out_x, 9)
            cross_parts(mix_new, mix_x, 4)

    def home_wait(k, dst):
        pltpu.make_async_copy(dst, dst, local.at[k]).wait()

    def arrived(ref, arrival):
        copy(ref, ref, 0, arrival, other).wait_recv()

    def gate_at(cc, ff):
        return gate_out.at[:, :, pl.ds(pl.multiple_of((ff * 4 + cc) * units, units), units)]

    def mix_at(cc, ff):
        return mix_out.at[pl.ds(pl.multiple_of((ff * 4 + cc) * 2 * HEAD, 2 * HEAD), 2 * HEAD)]

    def rows_at(ref, cc, count):
        return ref.at[pl.ds(pl.multiple_of(cc * count, count), count)]

    def out_at(cc, ff):
        return rows_at(out_out, cc, HEAD)

    def down_at(cc, ff):
        return rows_at(down_out, cc, units)

    origins = [lax.rem(f + k, 4) for k in (0, 3, 2, 1)]
    items = [(down_at, f)] + [(gate_at, one) for one in origins] + [(out_at, f)] + [(mix_at, one) for one in origins]

    def line(index, cc, slot, target):
        place, origin = items[index]
        return pltpu.make_async_remote_copy(
            place(cc, origin), place(cc, origin), line_send.at[slot], line_recv.at[cc * 10 + index],
            device_id={"ctx": target}, device_id_type=MESH,
        )

    def start_line(index):
        pl.when(c < 3)(line(index, c, index, above).start)
        pl.when(c > 0)(line(index, c, 10 + index, below).start)

    def fold(mine, theirs, arrival):
        arrived(theirs, arrival)
        mine[...] = (mine[...].astype(F32) + theirs[...].astype(F32)).astype(BF)

    def keep(src, dst):
        one = pltpu.make_async_copy(src, dst, local.at[4])
        one.start()
        one.wait()

    def whole_item(k, mine, theirs, arrival, place, index):
        home_wait(k, mine)
        fold(mine, theirs, arrival)
        keep(mine, place(c, f))
        start_line(index)

    def to_owner(k, mine, theirs, place, arrival_x, arrival_y, slot, index):
        owner = lax.rem(f + k, 4)
        rows = owner_part(owner)
        fold(mine.at[:, rows], theirs.at[:, rows], arrival_x + owner)
        if k:
            copy(mine.at[:, rows], place(c, f), slot + k, arrival_y + f, {"fsdp": owner}).start()
        else:
            keep(mine.at[:, rows], place(c, f))
            start_line(index)

    def from_owner(k, place, arrival, index):
        arrived(place(c, origins[k]), arrival + origins[k])
        start_line(index)

    gain_targets = [other, {"fsdp": f + 1 - 2 * lax.rem(f, 2)}, {"fsdp": f + 2 - 4 * (f // 2)},
                    {"ctx": c + 1 - 2 * lax.rem(c, 2)}, {"ctx": lax.rem(c + 2, 4)}]

    def gain_copy(k):
        return copy(gain_v.at[k], gain_x.at[k], 18 + k, 18 + k, gain_targets[k])

    def gain_sum(k):
        gain_copy(k).wait_recv()
        if k < 4:
            gain_v[k + 1] = gain_v[k] + gain_x[k]
            gain_copy(k + 1).start()
        else:
            gain_out[...] = gain_v[k] + gain_x[k]

    order = near_order(c)

    def onward(index, step):
        d = order[step]
        return line(index, d, 20 + (step - 1) * 10 + index, jnp.where(d < c, above, below))

    def pass_on(index, step):
        one = onward(index, step)
        one.wait_recv()
        pl.when(inner)(one.start)

    def near(index):
        pass_on(index, 1)
        pl.when(inner)(lambda: pass_on(index, 2))

    def far(index):
        pl.when(jnp.logical_not(inner))(lambda: pass_on(index, 2))
        pass_on(index, 3)

    def gate_first():
        home_wait(1, gate_v)
        to_owner(0, gate_v, gate_x, gate_at, 0, 10, 10, 1)

    def gate_rest(k):
        return lambda: to_owner(k, gate_v, gate_x, gate_at, 0, 10, 10, 1)

    def gate_from(k):
        return lambda: from_owner(k, gate_at, 10, 1 + k)

    def mix_first():
        home_wait(3, mix_v)
        to_owner(0, mix_v, mix_x, mix_at, 4, 14, 14, 6)

    def mix_rest(k):
        return lambda: to_owner(k, mix_v, mix_x, mix_at, 4, 14, 14, 6)

    def mix_from(k):
        return lambda: from_owner(k, mix_at, 14, 6 + k)

    def down_first():
        whole_item(0, down_v, down_x, 8, down_at, 0)

    def out_first():
        whole_item(2, out_v, out_x, 9, out_at, 5)

    def passing(*steps):
        return [functools.partial(near if sign > 0 else far, abs(sign) - 1) for sign in steps]

    after = [
        passing(1) + [gate_from(1), gate_from(2), gate_from(3), out_first, mix_first, mix_rest(1), mix_rest(2), mix_rest(3)],
        passing(2, -1, 3, -2, 4) + [mix_from(1), mix_from(2), mix_from(3)],
        passing(-3, 5, -4, 6, -5, 7),
        passing(-6, 8, -7, 9),
        passing(-8, 10, -9, -10),
    ]
    def begin_return():
        down_first()
        gate_first()
        for k in range(1, 4):
            gate_rest(k)()

    def steps_after():
        gain_copy(0).start()
        for k, steps in enumerate(after):
            for step in steps:
                step()
            gain_sum(k)

    def wait_all():
        for index in range(10):
            pl.when(c < 3)(line(index, c, index, above).wait_send)
            pl.when(c > 0)(line(index, c, 10 + index, below).wait_send)
            for step in range(1, 4):
                pl.when(inner)(onward(index, step).wait_send)
        for k in range(5):
            gain_copy(k).wait_send()
        for k in range(4):
            gate_part = gate_x.at[:, pl.ds(k * depth, depth)]
            mix_part = mix_x.at[:, pl.ds(k * depth, depth)]
            for slot in (k, 10 + k) if k else (k,):
                copy(gate_part, gate_part, slot, 0, other).wait_send()
                copy(mix_part, mix_part, 4 + slot, 0, other).wait_send()
        copy(down_x, down_x, 8, 0, other).wait_send()
        copy(out_x, out_x, 9, 0, other).wait_send()

    return begin_old, begin_feed, begin_mix, begin_return, steps_after, wait_all


def widen_kernel(mix, gate, out, down, gains, results, starts,
                 mix_f, gate_f, out_f, down_f, attention_f, feed_f, results_f, starts_f, places, turned):
    step = pl.program_id(0)
    rows = gate.shape[1]
    four = 4 * HEAD
    width = 4 * four

    @pl.when(step == 0)
    def _():
        s = lax.axis_index("section")
        f = lax.axis_index("fsdp")
        depth = attention_f.shape[1]
        columns = pl.ds(pl.multiple_of(f * depth, depth), depth)
        attention_f[...] = gains[pl.ds(2 * s, 1), columns]
        feed_f[...] = gains[pl.ds(2 * s + 1, 1), columns]
        results_f[...] = results[...]
        starts_f[...] = starts[...]
        source = lax.broadcasted_iota(jnp.int32, (2 * four, 2 * four), 0)
        column = lax.broadcasted_iota(jnp.int32, (2 * four, 2 * four), 1)
        query = (column // HEAD) * 2 * HEAD + lax.rem(column, HEAD)
        rest = column - four
        kind = rest // (2 * HEAD)
        rest = rest - kind * 2 * HEAD
        other = (2 * (rest // HEAD) + kind) * 2 * HEAD + HEAD + lax.rem(rest, HEAD)
        places[...] = jnp.where(source == jnp.where(column < four, query, other), 1.0, 0.0).astype(BF)
        groups = [kernel_dot_tn(mix[g * 2 * four : (g + 1) * 2 * four, :], places[...]) for g in range(4)]
        for g in range(4):
            turned[:, g * four : (g + 1) * four] = groups[g][:, :four]
        for g in range(2):
            for kind in range(2):
                at = width + kind * 2 * four + g * four
                low_part = four + kind * 2 * HEAD
                turned[:, at : at + four] = jnp.concatenate(
                    [groups[2 * g + k][:, low_part : low_part + 2 * HEAD] for k in range(2)], axis=1
                )

    mix_f[...] = turned[pl.ds(pl.multiple_of(step * rows, rows), rows), :]
    half = gate.shape[2]
    gate_f[:, :half] = gate[0].astype(F32)
    gate_f[:, half:] = gate[1].astype(F32)
    out_f[...] = out[...].astype(F32)
    down_f[...] = down[...].astype(F32)


def widen_call(results, starts, mix, gate, out, down, gains):
    steps = 8
    depth = gate.shape[1]
    width = out.shape[1]
    rows = depth // steps

    def whole(array):
        return pl.BlockSpec(array.shape, lambda i: (0,) * array.ndim)

    down_rows = down.shape[0] // steps
    return pl.pallas_call(
        widen_kernel,
        grid=(steps,),
        out_shape=shapes([
            full(depth, 2 * width), full(depth, 2 * gate.shape[2]), full(*out.shape), full(*down.shape),
            full(1, depth), full(1, depth), low(*results.shape), full(*starts.shape),
        ]),
        in_specs=[
            whole(mix),
            pl.BlockSpec((2, rows, gate.shape[2]), lambda i: (0, i, 0)),
            pl.BlockSpec((rows, width), lambda i: (i, 0)),
            pl.BlockSpec((down_rows, width), lambda i: (i, 0)),
            whole(gains),
            whole(results),
            whole(starts),
        ],
        out_specs=[
            pl.BlockSpec((rows, 2 * width), lambda i: (i, 0)),
            pl.BlockSpec((rows, 2 * gate.shape[2]), lambda i: (i, 0)),
            pl.BlockSpec((rows, width), lambda i: (i, 0)),
            pl.BlockSpec((down_rows, width), lambda i: (i, 0)),
            pl.BlockSpec((1, depth), lambda i: (0, 0)),
            pl.BlockSpec((1, depth), lambda i: (0, 0)),
            whole(results),
            whole(starts),
        ],
        scratch_shapes=rooms([low(8 * HEAD, 8 * HEAD), full(depth, 2 * width)]),
        compiler_params=pltpu.CompilerParams(vmem_limit_bytes=60 << 20),
    )(mix, gate, out, down, gains, results, starts)


def on_line():
    return lax.axis_size("ctx") == 4 and lax.axis_size("fsdp") == 4


def gather(own):
    return lax.all_gather(own, ("ctx", "fsdp"), axis=0, tiled=True)


def scatter(part):
    return lax.psum_scatter(part, ("ctx", "fsdp"), scatter_dimension=0, tiled=True)


def spread_halves(columns):
    halves = columns.reshape(columns.shape[:-1] + (2, HEAD // 2))
    halves = jnp.pad(halves, [(0, 0)] * (halves.ndim - 1) + [(0, SPAN - HEAD // 2)])
    return halves.reshape(columns.shape[:-1] + (LANES,))


def join_halves(columns):
    halves = columns.reshape(columns.shape[:-1] + (2, SPAN))[..., : HEAD // 2]
    return halves.reshape(columns.shape[:-1] + (HEAD,))


def angle_tables(positions):
    frequency = rope_base ** (-(jnp.arange(HEAD // 2, dtype=F32) * 2.0 / HEAD))
    frequency = jnp.pad(frequency, (0, SPAN - HEAD // 2))
    angles = positions.astype(F32)[:, None] * frequency[None, :]
    cosine = jnp.cos(angles)
    sine = jnp.sin(angles)
    return jnp.concatenate([cosine, cosine], axis=1), jnp.concatenate([-sine, sine], axis=1)


def rotate(values, cosine, sine):
    return values * cosine + jnp.roll(values, SPAN, axis=1) * sine


def rotate_back(grads, cosine, sine):
    return grads * cosine - jnp.roll(grads, SPAN, axis=1) * sine


def norm_rows(values):
    return lax.rsqrt(jnp.mean(values * values, axis=-1, keepdims=True) + norm_eps)


def norm_back(grad_out, values, factor, gain):
    shaped = grad_out * gain
    common = jnp.mean(shaped * values, axis=-1, keepdims=True)
    grad_in = factor * shaped - values * (factor * factor * factor) * common
    return grad_in, jnp.sum(grad_out * values * factor, axis=0)


def dot(left, right):
    return jnp.dot(left, right, preferred_element_type=F32)


def dot_nt(left, right):
    return lax.dot_general(left, right, (((1,), (1,)), ((), ())), preferred_element_type=F32)


def dot_tn(left, right):
    return lax.dot_general(left, right, (((0,), (0,)), ((), ())), preferred_element_type=F32)


class Plan:
    def __init__(self, width, hidden_units):
        self.c = lax.axis_index("ctx")
        self.f = lax.axis_index("fsdp")
        self.C = lax.axis_size("ctx")
        self.F = lax.axis_size("fsdp")
        self.heads = width // HEAD
        self.ratio = self.heads // KV_HEADS
        self.heads_f = self.heads // self.F
        self.groups_f = KV_HEADS // self.F
        self.share = self.C // self.heads_f
        self.units = hidden_units // (self.F * self.C)
        self.local_head = self.c // self.share
        self.part = self.c % self.share


def pick(array, index, axis):
    return lax.dynamic_index_in_dim(array, index, axis, keepdims=False)


def pack_weights(plan, mix, gate_up):
    depth = mix.shape[0]
    width = plan.heads * HEAD
    kv_width = KV_HEADS * HEAD
    F = plan.F
    queries = pick(mix[:, :width].reshape(depth, F, plan.heads_f, HEAD), plan.local_head, 2)
    group = plan.local_head // plan.ratio
    keys = pick(mix[:, width : width + kv_width].reshape(depth, F, plan.groups_f, HEAD), group, 2)
    values = pick(mix[:, width + kv_width :].reshape(depth, F, plan.groups_f, HEAD), group, 2)
    values = jnp.pad(values, ((0, 0), (0, 0), (0, LANES - HEAD)))
    half = gate_up.shape[1] // 2
    gate = pick(gate_up[:, :half].reshape(depth, F, plan.C, plan.units), plan.c, 2)
    up = pick(gate_up[:, half:].reshape(depth, F, plan.C, plan.units), plan.c, 2)
    packed = jnp.concatenate([spread_halves(queries), spread_halves(keys), values, gate, up], axis=2)
    return jnp.swapaxes(packed, 0, 1)


def attend(plan, q_part, k, v, positions, part_positions):
    scores = dot_nt(q_part, k) * HEAD ** (-0.5)
    allowed = positions[None, :] <= part_positions[:, None]
    scores = jnp.where(allowed, scores, masked_value)
    top = jnp.max(scores, axis=-1, keepdims=True)
    weights = jnp.exp(scores - top)
    total = jnp.sum(weights, axis=-1, keepdims=True)
    context = dot((weights / total).astype(BF), v)
    return context.astype(BF), top + jnp.log(total)


def attend_back(q_part, k, v, context_grad, context, log_total, positions, part_positions):
    scale = HEAD ** (-0.5)
    common = jnp.sum(context_grad.astype(F32) * context.astype(F32), axis=-1, keepdims=True)
    allowed = positions[None, :] <= part_positions[:, None]
    scores = dot_nt(q_part, k) * scale
    weights = jnp.exp(jnp.where(allowed, scores, masked_value) - log_total)
    weight_grad = dot_nt(context_grad, v)
    score_grad = (weights * (weight_grad - common)).astype(BF)
    value_grad = dot_tn(weights.astype(BF), context_grad)
    key_grad = dot_tn(score_grad, q_part) * scale
    query_grad = dot(score_grad, k) * scale
    return query_grad, key_grad, value_grad


def forward_layer(plan, x_own, weights, gains, positions, part_positions, tables):
    mix_cut, gate_cut, out, down = weights
    cosine, sine = tables
    length = positions.shape[0]
    x_all = gather(x_own)
    x32 = x_all.astype(F32)
    factor = norm_rows(x32)
    normed = (x32 * factor * gains[0]).astype(BF)
    mixed = dot(normed, mix_cut)
    q = rotate(mixed[:, :LANES], cosine, sine).astype(BF)
    k = rotate(mixed[:, LANES : 2 * LANES], cosine, sine).astype(BF)
    v = mixed[:, 2 * LANES :].astype(BF)
    rows = length // plan.share
    start = plan.part * rows
    q_part = lax.dynamic_slice_in_dim(q, start, rows, 0)
    context, log_total = attend(plan, q_part, k, v, positions, part_positions)
    partial = dot(context[:, :HEAD], out).astype(BF)
    if plan.share > 1:
        partial = lax.dynamic_update_slice_in_dim(
            jnp.zeros((length, partial.shape[1]), BF), partial, start, 0
        )
    middle = x_own.astype(F32) + scatter(partial)
    factor_two = norm_rows(middle)
    normed_two = gather((middle * factor_two * gains[1]).astype(BF))
    both = dot(normed_two, gate_cut)
    hidden = (jax.nn.silu(both[:, : plan.units]) * both[:, plan.units :]).astype(BF)
    result = middle + scatter(dot(hidden, down).astype(BF))
    kept = (x_own, normed, q_part, k, v, context, log_total, middle, normed_two, both, hidden)
    return result.astype(BF), kept


def backward_layer(plan, grad_own, weights, gains, kept, positions, part_positions, tables, part_tables):
    mix_cut, gate_cut, out, down = weights
    x_own, normed, q_part, k, v, context, log_total, middle, normed_two, both, hidden = kept
    length = positions.shape[0]
    rows = length // plan.share
    start = plan.part * rows
    grad_all = gather(grad_own)
    hidden_grad = dot_nt(grad_all, down)
    gate = both[:, : plan.units]
    up = both[:, plan.units :]
    sig = jax.nn.sigmoid(gate)
    gate_grad = hidden_grad * up * sig * (1.0 + gate * (1.0 - sig))
    up_grad = hidden_grad * gate * sig
    both_grad = jnp.concatenate([gate_grad, up_grad], axis=1).astype(BF)
    normed_two_grad = scatter(dot_nt(both_grad, gate_cut).astype(BF))
    middle_grad, feed_gain_grad = norm_back(normed_two_grad, middle, norm_rows(middle), gains[1])
    middle_grad = middle_grad + grad_own.astype(F32)
    middle_low = gather(middle_grad.astype(BF))
    middle_part = lax.dynamic_slice_in_dim(middle_low, start, rows, 0)
    context_grad = jnp.pad(dot_nt(middle_part, out), ((0, 0), (0, LANES - HEAD))).astype(BF)
    query_grad, key_grad, value_grad = attend_back(
        q_part, k, v, context_grad, context, log_total, positions, part_positions
    )
    query_grad = rotate_back(query_grad, *part_tables).astype(BF)
    if plan.share > 1:
        query_grad = lax.dynamic_update_slice_in_dim(
            jnp.zeros((length, LANES), BF), query_grad, start, 0
        )
    key_grad = rotate_back(key_grad, *tables).astype(BF)
    mixed_grad = jnp.concatenate([query_grad, key_grad, value_grad.astype(BF)], axis=1)
    normed_grad = scatter(dot_nt(mixed_grad, mix_cut).astype(BF))
    x32 = x_own.astype(F32)
    start_grad, attention_gain_grad = norm_back(normed_grad, x32, norm_rows(x32), gains[0])
    start_grad = start_grad + middle_grad
    mix_grad = jnp.stack(
        [dot_tn(normed, part).astype(BF) for part in (query_grad, key_grad, value_grad.astype(BF))]
    )
    gate_cut_grad = jnp.stack(
        [dot_tn(normed_two, part.astype(BF)).astype(BF) for part in (gate_grad, up_grad)]
    )
    out_grad = dot_tn(context, middle_part).astype(BF)[:HEAD]
    down_grad = dot_tn(hidden, grad_all).astype(BF)
    return start_grad, (mix_grad, gate_cut_grad, out_grad, down_grad), jnp.stack([attention_gain_grad, feed_gain_grad])


def swap_sections(array):
    return lax.ppermute(array, "section", [(0, 1), (1, 0)])


def by_layer_of(section, own, other):
    first = section == 0
    return jnp.where(first, own, other), jnp.where(first, other, own)


def shared_weights(plan, section, attention_gain, query_key_value, output_weight, feed_gain, gate_up, down_weight):
    depth = query_key_value.shape[1]
    width = depth * plan.F
    gains = lax.all_gather(
        jnp.stack([attention_gain[0], feed_gain[0]]), ("section", "fsdp"), axis=0, tiled=False
    )
    gains = gains.reshape(2, plan.F, 2, depth)
    gains = jnp.swapaxes(gains, 1, 2).reshape(2, 2, width).astype(F32)
    packed = pack_weights(plan, query_key_value[0], gate_up[0])
    own_cut = lax.all_to_all(packed, "fsdp", 0, 0).reshape(width, -1)
    own_out = lax.dynamic_slice_in_dim(output_weight[0], plan.local_head * HEAD, HEAD, 0)
    own_down = lax.dynamic_slice_in_dim(down_weight[0], plan.c * plan.units, plan.units, 0)
    cuts = by_layer_of(section, own_cut, swap_sections(own_cut))
    outs = by_layer_of(section, own_out, swap_sections(own_out))
    downs = by_layer_of(section, own_down, swap_sections(own_down))
    weights = [(cuts[s][:, : 3 * LANES], cuts[s][:, 3 * LANES :], outs[s], downs[s]) for s in range(2)]
    return weights, gains


def own_gain_sums(plan, section, gain_sum, depth):
    gain_sum = lax.dynamic_slice_in_dim(gain_sum, 2 * section, 2, 0)
    return lax.dynamic_slice_in_dim(gain_sum, plan.f * depth, depth, 1)


def returned_grads(plan, section, weight_grads, gain_grads, depth):
    C, F = plan.C, plan.F
    gain_sum = jnp.concatenate([gain_grads[0], gain_grads[1]])

    def collected(index):
        first, second = weight_grads[0][index], weight_grads[1][index]
        own = jnp.where(section == 0, first, second)
        away = jnp.where(section == 0, second, first)
        return (own.astype(F32) + swap_sections(away).astype(F32)).astype(BF)

    cut_grad = jnp.concatenate(list(collected(0)) + list(collected(1)), axis=1)
    cut_grad = lax.all_to_all(cut_grad.reshape(F, depth, -1), "fsdp", 0, 0)
    cut_grad = lax.all_gather(cut_grad, "ctx", axis=0, tiled=False)
    out_grad = lax.all_gather(collected(2), "ctx", axis=0, tiled=False)
    down_grad = lax.all_gather(collected(3), "ctx", axis=0, tiled=True).astype(F32)

    def heads_of(columns, count):
        folded = columns.astype(F32).reshape(count, C // count, F, depth, columns.shape[-1]).sum(axis=1)
        return jnp.transpose(folded, (2, 1, 0, 3))

    q_grad = join_halves(heads_of(cut_grad[..., :LANES], plan.heads_f)).reshape(depth, -1)
    k_grad = join_halves(heads_of(cut_grad[..., LANES : 2 * LANES], plan.groups_f)).reshape(depth, -1)
    v_grad = heads_of(cut_grad[..., 2 * LANES : 3 * LANES], plan.groups_f)[..., :HEAD].reshape(depth, -1)
    mix_grad = jnp.concatenate([q_grad, k_grad, v_grad], axis=1)
    both = jnp.transpose(cut_grad[..., 3 * LANES :], (2, 1, 0, 3)).astype(F32)
    gate_up_grad = jnp.concatenate(
        [both[..., : plan.units].reshape(depth, -1), both[..., plan.units :].reshape(depth, -1)], axis=1
    )
    out_grad = out_grad.astype(F32).reshape(plan.heads_f, plan.share, HEAD, depth * F).sum(axis=1).reshape(-1, depth * F)

    gain_sum = lax.psum(gain_sum, ("section", "ctx", "fsdp"))
    return mix_grad, gate_up_grad, out_grad, down_grad, own_gain_sums(plan, section, gain_sum, depth)


def on_device(
    inputs, cotangent, attention_gain, query_key_value, output_weight, feed_gain, gate_up, down_weight, block_order
):
    section = lax.axis_index("section")
    width = inputs.shape[2]
    hidden_units = down_weight.shape[1] * lax.axis_size("fsdp")
    plan = Plan(width, hidden_units)
    rows = inputs.shape[1]
    C, F = plan.C, plan.F
    length = rows * C * F
    depth = query_key_value.shape[1]

    def by_layer(own, other):
        first = section == 0
        return jnp.where(first, own, other), jnp.where(first, other, own)

    results = []
    input_grads = [None, None]
    weight_grads = [None, None]
    gain_grads = [None, None]
    kept = []
    if on_line():
        shards = (query_key_value, output_weight, gate_up, down_weight)
        first = forward_share_call(inputs, shards, (attention_gain, feed_gain), block_order)
        weights = first[10:15]
        common = first[15:]
        results.append(first[9])
        second = forward_call(1, first[9], weights, common)
        results.append(second[9])
        input_grads[1], *old, grad = backward_call(1, cotangent, weights, common, [first[9], *second[:9]])
        last = backward_call(
            0, grad, weights, common, [inputs, *first[:9]], [input_grads[1], *old], results
        )
        (mix_grad, gate_up_grad, out_grad, down_grad, attention_gain_grad, feed_gain_grad,
         section_outputs, section_input_grads) = widen_call(*last)
    else:
        order = pick(block_order, section, 0)
        positions = (order[:, None] * rows + jnp.arange(rows, dtype=jnp.int32)[None, :]).reshape(length)
        part_rows = length // plan.share
        part_positions = lax.dynamic_slice_in_dim(positions, plan.part * part_rows, part_rows, 0)
        tables = angle_tables(positions)
        part_tables = angle_tables(part_positions)

        x = pick(inputs, section, 0)
        grad = pick(cotangent, section, 0)
        weights, gains = shared_weights(
            plan, section, attention_gain, query_key_value, output_weight, feed_gain, gate_up, down_weight
        )
        for s in range(2):
            x, keep = forward_layer(plan, x, weights[s], gains[s], positions, part_positions, tables)
            kept.append(keep)
            results.append(x)
        for s in (1, 0):
            input_grads[s], weight_grads[s], gain_grads[s] = backward_layer(
                plan, grad, weights[s], gains[s], kept[s], positions, part_positions, tables, part_tables
            )
            grad = input_grads[s].astype(BF)
        def mine_and_theirs(first, second):
            return jnp.where(section == 0, first, second), jnp.where(section == 0, second, first)

        def by_batch(first, second):
            own, away = mine_and_theirs(first, second)
            return jnp.stack(by_layer(own, swap_sections(away)))

        section_outputs = by_batch(*results)
        section_input_grads = by_batch(*input_grads)

        shard_grads = returned_grads(plan, section, weight_grads, gain_grads, depth)
        mix_grad, gate_up_grad, out_grad, down_grad, gain_sum = shard_grads
        attention_gain_grad, feed_gain_grad = gain_sum[0][None], gain_sum[1][None]

    return (
        section_outputs[None],
        section_input_grads[None],
        attention_gain_grad,
        mix_grad[None],
        out_grad[None],
        feed_gain_grad,
        gate_up_grad[None],
        down_grad[None],
    )


def solution(mesh):
    placed = (
        P(None, ("ctx", "fsdp"), None),
        P(None, ("ctx", "fsdp"), None),
        P("section", "fsdp"),
        P("section", "fsdp", None),
        P("section", "fsdp", None),
        P("section", "fsdp"),
        P("section", "fsdp", None),
        P("section", "fsdp", None),
        P(),
    )
    return jax.shard_map(
        on_device,
        mesh=mesh,
        in_specs=placed,
        out_specs=(
            P("section", None, ("ctx", "fsdp"), None),
            P("section", None, ("ctx", "fsdp"), None),
            P("section", "fsdp"),
            P("section", "fsdp", None),
            P("section", "fsdp", None),
            P("section", "fsdp"),
            P("section", "fsdp", None),
            P("section", "fsdp", None),
        ),
        check_vma=False,
    )
```

```python
import functools

import jax
import jax.numpy as jnp
import numpy as np
from jax import lax
from jax.experimental import pallas as pl
from jax.experimental.pallas import tpu as pltpu
from jax.sharding import PartitionSpec as P

KV_HEADS = 8
HEAD = 96
LANES = 128
SPAN = 64
norm_eps = 1e-05
rope_base = 100000.0
masked_value = -1e30
BF = jnp.bfloat16
F32 = jnp.float32

MESH = pl.DeviceIdType.MESH


def greet():
    c = lax.axis_index("ctx")
    f = lax.axis_index("fsdp")
    barrier = pltpu.get_barrier_semaphore()
    inner = jnp.logical_and(c > 0, c < 3)
    for peer in (f + 2 - 4 * (f // 2), f + 1 - 2 * lax.rem(f, 2)):
        pl.semaphore_signal(barrier, inc=1, device_id={"fsdp": peer}, device_id_type=MESH)
    pl.semaphore_signal(barrier, inc=1, device_id={"ctx": lax.rem(c + 2, 4)}, device_id_type=MESH)

    @pl.when(c < 3)
    def _():
        pl.semaphore_signal(barrier, inc=1, device_id={"ctx": c + 1}, device_id_type=MESH)

    @pl.when(c > 0)
    def _():
        pl.semaphore_signal(barrier, inc=1, device_id={"ctx": c - 1}, device_id_type=MESH)

    @pl.when(inner)
    def _():
        pl.semaphore_wait(barrier, 5)

    @pl.when(jnp.logical_not(inner))
    def _():
        pl.semaphore_wait(barrier, 4)


def near_order(c):
    low = c < 2
    return [c, c + 1 - 2 * lax.rem(c, 2), jnp.where(low, 2, 1), jnp.where(low, 3, 0)]


def own_block(c, f):
    return c * 4 + lax.rem(f, 2) * 2 + f // 2


def begin_rows(whole, rows, send, recv, h):
    c = lax.axis_index("ctx")
    f = lax.axis_index("fsdp")
    half = rows // 2
    mine = whole.at[pl.ds(pl.multiple_of(own_block(c, f) * rows + h * half, half), half)]

    def copy(slot, arrival, peer):
        return pltpu.make_async_remote_copy(
            mine, mine, send.at[slot], recv.at[arrival], device_id=peer, device_id_type=MESH
        )

    pl.when(c < 3)(copy(0, 2 * c + h, {"ctx": jnp.minimum(c + 1, 3)}).start)
    pl.when(c > 0)(copy(1, 2 * c + h, {"ctx": jnp.maximum(c - 1, 0)}).start)
    copy(3, 8 + c, {"fsdp": f + 2 - 4 * (f // 2)}).start()


def gather_rows(whole, rows, send, recv, ready=None, started=None, begun=False):
    c = lax.axis_index("ctx")
    f = lax.axis_index("fsdp")
    y = f // 2
    lane = lax.rem(f, 2)
    inner = jnp.logical_and(c > 0, c < 3)
    outer = jnp.logical_not(inner)
    order = near_order(c)
    pair = order[1]
    half = rows // 2
    to_across = {"fsdp": f + 2 - 4 * y}
    to_twin = {"fsdp": f + 1 - 2 * lane}
    to_pair = {"ctx": pair}

    def at(d, k, yy, h):
        return whole.at[pl.ds(pl.multiple_of((d * 4 + k * 2 + yy) * rows + h * half, half), half)]

    def block(d, k, yy):
        return whole.at[pl.ds(pl.multiple_of((d * 4 + k * 2 + yy) * rows, rows), rows)]

    def two(d, k):
        return whole.at[pl.ds(pl.multiple_of((d * 4 + k * 2) * rows, rows), 2 * rows)]

    def copy(src, slot, arrival, peer):
        return pltpu.make_async_remote_copy(
            src, src, send.at[slot], recv.at[arrival], device_id=peer, device_id_type=MESH
        )

    def go(src, slot, arrival, peer, when=None):
        one = copy(src, slot, arrival, peer)
        if when is None:
            one.start()
        else:
            pl.when(when)(one.start)

    def arrived(ref, arrival):
        copy(ref, 0, arrival, to_twin).wait_recv()

    def gone(count, slot):
        copy(whole.at[pl.ds(0, count * half)], slot, 0, to_twin).wait_send()

    if not begun:
        for h in range(2):
            begin_rows(whole, rows, send, recv, h)
    if started is not None:
        started()

    events = [
        (pair, 0),
        (jnp.where(inner, order[2], pair), jnp.where(inner, 0, 1)),
        (jnp.where(inner, pair, order[2]), jnp.where(inner, 1, 0)),
        (order[2], 1),
        (order[3], 0),
        (order[3], 1),
    ]

    def along(index):
        d, h = events[index]
        piece = at(d, lane, y, h)
        arrived(piece, 2 * d + h)
        go(piece, 2, 2 * d + h, {"ctx": jnp.where(d < c, c + 1, c - 1)}, inner)
        go(piece, 3, 8 + d, to_across, jnp.logical_or(d != pair, h == 0) if index in (1, 2) else None)

    def complete(d):
        arrived(two(d, 1 - lane), 13 + d)
        if ready is not None:
            ready(d)

    def pair_half(when):
        go(at(c, lane, 1 - y, 1), 4, 12, to_pair, when)

    along(0)
    along(1)
    along(2)
    arrived(block(c, lane, 1 - y), 8 + c)
    pair_half(outer)
    go(two(c, lane), 5, 13 + c, to_twin)
    along(3)
    complete(c)
    along(4)
    along(5)
    pair_half(inner)
    arrived(block(order[2], lane, 1 - y), 8 + order[2])
    go(two(order[2], lane), 5, 13 + order[2], to_twin)
    go(block(order[3], lane, y), 5, 13 + order[3], to_twin)
    complete(order[2])
    arrived(at(pair, lane, 1 - y, 0), 8 + pair)
    arrived(at(pair, lane, 1 - y, 1), 12)
    go(two(pair, lane), 5, 13 + pair, to_twin)
    arrived(block(order[3], lane, 1 - y), 8 + order[3])
    go(block(order[3], lane, 1 - y), 5, 17, to_twin)
    complete(pair)
    arrived(block(order[3], 1 - lane, y), 13 + order[3])
    arrived(block(order[3], 1 - lane, 1 - y), 17)
    if ready is not None:
        ready(order[3])
    pl.when(c < 3)(lambda: gone(2, 0))
    pl.when(c > 0)(lambda: gone(2, 1))
    pl.when(inner)(lambda: gone(6, 2))
    gone(7, 3)
    gone(1, 4)
    gone(16, 5)


GATHER_SENDS = 6
GATHER_RECVS = 18


def scatter_sum(part, total, land, send, recv, produce=None, meanwhile=None, ending=None, done=None):
    c = lax.axis_index("ctx")
    f = lax.axis_index("fsdp")
    y = f // 2
    lane = lax.rem(f, 2)
    inner = jnp.logical_and(c > 0, c < 3)
    rows = total.shape[0]
    half = rows // 2
    order = near_order(c)[::-1]
    to_across = {"fsdp": f + 2 - 4 * y}
    to_twin = {"fsdp": f + 1 - 2 * lane}
    to_pair = {"ctx": order[2]}

    def rows_at(d, yy, h):
        return pl.ds(pl.multiple_of((d * 4 + lane * 2 + yy) * rows + h * half, half), half)

    def copy(src, dst, slot, arrival, peer):
        return pltpu.make_async_remote_copy(
            src, dst, send.at[slot], recv.at[arrival], device_id=peer, device_id_type=MESH
        )

    def go(src, dst, slot, arrival, peer):
        copy(src, dst, slot, arrival, peer).start()

    def gone(count, slot):
        ref = part.at[pl.ds(0, count * half)]
        copy(ref, ref, slot, 0, to_twin).wait_send()

    def piece(slot, h):
        return land.at[slot, pl.ds(h * half, half)]

    def landed(ref, arrival):
        copy(ref, ref, 0, arrival, to_twin).wait_recv()
        return ref[...].astype(F32)

    def begin(step):
        d = order[step]
        if produce is not None:
            produce(d)
        for yy, slot in ((1 - y, step), (y, 27 + step)):
            other = pl.ds(pl.multiple_of((d * 4 + 2 - lane * 2 + yy) * rows, rows), rows)
            go(part.at[other], land.at[2 * step + yy], 0, slot, to_twin)

    def twin_there(step, yy, slot):
        ref = land.at[2 * step + yy]
        copy(ref, ref, 0, slot, to_twin).wait_recv()

    def over(step, h, first=False):
        d = order[step]
        if first:
            twin_there(step, 1 - y, step)
        mine = rows_at(d, 1 - y, h)
        value = part[mine, :].astype(F32) + piece(2 * step + 1 - y, h)[...].astype(F32)
        if (step, h) == (3, 1):
            value = value + landed(piece(17, 0), 26)
        part[mine, :] = value.astype(BF)
        if (step, h) == (2, 1):
            go(part.at[mine], piece(17, 0), 3, 26, to_pair)
        else:
            go(part.at[mine], piece(8 + step, h), 1, 8 + 2 * step + h, to_across)

    def onward(step, h, first=False):
        d = order[step]
        mine = rows_at(d, y, h)
        if first:
            twin_there(step, y, 27 + step)
        value = part[mine, :].astype(F32) + piece(2 * step + y, h)[...].astype(F32)
        if (step, h) != (2, 1):
            value = value + landed(piece(8 + step, h), 8 + 2 * step + h)
        if step == 3:
            total[h * half : (h + 1) * half, :] = value
            return
        part[mine, :] = value.astype(BF)

        if step < 2:

            @pl.when(inner)
            def _():
                part[mine, :] = (part[mine, :].astype(F32) + landed(piece(12 + d, h), 16 + 2 * d + h)).astype(BF)

        here = jnp.logical_and(d < c, d == c - 1)
        target = jnp.where(d > c, c + 1, c - 1)
        slot = jnp.where(here, 16, 12 + d)
        arrival = jnp.where(here, 24, 16 + 2 * d) + h
        if step == 0:
            target = jnp.where(inner, d, target)
            slot = jnp.where(inner, 18, slot)
            arrival = jnp.where(inner, 31 + h, arrival)
        go(part.at[mine], piece(slot, h), 2, arrival, {"ctx": target})

    begin(0)
    over(0, 0, True)
    over(0, 1)
    begin(1)
    begin(2)
    over(2, 1, True)
    over(1, 0, True)
    onward(0, 0, True)
    over(1, 1)
    onward(0, 1)
    if meanwhile is not None:
        meanwhile()
    begin(3)
    over(2, 0)
    onward(1, 0, True)
    over(3, 0, True)
    onward(1, 1)
    over(3, 1)
    onward(2, 1, True)
    onward(2, 0)
    if ending is not None:
        ending()
    for h in range(2):
        onward(3, h, h == 0)

        @pl.when(c > 0)
        def _():
            total[h * half : (h + 1) * half, :] += landed(piece(12 + c, h), 16 + 2 * c + h)

        @pl.when(c < 3)
        def _():
            total[h * half : (h + 1) * half, :] += landed(piece(16, h), 24 + h)

        @pl.when(jnp.logical_not(inner))
        def _():
            total[h * half : (h + 1) * half, :] += landed(piece(18, h), 31 + h)

        if done is not None:
            done(h)

    gone(16, 0)
    gone(7, 1)
    gone(6, 2)
    gone(1, 3)


SCATTER_SENDS = 4
SCATTER_RECVS = 33


def kernel_dot(left, right):
    return jnp.dot(left, right, preferred_element_type=F32)


def kernel_dot_nt(left, right):
    return lax.dot_general(left, right, (((1,), (1,)), ((), ())), preferred_element_type=F32)


def kernel_dot_tn(left, right):
    return lax.dot_general(left, right, (((0,), (0,)), ((), ())), preferred_element_type=F32)


def turn(values):
    return pltpu.roll(values, SPAN, axis=1)


def mean_square(values):
    return lax.rsqrt(jnp.mean(values * values, axis=-1, keepdims=True) + norm_eps)


def greet_all(peers):
    barrier = pltpu.get_barrier_semaphore()
    for peer in peers:
        pl.semaphore_signal(barrier, inc=1, device_id=peer, device_id_type=MESH)
    return len(peers)


def greet_more(peers):
    c = lax.axis_index("ctx")
    barrier = pltpu.get_barrier_semaphore()
    count = greet_all(peers)
    inner = jnp.logical_and(c > 0, c < 3)

    @pl.when(c < 3)
    def _():
        pl.semaphore_signal(barrier, inc=1, device_id={"ctx": c + 1}, device_id_type=MESH)

    @pl.when(c > 0)
    def _():
        pl.semaphore_signal(barrier, inc=1, device_id={"ctx": c - 1}, device_id_type=MESH)

    @pl.when(inner)
    def _():
        pl.semaphore_wait(barrier, count + 2)

    @pl.when(jnp.logical_not(inner))
    def _():
        pl.semaphore_wait(barrier, count + 1)


class Share:
    def __init__(self, sources, targets, scratch, sems):
        self.mix, self.out, self.gate_up, self.down, self.attention_gain, self.feed_gain = sources
        self.w_mix, self.w_gate, self.w_out, self.w_down, self.w_gains = targets
        self.mix_v, self.heads_v, self.gate_s, self.out_s, self.down_s, self.gains = scratch
        self.local, self.send, self.recv = sems
        self.s = lax.axis_index("section")
        self.c = lax.axis_index("ctx")
        self.f = lax.axis_index("fsdp")
        self.other = 1 - self.s
        self.depth = self.mix.shape[1]
        self.units = self.w_down.shape[1]
        self.peers = [lax.rem(self.f + k, 4) for k in range(1, 4)]
        self.rows = pl.ds(pl.multiple_of(self.f * self.depth, self.depth), self.depth)
        self.pending = []

    def greeted(self):
        return (
            [{"fsdp": peer} for peer in self.peers]
            + [{"section": self.other}, {"ctx": lax.rem(self.c + 2, 4)}]
            + [{"section": self.other, "fsdp": peer} for peer in self.peers]
        )

    def copy(self, src, dst, slot, arrival, peer):
        return pltpu.make_async_remote_copy(
            src, dst, self.send.at[slot], self.recv.at[arrival], device_id=peer, device_id_type=MESH
        )

    def go(self, src, dst, slot, arrival, peer):
        one = self.copy(src, dst, slot, arrival, peer)
        one.start()
        self.pending.append(one)

    def keep(self, src, dst, slot):
        one = pltpu.make_async_copy(src, dst, self.local.at[slot])
        one.start()
        return one

    def load(self):
        self.gains[...] = jnp.zeros_like(self.gains)
        self.gains[0:1, :] = self.attention_gain[...]
        self.gains[1:2, :] = self.feed_gain[...]
        self.loaded = self.keep(self.mix.at[0], self.mix_v, 0)
        out_rows = self.out.at[0, pl.ds(pl.multiple_of(self.c * HEAD, HEAD), HEAD)]
        down_rows = self.down.at[0, pl.ds(pl.multiple_of(self.c * self.units, self.units), self.units)]
        self.staged = [
            self.keep(self.gate_piece(self.f, part), self.gate_s.at[:, pl.ds(part * self.units, self.units)], 5 + part)
            for part in range(2)
        ]
        self.staged.append(self.keep(out_rows, self.out_s, 7))
        self.staged.append(self.keep(down_rows, self.down_s, 8))

    def head_rows(self, peer, part):
        head = peer * 4 + self.c
        start = head * HEAD if part == 0 else (16 + 8 * (part - 1) + head // 2) * HEAD
        return self.heads_v.at[pl.ds(pl.multiple_of(start, HEAD), HEAD)]

    def put(self, part):
        return self.w_mix.at[self.s, pl.ds(part * HEAD, HEAD), self.rows]

    def send_mix(self):
        self.loaded.wait()
        for g in range(8):
            here = slice(g * 4 * HEAD, (g + 1) * 4 * HEAD)
            self.heads_v[here, :] = self.mix_v[:, here].T
        for k, peer in enumerate(self.peers):
            for part in range(3):
                self.copy(self.head_rows(peer, part), self.put(part), k, self.f, {"fsdp": peer}).start()
        self.own_mix = [self.keep(self.head_rows(self.f, part), self.put(part), 2 + part) for part in range(3)]
        for one in self.staged:
            one.wait()
        self.own_gate = self.keep(self.gate_s, self.slab(self.w_gate, self.f), 5)
        self.own_out = self.keep(self.out_s, self.w_out.at[self.s], 7)
        self.own_down = self.keep(self.down_s, self.w_down.at[self.s], 8)
        mine = self.w_gains.at[self.s, :, pl.ds(pl.multiple_of(self.f * self.depth, self.depth), self.depth)]
        for k, peer in enumerate(self.peers):
            self.go(self.gains, mine, 20 + k, 16 + 4 * self.s + self.f, {"fsdp": peer})
            self.go(self.gains, mine, 23 + k, 16 + 4 * self.s + self.f, {"section": self.other, "fsdp": peer})
        self.go(self.gains, mine, 26, 16 + 4 * self.s + self.f, {"section": self.other})
        self.own_gains = self.keep(self.gains, mine, 1)

    def gate_piece(self, peer, part):
        hidden_units = self.gate_up.shape[2] // 2
        start = pl.multiple_of(part * hidden_units + (peer * 4 + self.c) * self.units, self.units)
        return self.gate_up.at[0, :, pl.ds(start, self.units)]

    def gate_put(self, part):
        return self.w_gate.at[self.s, self.rows, pl.ds(part * self.units, self.units)]

    def send_gate(self):
        for k, peer in enumerate(self.peers):
            for part in range(2):
                self.copy(self.gate_piece(peer, part), self.gate_put(part), 3 + k, 4 + self.f, {"fsdp": peer}).start()

    def slab(self, ref, origin):
        part = pl.ds(pl.multiple_of(origin * self.depth, self.depth), self.depth)
        return ref.at[self.s, :, part] if ref is self.w_mix else ref.at[self.s, part]

    def cross_slab(self, ref, k, slot, arrival, base):
        origin = lax.rem(self.f + 3 - k, 4)
        block = self.slab(ref, origin)
        self.copy(block, block, 0, arrival + origin, {"fsdp": origin}).wait_recv()
        self.go(block, block, slot + k, base + origin, {"section": self.other})

    def cross_mix(self, between):
        for one in self.own_mix:
            one.wait()
        self.go(self.slab(self.w_mix, self.f), self.slab(self.w_mix, self.f), 6, 8 + self.f, {"section": self.other})
        between()
        for k in range(3):
            self.cross_slab(self.w_mix, k, 7, 0, 8)
        self.send_gate()
        self.go(self.out_s, self.w_out.at[self.s], 10, 24, {"section": self.other})
        self.go(self.gate_s, self.slab(self.w_gate, self.f), 11, 12 + self.f, {"section": self.other})

    def cross_gate(self):
        for k in range(3):
            self.cross_slab(self.w_gate, k, 12, 4, 12)
        self.go(self.down_s, self.w_down.at[self.s], 15, 25, {"section": self.other})

    def there(self, ref, arrival):
        self.copy(ref, ref, 0, arrival, {"section": self.other}).wait_recv()

    def mix_there(self):
        for one in (self.own_gains, self.own_gate, self.own_out, self.own_down):
            one.wait()
        for origin in range(4):
            rows = pl.ds(origin * self.depth, self.depth)
            self.there(self.w_mix.at[self.other, :, rows], 8 + origin)
            self.there(self.w_gains.at[self.other, :, rows], 16 + 4 * self.other + origin)
        for k in range(3):
            origin = lax.rem(self.f + 3 - k, 4)
            columns = pl.ds(pl.multiple_of(origin * self.depth, self.depth), self.depth)
            self.there(self.w_gains.at[self.s, :, columns], 16 + 4 * self.s + origin)
        self.there(self.w_out.at[self.other], 24)

    def gate_there(self):
        for origin in range(4):
            self.there(self.w_gate.at[self.other, pl.ds(origin * self.depth, self.depth)], 12 + origin)

    def down_there(self):
        self.there(self.w_down.at[self.other], 25)

    def finish(self):
        for k, peer in enumerate(self.peers):
            block = self.slab(self.w_mix, self.f)
            self.copy(block, block, k, 0, {"fsdp": peer}).wait_send()
            block = self.slab(self.w_gate, self.f)
            self.copy(block, block, 3 + k, 0, {"fsdp": peer}).wait_send()
        for one in self.pending:
            one.wait_send()


class Loads:
    def __init__(self, sems):
        self.sems = sems
        self.copies = []

    def start(self, src, dst):
        one = pltpu.make_async_copy(src, dst, self.sems.at[len(self.copies)])
        one.start()
        self.copies.append(one)
        return one


def load_heads(loads, source, target):
    half = HEAD // 2
    target[...] = jnp.zeros_like(target)
    pieces = [(part * HEAD + h * half, part * LANES + h * SPAN, half) for part in range(2) for h in range(2)]
    pieces.append((2 * HEAD, 2 * LANES, HEAD))
    return [loads.start(source.at[pl.ds(a, count)], target.at[pl.ds(b, count)]) for a, b, count in pieces]


def plane_rows(d, rows):
    return pl.ds(pl.multiple_of(d * 4 * rows, 4 * rows), 4 * rows)


def make_tables(block_order, frequency, cosine, sine, place_col, place_row):
    s = lax.axis_index("section")
    blocks = block_order.shape[1]
    rows = place_col.shape[0] // blocks
    order = jnp.where(s == 0, block_order[0:1, :], block_order[1:2, :])
    inside_col = lax.broadcasted_iota(jnp.int32, (rows, 1), 0)
    inside_row = lax.broadcasted_iota(jnp.int32, (1, 2 * rows), 1)
    firsts = []
    for b in range(blocks):
        source = b - b % 4 + (b % 2) * 2 + (b % 4) // 2
        firsts.append(order[:, source : source + 1] * rows)
        place_col[b * rows : (b + 1) * rows, :] = firsts[b] + inside_col
    for b in range(0, blocks, 2):
        place_row[:, b * rows : (b + 2) * rows] = jnp.where(
            inside_row < rows, firsts[b] + inside_row, firsts[b + 1] + inside_row - rows
        )
    lane = lax.broadcasted_iota(jnp.int32, (4 * rows, LANES), 1)
    for part in range(blocks // 4):
        here = pl.ds(part * 4 * rows, 4 * rows)
        angles = place_col[here, :].astype(F32) * frequency[...]
        wave = jnp.sin(angles)
        cosine[here, :] = jnp.cos(angles)
        sine[here, :] = jnp.where(lane < SPAN, -wave, wave)


def forward_body(layer, share, x_own, weights, tables, kept, scratch, sems, prepare=None, before=None, ending=None):
    w_mix, w_gate, w_out, w_down, w_gains = weights
    cosine, sine, place_col, place_row = tables
    normed_o, q_o, k_o, v_o, context_o, log_o, middle_o, normed_two_o, both_o, result_o = kept
    (x_v, normed_v, q_v, k_v, v_v, context_v, log_v, middle_v, two_v, both_v, hidden_v, result_v,
     mix_v, gate_v, out_v, down_v, gains_v, part_v, land_a, land_b, total_v) = scratch
    local, save, send_a, recv_a, send_b, recv_b, send_c, recv_c, send_d, recv_d = sems
    c = lax.axis_index("ctx")
    f = lax.axis_index("fsdp")
    rows = x_own.shape[0]
    units = down_v.shape[0]
    own_rows = pl.ds(pl.multiple_of(own_block(c, f) * rows, rows), rows)
    loads = Loads(local)
    saves = Loads(save)

    def save_to(src, dst):
        if dst is not None:
            saves.start(src, dst)

    load_x = loads.start(x_own, x_v.at[own_rows])
    out_v[...] = jnp.zeros_like(out_v)

    def load_first():
        return [
            loads.start(w_gains.at[layer], gains_v),
            loads.start(w_out.at[layer], out_v.at[pl.ds(0, HEAD)]),
        ] + load_heads(loads, w_mix.at[layer], mix_v)

    def project(d):
        here = plane_rows(d, rows)
        x = x_v[here, :].astype(F32)
        normed = (x * mean_square(x) * gains_v[0:1, :].astype(F32)).astype(BF)
        normed_v[here, :] = normed
        mixed = kernel_dot_nt(normed, mix_v[...])
        cos = cosine[here, :]
        sin = sine[here, :]
        q = mixed[:, :LANES]
        k = mixed[:, LANES : 2 * LANES]
        q_v[here, :] = (q * cos + turn(q) * sin).astype(BF)
        k_v[here, :] = (k * cos + turn(k) * sin).astype(BF)
        v_v[here, :] = mixed[:, 2 * LANES :].astype(BF)

    if share is None:
        first = load_first()
        load_gate = loads.start(w_gate.at[layer], gate_v)
        load_down = loads.start(w_down.at[layer], down_v)
        greet()
        load_x.wait()
        for one in first:
            one.wait()
        gather_rows(x_v, rows, send_a, recv_a, project)
    else:
        share.load()
        greet_more(share.greeted())
        load_x.wait()
        share.send_mix()
        gather_rows(x_v, rows, send_a, recv_a, started=lambda: share.cross_mix(prepare))
        share.mix_there()
        first = load_first()
        for one in first:
            one.wait()
        for d in range(4):
            project(d)
        share.cross_gate()
    for src, dst in ((normed_v, normed_o), (q_v, q_o), (k_v, k_o), (v_v, v_o)):
        save_to(src, dst)
    scale = HEAD ** (-0.5)

    def attention(d):
        here = plane_rows(d, rows)
        scores = kernel_dot_nt(q_v[here, :], k_v[...]) * scale
        allowed = place_row[...] <= place_col[here, :]
        scores = jnp.where(allowed, scores, masked_value)
        top = jnp.max(scores, axis=-1, keepdims=True)
        weights = jnp.exp(scores - top)
        amount = jnp.sum(weights, axis=-1, keepdims=True)
        context = (kernel_dot(weights.astype(BF), v_v[...]) / amount).astype(BF)
        context_v[here, :] = context
        log_v[here, :] = jnp.broadcast_to(top + jnp.log(amount), (4 * rows, LANES))
        part_v[here, :] = kernel_dot(context, out_v[...]).astype(BF)

    half = rows // 2

    def own_half(h):
        return pl.ds(pl.multiple_of(own_block(c, f) * rows + h * half, half), half)

    def middle_half(h):
        part = slice(h * half, (h + 1) * half)
        middle = x_v[own_half(h), :].astype(F32) + total_v[part, :]
        middle_v[part, :] = middle
        two_v[own_half(h), :] = (middle * mean_square(middle) * gains_v[1:2, :].astype(F32)).astype(BF)
        begin_rows(two_v, rows, send_c, recv_c, h)

    scatter_sum(part_v, total_v, land_a, send_b, recv_b, attention, done=middle_half)
    save_to(context_v, context_o)
    save_to(log_v, log_o)
    save_to(middle_v, middle_o)

    def gate_ready():
        if share is None:
            load_gate.wait()
        else:
            share.gate_there()
            loads.start(w_gate.at[layer], gate_v).wait()

    def feed(d):
        here = plane_rows(d, rows)
        both = kernel_dot(two_v[here, :], gate_v[...])
        both_v[here, :] = both
        gate = both[:, :units]
        hidden_v[here, :] = (gate * jax.nn.sigmoid(gate) * both[:, units:]).astype(BF)

    first = iter((True, False, False, False))

    def feed_when_ready(d):
        if next(first):
            gate_ready()
        feed(d)

    gather_rows(two_v, rows, send_c, recv_c, feed_when_ready, begun=True)
    save_to(two_v, normed_two_o)
    save_to(both_v, both_o)
    if share is None:
        load_down.wait()
    else:
        share.down_there()
        loads.start(w_down.at[layer], down_v).wait()

    def lower(d):
        here = plane_rows(d, rows)
        part_v[here, :] = kernel_dot(hidden_v[here, :], down_v[...]).astype(BF)

    if before is not None:
        before()
    scatter_sum(part_v, total_v, land_b, send_d, recv_d, lower, ending=ending)
    result_v[...] = (middle_v[...] + total_v[...]).astype(BF)
    saves.start(result_v, result_o)
    for one in saves.copies:
        one.wait()
    if share is not None:
        share.finish()


def forward_share_kernel(*refs):
    inputs, *refs = refs
    sources, refs = refs[:6], refs[6:]
    (block_order, frequency), refs = refs[:2], refs[2:]
    kept, refs = refs[:10], refs[10:]
    weights, refs = refs[:5], refs[5:]
    tables, refs = refs[:4], refs[4:]
    scratch, refs = refs[:21], refs[21:]
    packing, refs = refs[:6], refs[6:]
    sems, share_sems = refs[:10], refs[10:]
    share = Share(sources, weights, packing, share_sems)
    forward_body(
        0, share, inputs.at[lax.axis_index("section")], weights, tables, kept, scratch, sems,
        lambda: make_tables(block_order, frequency, *tables),
    )


def backward_body(layer, grad_own, weights, tables, saved, outs, scratch, sems, returning, forward=None):
    w_mix, w_gate, w_out, w_down, w_gains = weights
    cosine, sine, place_col, place_row = tables
    (grad_v, x_v, normed_v, q_v, k_v, v_v, context_v, log_v, middle_v, two_v, both_v, both_grad_v, hidden_v,
     low_v, mixed_v, kv_land, kv_v, key_grad_v, value_grad_v, start_v, start_low_v,
     mix_grad_v, gate_grad_v, out_grad_v, down_grad_v, gain_grad_v,
     mix_v, gate_v, out_v, down_v, gains_v, part_v, land_a, land_b, total_v) = scratch
    local, save, pair_sems, send_a, recv_a, send_b, recv_b, send_c, recv_c, send_d, recv_d = sems
    c = lax.axis_index("ctx")
    f = lax.axis_index("fsdp")
    odd = lax.rem(c, 2)
    rows = x_v.shape[0]
    units = down_v.shape[0]
    own_rows = pl.ds(pl.multiple_of(own_block(c, f) * rows, rows), rows)
    loads = Loads(local)
    saves = Loads(save)
    load_grad = loads.start(grad_own, grad_v.at[own_rows])
    key_grad_v[...] = jnp.zeros_like(key_grad_v)
    value_grad_v[...] = jnp.zeros_like(value_grad_v)
    gain_grad_v[...] = jnp.zeros_like(gain_grad_v)
    if forward is None:
        x_own, normed, q, k, v, context, log, middle, normed_two, both = saved
        load_down = loads.start(w_down.at[layer], down_v)
        load_both = loads.start(both, both_v)
        load_gate = loads.start(w_gate.at[layer], gate_v)
        out_v[...] = jnp.zeros_like(out_v)
        if returning is None:
            greet()
        else:
            peers = [{"fsdp": lax.rem(f + k, 4)} for k in range(1, 4)]
            greet_more(peers + [{"section": 1 - lax.axis_index("section")}, {"ctx": lax.rem(c + 2, 4)}])
        load_grad.wait()
        later = [
            loads.start(src, dst)
            for src, dst in (
                (normed_two, two_v), (middle, middle_v), (w_gains.at[layer], gains_v),
                (w_out.at[layer], out_v.at[pl.ds(0, HEAD)]), (q, q_v), (k, k_v), (v, v_v),
                (context, context_v), (log, log_v), (normed, normed_v), (x_own, x_v),
            )
        ] + load_heads(loads, w_mix.at[layer], mix_v)
        load_down.wait()
        load_both.wait()
    else:
        later = []
    if returning is not None:
        begin_old, begin_feed, begin_mix, begin_return, finish = returning
        begin_old()

    def feed(d):
        here = plane_rows(d, rows)
        hidden_grad = kernel_dot_nt(grad_v[here, :], down_v[...])
        gate = both_v[here, :units]
        up = both_v[here, units:]
        sig = jax.nn.sigmoid(gate)
        silu = gate * sig
        hidden_v[here, :] = (silu * up).astype(BF)
        both_grad_v[here, :units] = (hidden_grad * up * sig * (1.0 + gate * (1.0 - sig))).astype(BF)
        both_grad_v[here, units:] = (hidden_grad * silu).astype(BF)

    if forward is None:
        gather_rows(grad_v, rows, send_a, recv_a, feed)
        load_gate.wait()
    else:

        def before():
            load_grad.wait()
            for h in range(2):
                begin_rows(grad_v, rows, send_a, recv_a, h)

        forward(before, lambda: gather_rows(grad_v, rows, send_a, recv_a, feed, begun=True))

    def spread(d):
        here = plane_rows(d, rows)
        part_v[here, :] = kernel_dot_nt(both_grad_v[here, :], gate_v[...]).astype(BF)

    def feed_weights():
        for one in later[:1]:
            one.wait()
        down_grad_v[...] = kernel_dot_tn(hidden_v[...], grad_v[...]).astype(BF)
        for part in range(2):
            gate_grad_v[part] = kernel_dot_tn(
                two_v[...], both_grad_v[:, part * units : (part + 1) * units]
            ).astype(BF)
        if returning is None:
            saves.start(down_grad_v, outs[4])
            saves.start(gate_grad_v, outs[2])
        else:
            begin_feed()

    def norm_grads(error, value, gain, row):
        factor = mean_square(value)
        shaped = error * gain
        common = jnp.mean(shaped * value, axis=-1, keepdims=True)
        gain_grad_v[row : row + 1, :] += jnp.sum(error * value * factor, axis=0, keepdims=True)
        return factor * shaped - value * (factor * factor * factor) * common

    half = rows // 2

    def middle_half(h):
        part = slice(h * half, (h + 1) * half)
        own_half = pl.ds(pl.multiple_of(own_block(c, f) * rows + h * half, half), half)
        if h == 0:
            for one in later[1:]:
                one.wait()
        middle_grad = norm_grads(total_v[part, :], middle_v[part, :], gains_v[1:2, :].astype(F32), 1)
        middle_grad = middle_grad + grad_v[own_half, :].astype(F32)
        middle_v[part, :] = middle_grad
        low_v[own_half, :] = middle_grad.astype(BF)
        begin_rows(low_v, rows, send_c, recv_c, h)

    scatter_sum(part_v, total_v, land_a, send_b, recv_b, spread, feed_weights, done=middle_half)
    scale = HEAD ** (-0.5)

    def attention(d):
        here = plane_rows(d, rows)
        context_grad = kernel_dot_nt(low_v[here, :], out_v[...])
        common = jnp.sum(context_grad * context_v[here, :].astype(F32), axis=-1, keepdims=True)
        context_grad = context_grad.astype(BF)
        queries = q_v[here, :]
        scores = kernel_dot_nt(queries, k_v[...]) * scale
        allowed = place_row[...] <= place_col[here, :]
        weights = jnp.exp(jnp.where(allowed, scores, masked_value) - log_v[here, 0:1])
        weight_grad = kernel_dot_nt(context_grad, v_v[...])
        score_grad = (weights * (weight_grad - common)).astype(BF)
        value_grad_v[...] += kernel_dot_tn(weights.astype(BF), context_grad)
        key_grad_v[...] += kernel_dot_tn(score_grad, queries)
        query_grad = kernel_dot(score_grad, k_v[...]) * scale
        mixed_v[here, :LANES] = (query_grad * cosine[here, :] - turn(query_grad) * sine[here, :]).astype(BF)

    gather_rows(low_v, rows, send_c, recv_c, attention, begun=True)
    key_grad = key_grad_v[...] * scale
    mixed_v[:, LANES : 2 * LANES] = (key_grad * cosine[...] - turn(key_grad) * sine[...]).astype(BF)
    mixed_v[:, 2 * LANES :] = value_grad_v[...].astype(BF)
    pair = {"ctx": c + 1 - 2 * odd}

    def pair_copy(part):
        return pltpu.make_async_remote_copy(
            mixed_v.at[:, pl.ds(part * LANES, LANES)], kv_land, pair_sems.at[0], pair_sems.at[1],
            device_id=pair, device_id_type=MESH,
        )

    pl.when(odd == 0)(pair_copy(2).start)
    pl.when(odd == 1)(pair_copy(1).start)

    def spread_two(d):
        here = plane_rows(d, rows)
        part_v[here, :] = kernel_dot(mixed_v[here, :], mix_v[...]).astype(BF)

    def mix_weights():
        out_grad_v[...] = kernel_dot_tn(context_v[...], low_v[...])[:HEAD].astype(BF)
        short = HEAD // 2
        columns = kernel_dot_tn(mixed_v[:, :LANES], normed_v[...])
        mix_grad_v[:short, :] = columns[:short].astype(BF)
        mix_grad_v[short:HEAD, :] = columns[SPAN : SPAN + short].astype(BF)
        pair_copy(1).wait_recv()
        mine = jnp.where(odd == 0, mixed_v[:, LANES : 2 * LANES].astype(F32), mixed_v[:, 2 * LANES :].astype(F32))
        kv_v[...] = (mine + kv_land[...].astype(F32)).astype(BF)
        columns = kernel_dot_tn(kv_v[...], normed_v[...])
        mix_grad_v[HEAD : HEAD + short, :] = columns[:short].astype(BF)
        mix_grad_v[HEAD + short :, :] = jnp.where(
            odd == 0, columns[SPAN : SPAN + short], columns[short:HEAD]
        ).astype(BF)
        if returning is None:
            saves.start(out_grad_v, outs[3])
            saves.start(mix_grad_v, outs[1])
        else:
            begin_mix()

    scatter_sum(part_v, total_v, land_b, send_d, recv_d, spread_two, mix_weights,
                None if returning is None else begin_return)
    start_grad = norm_grads(total_v[...], x_v[...].astype(F32), gains_v[0:1, :].astype(F32), 0) + middle_v[...]
    start_v[...] = start_grad
    if returning is None:
        saves.start(start_v, outs[0])
        start_low_v[...] = start_grad.astype(BF)
        saves.start(start_low_v, outs[6])
        saves.start(gain_grad_v, outs[5])
    else:
        finish(gain_grad_v)
    pair_copy(1).wait_send()
    for one in saves.copies:
        one.wait()


SAVED = 10
BACK_SCRATCH = 35


def forward_backward_kernel(layer, *refs):
    (x_own, cotangent), refs = refs[:2], refs[2:]
    weights, refs = refs[:5], refs[5:]
    tables, refs = refs[:4], refs[4:]
    result_o, *refs = refs
    outs, refs = refs[:7], refs[7:]
    ahead, refs = refs[:21], refs[21:]
    more, refs = refs[:16], refs[16:]
    ahead_sems, sems = refs[:10], refs[10:]
    (x_v, normed_v, q_v, k_v, v_v, context_v, log_v, middle_v, two_v, both_v, hidden_v, result_v,
     mix_v, gate_v, out_v, down_v, gains_v, part_v, land_a, land_b, total_v) = ahead
    grad_v, own_v, both_grad_v, low_v = more[:4]
    scratch = [
        grad_v, own_v, normed_v, q_v, k_v, v_v, context_v, log_v, middle_v, two_v, both_v, both_grad_v, hidden_v,
        low_v, *more[4:], mix_v, gate_v, out_v, down_v, gains_v, part_v, land_a, land_b, total_v,
    ]

    def forward(before, ending):
        forward_body(
            layer, None, x_own, weights, tables, [None] * 9 + [result_o], ahead, ahead_sems, None, before, ending
        )
        rows = own_v.shape[0]
        place = own_block(lax.axis_index("ctx"), lax.axis_index("fsdp"))
        own_v[...] = x_v[pl.ds(pl.multiple_of(place * rows, rows), rows), :]

    backward_body(
        layer, cotangent.at[lax.axis_index("section")], weights, tables, None, outs, scratch, sems, None, forward
    )


def backward_return_kernel(*refs):
    grad_own, *refs = refs
    weights, refs = refs[:5], refs[5:]
    tables, refs = refs[:4], refs[4:]
    saved, refs = refs[:SAVED], refs[SAVED:]
    (start_old, mix_old, gate_old, out_old, down_old, gain_old), refs = refs[:6], refs[6:]
    (result_new, result_old), refs = refs[:2], refs[2:]
    (results_o, starts_o), refs = refs[:2], refs[2:]
    finals, refs = refs[:5], refs[5:]
    scratch, refs = refs[:BACK_SCRATCH], refs[BACK_SCRATCH:]
    own, refs = refs[:10], refs[10:]
    sems, return_sems, swap_sems = refs[:11], refs[11:16], refs[16]
    start_new = scratch[19]
    mix_new, gate_new, out_new, down_new, gain_new = scratch[21:26]
    gain_v = own[8]
    s = lax.axis_index("section")
    begin_old, begin_feed, begin_mix, begin_return, steps_after, wait_all = returner(
        tuple(finals) + tuple(own), return_sems,
        gate_new, down_new, mix_new, out_new, gate_old, down_old, mix_old, out_old,
    )

    def swap_copy(src, dst, slot):
        return pltpu.make_async_remote_copy(
            src, dst, swap_sems.at[slot], swap_sems.at[2 + slot], device_id={"section": 1 - s}, device_id_type=MESH
        )

    def swap_rows(away, home, out, slot):
        swap_copy(away, out.at[s], slot).start()
        pltpu.make_async_copy(home, out.at[s], swap_sems.at[4 + slot]).start()

    def finish(gain_grad_v):
        @pl.when(s == 0)
        def _():
            swap_rows(result_old, result_new, results_o, 0)
            swap_rows(start_old, start_new, starts_o, 1)

        @pl.when(s == 1)
        def _():
            swap_rows(result_new, result_old, results_o, 0)
            swap_rows(start_new, start_old, starts_o, 1)

        gain_v[0] = jnp.zeros(gain_v.shape[1:], F32)
        gain_v[0, 0:2, :] = gain_grad_v[...]
        gain_v[0, 2:4, :] = gain_old[...]
        steps_after()
        wait_all()
        for slot, out in enumerate((results_o, starts_o)):
            pltpu.make_async_copy(out.at[s], out.at[s], swap_sems.at[4 + slot]).wait()
            swap_copy(out.at[s], out.at[1 - s], slot).wait()

    saved = [saved[0].at[s], *saved[1:]]
    backward_body(0, grad_own, weights, tables, saved, None, scratch, sems, (begin_old, begin_feed, begin_mix, begin_return, finish))


def link_sems():
    dma = pltpu.SemaphoreType.DMA
    return [dma((GATHER_SENDS,)), dma((GATHER_RECVS,)), dma((SCATTER_SENDS,)), dma((SCATTER_RECVS,))] * 2


def low(*shape):
    return (shape, BF)


def full(*shape):
    return (shape, F32)


def shapes(specs):
    return [jax.ShapeDtypeStruct(*one) for one in specs]


def rooms(specs):
    return [pltpu.VMEM(*one) for one in specs]


def signals(*counts):
    return [pltpu.SemaphoreType.DMA((count,)) for count in counts]


def forward_scratch(rows, width, units):
    length = 16 * rows
    return [low(length, width), low(length, width)] + [low(length, LANES)] * 4 + [
        full(length, LANES), full(rows, width), low(length, width), full(length, 2 * units), low(length, units),
        low(rows, width), low(3 * LANES, width), low(width, 2 * units), low(LANES, width), low(units, width),
        low(16, width), low(length, width), low(19, rows, width), low(19, rows, width), full(rows, width)]


def forward_kept(rows, width, units):
    length = 16 * rows
    return [low(length, width)] + [low(length, LANES)] * 4 + [
        full(length, LANES), full(rows, width), low(length, width), full(length, 2 * units), low(rows, width)]


ANYWHERE = pl.BlockSpec(memory_space=pl.ANY)
INSIDE = pl.BlockSpec(memory_space=pltpu.VMEM)


def forward_share_call(inputs, shards, gains, block_order):
    rows, width = inputs.shape[1:]
    length = 16 * rows
    depth = shards[0].shape[1]
    units = shards[2].shape[2] // 32
    frequency = np.zeros((2, SPAN), np.float32)
    frequency[:, : HEAD // 2] = np.float32(rope_base) ** (-(np.arange(HEAD // 2, dtype=np.float32) * 2.0 / HEAD))
    packing = [low(depth, shards[0].shape[2]), low(shards[0].shape[2], depth), low(depth, 2 * units), low(HEAD, width),
               low(units, width), low(16, depth)]
    kept = forward_kept(rows, width, units)
    weights = [low(2, 3 * HEAD, width), low(2, width, 2 * units), low(2, HEAD, width), low(2, units, width), low(2, 16, width)]
    tables = [full(length, LANES), full(length, LANES), ((length, 1), jnp.int32), ((1, length), jnp.int32)]
    return pl.pallas_call(
        forward_share_kernel,
        out_shape=shapes(kept + weights + tables),
        in_specs=[ANYWHERE] * 5 + [INSIDE] * 4,
        out_specs=[ANYWHERE] * 15 + [INSIDE] * 4,
        scratch_shapes=rooms(forward_scratch(rows, width, units) + packing) + signals(10, 10) + link_sems()
        + signals(9, 27, 26),
        compiler_params=pltpu.CompilerParams(collective_id=0, has_side_effects=True, vmem_limit_bytes=60 << 20),
    )(inputs, *shards, *gains, block_order, jnp.asarray(frequency.reshape(1, LANES)))


def backward_grads(width, units):
    return [low(2 * HEAD, width), low(2, width, units), low(HEAD, width), low(units, width), full(2, width)]


def forward_backward_call(layer, x_own, cotangent, weights, tables):
    rows, width = x_own.shape
    length = 16 * rows
    units = weights[3].shape[1]
    grads = backward_grads(width, units)
    more = [low(length, width), low(rows, width), low(length, 2 * units), low(length, width), low(length, 3 * LANES),
            low(length, LANES), low(length, LANES), full(length, LANES), full(length, LANES), full(rows, width),
            low(rows, width)] + grads
    outs = [low(rows, width), full(rows, width)] + grads + [low(rows, width)]
    return pl.pallas_call(
        functools.partial(forward_backward_kernel, layer),
        out_shape=shapes(outs),
        in_specs=[ANYWHERE] * 7 + [INSIDE] * 4,
        out_specs=[ANYWHERE] * len(outs),
        scratch_shapes=rooms(forward_scratch(rows, width, units) + more) + signals(10, 10) + link_sems()
        + signals(20, 7, 2) + link_sems(),
        compiler_params=pltpu.CompilerParams(collective_id=layer, has_side_effects=True, vmem_limit_bytes=60 << 20),
    )(x_own, cotangent, *weights, *tables)


def backward_return_call(grad_own, weights, tables, saved, old, results):
    rows, width = grad_own.shape
    length = 16 * rows
    units = weights[3].shape[1]
    depth = width // 4
    grads = backward_grads(width, units)
    scratch = [low(length, width), low(rows, width), low(length, width)] + [low(length, LANES)] * 4 + [
        full(length, LANES), full(rows, width), low(length, width), full(length, 2 * units), low(length, 2 * units),
        low(length, units), low(length, width), low(length, 3 * LANES), low(length, LANES), low(length, LANES),
        full(length, LANES), full(length, LANES),
        full(rows, width), low(rows, width)] + grads + [
        low(3 * LANES, width), low(width, 2 * units), low(LANES, width), low(units, width),
        low(16, width), low(length, width), low(19, rows, width), low(19, rows, width), full(rows, width)]
    scratch += grads[:4] + grads[:4] + [full(5, 8, width), full(5, 8, width)]
    outs = [low(2, rows, width), full(2, rows, width), low(16 * 2 * HEAD, depth), low(2, depth, 16 * units),
            low(4 * HEAD, width), low(4 * units, width), full(8, width)]
    return pl.pallas_call(
        backward_return_kernel,
        out_shape=shapes(outs),
        in_specs=[ANYWHERE] * 6 + [INSIDE] * 4 + [ANYWHERE] * SAVED + [ANYWHERE] * 5 + [INSIDE] + [ANYWHERE] * 2,
        out_specs=[ANYWHERE] * 6 + [INSIDE],
        scratch_shapes=rooms(scratch) + signals(20, 7, 2) + link_sems() + signals(5, 23, 23, 50, 40, 6),
        compiler_params=pltpu.CompilerParams(collective_id=2, has_side_effects=True, vmem_limit_bytes=60 << 20),
    )(grad_own, *weights, *tables, *saved, *old, *results)


def returner(refs, sems, gate_new, down_new, mix_new, out_new, gate_old, down_old, mix_old, out_old):
    (mix_out, gate_out, out_out, down_out, gain_out,
     mix_v, gate_v, out_v, down_v, mix_x, gate_x, out_x, down_x, gain_v, gain_x) = refs
    local, send, recv, line_send, line_recv = sems
    s = lax.axis_index("section")
    c = lax.axis_index("ctx")
    f = lax.axis_index("fsdp")
    other = {"section": 1 - s}
    units = down_v.shape[0]
    depth = gate_out.shape[1]
    inner = jnp.logical_and(c > 0, c < 3)
    above = jnp.minimum(c + 1, 3)
    below = jnp.maximum(c - 1, 0)

    def copy(src, dst, slot, arrival, peer):
        return pltpu.make_async_remote_copy(
            src, dst, send.at[slot], recv.at[arrival], device_id=peer, device_id_type=MESH
        )

    def owner_part(owner):
        return pl.ds(pl.multiple_of(owner * depth, depth), depth)

    def cross_parts(away, theirs, first):
        for k in range(4):
            owner = lax.rem(f + k, 4)
            part = owner_part(owner)
            copy(away.at[:, part], theirs.at[:, part], first + k, first + owner, other).start()

    def cross_whole(away, theirs, slot):
        copy(away, theirs, slot, slot, other).start()

    def home(src, dst, k):
        pltpu.make_async_copy(src, dst, local.at[k]).start()

    def begin_old():
        @pl.when(s == 0)
        def _():
            cross_whole(down_old, down_x, 8)
            cross_parts(gate_old, gate_x, 0)
            cross_whole(out_old, out_x, 9)
            cross_parts(mix_old, mix_x, 4)

        @pl.when(s == 1)
        def _():
            home(down_old, down_v, 0)
            home(gate_old, gate_v, 1)
            home(out_old, out_v, 2)
            home(mix_old, mix_v, 3)

    def begin_feed():
        @pl.when(s == 0)
        def _():
            home(down_new, down_v, 0)
            home(gate_new, gate_v, 1)

        @pl.when(s == 1)
        def _():
            cross_whole(down_new, down_x, 8)
            cross_parts(gate_new, gate_x, 0)

    def begin_mix():
        @pl.when(s == 0)
        def _():
            home(out_new, out_v, 2)
            home(mix_new, mix_v, 3)

        @pl.when(s == 1)
        def _():
            cross_whole(out_new, out_x, 9)
            cross_parts(mix_new, mix_x, 4)

    def home_wait(k, dst):
        pltpu.make_async_copy(dst, dst, local.at[k]).wait()

    def arrived(ref, arrival):
        copy(ref, ref, 0, arrival, other).wait_recv()

    def gate_at(cc, ff):
        return gate_out.at[:, :, pl.ds(pl.multiple_of((ff * 4 + cc) * units, units), units)]

    def mix_at(cc, ff):
        return mix_out.at[pl.ds(pl.multiple_of((ff * 4 + cc) * 2 * HEAD, 2 * HEAD), 2 * HEAD)]

    def rows_at(ref, cc, count):
        return ref.at[pl.ds(pl.multiple_of(cc * count, count), count)]

    def out_at(cc, ff):
        return rows_at(out_out, cc, HEAD)

    def down_at(cc, ff):
        return rows_at(down_out, cc, units)

    origins = [lax.rem(f + k, 4) for k in (0, 3, 2, 1)]
    items = [(down_at, f)] + [(gate_at, one) for one in origins] + [(out_at, f)] + [(mix_at, one) for one in origins]

    def line(index, cc, slot, target):
        place, origin = items[index]
        return pltpu.make_async_remote_copy(
            place(cc, origin), place(cc, origin), line_send.at[slot], line_recv.at[cc * 10 + index],
            device_id={"ctx": target}, device_id_type=MESH,
        )

    def start_line(index):
        pl.when(c < 3)(line(index, c, index, above).start)
        pl.when(c > 0)(line(index, c, 10 + index, below).start)

    def fold(mine, theirs, arrival):
        arrived(theirs, arrival)
        mine[...] = (mine[...].astype(F32) + theirs[...].astype(F32)).astype(BF)

    def keep(src, dst):
        one = pltpu.make_async_copy(src, dst, local.at[4])
        one.start()
        one.wait()

    def whole_item(k, mine, theirs, arrival, place, index):
        home_wait(k, mine)
        fold(mine, theirs, arrival)
        keep(mine, place(c, f))
        start_line(index)

    def to_owner(k, mine, theirs, place, arrival_x, arrival_y, slot, index):
        owner = lax.rem(f + k, 4)
        rows = owner_part(owner)
        fold(mine.at[:, rows], theirs.at[:, rows], arrival_x + owner)
        if k:
            copy(mine.at[:, rows], place(c, f), slot + k, arrival_y + f, {"fsdp": owner}).start()
        else:
            keep(mine.at[:, rows], place(c, f))
            start_line(index)

    def from_owner(k, place, arrival, index):
        arrived(place(c, origins[k]), arrival + origins[k])
        start_line(index)

    gain_targets = [other, {"fsdp": f + 1 - 2 * lax.rem(f, 2)}, {"fsdp": f + 2 - 4 * (f // 2)},
                    {"ctx": c + 1 - 2 * lax.rem(c, 2)}, {"ctx": lax.rem(c + 2, 4)}]

    def gain_copy(k):
        return copy(gain_v.at[k], gain_x.at[k], 18 + k, 18 + k, gain_targets[k])

    def gain_sum(k):
        gain_copy(k).wait_recv()
        if k < 4:
            gain_v[k + 1] = gain_v[k] + gain_x[k]
            gain_copy(k + 1).start()
        else:
            gain_out[...] = gain_v[k] + gain_x[k]

    order = near_order(c)

    def onward(index, step):
        d = order[step]
        return line(index, d, 20 + (step - 1) * 10 + index, jnp.where(d < c, above, below))

    def pass_on(index, step):
        one = onward(index, step)
        one.wait_recv()
        pl.when(inner)(one.start)

    def near(index):
        pass_on(index, 1)
        pl.when(inner)(lambda: pass_on(index, 2))

    def far(index):
        pl.when(jnp.logical_not(inner))(lambda: pass_on(index, 2))
        pass_on(index, 3)

    def gate_first():
        home_wait(1, gate_v)
        to_owner(0, gate_v, gate_x, gate_at, 0, 10, 10, 1)

    def gate_rest(k):
        return lambda: to_owner(k, gate_v, gate_x, gate_at, 0, 10, 10, 1)

    def gate_from(k):
        return lambda: from_owner(k, gate_at, 10, 1 + k)

    def mix_first():
        home_wait(3, mix_v)
        to_owner(0, mix_v, mix_x, mix_at, 4, 14, 14, 6)

    def mix_rest(k):
        return lambda: to_owner(k, mix_v, mix_x, mix_at, 4, 14, 14, 6)

    def mix_from(k):
        return lambda: from_owner(k, mix_at, 14, 6 + k)

    def down_first():
        whole_item(0, down_v, down_x, 8, down_at, 0)

    def out_first():
        whole_item(2, out_v, out_x, 9, out_at, 5)

    def passing(*steps):
        return [functools.partial(near if sign > 0 else far, abs(sign) - 1) for sign in steps]

    after = [
        passing(1) + [gate_from(1), gate_from(2), gate_from(3), out_first, mix_first, mix_rest(1), mix_rest(2), mix_rest(3)],
        passing(2, -1, 3, -2, 4) + [mix_from(1), mix_from(2), mix_from(3)],
        passing(-3, 5, -4, 6, -5, 7),
        passing(-6, 8, -7, 9),
        passing(-8, 10, -9, -10),
    ]
    def begin_return():
        down_first()
        gate_first()
        for k in range(1, 4):
            gate_rest(k)()

    def steps_after():
        gain_copy(0).start()
        for k, steps in enumerate(after):
            for step in steps:
                step()
            gain_sum(k)

    def wait_all():
        for index in range(10):
            pl.when(c < 3)(line(index, c, index, above).wait_send)
            pl.when(c > 0)(line(index, c, 10 + index, below).wait_send)
            for step in range(1, 4):
                pl.when(inner)(onward(index, step).wait_send)
        for k in range(5):
            gain_copy(k).wait_send()
        for k in range(4):
            gate_part = gate_x.at[:, pl.ds(k * depth, depth)]
            mix_part = mix_x.at[:, pl.ds(k * depth, depth)]
            for slot in (k, 10 + k) if k else (k,):
                copy(gate_part, gate_part, slot, 0, other).wait_send()
                copy(mix_part, mix_part, 4 + slot, 0, other).wait_send()
        copy(down_x, down_x, 8, 0, other).wait_send()
        copy(out_x, out_x, 9, 0, other).wait_send()

    return begin_old, begin_feed, begin_mix, begin_return, steps_after, wait_all


def widen_kernel(mix, gate, out, down, gains, results, starts,
                 mix_f, gate_f, out_f, down_f, attention_f, feed_f, results_f, starts_f, places, turned, rest):
    step = pl.program_id(0)
    rows = gate.shape[1]
    four = 4 * HEAD
    width = 4 * four

    @pl.when(step == 0)
    def _():
        s = lax.axis_index("section")
        f = lax.axis_index("fsdp")
        depth = attention_f.shape[1]
        columns = pl.ds(pl.multiple_of(f * depth, depth), depth)
        attention_f[...] = gains[pl.ds(2 * s, 1), columns]
        feed_f[...] = gains[pl.ds(2 * s + 1, 1), columns]
        results_f[...] = results[...]
        starts_f[...] = starts[...]
        source = lax.broadcasted_iota(jnp.int32, (2 * four, 2 * four), 0)
        column = lax.broadcasted_iota(jnp.int32, (2 * four, 2 * four), 1)
        query = (column // HEAD) * 2 * HEAD + lax.rem(column, HEAD)
        beyond = column - four
        kind = beyond // (2 * HEAD)
        beyond = beyond - kind * 2 * HEAD
        other = (2 * (beyond // HEAD) + kind) * 2 * HEAD + HEAD + lax.rem(beyond, HEAD)
        places[...] = jnp.where(source == jnp.where(column < four, query, other), 1.0, 0.0).astype(BF)

    @pl.when(step < 4)
    def _():
        group = kernel_dot_tn(mix[...], places[...])
        turned[:, pl.ds(pl.multiple_of(step * four, four), four)] = group[:, :four]
        rest[step] = group[:, four:]

    @pl.when(step >= 4)
    def _():
        here = pl.ds(pl.multiple_of((step - 4) * 2 * rows, 2 * rows), 2 * rows)
        mix_f[:, :width] = turned[here, :]
        for g in range(2):
            for kind in range(2):
                at = width + kind * 2 * four + g * four
                part = slice(kind * 2 * HEAD, (kind + 1) * 2 * HEAD)
                mix_f[:, at : at + four] = jnp.concatenate([rest[2 * g + k, here, part] for k in range(2)], axis=1)

    half = gate.shape[2]
    gate_f[:, :half] = gate[0].astype(F32)
    gate_f[:, half:] = gate[1].astype(F32)
    out_f[...] = out[...].astype(F32)
    down_f[...] = down[...].astype(F32)


def widen_call(results, starts, mix, gate, out, down, gains):
    steps = 8
    depth = gate.shape[1]
    width = out.shape[1]
    rows = depth // steps

    def whole(array):
        return pl.BlockSpec(array.shape, lambda i: (0,) * array.ndim)

    down_rows = down.shape[0] // steps
    return pl.pallas_call(
        widen_kernel,
        grid=(steps,),
        out_shape=shapes([
            full(depth, 2 * width), full(depth, 2 * gate.shape[2]), full(*out.shape), full(*down.shape),
            full(1, depth), full(1, depth), low(*results.shape), full(*starts.shape),
        ]),
        in_specs=[
            pl.BlockSpec((8 * HEAD, depth), lambda i: (jnp.minimum(i, 3), 0)),
            pl.BlockSpec((2, rows, gate.shape[2]), lambda i: (0, i, 0)),
            pl.BlockSpec((rows, width), lambda i: (i, 0)),
            pl.BlockSpec((down_rows, width), lambda i: (i, 0)),
            whole(gains),
            whole(results),
            whole(starts),
        ],
        out_specs=[
            pl.BlockSpec((2 * rows, 2 * width), lambda i: (jnp.maximum(i - 4, 0), 0)),
            pl.BlockSpec((rows, 2 * gate.shape[2]), lambda i: (i, 0)),
            pl.BlockSpec((rows, width), lambda i: (i, 0)),
            pl.BlockSpec((down_rows, width), lambda i: (i, 0)),
            pl.BlockSpec((1, depth), lambda i: (0, 0)),
            pl.BlockSpec((1, depth), lambda i: (0, 0)),
            whole(results),
            whole(starts),
        ],
        scratch_shapes=rooms([low(8 * HEAD, 8 * HEAD), full(depth, width), full(4, depth, 4 * HEAD)]),
        compiler_params=pltpu.CompilerParams(vmem_limit_bytes=60 << 20),
    )(mix, gate, out, down, gains, results, starts)


def on_line():
    return lax.axis_size("ctx") == 4 and lax.axis_size("fsdp") == 4


def gather(own):
    return lax.all_gather(own, ("ctx", "fsdp"), axis=0, tiled=True)


def scatter(part):
    return lax.psum_scatter(part, ("ctx", "fsdp"), scatter_dimension=0, tiled=True)


def spread_halves(columns):
    halves = columns.reshape(columns.shape[:-1] + (2, HEAD // 2))
    halves = jnp.pad(halves, [(0, 0)] * (halves.ndim - 1) + [(0, SPAN - HEAD // 2)])
    return halves.reshape(columns.shape[:-1] + (LANES,))


def join_halves(columns):
    halves = columns.reshape(columns.shape[:-1] + (2, SPAN))[..., : HEAD // 2]
    return halves.reshape(columns.shape[:-1] + (HEAD,))


def angle_tables(positions):
    frequency = rope_base ** (-(jnp.arange(HEAD // 2, dtype=F32) * 2.0 / HEAD))
    frequency = jnp.pad(frequency, (0, SPAN - HEAD // 2))
    angles = positions.astype(F32)[:, None] * frequency[None, :]
    cosine = jnp.cos(angles)
    sine = jnp.sin(angles)
    return jnp.concatenate([cosine, cosine], axis=1), jnp.concatenate([-sine, sine], axis=1)


def rotate(values, cosine, sine):
    return values * cosine + jnp.roll(values, SPAN, axis=1) * sine


def rotate_back(grads, cosine, sine):
    return grads * cosine - jnp.roll(grads, SPAN, axis=1) * sine


def norm_rows(values):
    return lax.rsqrt(jnp.mean(values * values, axis=-1, keepdims=True) + norm_eps)


def norm_back(grad_out, values, factor, gain):
    shaped = grad_out * gain
    common = jnp.mean(shaped * values, axis=-1, keepdims=True)
    grad_in = factor * shaped - values * (factor * factor * factor) * common
    return grad_in, jnp.sum(grad_out * values * factor, axis=0)


def dot(left, right):
    return jnp.dot(left, right, preferred_element_type=F32)


def dot_nt(left, right):
    return lax.dot_general(left, right, (((1,), (1,)), ((), ())), preferred_element_type=F32)


def dot_tn(left, right):
    return lax.dot_general(left, right, (((0,), (0,)), ((), ())), preferred_element_type=F32)


class Plan:
    def __init__(self, width, hidden_units):
        self.c = lax.axis_index("ctx")
        self.f = lax.axis_index("fsdp")
        self.C = lax.axis_size("ctx")
        self.F = lax.axis_size("fsdp")
        self.heads = width // HEAD
        self.ratio = self.heads // KV_HEADS
        self.heads_f = self.heads // self.F
        self.groups_f = KV_HEADS // self.F
        self.share = self.C // self.heads_f
        self.units = hidden_units // (self.F * self.C)
        self.local_head = self.c // self.share
        self.part = self.c % self.share


def pick(array, index, axis):
    return lax.dynamic_index_in_dim(array, index, axis, keepdims=False)


def pack_weights(plan, mix, gate_up):
    depth = mix.shape[0]
    width = plan.heads * HEAD
    kv_width = KV_HEADS * HEAD
    F = plan.F
    queries = pick(mix[:, :width].reshape(depth, F, plan.heads_f, HEAD), plan.local_head, 2)
    group = plan.local_head // plan.ratio
    keys = pick(mix[:, width : width + kv_width].reshape(depth, F, plan.groups_f, HEAD), group, 2)
    values = pick(mix[:, width + kv_width :].reshape(depth, F, plan.groups_f, HEAD), group, 2)
    values = jnp.pad(values, ((0, 0), (0, 0), (0, LANES - HEAD)))
    half = gate_up.shape[1] // 2
    gate = pick(gate_up[:, :half].reshape(depth, F, plan.C, plan.units), plan.c, 2)
    up = pick(gate_up[:, half:].reshape(depth, F, plan.C, plan.units), plan.c, 2)
    packed = jnp.concatenate([spread_halves(queries), spread_halves(keys), values, gate, up], axis=2)
    return jnp.swapaxes(packed, 0, 1)


def attend(plan, q_part, k, v, positions, part_positions):
    scores = dot_nt(q_part, k) * HEAD ** (-0.5)
    allowed = positions[None, :] <= part_positions[:, None]
    scores = jnp.where(allowed, scores, masked_value)
    top = jnp.max(scores, axis=-1, keepdims=True)
    weights = jnp.exp(scores - top)
    total = jnp.sum(weights, axis=-1, keepdims=True)
    context = dot((weights / total).astype(BF), v)
    return context.astype(BF), top + jnp.log(total)


def attend_back(q_part, k, v, context_grad, context, log_total, positions, part_positions):
    scale = HEAD ** (-0.5)
    common = jnp.sum(context_grad.astype(F32) * context.astype(F32), axis=-1, keepdims=True)
    allowed = positions[None, :] <= part_positions[:, None]
    scores = dot_nt(q_part, k) * scale
    weights = jnp.exp(jnp.where(allowed, scores, masked_value) - log_total)
    weight_grad = dot_nt(context_grad, v)
    score_grad = (weights * (weight_grad - common)).astype(BF)
    value_grad = dot_tn(weights.astype(BF), context_grad)
    key_grad = dot_tn(score_grad, q_part) * scale
    query_grad = dot(score_grad, k) * scale
    return query_grad, key_grad, value_grad


def forward_layer(plan, x_own, weights, gains, positions, part_positions, tables):
    mix_cut, gate_cut, out, down = weights
    cosine, sine = tables
    length = positions.shape[0]
    x_all = gather(x_own)
    x32 = x_all.astype(F32)
    factor = norm_rows(x32)
    normed = (x32 * factor * gains[0]).astype(BF)
    mixed = dot(normed, mix_cut)
    q = rotate(mixed[:, :LANES], cosine, sine).astype(BF)
    k = rotate(mixed[:, LANES : 2 * LANES], cosine, sine).astype(BF)
    v = mixed[:, 2 * LANES :].astype(BF)
    rows = length // plan.share
    start = plan.part * rows
    q_part = lax.dynamic_slice_in_dim(q, start, rows, 0)
    context, log_total = attend(plan, q_part, k, v, positions, part_positions)
    partial = dot(context[:, :HEAD], out).astype(BF)
    if plan.share > 1:
        partial = lax.dynamic_update_slice_in_dim(
            jnp.zeros((length, partial.shape[1]), BF), partial, start, 0
        )
    middle = x_own.astype(F32) + scatter(partial)
    factor_two = norm_rows(middle)
    normed_two = gather((middle * factor_two * gains[1]).astype(BF))
    both = dot(normed_two, gate_cut)
    hidden = (jax.nn.silu(both[:, : plan.units]) * both[:, plan.units :]).astype(BF)
    result = middle + scatter(dot(hidden, down).astype(BF))
    kept = (x_own, normed, q_part, k, v, context, log_total, middle, normed_two, both, hidden)
    return result.astype(BF), kept


def backward_layer(plan, grad_own, weights, gains, kept, positions, part_positions, tables, part_tables):
    mix_cut, gate_cut, out, down = weights
    x_own, normed, q_part, k, v, context, log_total, middle, normed_two, both, hidden = kept
    length = positions.shape[0]
    rows = length // plan.share
    start = plan.part * rows
    grad_all = gather(grad_own)
    hidden_grad = dot_nt(grad_all, down)
    gate = both[:, : plan.units]
    up = both[:, plan.units :]
    sig = jax.nn.sigmoid(gate)
    gate_grad = hidden_grad * up * sig * (1.0 + gate * (1.0 - sig))
    up_grad = hidden_grad * gate * sig
    both_grad = jnp.concatenate([gate_grad, up_grad], axis=1).astype(BF)
    normed_two_grad = scatter(dot_nt(both_grad, gate_cut).astype(BF))
    middle_grad, feed_gain_grad = norm_back(normed_two_grad, middle, norm_rows(middle), gains[1])
    middle_grad = middle_grad + grad_own.astype(F32)
    middle_low = gather(middle_grad.astype(BF))
    middle_part = lax.dynamic_slice_in_dim(middle_low, start, rows, 0)
    context_grad = jnp.pad(dot_nt(middle_part, out), ((0, 0), (0, LANES - HEAD))).astype(BF)
    query_grad, key_grad, value_grad = attend_back(
        q_part, k, v, context_grad, context, log_total, positions, part_positions
    )
    query_grad = rotate_back(query_grad, *part_tables).astype(BF)
    if plan.share > 1:
        query_grad = lax.dynamic_update_slice_in_dim(
            jnp.zeros((length, LANES), BF), query_grad, start, 0
        )
    key_grad = rotate_back(key_grad, *tables).astype(BF)
    mixed_grad = jnp.concatenate([query_grad, key_grad, value_grad.astype(BF)], axis=1)
    normed_grad = scatter(dot_nt(mixed_grad, mix_cut).astype(BF))
    x32 = x_own.astype(F32)
    start_grad, attention_gain_grad = norm_back(normed_grad, x32, norm_rows(x32), gains[0])
    start_grad = start_grad + middle_grad
    mix_grad = jnp.stack(
        [dot_tn(normed, part).astype(BF) for part in (query_grad, key_grad, value_grad.astype(BF))]
    )
    gate_cut_grad = jnp.stack(
        [dot_tn(normed_two, part.astype(BF)).astype(BF) for part in (gate_grad, up_grad)]
    )
    out_grad = dot_tn(context, middle_part).astype(BF)[:HEAD]
    down_grad = dot_tn(hidden, grad_all).astype(BF)
    return start_grad, (mix_grad, gate_cut_grad, out_grad, down_grad), jnp.stack([attention_gain_grad, feed_gain_grad])


def swap_sections(array):
    return lax.ppermute(array, "section", [(0, 1), (1, 0)])


def by_layer_of(section, own, other):
    first = section == 0
    return jnp.where(first, own, other), jnp.where(first, other, own)


def shared_weights(plan, section, attention_gain, query_key_value, output_weight, feed_gain, gate_up, down_weight):
    depth = query_key_value.shape[1]
    width = depth * plan.F
    gains = lax.all_gather(
        jnp.stack([attention_gain[0], feed_gain[0]]), ("section", "fsdp"), axis=0, tiled=False
    )
    gains = gains.reshape(2, plan.F, 2, depth)
    gains = jnp.swapaxes(gains, 1, 2).reshape(2, 2, width).astype(F32)
    packed = pack_weights(plan, query_key_value[0], gate_up[0])
    own_cut = lax.all_to_all(packed, "fsdp", 0, 0).reshape(width, -1)
    own_out = lax.dynamic_slice_in_dim(output_weight[0], plan.local_head * HEAD, HEAD, 0)
    own_down = lax.dynamic_slice_in_dim(down_weight[0], plan.c * plan.units, plan.units, 0)
    cuts = by_layer_of(section, own_cut, swap_sections(own_cut))
    outs = by_layer_of(section, own_out, swap_sections(own_out))
    downs = by_layer_of(section, own_down, swap_sections(own_down))
    weights = [(cuts[s][:, : 3 * LANES], cuts[s][:, 3 * LANES :], outs[s], downs[s]) for s in range(2)]
    return weights, gains


def own_gain_sums(plan, section, gain_sum, depth):
    gain_sum = lax.dynamic_slice_in_dim(gain_sum, 2 * section, 2, 0)
    return lax.dynamic_slice_in_dim(gain_sum, plan.f * depth, depth, 1)


def returned_grads(plan, section, weight_grads, gain_grads, depth):
    C, F = plan.C, plan.F
    gain_sum = jnp.concatenate([gain_grads[0], gain_grads[1]])

    def collected(index):
        first, second = weight_grads[0][index], weight_grads[1][index]
        own = jnp.where(section == 0, first, second)
        away = jnp.where(section == 0, second, first)
        return (own.astype(F32) + swap_sections(away).astype(F32)).astype(BF)

    cut_grad = jnp.concatenate(list(collected(0)) + list(collected(1)), axis=1)
    cut_grad = lax.all_to_all(cut_grad.reshape(F, depth, -1), "fsdp", 0, 0)
    cut_grad = lax.all_gather(cut_grad, "ctx", axis=0, tiled=False)
    out_grad = lax.all_gather(collected(2), "ctx", axis=0, tiled=False)
    down_grad = lax.all_gather(collected(3), "ctx", axis=0, tiled=True).astype(F32)

    def heads_of(columns, count):
        folded = columns.astype(F32).reshape(count, C // count, F, depth, columns.shape[-1]).sum(axis=1)
        return jnp.transpose(folded, (2, 1, 0, 3))

    q_grad = join_halves(heads_of(cut_grad[..., :LANES], plan.heads_f)).reshape(depth, -1)
    k_grad = join_halves(heads_of(cut_grad[..., LANES : 2 * LANES], plan.groups_f)).reshape(depth, -1)
    v_grad = heads_of(cut_grad[..., 2 * LANES : 3 * LANES], plan.groups_f)[..., :HEAD].reshape(depth, -1)
    mix_grad = jnp.concatenate([q_grad, k_grad, v_grad], axis=1)
    both = jnp.transpose(cut_grad[..., 3 * LANES :], (2, 1, 0, 3)).astype(F32)
    gate_up_grad = jnp.concatenate(
        [both[..., : plan.units].reshape(depth, -1), both[..., plan.units :].reshape(depth, -1)], axis=1
    )
    out_grad = out_grad.astype(F32).reshape(plan.heads_f, plan.share, HEAD, depth * F).sum(axis=1).reshape(-1, depth * F)

    gain_sum = lax.psum(gain_sum, ("section", "ctx", "fsdp"))
    return mix_grad, gate_up_grad, out_grad, down_grad, own_gain_sums(plan, section, gain_sum, depth)


def on_device(
    inputs, cotangent, attention_gain, query_key_value, output_weight, feed_gain, gate_up, down_weight, block_order
):
    section = lax.axis_index("section")
    width = inputs.shape[2]
    hidden_units = down_weight.shape[1] * lax.axis_size("fsdp")
    plan = Plan(width, hidden_units)
    rows = inputs.shape[1]
    C, F = plan.C, plan.F
    length = rows * C * F
    depth = query_key_value.shape[1]

    def by_layer(own, other):
        first = section == 0
        return jnp.where(first, own, other), jnp.where(first, other, own)

    results = []
    input_grads = [None, None]
    weight_grads = [None, None]
    gain_grads = [None, None]
    kept = []
    if on_line():
        shards = (query_key_value, output_weight, gate_up, down_weight)
        first = forward_share_call(inputs, shards, (attention_gain, feed_gain), block_order)
        weights = first[10:15]
        common = first[15:]
        results.append(first[9])
        result, *old, grad = forward_backward_call(1, first[9], cotangent, weights, common)
        results.append(result)
        last = backward_return_call(grad, weights, common, [inputs, *first[:9]], old, results)
        (mix_grad, gate_up_grad, out_grad, down_grad, attention_gain_grad, feed_gain_grad,
         section_outputs, section_input_grads) = widen_call(*last)
    else:
        order = pick(block_order, section, 0)
        positions = (order[:, None] * rows + jnp.arange(rows, dtype=jnp.int32)[None, :]).reshape(length)
        part_rows = length // plan.share
        part_positions = lax.dynamic_slice_in_dim(positions, plan.part * part_rows, part_rows, 0)
        tables = angle_tables(positions)
        part_tables = angle_tables(part_positions)

        x = pick(inputs, section, 0)
        grad = pick(cotangent, section, 0)
        weights, gains = shared_weights(
            plan, section, attention_gain, query_key_value, output_weight, feed_gain, gate_up, down_weight
        )
        for s in range(2):
            x, keep = forward_layer(plan, x, weights[s], gains[s], positions, part_positions, tables)
            kept.append(keep)
            results.append(x)
        for s in (1, 0):
            input_grads[s], weight_grads[s], gain_grads[s] = backward_layer(
                plan, grad, weights[s], gains[s], kept[s], positions, part_positions, tables, part_tables
            )
            grad = input_grads[s].astype(BF)
        def mine_and_theirs(first, second):
            return jnp.where(section == 0, first, second), jnp.where(section == 0, second, first)

        def by_batch(first, second):
            own, away = mine_and_theirs(first, second)
            return jnp.stack(by_layer(own, swap_sections(away)))

        section_outputs = by_batch(*results)
        section_input_grads = by_batch(*input_grads)

        shard_grads = returned_grads(plan, section, weight_grads, gain_grads, depth)
        mix_grad, gate_up_grad, out_grad, down_grad, gain_sum = shard_grads
        attention_gain_grad, feed_gain_grad = gain_sum[0][None], gain_sum[1][None]

    return (
        section_outputs[None],
        section_input_grads[None],
        attention_gain_grad,
        mix_grad[None],
        out_grad[None],
        feed_gain_grad,
        gate_up_grad[None],
        down_grad[None],
    )


def solution(mesh):
    placed = (
        P(None, ("ctx", "fsdp"), None),
        P(None, ("ctx", "fsdp"), None),
        P("section", "fsdp"),
        P("section", "fsdp", None),
        P("section", "fsdp", None),
        P("section", "fsdp"),
        P("section", "fsdp", None),
        P("section", "fsdp", None),
        P(),
    )
    return jax.shard_map(
        on_device,
        mesh=mesh,
        in_specs=placed,
        out_specs=(
            P("section", None, ("ctx", "fsdp"), None),
            P("section", None, ("ctx", "fsdp"), None),
            P("section", "fsdp"),
            P("section", "fsdp", None),
            P("section", "fsdp", None),
            P("section", "fsdp"),
            P("section", "fsdp", None),
            P("section", "fsdp", None),
        ),
        check_vma=False,
    )
```

```python
import functools

import jax
import jax.numpy as jnp
import numpy as np
from jax import lax
from jax.experimental import pallas as pl
from jax.experimental.pallas import tpu as pltpu
from jax.sharding import PartitionSpec as P

KV_HEADS = 8
HEAD = 96
LANES = 128
SPAN = 64
norm_eps = 1e-05
rope_base = 100000.0
masked_value = -1e30
BF = jnp.bfloat16
F32 = jnp.float32

MESH = pl.DeviceIdType.MESH


def greet():
    c = lax.axis_index("ctx")
    f = lax.axis_index("fsdp")
    barrier = pltpu.get_barrier_semaphore()
    inner = jnp.logical_and(c > 0, c < 3)
    for peer in (f + 2 - 4 * (f // 2), f + 1 - 2 * lax.rem(f, 2)):
        pl.semaphore_signal(barrier, inc=1, device_id={"fsdp": peer}, device_id_type=MESH)
    pl.semaphore_signal(barrier, inc=1, device_id={"ctx": lax.rem(c + 2, 4)}, device_id_type=MESH)

    @pl.when(c < 3)
    def _():
        pl.semaphore_signal(barrier, inc=1, device_id={"ctx": c + 1}, device_id_type=MESH)

    @pl.when(c > 0)
    def _():
        pl.semaphore_signal(barrier, inc=1, device_id={"ctx": c - 1}, device_id_type=MESH)

    @pl.when(inner)
    def _():
        pl.semaphore_wait(barrier, 5)

    @pl.when(jnp.logical_not(inner))
    def _():
        pl.semaphore_wait(barrier, 4)


def near_order(c):
    low = c < 2
    return [c, c + 1 - 2 * lax.rem(c, 2), jnp.where(low, 2, 1), jnp.where(low, 3, 0)]


def own_block(c, f):
    return c * 4 + lax.rem(f, 2) * 2 + f // 2


def begin_rows(whole, rows, send, recv, h):
    c = lax.axis_index("ctx")
    f = lax.axis_index("fsdp")
    half = rows // 2
    mine = whole.at[pl.ds(pl.multiple_of(own_block(c, f) * rows + h * half, half), half)]

    def copy(slot, arrival, peer):
        return pltpu.make_async_remote_copy(
            mine, mine, send.at[slot], recv.at[arrival], device_id=peer, device_id_type=MESH
        )

    pl.when(c < 3)(copy(0, 2 * c + h, {"ctx": jnp.minimum(c + 1, 3)}).start)
    pl.when(c > 0)(copy(1, 2 * c + h, {"ctx": jnp.maximum(c - 1, 0)}).start)
    copy(3, 8 + c, {"fsdp": f + 2 - 4 * (f // 2)}).start()


def gather_rows(whole, rows, send, recv, ready=None, started=None, begun=False):
    c = lax.axis_index("ctx")
    f = lax.axis_index("fsdp")
    y = f // 2
    lane = lax.rem(f, 2)
    inner = jnp.logical_and(c > 0, c < 3)
    outer = jnp.logical_not(inner)
    order = near_order(c)
    pair = order[1]
    half = rows // 2
    to_across = {"fsdp": f + 2 - 4 * y}
    to_twin = {"fsdp": f + 1 - 2 * lane}
    to_pair = {"ctx": pair}

    def at(d, k, yy, h):
        return whole.at[pl.ds(pl.multiple_of((d * 4 + k * 2 + yy) * rows + h * half, half), half)]

    def block(d, k, yy):
        return whole.at[pl.ds(pl.multiple_of((d * 4 + k * 2 + yy) * rows, rows), rows)]

    def two(d, k):
        return whole.at[pl.ds(pl.multiple_of((d * 4 + k * 2) * rows, rows), 2 * rows)]

    def copy(src, slot, arrival, peer):
        return pltpu.make_async_remote_copy(
            src, src, send.at[slot], recv.at[arrival], device_id=peer, device_id_type=MESH
        )

    def go(src, slot, arrival, peer, when=None):
        one = copy(src, slot, arrival, peer)
        if when is None:
            one.start()
        else:
            pl.when(when)(one.start)

    def arrived(ref, arrival):
        copy(ref, 0, arrival, to_twin).wait_recv()

    def gone(count, slot):
        copy(whole.at[pl.ds(0, count * half)], slot, 0, to_twin).wait_send()

    if not begun:
        for h in range(2):
            begin_rows(whole, rows, send, recv, h)
    if started is not None:
        started()

    events = [
        (pair, 0),
        (jnp.where(inner, order[2], pair), jnp.where(inner, 0, 1)),
        (jnp.where(inner, pair, order[2]), jnp.where(inner, 1, 0)),
        (order[2], 1),
        (order[3], 0),
        (order[3], 1),
    ]

    def along(index):
        d, h = events[index]
        piece = at(d, lane, y, h)
        arrived(piece, 2 * d + h)
        go(piece, 2, 2 * d + h, {"ctx": jnp.where(d < c, c + 1, c - 1)}, inner)
        go(piece, 3, 8 + d, to_across, jnp.logical_or(d != pair, h == 0) if index in (1, 2) else None)

    def complete(d):
        arrived(two(d, 1 - lane), 13 + d)
        if ready is not None:
            ready(d)

    def pair_half(when):
        go(at(c, lane, 1 - y, 1), 4, 12, to_pair, when)

    along(0)
    along(1)
    along(2)
    arrived(block(c, lane, 1 - y), 8 + c)
    pair_half(outer)
    go(two(c, lane), 5, 13 + c, to_twin)
    along(3)
    complete(c)
    along(4)
    along(5)
    pair_half(inner)
    arrived(block(order[2], lane, 1 - y), 8 + order[2])
    go(two(order[2], lane), 5, 13 + order[2], to_twin)
    go(block(order[3], lane, y), 5, 13 + order[3], to_twin)
    complete(order[2])
    arrived(at(pair, lane, 1 - y, 0), 8 + pair)
    arrived(at(pair, lane, 1 - y, 1), 12)
    go(two(pair, lane), 5, 13 + pair, to_twin)
    arrived(block(order[3], lane, 1 - y), 8 + order[3])
    go(block(order[3], lane, 1 - y), 5, 17, to_twin)
    complete(pair)
    arrived(block(order[3], 1 - lane, y), 13 + order[3])
    arrived(block(order[3], 1 - lane, 1 - y), 17)
    if ready is not None:
        ready(order[3])
    pl.when(c < 3)(lambda: gone(2, 0))
    pl.when(c > 0)(lambda: gone(2, 1))
    pl.when(inner)(lambda: gone(6, 2))
    gone(7, 3)
    gone(1, 4)
    gone(16, 5)


GATHER_SENDS = 6
GATHER_RECVS = 18


def scatter_sum(part, total, land, send, recv, produce=None, meanwhile=None, ending=None, done=None):
    c = lax.axis_index("ctx")
    f = lax.axis_index("fsdp")
    y = f // 2
    lane = lax.rem(f, 2)
    inner = jnp.logical_and(c > 0, c < 3)
    rows = total.shape[0]
    half = rows // 2
    order = near_order(c)[::-1]
    to_across = {"fsdp": f + 2 - 4 * y}
    to_twin = {"fsdp": f + 1 - 2 * lane}
    to_pair = {"ctx": order[2]}

    def rows_at(d, yy, h):
        return pl.ds(pl.multiple_of((d * 4 + lane * 2 + yy) * rows + h * half, half), half)

    def copy(src, dst, slot, arrival, peer):
        return pltpu.make_async_remote_copy(
            src, dst, send.at[slot], recv.at[arrival], device_id=peer, device_id_type=MESH
        )

    def go(src, dst, slot, arrival, peer):
        copy(src, dst, slot, arrival, peer).start()

    def gone(count, slot):
        ref = part.at[pl.ds(0, count * half)]
        copy(ref, ref, slot, 0, to_twin).wait_send()

    def piece(slot, h):
        return land.at[slot, pl.ds(h * half, half)]

    def landed(ref, arrival):
        copy(ref, ref, 0, arrival, to_twin).wait_recv()
        return ref[...].astype(F32)

    def begin(step):
        d = order[step]
        if produce is not None:
            produce(d)
        for yy, slot in ((1 - y, step), (y, 27 + step)):
            other = pl.ds(pl.multiple_of((d * 4 + 2 - lane * 2 + yy) * rows, rows), rows)
            go(part.at[other], land.at[2 * step + yy], 0, slot, to_twin)

    def twin_there(step, yy, slot):
        ref = land.at[2 * step + yy]
        copy(ref, ref, 0, slot, to_twin).wait_recv()

    def over(step, h, first=False):
        d = order[step]
        if first:
            twin_there(step, 1 - y, step)
        mine = rows_at(d, 1 - y, h)
        value = part[mine, :].astype(F32) + piece(2 * step + 1 - y, h)[...].astype(F32)
        if (step, h) == (3, 1):
            value = value + landed(piece(17, 0), 26)
        part[mine, :] = value.astype(BF)
        if (step, h) == (2, 1):
            go(part.at[mine], piece(17, 0), 3, 26, to_pair)
        else:
            go(part.at[mine], piece(8 + step, h), 1, 8 + 2 * step + h, to_across)

    def onward(step, h, first=False):
        d = order[step]
        mine = rows_at(d, y, h)
        if first:
            twin_there(step, y, 27 + step)
        value = part[mine, :].astype(F32) + piece(2 * step + y, h)[...].astype(F32)
        if (step, h) != (2, 1):
            value = value + landed(piece(8 + step, h), 8 + 2 * step + h)
        if step == 3:
            total[h * half : (h + 1) * half, :] = value
            return
        part[mine, :] = value.astype(BF)

        if step < 2:

            @pl.when(inner)
            def _():
                part[mine, :] = (part[mine, :].astype(F32) + landed(piece(12 + d, h), 16 + 2 * d + h)).astype(BF)

        here = jnp.logical_and(d < c, d == c - 1)
        target = jnp.where(d > c, c + 1, c - 1)
        slot = jnp.where(here, 16, 12 + d)
        arrival = jnp.where(here, 24, 16 + 2 * d) + h
        if step == 0:
            target = jnp.where(inner, d, target)
            slot = jnp.where(inner, 18, slot)
            arrival = jnp.where(inner, 31 + h, arrival)
        go(part.at[mine], piece(slot, h), 2, arrival, {"ctx": target})

    begin(0)
    over(0, 0, True)
    over(0, 1)
    begin(1)
    begin(2)
    over(2, 1, True)
    over(1, 0, True)
    onward(0, 0, True)
    over(1, 1)
    onward(0, 1)
    if meanwhile is not None:
        meanwhile()
    begin(3)
    over(2, 0)
    onward(1, 0, True)
    over(3, 0, True)
    onward(1, 1)
    over(3, 1)
    onward(2, 1, True)
    onward(2, 0)
    if ending is not None:
        ending()
    for h in range(2):
        onward(3, h, h == 0)

        @pl.when(c > 0)
        def _():
            total[h * half : (h + 1) * half, :] += landed(piece(12 + c, h), 16 + 2 * c + h)

        @pl.when(c < 3)
        def _():
            total[h * half : (h + 1) * half, :] += landed(piece(16, h), 24 + h)

        @pl.when(jnp.logical_not(inner))
        def _():
            total[h * half : (h + 1) * half, :] += landed(piece(18, h), 31 + h)

        if done is not None:
            done(h)

    gone(16, 0)
    gone(7, 1)
    gone(6, 2)
    gone(1, 3)


SCATTER_SENDS = 4
SCATTER_RECVS = 33


def kernel_dot(left, right):
    return jnp.dot(left, right, preferred_element_type=F32)


def kernel_dot_nt(left, right):
    return lax.dot_general(left, right, (((1,), (1,)), ((), ())), preferred_element_type=F32)


def kernel_dot_tn(left, right):
    return lax.dot_general(left, right, (((0,), (0,)), ((), ())), preferred_element_type=F32)


def turn(values):
    return pltpu.roll(values, SPAN, axis=1)


def mean_square(values):
    return lax.rsqrt(jnp.mean(values * values, axis=-1, keepdims=True) + norm_eps)


def greet_all(peers):
    barrier = pltpu.get_barrier_semaphore()
    for peer in peers:
        pl.semaphore_signal(barrier, inc=1, device_id=peer, device_id_type=MESH)
    return len(peers)


def greet_more(peers):
    c = lax.axis_index("ctx")
    barrier = pltpu.get_barrier_semaphore()
    count = greet_all(peers)
    inner = jnp.logical_and(c > 0, c < 3)

    @pl.when(c < 3)
    def _():
        pl.semaphore_signal(barrier, inc=1, device_id={"ctx": c + 1}, device_id_type=MESH)

    @pl.when(c > 0)
    def _():
        pl.semaphore_signal(barrier, inc=1, device_id={"ctx": c - 1}, device_id_type=MESH)

    @pl.when(inner)
    def _():
        pl.semaphore_wait(barrier, count + 2)

    @pl.when(jnp.logical_not(inner))
    def _():
        pl.semaphore_wait(barrier, count + 1)


class Share:
    def __init__(self, sources, targets, scratch, sems):
        self.mix, self.out, self.gate_up, self.down, self.attention_gain, self.feed_gain = sources
        self.w_mix, self.w_gate, self.w_out, self.w_down, self.w_gains = targets
        self.mix_v, self.heads_v, self.gate_s, self.out_s, self.down_s, self.gains = scratch
        self.local, self.send, self.recv = sems
        self.s = lax.axis_index("section")
        self.c = lax.axis_index("ctx")
        self.f = lax.axis_index("fsdp")
        self.other = 1 - self.s
        self.depth = self.mix.shape[1]
        self.units = self.w_down.shape[1]
        self.peers = [lax.rem(self.f + k, 4) for k in range(1, 4)]
        self.rows = pl.ds(pl.multiple_of(self.f * self.depth, self.depth), self.depth)
        self.pending = []

    def greeted(self):
        return (
            [{"fsdp": peer} for peer in self.peers]
            + [{"section": self.other}, {"ctx": lax.rem(self.c + 2, 4)}]
            + [{"section": self.other, "fsdp": peer} for peer in self.peers]
        )

    def copy(self, src, dst, slot, arrival, peer):
        return pltpu.make_async_remote_copy(
            src, dst, self.send.at[slot], self.recv.at[arrival], device_id=peer, device_id_type=MESH
        )

    def go(self, src, dst, slot, arrival, peer):
        one = self.copy(src, dst, slot, arrival, peer)
        one.start()
        self.pending.append(one)

    def keep(self, src, dst, slot):
        one = pltpu.make_async_copy(src, dst, self.local.at[slot])
        one.start()
        return one

    def load(self):
        self.gains[...] = jnp.zeros_like(self.gains)
        self.gains[0:1, :] = self.attention_gain[...]
        self.gains[1:2, :] = self.feed_gain[...]
        self.loaded = self.keep(self.mix.at[0], self.mix_v, 0)
        out_rows = self.out.at[0, pl.ds(pl.multiple_of(self.c * HEAD, HEAD), HEAD)]
        down_rows = self.down.at[0, pl.ds(pl.multiple_of(self.c * self.units, self.units), self.units)]
        self.staged = [
            self.keep(self.gate_piece(self.f, part), self.gate_s.at[:, pl.ds(part * self.units, self.units)], 5 + part)
            for part in range(2)
        ]
        self.staged.append(self.keep(out_rows, self.out_s, 7))
        self.staged.append(self.keep(down_rows, self.down_s, 8))

    def head_rows(self, peer, part):
        head = peer * 4 + self.c
        start = head * HEAD if part == 0 else (16 + 8 * (part - 1) + head // 2) * HEAD
        return self.heads_v.at[pl.ds(pl.multiple_of(start, HEAD), HEAD)]

    def put(self, part):
        return self.w_mix.at[self.s, pl.ds(part * HEAD, HEAD), self.rows]

    def send_mix(self):
        self.loaded.wait()
        for g in range(8):
            here = slice(g * 4 * HEAD, (g + 1) * 4 * HEAD)
            self.heads_v[here, :] = self.mix_v[:, here].T
        for k, peer in enumerate(self.peers):
            for part in range(3):
                self.copy(self.head_rows(peer, part), self.put(part), k, self.f, {"fsdp": peer}).start()
        self.own_mix = [self.keep(self.head_rows(self.f, part), self.put(part), 2 + part) for part in range(3)]
        for one in self.staged:
            one.wait()
        self.own_gate = self.keep(self.gate_s, self.slab(self.w_gate, self.f), 5)
        self.own_out = self.keep(self.out_s, self.w_out.at[self.s], 7)
        self.own_down = self.keep(self.down_s, self.w_down.at[self.s], 8)
        mine = self.w_gains.at[self.s, :, pl.ds(pl.multiple_of(self.f * self.depth, self.depth), self.depth)]
        for k, peer in enumerate(self.peers):
            self.go(self.gains, mine, 20 + k, 16 + 4 * self.s + self.f, {"fsdp": peer})
            self.go(self.gains, mine, 23 + k, 16 + 4 * self.s + self.f, {"section": self.other, "fsdp": peer})
        self.go(self.gains, mine, 26, 16 + 4 * self.s + self.f, {"section": self.other})
        self.own_gains = self.keep(self.gains, mine, 1)

    def gate_piece(self, peer, part):
        hidden_units = self.gate_up.shape[2] // 2
        start = pl.multiple_of(part * hidden_units + (peer * 4 + self.c) * self.units, self.units)
        return self.gate_up.at[0, :, pl.ds(start, self.units)]

    def gate_put(self, part):
        return self.w_gate.at[self.s, self.rows, pl.ds(part * self.units, self.units)]

    def send_gate(self):
        for k, peer in enumerate(self.peers):
            for part in range(2):
                self.copy(self.gate_piece(peer, part), self.gate_put(part), 3 + k, 4 + self.f, {"fsdp": peer}).start()

    def slab(self, ref, origin):
        part = pl.ds(pl.multiple_of(origin * self.depth, self.depth), self.depth)
        return ref.at[self.s, :, part] if ref is self.w_mix else ref.at[self.s, part]

    def cross_slab(self, ref, k, slot, arrival, base):
        origin = lax.rem(self.f + 3 - k, 4)
        block = self.slab(ref, origin)
        self.copy(block, block, 0, arrival + origin, {"fsdp": origin}).wait_recv()
        self.go(block, block, slot + k, base + origin, {"section": self.other})

    def cross_mix(self, between):
        for one in self.own_mix:
            one.wait()
        self.go(self.slab(self.w_mix, self.f), self.slab(self.w_mix, self.f), 6, 8 + self.f, {"section": self.other})
        between()
        for k in range(3):
            self.cross_slab(self.w_mix, k, 7, 0, 8)
        self.send_gate()
        self.go(self.out_s, self.w_out.at[self.s], 10, 24, {"section": self.other})
        self.go(self.gate_s, self.slab(self.w_gate, self.f), 11, 12 + self.f, {"section": self.other})

    def cross_gate(self):
        for k in range(3):
            self.cross_slab(self.w_gate, k, 12, 4, 12)
        self.go(self.down_s, self.w_down.at[self.s], 15, 25, {"section": self.other})

    def there(self, ref, arrival):
        self.copy(ref, ref, 0, arrival, {"section": self.other}).wait_recv()

    def mix_there(self):
        for one in (self.own_gains, self.own_gate, self.own_out, self.own_down):
            one.wait()
        for origin in range(4):
            rows = pl.ds(origin * self.depth, self.depth)
            self.there(self.w_mix.at[self.other, :, rows], 8 + origin)
            self.there(self.w_gains.at[self.other, :, rows], 16 + 4 * self.other + origin)
        for k in range(3):
            origin = lax.rem(self.f + 3 - k, 4)
            columns = pl.ds(pl.multiple_of(origin * self.depth, self.depth), self.depth)
            self.there(self.w_gains.at[self.s, :, columns], 16 + 4 * self.s + origin)
        self.there(self.w_out.at[self.other], 24)

    def gate_there(self):
        for origin in range(4):
            self.there(self.w_gate.at[self.other, pl.ds(origin * self.depth, self.depth)], 12 + origin)

    def down_there(self):
        self.there(self.w_down.at[self.other], 25)

    def finish(self):
        for k, peer in enumerate(self.peers):
            block = self.slab(self.w_mix, self.f)
            self.copy(block, block, k, 0, {"fsdp": peer}).wait_send()
            block = self.slab(self.w_gate, self.f)
            self.copy(block, block, 3 + k, 0, {"fsdp": peer}).wait_send()
        for one in self.pending:
            one.wait_send()


class Loads:
    def __init__(self, sems):
        self.sems = sems
        self.copies = []

    def start(self, src, dst):
        one = pltpu.make_async_copy(src, dst, self.sems.at[len(self.copies)])
        one.start()
        self.copies.append(one)
        return one


def load_heads(loads, source, target):
    half = HEAD // 2
    target[...] = jnp.zeros_like(target)
    pieces = [(part * HEAD + h * half, part * LANES + h * SPAN, half) for part in range(2) for h in range(2)]
    pieces.append((2 * HEAD, 2 * LANES, HEAD))
    return [loads.start(source.at[pl.ds(a, count)], target.at[pl.ds(b, count)]) for a, b, count in pieces]


def plane_rows(d, rows):
    return pl.ds(pl.multiple_of(d * 4 * rows, 4 * rows), 4 * rows)


def make_tables(block_order, frequency, cosine, sine, place_col, place_row):
    s = lax.axis_index("section")
    blocks = block_order.shape[1]
    rows = place_col.shape[0] // blocks
    order = jnp.where(s == 0, block_order[0:1, :], block_order[1:2, :])
    inside_col = lax.broadcasted_iota(jnp.int32, (rows, 1), 0)
    inside_row = lax.broadcasted_iota(jnp.int32, (1, 2 * rows), 1)
    firsts = []
    for b in range(blocks):
        source = b - b % 4 + (b % 2) * 2 + (b % 4) // 2
        firsts.append(order[:, source : source + 1] * rows)
        place_col[b * rows : (b + 1) * rows, :] = firsts[b] + inside_col
    for b in range(0, blocks, 2):
        place_row[:, b * rows : (b + 2) * rows] = jnp.where(
            inside_row < rows, firsts[b] + inside_row, firsts[b + 1] + inside_row - rows
        )
    lane = lax.broadcasted_iota(jnp.int32, (4 * rows, LANES), 1)
    for part in range(blocks // 4):
        here = pl.ds(part * 4 * rows, 4 * rows)
        angles = place_col[here, :].astype(F32) * frequency[...]
        wave = jnp.sin(angles)
        cosine[here, :] = jnp.cos(angles)
        sine[here, :] = jnp.where(lane < SPAN, -wave, wave)


def forward_body(layer, share, x_own, weights, tables, kept, scratch, sems, prepare=None, before=None, ending=None, meet=None):
    w_mix, w_gate, w_out, w_down, w_gains = weights
    cosine, sine, place_col, place_row = tables
    normed_o, q_o, k_o, v_o, context_o, log_o, middle_o, normed_two_o, both_o, result_o = kept
    (x_v, normed_v, q_v, k_v, v_v, context_v, log_v, middle_v, two_v, both_v, hidden_v, result_v,
     mix_v, gate_v, out_v, down_v, gains_v, part_v, land_a, land_b, total_v) = scratch
    local, save, send_a, recv_a, send_b, recv_b, send_c, recv_c, send_d, recv_d = sems
    c = lax.axis_index("ctx")
    f = lax.axis_index("fsdp")
    rows = x_own.shape[0]
    units = down_v.shape[0]
    own_rows = pl.ds(pl.multiple_of(own_block(c, f) * rows, rows), rows)
    loads = Loads(local)
    saves = Loads(save)

    def save_to(src, dst):
        if dst is not None:
            saves.start(src, dst)

    load_x = loads.start(x_own, x_v.at[own_rows])
    out_v[...] = jnp.zeros_like(out_v)

    def load_first():
        return [
            loads.start(w_gains.at[layer], gains_v),
            loads.start(w_out.at[layer], out_v.at[pl.ds(0, HEAD)]),
        ] + load_heads(loads, w_mix.at[layer], mix_v)

    def project(d):
        here = plane_rows(d, rows)
        x = x_v[here, :].astype(F32)
        normed = (x * mean_square(x) * gains_v[0:1, :].astype(F32)).astype(BF)
        normed_v[here, :] = normed
        mixed = kernel_dot_nt(normed, mix_v[...])
        cos = cosine[here, :]
        sin = sine[here, :]
        q = mixed[:, :LANES]
        k = mixed[:, LANES : 2 * LANES]
        q_v[here, :] = (q * cos + turn(q) * sin).astype(BF)
        k_v[here, :] = (k * cos + turn(k) * sin).astype(BF)
        v_v[here, :] = mixed[:, 2 * LANES :].astype(BF)

    if share is None:
        first = load_first()
        load_gate = loads.start(w_gate.at[layer], gate_v)
        load_down = loads.start(w_down.at[layer], down_v)
        meet()
        load_x.wait()
        for one in first:
            one.wait()
        gather_rows(x_v, rows, send_a, recv_a, project)
    else:
        share.load()
        greet_more(share.greeted())
        load_x.wait()
        share.send_mix()
        gather_rows(x_v, rows, send_a, recv_a, started=lambda: share.cross_mix(prepare))
        share.mix_there()
        first = load_first()
        for one in first:
            one.wait()
        for d in range(4):
            project(d)
        share.cross_gate()
    for src, dst in ((normed_v, normed_o), (q_v, q_o), (k_v, k_o), (v_v, v_o)):
        save_to(src, dst)
    scale = HEAD ** (-0.5)

    def attention(d):
        here = plane_rows(d, rows)
        scores = kernel_dot_nt(q_v[here, :], k_v[...]) * scale
        allowed = place_row[...] <= place_col[here, :]
        scores = jnp.where(allowed, scores, masked_value)
        top = jnp.max(scores, axis=-1, keepdims=True)
        weights = jnp.exp(scores - top)
        amount = jnp.sum(weights, axis=-1, keepdims=True)
        context = (kernel_dot(weights.astype(BF), v_v[...]) / amount).astype(BF)
        context_v[here, :] = context
        log_v[here, :] = jnp.broadcast_to(top + jnp.log(amount), (4 * rows, LANES))
        part_v[here, :] = kernel_dot(context, out_v[...]).astype(BF)

    half = rows // 2

    def own_half(h):
        return pl.ds(pl.multiple_of(own_block(c, f) * rows + h * half, half), half)

    def middle_half(h):
        part = slice(h * half, (h + 1) * half)
        middle = x_v[own_half(h), :].astype(F32) + total_v[part, :]
        middle_v[part, :] = middle
        two_v[own_half(h), :] = (middle * mean_square(middle) * gains_v[1:2, :].astype(F32)).astype(BF)
        begin_rows(two_v, rows, send_c, recv_c, h)

    scatter_sum(part_v, total_v, land_a, send_b, recv_b, attention, done=middle_half)
    save_to(context_v, context_o)
    save_to(log_v, log_o)
    save_to(middle_v, middle_o)

    def gate_ready():
        if share is None:
            load_gate.wait()
        else:
            share.gate_there()
            loads.start(w_gate.at[layer], gate_v).wait()

    def feed(d):
        here = plane_rows(d, rows)
        both = kernel_dot(two_v[here, :], gate_v[...])
        both_v[here, :] = both
        gate = both[:, :units]
        hidden_v[here, :] = (gate * jax.nn.sigmoid(gate) * both[:, units:]).astype(BF)

    first = iter((True, False, False, False))

    def feed_when_ready(d):
        if next(first):
            gate_ready()
        feed(d)

    gather_rows(two_v, rows, send_c, recv_c, feed_when_ready, begun=True)
    save_to(two_v, normed_two_o)
    save_to(both_v, both_o)
    if share is None:
        load_down.wait()
    else:
        share.down_there()
        loads.start(w_down.at[layer], down_v).wait()

    def lower(d):
        here = plane_rows(d, rows)
        part_v[here, :] = kernel_dot(hidden_v[here, :], down_v[...]).astype(BF)

    if before is not None:
        before()
    scatter_sum(part_v, total_v, land_b, send_d, recv_d, lower, ending=ending)
    result_v[...] = (middle_v[...] + total_v[...]).astype(BF)
    saves.start(result_v, result_o)
    for one in saves.copies:
        one.wait()
    if share is not None:
        share.finish()


def forward_share_kernel(*refs):
    inputs, *refs = refs
    sources, refs = refs[:6], refs[6:]
    (block_order, frequency), refs = refs[:2], refs[2:]
    kept, refs = refs[:10], refs[10:]
    weights, refs = refs[:5], refs[5:]
    tables, refs = refs[:4], refs[4:]
    scratch, refs = refs[:21], refs[21:]
    packing, refs = refs[:6], refs[6:]
    sems, share_sems = refs[:10], refs[10:]
    share = Share(sources, weights, packing, share_sems)
    forward_body(
        0, share, inputs.at[lax.axis_index("section")], weights, tables, kept, scratch, sems,
        lambda: make_tables(block_order, frequency, *tables),
    )


def backward_body(layer, grad_own, weights, tables, saved, outs, scratch, sems, returning, forward=None, hand_on=None):
    w_mix, w_gate, w_out, w_down, w_gains = weights
    cosine, sine, place_col, place_row = tables
    (grad_v, x_v, normed_v, q_v, k_v, v_v, context_v, log_v, middle_v, two_v, both_v, both_grad_v, hidden_v,
     low_v, mixed_v, kv_land, kv_v, key_grad_v, value_grad_v, start_v,
     mix_grad_v, gate_grad_v, out_grad_v, down_grad_v, gain_grad_v,
     mix_v, gate_v, out_v, down_v, gains_v, part_v, land_a, land_b, total_v) = scratch
    local, save, pair_sems, send_a, recv_a, send_b, recv_b, send_c, recv_c, send_d, recv_d = sems
    c = lax.axis_index("ctx")
    f = lax.axis_index("fsdp")
    odd = lax.rem(c, 2)
    rows = x_v.shape[0]
    units = down_v.shape[0]
    own_rows = pl.ds(pl.multiple_of(own_block(c, f) * rows, rows), rows)
    loads = Loads(local)
    saves = Loads(save)
    key_grad_v[...] = jnp.zeros_like(key_grad_v)
    value_grad_v[...] = jnp.zeros_like(value_grad_v)
    gain_grad_v[...] = jnp.zeros_like(gain_grad_v)
    if forward is None:
        x_own, normed, q, k, v, context, log, middle, normed_two, both = saved
        load_down = loads.start(w_down.at[layer], down_v)
        load_both = loads.start(both, both_v)
        load_gate = loads.start(w_gate.at[layer], gate_v)
        out_v[...] = jnp.zeros_like(out_v)
        later = [
            loads.start(src, dst)
            for src, dst in (
                (normed_two, two_v), (middle, middle_v), (w_gains.at[layer], gains_v),
                (w_out.at[layer], out_v.at[pl.ds(0, HEAD)]), (q, q_v), (k, k_v), (v, v_v),
                (context, context_v), (log, log_v), (normed, normed_v), (x_own, x_v),
            )
        ] + load_heads(loads, w_mix.at[layer], mix_v)
        load_down.wait()
        load_both.wait()
    else:
        later = []
        load_grad = loads.start(grad_own, grad_v.at[own_rows])
    if returning is not None:
        begin_old, begin_feed, begin_mix, begin_return, finish = returning
        begin_old()

    def feed(d):
        here = plane_rows(d, rows)
        hidden_grad = kernel_dot_nt(grad_v[here, :], down_v[...])
        gate = both_v[here, :units]
        up = both_v[here, units:]
        sig = jax.nn.sigmoid(gate)
        silu = gate * sig
        hidden_v[here, :] = (silu * up).astype(BF)
        both_grad_v[here, :units] = (hidden_grad * up * sig * (1.0 + gate * (1.0 - sig))).astype(BF)
        both_grad_v[here, units:] = (hidden_grad * silu).astype(BF)

    if forward is None:
        gather_rows(grad_v, rows, send_a, recv_a, feed, begun=True)
        load_gate.wait()
    else:

        def before():
            load_grad.wait()
            for h in range(2):
                begin_rows(grad_v, rows, send_a, recv_a, h)

        forward(before, lambda: gather_rows(grad_v, rows, send_a, recv_a, feed, begun=True))

    def spread(d):
        here = plane_rows(d, rows)
        part_v[here, :] = kernel_dot_nt(both_grad_v[here, :], gate_v[...]).astype(BF)

    def feed_weights():
        for one in later[:1]:
            one.wait()
        down_grad_v[...] = kernel_dot_tn(hidden_v[...], grad_v[...]).astype(BF)
        for part in range(2):
            gate_grad_v[part] = kernel_dot_tn(
                two_v[...], both_grad_v[:, part * units : (part + 1) * units]
            ).astype(BF)
        if returning is None:
            saves.start(down_grad_v, outs[4])
            saves.start(gate_grad_v, outs[2])
        else:
            begin_feed()

    def norm_grads(error, value, gain, row):
        factor = mean_square(value)
        shaped = error * gain
        common = jnp.mean(shaped * value, axis=-1, keepdims=True)
        gain_grad_v[row : row + 1, :] += jnp.sum(error * value * factor, axis=0, keepdims=True)
        return factor * shaped - value * (factor * factor * factor) * common

    half = rows // 2

    def middle_half(h):
        part = slice(h * half, (h + 1) * half)
        own_half = pl.ds(pl.multiple_of(own_block(c, f) * rows + h * half, half), half)
        if h == 0:
            for one in later[1:]:
                one.wait()
        middle_grad = norm_grads(total_v[part, :], middle_v[part, :], gains_v[1:2, :].astype(F32), 1)
        middle_grad = middle_grad + grad_v[own_half, :].astype(F32)
        middle_v[part, :] = middle_grad
        low_v[own_half, :] = middle_grad.astype(BF)
        begin_rows(low_v, rows, send_c, recv_c, h)

    scatter_sum(part_v, total_v, land_a, send_b, recv_b, spread, feed_weights, done=middle_half)
    scale = HEAD ** (-0.5)

    def attention(d):
        here = plane_rows(d, rows)
        context_grad = kernel_dot_nt(low_v[here, :], out_v[...])
        common = jnp.sum(context_grad * context_v[here, :].astype(F32), axis=-1, keepdims=True)
        context_grad = context_grad.astype(BF)
        queries = q_v[here, :]
        scores = kernel_dot_nt(queries, k_v[...]) * scale
        allowed = place_row[...] <= place_col[here, :]
        weights = jnp.exp(jnp.where(allowed, scores, masked_value) - log_v[here, 0:1])
        weight_grad = kernel_dot_nt(context_grad, v_v[...])
        score_grad = (weights * (weight_grad - common)).astype(BF)
        value_grad_v[...] += kernel_dot_tn(weights.astype(BF), context_grad)
        key_grad_v[...] += kernel_dot_tn(score_grad, queries)
        query_grad = kernel_dot(score_grad, k_v[...]) * scale
        mixed_v[here, :LANES] = (query_grad * cosine[here, :] - turn(query_grad) * sine[here, :]).astype(BF)

    gather_rows(low_v, rows, send_c, recv_c, attention, begun=True)
    key_grad = key_grad_v[...] * scale
    mixed_v[:, LANES : 2 * LANES] = (key_grad * cosine[...] - turn(key_grad) * sine[...]).astype(BF)
    mixed_v[:, 2 * LANES :] = value_grad_v[...].astype(BF)
    pair = {"ctx": c + 1 - 2 * odd}

    def pair_copy(part):
        return pltpu.make_async_remote_copy(
            mixed_v.at[:, pl.ds(part * LANES, LANES)], kv_land, pair_sems.at[0], pair_sems.at[1],
            device_id=pair, device_id_type=MESH,
        )

    pl.when(odd == 0)(pair_copy(2).start)
    pl.when(odd == 1)(pair_copy(1).start)

    def spread_two(d):
        here = plane_rows(d, rows)
        part_v[here, :] = kernel_dot(mixed_v[here, :], mix_v[...]).astype(BF)

    def mix_weights():
        out_grad_v[...] = kernel_dot_tn(context_v[...], low_v[...])[:HEAD].astype(BF)
        short = HEAD // 2
        columns = kernel_dot_tn(mixed_v[:, :LANES], normed_v[...])
        mix_grad_v[:short, :] = columns[:short].astype(BF)
        mix_grad_v[short:HEAD, :] = columns[SPAN : SPAN + short].astype(BF)
        pair_copy(1).wait_recv()
        mine = jnp.where(odd == 0, mixed_v[:, LANES : 2 * LANES].astype(F32), mixed_v[:, 2 * LANES :].astype(F32))
        kv_v[...] = (mine + kv_land[...].astype(F32)).astype(BF)
        columns = kernel_dot_tn(kv_v[...], normed_v[...])
        mix_grad_v[HEAD : HEAD + short, :] = columns[:short].astype(BF)
        mix_grad_v[HEAD + short :, :] = jnp.where(
            odd == 0, columns[SPAN : SPAN + short], columns[short:HEAD]
        ).astype(BF)
        if returning is None:
            saves.start(out_grad_v, outs[3])
            saves.start(mix_grad_v, outs[1])
        else:
            begin_mix()

    def start_half(h):
        part = slice(h * half, (h + 1) * half)
        start_grad = norm_grads(total_v[part, :], x_v[part, :].astype(F32), gains_v[0:1, :].astype(F32), 0)
        start_grad = start_grad + middle_v[part, :]
        start_v[part, :] = start_grad
        if hand_on is not None:
            hand_on(h, start_grad)

    scatter_sum(part_v, total_v, land_b, send_d, recv_d, spread_two, mix_weights,
                None if returning is None else begin_return, start_half)
    if returning is None:
        saves.start(start_v, outs[0])
        saves.start(gain_grad_v, outs[5])
    else:
        finish(gain_grad_v)
    pair_copy(1).wait_send()
    for one in saves.copies:
        one.wait()


def turn_kernel(*refs):
    (x_own, cotangent, inputs), refs = refs[:3], refs[3:]
    weights, refs = refs[:5], refs[5:]
    tables, refs = refs[:4], refs[4:]
    saved, refs = refs[:9], refs[9:]
    (results_o, starts_o), refs = refs[:2], refs[2:]
    finals, refs = refs[:5], refs[5:]
    (result_old, start_old, mix_old, gate_old, out_old, down_old), refs = refs[:6], refs[6:]
    ahead, refs = refs[:21], refs[21:]
    more, refs = refs[:15], refs[15:]
    own, refs = refs[:10], refs[10:]
    gain_old, *refs = refs
    ahead_sems, first_sems, second_sems = refs[:10], refs[10:21], refs[21:32]
    return_sems, swap_sems = refs[32:37], refs[37]
    (x_v, normed_v, q_v, k_v, v_v, context_v, log_v, middle_v, two_v, both_v, hidden_v, result_v,
     mix_v, gate_v, out_v, down_v, gains_v, part_v, land_a, land_b, total_v) = ahead
    grad_v, own_v, both_grad_v, low_v = more[:4]
    scratch = [
        grad_v, own_v, normed_v, q_v, k_v, v_v, context_v, log_v, middle_v, two_v, both_v, both_grad_v, hidden_v,
        low_v, *more[4:], mix_v, gate_v, out_v, down_v, gains_v, part_v, land_a, land_b, total_v,
    ]
    start_new = more[9]
    mix_new, gate_new, out_new, down_new, gain_new = more[10:]
    gain_v = own[8]
    s = lax.axis_index("section")
    c = lax.axis_index("ctx")
    f = lax.axis_index("fsdp")
    rows = own_v.shape[0]
    half = rows // 2
    first_row = own_block(c, f) * rows

    def meet():
        peers = [{"fsdp": lax.rem(f + k, 4)} for k in range(1, 4)]
        greet_more(peers + [{"section": 1 - s}, {"ctx": lax.rem(c + 2, 4)}])

    def forward(before, ending):
        forward_body(
            1, None, x_own, weights, tables, [None] * 9 + [result_old], ahead, ahead_sems, None, before, ending, meet
        )
        own_v[...] = x_v[pl.ds(pl.multiple_of(first_row, rows), rows), :]

    def hand_on(h, start_grad):
        grad_v[pl.ds(pl.multiple_of(first_row + h * half, half), half), :] = start_grad.astype(BF)
        begin_rows(grad_v, rows, second_sems[3], second_sems[4], h)

    backward_body(
        1, cotangent.at[s], weights, tables, None, (start_old, mix_old, gate_old, out_old, down_old, gain_old),
        scratch, first_sems, None, forward, hand_on,
    )
    begin_old, begin_feed, begin_mix, begin_return, steps_after, wait_all = returner(
        tuple(finals) + tuple(own), return_sems,
        gate_new, down_new, mix_new, out_new, gate_old, down_old, mix_old, out_old,
    )

    def swap_copy(src, dst, slot):
        return pltpu.make_async_remote_copy(
            src, dst, swap_sems.at[slot], swap_sems.at[2 + slot], device_id={"section": 1 - s}, device_id_type=MESH
        )

    def swap_rows(away, home, out, slot):
        swap_copy(away, out.at[s], slot).start()
        pltpu.make_async_copy(home, out.at[s], swap_sems.at[4 + slot]).start()

    result_new = x_own

    def finish(gain_grad_v):
        @pl.when(s == 0)
        def _():
            swap_rows(result_old, result_new, results_o, 0)
            swap_rows(start_old, start_new, starts_o, 1)

        @pl.when(s == 1)
        def _():
            swap_rows(result_new, result_old, results_o, 0)
            swap_rows(start_new, start_old, starts_o, 1)

        gain_v[0] = jnp.zeros(gain_v.shape[1:], F32)
        gain_v[0, 0:2, :] = gain_grad_v[...]
        gain_v[0, 2:4, :] = gain_old[...]
        steps_after()
        wait_all()
        for slot, out in enumerate((results_o, starts_o)):
            pltpu.make_async_copy(out.at[s], out.at[s], swap_sems.at[4 + slot]).wait()
            swap_copy(out.at[s], out.at[1 - s], slot).wait()

    backward_body(
        0, None, weights, tables, [inputs.at[s], *saved], None, scratch, second_sems,
        (begin_old, begin_feed, begin_mix, begin_return, finish),
    )


def link_sems():
    dma = pltpu.SemaphoreType.DMA
    return [dma((GATHER_SENDS,)), dma((GATHER_RECVS,)), dma((SCATTER_SENDS,)), dma((SCATTER_RECVS,))] * 2


def low(*shape):
    return (shape, BF)


def full(*shape):
    return (shape, F32)


def shapes(specs):
    return [jax.ShapeDtypeStruct(*one) for one in specs]


def rooms(specs):
    return [pltpu.VMEM(*one) for one in specs]


def signals(*counts):
    return [pltpu.SemaphoreType.DMA((count,)) for count in counts]


def forward_scratch(rows, width, units):
    length = 16 * rows
    return [low(length, width), low(length, width)] + [low(length, LANES)] * 4 + [
        full(length, LANES), full(rows, width), low(length, width), full(length, 2 * units), low(length, units),
        low(rows, width), low(3 * LANES, width), low(width, 2 * units), low(LANES, width), low(units, width),
        low(16, width), low(length, width), low(19, rows, width), low(19, rows, width), full(rows, width)]


def forward_kept(rows, width, units):
    length = 16 * rows
    return [low(length, width)] + [low(length, LANES)] * 4 + [
        full(length, LANES), full(rows, width), low(length, width), full(length, 2 * units), low(rows, width)]


ANYWHERE = pl.BlockSpec(memory_space=pl.ANY)
INSIDE = pl.BlockSpec(memory_space=pltpu.VMEM)


def forward_share_call(inputs, shards, gains, block_order):
    rows, width = inputs.shape[1:]
    length = 16 * rows
    depth = shards[0].shape[1]
    units = shards[2].shape[2] // 32
    frequency = np.zeros((2, SPAN), np.float32)
    frequency[:, : HEAD // 2] = np.float32(rope_base) ** (-(np.arange(HEAD // 2, dtype=np.float32) * 2.0 / HEAD))
    packing = [low(depth, shards[0].shape[2]), low(shards[0].shape[2], depth), low(depth, 2 * units), low(HEAD, width),
               low(units, width), low(16, depth)]
    kept = forward_kept(rows, width, units)
    weights = [low(2, 3 * HEAD, width), low(2, width, 2 * units), low(2, HEAD, width), low(2, units, width), low(2, 16, width)]
    tables = [full(length, LANES), full(length, LANES), ((length, 1), jnp.int32), ((1, length), jnp.int32)]
    return pl.pallas_call(
        forward_share_kernel,
        out_shape=shapes(kept + weights + tables),
        in_specs=[ANYWHERE] * 5 + [INSIDE] * 4,
        out_specs=[ANYWHERE] * 15 + [INSIDE] * 4,
        scratch_shapes=rooms(forward_scratch(rows, width, units) + packing) + signals(10, 10) + link_sems()
        + signals(9, 27, 26),
        compiler_params=pltpu.CompilerParams(collective_id=0, has_side_effects=True, vmem_limit_bytes=60 << 20),
    )(inputs, *shards, *gains, block_order, jnp.asarray(frequency.reshape(1, LANES)))


def backward_grads(width, units):
    return [low(2 * HEAD, width), low(2, width, units), low(HEAD, width), low(units, width), full(2, width)]


def turn_call(x_own, cotangent, inputs, weights, tables, saved):
    rows, width = x_own.shape
    length = 16 * rows
    depth = width // 4
    units = weights[3].shape[1]
    grads = backward_grads(width, units)
    more = [low(length, width), low(rows, width), low(length, 2 * units), low(length, width), low(length, 3 * LANES),
            low(length, LANES), low(length, LANES), full(length, LANES), full(length, LANES), full(rows, width)] + grads
    own = grads[:4] + grads[:4] + [full(5, 8, width), full(5, 8, width)]
    finals = [low(2, rows, width), full(2, rows, width), low(16 * 2 * HEAD, depth), low(2, depth, 16 * units),
              low(4 * HEAD, width), low(4 * units, width), full(8, width)]
    old = [low(rows, width), full(rows, width)] + grads[:4]
    return pl.pallas_call(
        turn_kernel,
        out_shape=shapes(finals + old),
        in_specs=[ANYWHERE] * 8 + [INSIDE] * 4 + [ANYWHERE] * 9,
        out_specs=[ANYWHERE] * 6 + [INSIDE] + [ANYWHERE] * 6,
        scratch_shapes=rooms(forward_scratch(rows, width, units) + more + own + grads[4:]) + signals(10, 10) + link_sems()
        + signals(20, 7, 2) + link_sems() + signals(20, 7, 2) + link_sems() + signals(5, 23, 23, 50, 40, 6),
        compiler_params=pltpu.CompilerParams(collective_id=1, has_side_effects=True, vmem_limit_bytes=60 << 20),
    )(x_own, cotangent, inputs, *weights, *tables, *saved)


def returner(refs, sems, gate_new, down_new, mix_new, out_new, gate_old, down_old, mix_old, out_old):
    (mix_out, gate_out, out_out, down_out, gain_out,
     mix_v, gate_v, out_v, down_v, mix_x, gate_x, out_x, down_x, gain_v, gain_x) = refs
    local, send, recv, line_send, line_recv = sems
    s = lax.axis_index("section")
    c = lax.axis_index("ctx")
    f = lax.axis_index("fsdp")
    other = {"section": 1 - s}
    units = down_v.shape[0]
    depth = gate_out.shape[1]
    inner = jnp.logical_and(c > 0, c < 3)
    above = jnp.minimum(c + 1, 3)
    below = jnp.maximum(c - 1, 0)

    def copy(src, dst, slot, arrival, peer):
        return pltpu.make_async_remote_copy(
            src, dst, send.at[slot], recv.at[arrival], device_id=peer, device_id_type=MESH
        )

    def owner_part(owner):
        return pl.ds(pl.multiple_of(owner * depth, depth), depth)

    def cross_parts(away, theirs, first):
        for k in range(4):
            owner = lax.rem(f + k, 4)
            part = owner_part(owner)
            copy(away.at[:, part], theirs.at[:, part], first + k, first + owner, other).start()

    def cross_whole(away, theirs, slot):
        copy(away, theirs, slot, slot, other).start()

    def home(src, dst, k):
        pltpu.make_async_copy(src, dst, local.at[k]).start()

    def begin_old():
        @pl.when(s == 0)
        def _():
            cross_whole(down_old, down_x, 8)
            cross_parts(gate_old, gate_x, 0)
            cross_whole(out_old, out_x, 9)
            cross_parts(mix_old, mix_x, 4)

        @pl.when(s == 1)
        def _():
            home(down_old, down_v, 0)
            home(gate_old, gate_v, 1)
            home(out_old, out_v, 2)
            home(mix_old, mix_v, 3)

    def begin_feed():
        @pl.when(s == 0)
        def _():
            home(down_new, down_v, 0)
            home(gate_new, gate_v, 1)

        @pl.when(s == 1)
        def _():
            cross_whole(down_new, down_x, 8)
            cross_parts(gate_new, gate_x, 0)

    def begin_mix():
        @pl.when(s == 0)
        def _():
            home(out_new, out_v, 2)
            home(mix_new, mix_v, 3)

        @pl.when(s == 1)
        def _():
            cross_whole(out_new, out_x, 9)
            cross_parts(mix_new, mix_x, 4)

    def home_wait(k, dst):
        pltpu.make_async_copy(dst, dst, local.at[k]).wait()

    def arrived(ref, arrival):
        copy(ref, ref, 0, arrival, other).wait_recv()

    def gate_at(cc, ff):
        return gate_out.at[:, :, pl.ds(pl.multiple_of((ff * 4 + cc) * units, units), units)]

    def mix_at(cc, ff):
        return mix_out.at[pl.ds(pl.multiple_of((ff * 4 + cc) * 2 * HEAD, 2 * HEAD), 2 * HEAD)]

    def rows_at(ref, cc, count):
        return ref.at[pl.ds(pl.multiple_of(cc * count, count), count)]

    def out_at(cc, ff):
        return rows_at(out_out, cc, HEAD)

    def down_at(cc, ff):
        return rows_at(down_out, cc, units)

    origins = [lax.rem(f + k, 4) for k in (0, 3, 2, 1)]
    items = [(down_at, f)] + [(gate_at, one) for one in origins] + [(out_at, f)] + [(mix_at, one) for one in origins]

    def line(index, cc, slot, target):
        place, origin = items[index]
        return pltpu.make_async_remote_copy(
            place(cc, origin), place(cc, origin), line_send.at[slot], line_recv.at[cc * 10 + index],
            device_id={"ctx": target}, device_id_type=MESH,
        )

    def start_line(index):
        pl.when(c < 3)(line(index, c, index, above).start)
        pl.when(c > 0)(line(index, c, 10 + index, below).start)

    def fold(mine, theirs, arrival):
        arrived(theirs, arrival)
        mine[...] = (mine[...].astype(F32) + theirs[...].astype(F32)).astype(BF)

    def keep(src, dst):
        one = pltpu.make_async_copy(src, dst, local.at[4])
        one.start()
        one.wait()

    def whole_item(k, mine, theirs, arrival, place, index):
        home_wait(k, mine)
        fold(mine, theirs, arrival)
        keep(mine, place(c, f))
        start_line(index)

    def to_owner(k, mine, theirs, place, arrival_x, arrival_y, slot, index):
        owner = lax.rem(f + k, 4)
        rows = owner_part(owner)
        fold(mine.at[:, rows], theirs.at[:, rows], arrival_x + owner)
        if k:
            copy(mine.at[:, rows], place(c, f), slot + k, arrival_y + f, {"fsdp": owner}).start()
        else:
            keep(mine.at[:, rows], place(c, f))
            start_line(index)

    def from_owner(k, place, arrival, index):
        arrived(place(c, origins[k]), arrival + origins[k])
        start_line(index)

    gain_targets = [other, {"fsdp": f + 1 - 2 * lax.rem(f, 2)}, {"fsdp": f + 2 - 4 * (f // 2)},
                    {"ctx": c + 1 - 2 * lax.rem(c, 2)}, {"ctx": lax.rem(c + 2, 4)}]

    def gain_copy(k):
        return copy(gain_v.at[k], gain_x.at[k], 18 + k, 18 + k, gain_targets[k])

    def gain_sum(k):
        gain_copy(k).wait_recv()
        if k < 4:
            gain_v[k + 1] = gain_v[k] + gain_x[k]
            gain_copy(k + 1).start()
        else:
            gain_out[...] = gain_v[k] + gain_x[k]

    order = near_order(c)

    def onward(index, step):
        d = order[step]
        return line(index, d, 20 + (step - 1) * 10 + index, jnp.where(d < c, above, below))

    def pass_on(index, step):
        one = onward(index, step)
        one.wait_recv()
        pl.when(inner)(one.start)

    def near(index):
        pass_on(index, 1)
        pl.when(inner)(lambda: pass_on(index, 2))

    def far(index):
        pl.when(jnp.logical_not(inner))(lambda: pass_on(index, 2))
        pass_on(index, 3)

    def gate_first():
        home_wait(1, gate_v)
        to_owner(0, gate_v, gate_x, gate_at, 0, 10, 10, 1)

    def gate_rest(k):
        return lambda: to_owner(k, gate_v, gate_x, gate_at, 0, 10, 10, 1)

    def gate_from(k):
        return lambda: from_owner(k, gate_at, 10, 1 + k)

    def mix_first():
        home_wait(3, mix_v)
        to_owner(0, mix_v, mix_x, mix_at, 4, 14, 14, 6)

    def mix_rest(k):
        return lambda: to_owner(k, mix_v, mix_x, mix_at, 4, 14, 14, 6)

    def mix_from(k):
        return lambda: from_owner(k, mix_at, 14, 6 + k)

    def down_first():
        whole_item(0, down_v, down_x, 8, down_at, 0)

    def out_first():
        whole_item(2, out_v, out_x, 9, out_at, 5)

    def passing(*steps):
        return [functools.partial(near if sign > 0 else far, abs(sign) - 1) for sign in steps]

    after = [
        passing(1) + [gate_from(1), gate_from(2), gate_from(3), out_first, mix_first, mix_rest(1), mix_rest(2), mix_rest(3)],
        passing(2, -1, 3, -2, 4) + [mix_from(1), mix_from(2), mix_from(3)],
        passing(-3, 5, -4, 6, -5, 7),
        passing(-6, 8, -7, 9),
        passing(-8, 10, -9, -10),
    ]
    def begin_return():
        down_first()
        gate_first()
        for k in range(1, 4):
            gate_rest(k)()

    def steps_after():
        gain_copy(0).start()
        for k, steps in enumerate(after):
            for step in steps:
                step()
            gain_sum(k)

    def wait_all():
        for index in range(10):
            pl.when(c < 3)(line(index, c, index, above).wait_send)
            pl.when(c > 0)(line(index, c, 10 + index, below).wait_send)
            for step in range(1, 4):
                pl.when(inner)(onward(index, step).wait_send)
        for k in range(5):
            gain_copy(k).wait_send()
        for k in range(4):
            gate_part = gate_x.at[:, pl.ds(k * depth, depth)]
            mix_part = mix_x.at[:, pl.ds(k * depth, depth)]
            for slot in (k, 10 + k) if k else (k,):
                copy(gate_part, gate_part, slot, 0, other).wait_send()
                copy(mix_part, mix_part, 4 + slot, 0, other).wait_send()
        copy(down_x, down_x, 8, 0, other).wait_send()
        copy(out_x, out_x, 9, 0, other).wait_send()

    return begin_old, begin_feed, begin_mix, begin_return, steps_after, wait_all


def widen_kernel(mix, gate, out, down, gains, results, starts,
                 mix_f, gate_f, out_f, down_f, attention_f, feed_f, results_f, starts_f, places, turned, rest):
    step = pl.program_id(0)
    rows = gate.shape[1]
    four = 4 * HEAD
    width = 4 * four

    @pl.when(step == 0)
    def _():
        s = lax.axis_index("section")
        f = lax.axis_index("fsdp")
        depth = attention_f.shape[1]
        columns = pl.ds(pl.multiple_of(f * depth, depth), depth)
        attention_f[...] = gains[pl.ds(2 * s, 1), columns]
        feed_f[...] = gains[pl.ds(2 * s + 1, 1), columns]
        results_f[...] = results[...]
        starts_f[...] = starts[...]
        source = lax.broadcasted_iota(jnp.int32, (2 * four, 2 * four), 0)
        column = lax.broadcasted_iota(jnp.int32, (2 * four, 2 * four), 1)
        query = (column // HEAD) * 2 * HEAD + lax.rem(column, HEAD)
        beyond = column - four
        kind = beyond // (2 * HEAD)
        beyond = beyond - kind * 2 * HEAD
        other = (2 * (beyond // HEAD) + kind) * 2 * HEAD + HEAD + lax.rem(beyond, HEAD)
        places[...] = jnp.where(source == jnp.where(column < four, query, other), 1.0, 0.0).astype(BF)

    @pl.when(step < 4)
    def _():
        group = kernel_dot_tn(mix[...], places[...])
        turned[:, pl.ds(pl.multiple_of(step * four, four), four)] = group[:, :four]
        rest[step] = group[:, four:]

    @pl.when(step >= 4)
    def _():
        here = pl.ds(pl.multiple_of((step - 4) * 2 * rows, 2 * rows), 2 * rows)
        mix_f[:, :width] = turned[here, :]
        for g in range(2):
            for kind in range(2):
                at = width + kind * 2 * four + g * four
                part = slice(kind * 2 * HEAD, (kind + 1) * 2 * HEAD)
                mix_f[:, at : at + four] = jnp.concatenate([rest[2 * g + k, here, part] for k in range(2)], axis=1)

    half = gate.shape[2]
    gate_f[:, :half] = gate[0].astype(F32)
    gate_f[:, half:] = gate[1].astype(F32)
    out_f[...] = out[...].astype(F32)
    down_f[...] = down[...].astype(F32)


def widen_call(results, starts, mix, gate, out, down, gains):
    steps = 8
    depth = gate.shape[1]
    width = out.shape[1]
    rows = depth // steps

    def whole(array):
        return pl.BlockSpec(array.shape, lambda i: (0,) * array.ndim)

    down_rows = down.shape[0] // steps
    return pl.pallas_call(
        widen_kernel,
        grid=(steps,),
        out_shape=shapes([
            full(depth, 2 * width), full(depth, 2 * gate.shape[2]), full(*out.shape), full(*down.shape),
            full(1, depth), full(1, depth), low(*results.shape), full(*starts.shape),
        ]),
        in_specs=[
            pl.BlockSpec((8 * HEAD, depth), lambda i: (jnp.minimum(i, 3), 0)),
            pl.BlockSpec((2, rows, gate.shape[2]), lambda i: (0, i, 0)),
            pl.BlockSpec((rows, width), lambda i: (i, 0)),
            pl.BlockSpec((down_rows, width), lambda i: (i, 0)),
            whole(gains),
            whole(results),
            whole(starts),
        ],
        out_specs=[
            pl.BlockSpec((2 * rows, 2 * width), lambda i: (jnp.maximum(i - 4, 0), 0)),
            pl.BlockSpec((rows, 2 * gate.shape[2]), lambda i: (i, 0)),
            pl.BlockSpec((rows, width), lambda i: (i, 0)),
            pl.BlockSpec((down_rows, width), lambda i: (i, 0)),
            pl.BlockSpec((1, depth), lambda i: (0, 0)),
            pl.BlockSpec((1, depth), lambda i: (0, 0)),
            whole(results),
            whole(starts),
        ],
        scratch_shapes=rooms([low(8 * HEAD, 8 * HEAD), full(depth, width), full(4, depth, 4 * HEAD)]),
        compiler_params=pltpu.CompilerParams(vmem_limit_bytes=60 << 20),
    )(mix, gate, out, down, gains, results, starts)


def on_line():
    return lax.axis_size("ctx") == 4 and lax.axis_size("fsdp") == 4


def gather(own):
    return lax.all_gather(own, ("ctx", "fsdp"), axis=0, tiled=True)


def scatter(part):
    return lax.psum_scatter(part, ("ctx", "fsdp"), scatter_dimension=0, tiled=True)


def spread_halves(columns):
    halves = columns.reshape(columns.shape[:-1] + (2, HEAD // 2))
    halves = jnp.pad(halves, [(0, 0)] * (halves.ndim - 1) + [(0, SPAN - HEAD // 2)])
    return halves.reshape(columns.shape[:-1] + (LANES,))


def join_halves(columns):
    halves = columns.reshape(columns.shape[:-1] + (2, SPAN))[..., : HEAD // 2]
    return halves.reshape(columns.shape[:-1] + (HEAD,))


def angle_tables(positions):
    frequency = rope_base ** (-(jnp.arange(HEAD // 2, dtype=F32) * 2.0 / HEAD))
    frequency = jnp.pad(frequency, (0, SPAN - HEAD // 2))
    angles = positions.astype(F32)[:, None] * frequency[None, :]
    cosine = jnp.cos(angles)
    sine = jnp.sin(angles)
    return jnp.concatenate([cosine, cosine], axis=1), jnp.concatenate([-sine, sine], axis=1)


def rotate(values, cosine, sine):
    return values * cosine + jnp.roll(values, SPAN, axis=1) * sine


def rotate_back(grads, cosine, sine):
    return grads * cosine - jnp.roll(grads, SPAN, axis=1) * sine


def norm_rows(values):
    return lax.rsqrt(jnp.mean(values * values, axis=-1, keepdims=True) + norm_eps)


def norm_back(grad_out, values, factor, gain):
    shaped = grad_out * gain
    common = jnp.mean(shaped * values, axis=-1, keepdims=True)
    grad_in = factor * shaped - values * (factor * factor * factor) * common
    return grad_in, jnp.sum(grad_out * values * factor, axis=0)


def dot(left, right):
    return jnp.dot(left, right, preferred_element_type=F32)


def dot_nt(left, right):
    return lax.dot_general(left, right, (((1,), (1,)), ((), ())), preferred_element_type=F32)


def dot_tn(left, right):
    return lax.dot_general(left, right, (((0,), (0,)), ((), ())), preferred_element_type=F32)


class Plan:
    def __init__(self, width, hidden_units):
        self.c = lax.axis_index("ctx")
        self.f = lax.axis_index("fsdp")
        self.C = lax.axis_size("ctx")
        self.F = lax.axis_size("fsdp")
        self.heads = width // HEAD
        self.ratio = self.heads // KV_HEADS
        self.heads_f = self.heads // self.F
        self.groups_f = KV_HEADS // self.F
        self.share = self.C // self.heads_f
        self.units = hidden_units // (self.F * self.C)
        self.local_head = self.c // self.share
        self.part = self.c % self.share


def pick(array, index, axis):
    return lax.dynamic_index_in_dim(array, index, axis, keepdims=False)


def pack_weights(plan, mix, gate_up):
    depth = mix.shape[0]
    width = plan.heads * HEAD
    kv_width = KV_HEADS * HEAD
    F = plan.F
    queries = pick(mix[:, :width].reshape(depth, F, plan.heads_f, HEAD), plan.local_head, 2)
    group = plan.local_head // plan.ratio
    keys = pick(mix[:, width : width + kv_width].reshape(depth, F, plan.groups_f, HEAD), group, 2)
    values = pick(mix[:, width + kv_width :].reshape(depth, F, plan.groups_f, HEAD), group, 2)
    values = jnp.pad(values, ((0, 0), (0, 0), (0, LANES - HEAD)))
    half = gate_up.shape[1] // 2
    gate = pick(gate_up[:, :half].reshape(depth, F, plan.C, plan.units), plan.c, 2)
    up = pick(gate_up[:, half:].reshape(depth, F, plan.C, plan.units), plan.c, 2)
    packed = jnp.concatenate([spread_halves(queries), spread_halves(keys), values, gate, up], axis=2)
    return jnp.swapaxes(packed, 0, 1)


def attend(plan, q_part, k, v, positions, part_positions):
    scores = dot_nt(q_part, k) * HEAD ** (-0.5)
    allowed = positions[None, :] <= part_positions[:, None]
    scores = jnp.where(allowed, scores, masked_value)
    top = jnp.max(scores, axis=-1, keepdims=True)
    weights = jnp.exp(scores - top)
    total = jnp.sum(weights, axis=-1, keepdims=True)
    context = dot((weights / total).astype(BF), v)
    return context.astype(BF), top + jnp.log(total)


def attend_back(q_part, k, v, context_grad, context, log_total, positions, part_positions):
    scale = HEAD ** (-0.5)
    common = jnp.sum(context_grad.astype(F32) * context.astype(F32), axis=-1, keepdims=True)
    allowed = positions[None, :] <= part_positions[:, None]
    scores = dot_nt(q_part, k) * scale
    weights = jnp.exp(jnp.where(allowed, scores, masked_value) - log_total)
    weight_grad = dot_nt(context_grad, v)
    score_grad = (weights * (weight_grad - common)).astype(BF)
    value_grad = dot_tn(weights.astype(BF), context_grad)
    key_grad = dot_tn(score_grad, q_part) * scale
    query_grad = dot(score_grad, k) * scale
    return query_grad, key_grad, value_grad


def forward_layer(plan, x_own, weights, gains, positions, part_positions, tables):
    mix_cut, gate_cut, out, down = weights
    cosine, sine = tables
    length = positions.shape[0]
    x_all = gather(x_own)
    x32 = x_all.astype(F32)
    factor = norm_rows(x32)
    normed = (x32 * factor * gains[0]).astype(BF)
    mixed = dot(normed, mix_cut)
    q = rotate(mixed[:, :LANES], cosine, sine).astype(BF)
    k = rotate(mixed[:, LANES : 2 * LANES], cosine, sine).astype(BF)
    v = mixed[:, 2 * LANES :].astype(BF)
    rows = length // plan.share
    start = plan.part * rows
    q_part = lax.dynamic_slice_in_dim(q, start, rows, 0)
    context, log_total = attend(plan, q_part, k, v, positions, part_positions)
    partial = dot(context[:, :HEAD], out).astype(BF)
    if plan.share > 1:
        partial = lax.dynamic_update_slice_in_dim(
            jnp.zeros((length, partial.shape[1]), BF), partial, start, 0
        )
    middle = x_own.astype(F32) + scatter(partial)
    factor_two = norm_rows(middle)
    normed_two = gather((middle * factor_two * gains[1]).astype(BF))
    both = dot(normed_two, gate_cut)
    hidden = (jax.nn.silu(both[:, : plan.units]) * both[:, plan.units :]).astype(BF)
    result = middle + scatter(dot(hidden, down).astype(BF))
    kept = (x_own, normed, q_part, k, v, context, log_total, middle, normed_two, both, hidden)
    return result.astype(BF), kept


def backward_layer(plan, grad_own, weights, gains, kept, positions, part_positions, tables, part_tables):
    mix_cut, gate_cut, out, down = weights
    x_own, normed, q_part, k, v, context, log_total, middle, normed_two, both, hidden = kept
    length = positions.shape[0]
    rows = length // plan.share
    start = plan.part * rows
    grad_all = gather(grad_own)
    hidden_grad = dot_nt(grad_all, down)
    gate = both[:, : plan.units]
    up = both[:, plan.units :]
    sig = jax.nn.sigmoid(gate)
    gate_grad = hidden_grad * up * sig * (1.0 + gate * (1.0 - sig))
    up_grad = hidden_grad * gate * sig
    both_grad = jnp.concatenate([gate_grad, up_grad], axis=1).astype(BF)
    normed_two_grad = scatter(dot_nt(both_grad, gate_cut).astype(BF))
    middle_grad, feed_gain_grad = norm_back(normed_two_grad, middle, norm_rows(middle), gains[1])
    middle_grad = middle_grad + grad_own.astype(F32)
    middle_low = gather(middle_grad.astype(BF))
    middle_part = lax.dynamic_slice_in_dim(middle_low, start, rows, 0)
    context_grad = jnp.pad(dot_nt(middle_part, out), ((0, 0), (0, LANES - HEAD))).astype(BF)
    query_grad, key_grad, value_grad = attend_back(
        q_part, k, v, context_grad, context, log_total, positions, part_positions
    )
    query_grad = rotate_back(query_grad, *part_tables).astype(BF)
    if plan.share > 1:
        query_grad = lax.dynamic_update_slice_in_dim(
            jnp.zeros((length, LANES), BF), query_grad, start, 0
        )
    key_grad = rotate_back(key_grad, *tables).astype(BF)
    mixed_grad = jnp.concatenate([query_grad, key_grad, value_grad.astype(BF)], axis=1)
    normed_grad = scatter(dot_nt(mixed_grad, mix_cut).astype(BF))
    x32 = x_own.astype(F32)
    start_grad, attention_gain_grad = norm_back(normed_grad, x32, norm_rows(x32), gains[0])
    start_grad = start_grad + middle_grad
    mix_grad = jnp.stack(
        [dot_tn(normed, part).astype(BF) for part in (query_grad, key_grad, value_grad.astype(BF))]
    )
    gate_cut_grad = jnp.stack(
        [dot_tn(normed_two, part.astype(BF)).astype(BF) for part in (gate_grad, up_grad)]
    )
    out_grad = dot_tn(context, middle_part).astype(BF)[:HEAD]
    down_grad = dot_tn(hidden, grad_all).astype(BF)
    return start_grad, (mix_grad, gate_cut_grad, out_grad, down_grad), jnp.stack([attention_gain_grad, feed_gain_grad])


def swap_sections(array):
    return lax.ppermute(array, "section", [(0, 1), (1, 0)])


def by_layer_of(section, own, other):
    first = section == 0
    return jnp.where(first, own, other), jnp.where(first, other, own)


def shared_weights(plan, section, attention_gain, query_key_value, output_weight, feed_gain, gate_up, down_weight):
    depth = query_key_value.shape[1]
    width = depth * plan.F
    gains = lax.all_gather(
        jnp.stack([attention_gain[0], feed_gain[0]]), ("section", "fsdp"), axis=0, tiled=False
    )
    gains = gains.reshape(2, plan.F, 2, depth)
    gains = jnp.swapaxes(gains, 1, 2).reshape(2, 2, width).astype(F32)
    packed = pack_weights(plan, query_key_value[0], gate_up[0])
    own_cut = lax.all_to_all(packed, "fsdp", 0, 0).reshape(width, -1)
    own_out = lax.dynamic_slice_in_dim(output_weight[0], plan.local_head * HEAD, HEAD, 0)
    own_down = lax.dynamic_slice_in_dim(down_weight[0], plan.c * plan.units, plan.units, 0)
    cuts = by_layer_of(section, own_cut, swap_sections(own_cut))
    outs = by_layer_of(section, own_out, swap_sections(own_out))
    downs = by_layer_of(section, own_down, swap_sections(own_down))
    weights = [(cuts[s][:, : 3 * LANES], cuts[s][:, 3 * LANES :], outs[s], downs[s]) for s in range(2)]
    return weights, gains


def own_gain_sums(plan, section, gain_sum, depth):
    gain_sum = lax.dynamic_slice_in_dim(gain_sum, 2 * section, 2, 0)
    return lax.dynamic_slice_in_dim(gain_sum, plan.f * depth, depth, 1)


def returned_grads(plan, section, weight_grads, gain_grads, depth):
    C, F = plan.C, plan.F
    gain_sum = jnp.concatenate([gain_grads[0], gain_grads[1]])

    def collected(index):
        first, second = weight_grads[0][index], weight_grads[1][index]
        own = jnp.where(section == 0, first, second)
        away = jnp.where(section == 0, second, first)
        return (own.astype(F32) + swap_sections(away).astype(F32)).astype(BF)

    cut_grad = jnp.concatenate(list(collected(0)) + list(collected(1)), axis=1)
    cut_grad = lax.all_to_all(cut_grad.reshape(F, depth, -1), "fsdp", 0, 0)
    cut_grad = lax.all_gather(cut_grad, "ctx", axis=0, tiled=False)
    out_grad = lax.all_gather(collected(2), "ctx", axis=0, tiled=False)
    down_grad = lax.all_gather(collected(3), "ctx", axis=0, tiled=True).astype(F32)

    def heads_of(columns, count):
        folded = columns.astype(F32).reshape(count, C // count, F, depth, columns.shape[-1]).sum(axis=1)
        return jnp.transpose(folded, (2, 1, 0, 3))

    q_grad = join_halves(heads_of(cut_grad[..., :LANES], plan.heads_f)).reshape(depth, -1)
    k_grad = join_halves(heads_of(cut_grad[..., LANES : 2 * LANES], plan.groups_f)).reshape(depth, -1)
    v_grad = heads_of(cut_grad[..., 2 * LANES : 3 * LANES], plan.groups_f)[..., :HEAD].reshape(depth, -1)
    mix_grad = jnp.concatenate([q_grad, k_grad, v_grad], axis=1)
    both = jnp.transpose(cut_grad[..., 3 * LANES :], (2, 1, 0, 3)).astype(F32)
    gate_up_grad = jnp.concatenate(
        [both[..., : plan.units].reshape(depth, -1), both[..., plan.units :].reshape(depth, -1)], axis=1
    )
    out_grad = out_grad.astype(F32).reshape(plan.heads_f, plan.share, HEAD, depth * F).sum(axis=1).reshape(-1, depth * F)

    gain_sum = lax.psum(gain_sum, ("section", "ctx", "fsdp"))
    return mix_grad, gate_up_grad, out_grad, down_grad, own_gain_sums(plan, section, gain_sum, depth)


def on_device(
    inputs, cotangent, attention_gain, query_key_value, output_weight, feed_gain, gate_up, down_weight, block_order
):
    section = lax.axis_index("section")
    width = inputs.shape[2]
    hidden_units = down_weight.shape[1] * lax.axis_size("fsdp")
    plan = Plan(width, hidden_units)
    rows = inputs.shape[1]
    C, F = plan.C, plan.F
    length = rows * C * F
    depth = query_key_value.shape[1]

    def by_layer(own, other):
        first = section == 0
        return jnp.where(first, own, other), jnp.where(first, other, own)

    results = []
    input_grads = [None, None]
    weight_grads = [None, None]
    gain_grads = [None, None]
    kept = []
    if on_line():
        shards = (query_key_value, output_weight, gate_up, down_weight)
        first = forward_share_call(inputs, shards, (attention_gain, feed_gain), block_order)
        weights = first[10:15]
        common = first[15:]
        last = turn_call(first[9], cotangent, inputs, weights, common, first[:9])[:7]
        (mix_grad, gate_up_grad, out_grad, down_grad, attention_gain_grad, feed_gain_grad,
         section_outputs, section_input_grads) = widen_call(*last)
    else:
        order = pick(block_order, section, 0)
        positions = (order[:, None] * rows + jnp.arange(rows, dtype=jnp.int32)[None, :]).reshape(length)
        part_rows = length // plan.share
        part_positions = lax.dynamic_slice_in_dim(positions, plan.part * part_rows, part_rows, 0)
        tables = angle_tables(positions)
        part_tables = angle_tables(part_positions)

        x = pick(inputs, section, 0)
        grad = pick(cotangent, section, 0)
        weights, gains = shared_weights(
            plan, section, attention_gain, query_key_value, output_weight, feed_gain, gate_up, down_weight
        )
        for s in range(2):
            x, keep = forward_layer(plan, x, weights[s], gains[s], positions, part_positions, tables)
            kept.append(keep)
            results.append(x)
        for s in (1, 0):
            input_grads[s], weight_grads[s], gain_grads[s] = backward_layer(
                plan, grad, weights[s], gains[s], kept[s], positions, part_positions, tables, part_tables
            )
            grad = input_grads[s].astype(BF)
        def mine_and_theirs(first, second):
            return jnp.where(section == 0, first, second), jnp.where(section == 0, second, first)

        def by_batch(first, second):
            own, away = mine_and_theirs(first, second)
            return jnp.stack(by_layer(own, swap_sections(away)))

        section_outputs = by_batch(*results)
        section_input_grads = by_batch(*input_grads)

        shard_grads = returned_grads(plan, section, weight_grads, gain_grads, depth)
        mix_grad, gate_up_grad, out_grad, down_grad, gain_sum = shard_grads
        attention_gain_grad, feed_gain_grad = gain_sum[0][None], gain_sum[1][None]

    return (
        section_outputs[None],
        section_input_grads[None],
        attention_gain_grad,
        mix_grad[None],
        out_grad[None],
        feed_gain_grad,
        gate_up_grad[None],
        down_grad[None],
    )


def solution(mesh):
    placed = (
        P(None, ("ctx", "fsdp"), None),
        P(None, ("ctx", "fsdp"), None),
        P("section", "fsdp"),
        P("section", "fsdp", None),
        P("section", "fsdp", None),
        P("section", "fsdp"),
        P("section", "fsdp", None),
        P("section", "fsdp", None),
        P(),
    )
    return jax.shard_map(
        on_device,
        mesh=mesh,
        in_specs=placed,
        out_specs=(
            P("section", None, ("ctx", "fsdp"), None),
            P("section", None, ("ctx", "fsdp"), None),
            P("section", "fsdp"),
            P("section", "fsdp", None),
            P("section", "fsdp", None),
            P("section", "fsdp"),
            P("section", "fsdp", None),
            P("section", "fsdp", None),
        ),
        check_vma=False,
    )
```

```python
import functools

import jax
import jax.numpy as jnp
import numpy as np
from jax import lax
from jax.experimental import pallas as pl
from jax.experimental.pallas import tpu as pltpu
from jax.sharding import PartitionSpec as P

KV_HEADS = 8
HEAD = 96
LANES = 128
SPAN = 64
norm_eps = 1e-05
rope_base = 100000.0
masked_value = -1e30
BF = jnp.bfloat16
F32 = jnp.float32

MESH = pl.DeviceIdType.MESH


def greet():
    c = lax.axis_index("ctx")
    f = lax.axis_index("fsdp")
    barrier = pltpu.get_barrier_semaphore()
    inner = jnp.logical_and(c > 0, c < 3)
    for peer in (f + 2 - 4 * (f // 2), f + 1 - 2 * lax.rem(f, 2)):
        pl.semaphore_signal(barrier, inc=1, device_id={"fsdp": peer}, device_id_type=MESH)
    pl.semaphore_signal(barrier, inc=1, device_id={"ctx": lax.rem(c + 2, 4)}, device_id_type=MESH)

    @pl.when(c < 3)
    def _():
        pl.semaphore_signal(barrier, inc=1, device_id={"ctx": c + 1}, device_id_type=MESH)

    @pl.when(c > 0)
    def _():
        pl.semaphore_signal(barrier, inc=1, device_id={"ctx": c - 1}, device_id_type=MESH)

    @pl.when(inner)
    def _():
        pl.semaphore_wait(barrier, 5)

    @pl.when(jnp.logical_not(inner))
    def _():
        pl.semaphore_wait(barrier, 4)


def near_order(c):
    low = c < 2
    return [c, c + 1 - 2 * lax.rem(c, 2), jnp.where(low, 2, 1), jnp.where(low, 3, 0)]


def own_block(c, f):
    return c * 4 + lax.rem(f, 2) * 2 + f // 2


def begin_rows(whole, rows, send, recv, h):
    c = lax.axis_index("ctx")
    f = lax.axis_index("fsdp")
    half = rows // 2
    mine = whole.at[pl.ds(pl.multiple_of(own_block(c, f) * rows + h * half, half), half)]

    def copy(slot, arrival, peer):
        return pltpu.make_async_remote_copy(
            mine, mine, send.at[slot], recv.at[arrival], device_id=peer, device_id_type=MESH
        )

    pl.when(c < 3)(copy(0, 2 * c + h, {"ctx": jnp.minimum(c + 1, 3)}).start)
    pl.when(c > 0)(copy(1, 2 * c + h, {"ctx": jnp.maximum(c - 1, 0)}).start)
    copy(3, 8 + c, {"fsdp": f + 2 - 4 * (f // 2)}).start()


def gather_rows(whole, rows, send, recv, ready=None, started=None, begun=False):
    c = lax.axis_index("ctx")
    f = lax.axis_index("fsdp")
    y = f // 2
    lane = lax.rem(f, 2)
    inner = jnp.logical_and(c > 0, c < 3)
    outer = jnp.logical_not(inner)
    order = near_order(c)
    pair = order[1]
    half = rows // 2
    to_across = {"fsdp": f + 2 - 4 * y}
    to_twin = {"fsdp": f + 1 - 2 * lane}
    to_pair = {"ctx": pair}

    def at(d, k, yy, h):
        return whole.at[pl.ds(pl.multiple_of((d * 4 + k * 2 + yy) * rows + h * half, half), half)]

    def block(d, k, yy):
        return whole.at[pl.ds(pl.multiple_of((d * 4 + k * 2 + yy) * rows, rows), rows)]

    def two(d, k):
        return whole.at[pl.ds(pl.multiple_of((d * 4 + k * 2) * rows, rows), 2 * rows)]

    def copy(src, slot, arrival, peer):
        return pltpu.make_async_remote_copy(
            src, src, send.at[slot], recv.at[arrival], device_id=peer, device_id_type=MESH
        )

    def go(src, slot, arrival, peer, when=None):
        one = copy(src, slot, arrival, peer)
        if when is None:
            one.start()
        else:
            pl.when(when)(one.start)

    def arrived(ref, arrival):
        copy(ref, 0, arrival, to_twin).wait_recv()

    def gone(count, slot):
        copy(whole.at[pl.ds(0, count * half)], slot, 0, to_twin).wait_send()

    if not begun:
        for h in range(2):
            begin_rows(whole, rows, send, recv, h)
    if started is not None:
        started()

    events = [
        (pair, 0),
        (jnp.where(inner, order[2], pair), jnp.where(inner, 0, 1)),
        (jnp.where(inner, pair, order[2]), jnp.where(inner, 1, 0)),
        (order[2], 1),
        (order[3], 0),
        (order[3], 1),
    ]

    def along(index):
        d, h = events[index]
        piece = at(d, lane, y, h)
        arrived(piece, 2 * d + h)
        go(piece, 2, 2 * d + h, {"ctx": jnp.where(d < c, c + 1, c - 1)}, inner)
        go(piece, 3, 8 + d, to_across, jnp.logical_or(d != pair, h == 0) if index in (1, 2) else None)

    def complete(d):
        arrived(two(d, 1 - lane), 13 + d)
        if ready is not None:
            ready(d)

    def pair_half(when):
        go(at(c, lane, 1 - y, 1), 4, 12, to_pair, when)

    along(0)
    along(1)
    along(2)
    arrived(block(c, lane, 1 - y), 8 + c)
    pair_half(outer)
    go(two(c, lane), 5, 13 + c, to_twin)
    along(3)
    complete(c)
    along(4)
    along(5)
    pair_half(inner)
    arrived(block(order[2], lane, 1 - y), 8 + order[2])
    go(two(order[2], lane), 5, 13 + order[2], to_twin)
    go(block(order[3], lane, y), 5, 13 + order[3], to_twin)
    complete(order[2])
    arrived(at(pair, lane, 1 - y, 0), 8 + pair)
    arrived(at(pair, lane, 1 - y, 1), 12)
    go(two(pair, lane), 5, 13 + pair, to_twin)
    arrived(block(order[3], lane, 1 - y), 8 + order[3])
    go(block(order[3], lane, 1 - y), 5, 17, to_twin)
    complete(pair)
    arrived(block(order[3], 1 - lane, y), 13 + order[3])
    arrived(block(order[3], 1 - lane, 1 - y), 17)
    if ready is not None:
        ready(order[3])
    pl.when(c < 3)(lambda: gone(2, 0))
    pl.when(c > 0)(lambda: gone(2, 1))
    pl.when(inner)(lambda: gone(6, 2))
    gone(7, 3)
    gone(1, 4)
    gone(16, 5)


GATHER_SENDS = 6
GATHER_RECVS = 18


def scatter_sum(part, total, land, send, recv, produce=None, meanwhile=None, ending=None, done=None):
    c = lax.axis_index("ctx")
    f = lax.axis_index("fsdp")
    y = f // 2
    lane = lax.rem(f, 2)
    inner = jnp.logical_and(c > 0, c < 3)
    rows = total.shape[0]
    half = rows // 2
    order = near_order(c)[::-1]
    to_across = {"fsdp": f + 2 - 4 * y}
    to_twin = {"fsdp": f + 1 - 2 * lane}
    to_pair = {"ctx": order[2]}

    def rows_at(d, yy, h):
        return pl.ds(pl.multiple_of((d * 4 + lane * 2 + yy) * rows + h * half, half), half)

    def copy(src, dst, slot, arrival, peer):
        return pltpu.make_async_remote_copy(
            src, dst, send.at[slot], recv.at[arrival], device_id=peer, device_id_type=MESH
        )

    def go(src, dst, slot, arrival, peer):
        copy(src, dst, slot, arrival, peer).start()

    def gone(count, slot):
        ref = part.at[pl.ds(0, count * half)]
        copy(ref, ref, slot, 0, to_twin).wait_send()

    def piece(slot, h):
        return land.at[slot, pl.ds(h * half, half)]

    def landed(ref, arrival):
        copy(ref, ref, 0, arrival, to_twin).wait_recv()
        return ref[...].astype(F32)

    def begin(step):
        d = order[step]
        if produce is not None:
            produce(d)
        for yy, slot in ((1 - y, step), (y, 27 + step)):
            other = pl.ds(pl.multiple_of((d * 4 + 2 - lane * 2 + yy) * rows, rows), rows)
            go(part.at[other], land.at[2 * step + yy], 0, slot, to_twin)

    def twin_there(step, yy, slot):
        ref = land.at[2 * step + yy]
        copy(ref, ref, 0, slot, to_twin).wait_recv()

    def over(step, h, first=False):
        d = order[step]
        if first:
            twin_there(step, 1 - y, step)
        mine = rows_at(d, 1 - y, h)
        value = part[mine, :].astype(F32) + piece(2 * step + 1 - y, h)[...].astype(F32)
        if (step, h) == (3, 1):
            value = value + landed(piece(17, 0), 26)
        part[mine, :] = value.astype(BF)
        if (step, h) == (2, 1):
            go(part.at[mine], piece(17, 0), 3, 26, to_pair)
        else:
            go(part.at[mine], piece(8 + step, h), 1, 8 + 2 * step + h, to_across)

    def onward(step, h, first=False):
        d = order[step]
        mine = rows_at(d, y, h)
        if first:
            twin_there(step, y, 27 + step)
        value = part[mine, :].astype(F32) + piece(2 * step + y, h)[...].astype(F32)
        if (step, h) != (2, 1):
            value = value + landed(piece(8 + step, h), 8 + 2 * step + h)
        if step == 3:
            total[h * half : (h + 1) * half, :] = value
            return
        part[mine, :] = value.astype(BF)

        if step < 2:

            @pl.when(inner)
            def _():
                part[mine, :] = (part[mine, :].astype(F32) + landed(piece(12 + d, h), 16 + 2 * d + h)).astype(BF)

        here = jnp.logical_and(d < c, d == c - 1)
        target = jnp.where(d > c, c + 1, c - 1)
        slot = jnp.where(here, 16, 12 + d)
        arrival = jnp.where(here, 24, 16 + 2 * d) + h
        if step == 0:
            target = jnp.where(inner, d, target)
            slot = jnp.where(inner, 18, slot)
            arrival = jnp.where(inner, 31 + h, arrival)
        go(part.at[mine], piece(slot, h), 2, arrival, {"ctx": target})

    begin(0)
    over(0, 0, True)
    over(0, 1)
    begin(2)
    over(2, 1, True)
    begin(1)
    over(1, 0, True)
    onward(0, 0, True)
    over(1, 1)
    onward(0, 1)
    if meanwhile is not None:
        meanwhile()
    begin(3)
    over(2, 0)
    onward(1, 0, True)
    over(3, 0, True)
    onward(1, 1)
    over(3, 1)
    onward(2, 1, True)
    onward(2, 0)
    if ending is not None:
        ending()
    for h in range(2):
        onward(3, h, h == 0)

        @pl.when(c > 0)
        def _():
            total[h * half : (h + 1) * half, :] += landed(piece(12 + c, h), 16 + 2 * c + h)

        @pl.when(c < 3)
        def _():
            total[h * half : (h + 1) * half, :] += landed(piece(16, h), 24 + h)

        @pl.when(jnp.logical_not(inner))
        def _():
            total[h * half : (h + 1) * half, :] += landed(piece(18, h), 31 + h)

        if done is not None:
            done(h)

    gone(16, 0)
    gone(7, 1)
    gone(6, 2)
    gone(1, 3)


SCATTER_SENDS = 4
SCATTER_RECVS = 33


def kernel_dot(left, right):
    return jnp.dot(left, right, preferred_element_type=F32)


def kernel_dot_nt(left, right):
    return lax.dot_general(left, right, (((1,), (1,)), ((), ())), preferred_element_type=F32)


def kernel_dot_tn(left, right):
    return lax.dot_general(left, right, (((0,), (0,)), ((), ())), preferred_element_type=F32)


def turn(values):
    return pltpu.roll(values, SPAN, axis=1)


def mean_square(values):
    return lax.rsqrt(jnp.mean(values * values, axis=-1, keepdims=True) + norm_eps)


def greet_all(peers):
    barrier = pltpu.get_barrier_semaphore()
    for peer in peers:
        pl.semaphore_signal(barrier, inc=1, device_id=peer, device_id_type=MESH)
    return len(peers)


def greet_more(peers):
    c = lax.axis_index("ctx")
    barrier = pltpu.get_barrier_semaphore()
    count = greet_all(peers)
    inner = jnp.logical_and(c > 0, c < 3)

    @pl.when(c < 3)
    def _():
        pl.semaphore_signal(barrier, inc=1, device_id={"ctx": c + 1}, device_id_type=MESH)

    @pl.when(c > 0)
    def _():
        pl.semaphore_signal(barrier, inc=1, device_id={"ctx": c - 1}, device_id_type=MESH)

    @pl.when(inner)
    def _():
        pl.semaphore_wait(barrier, count + 2)

    @pl.when(jnp.logical_not(inner))
    def _():
        pl.semaphore_wait(barrier, count + 1)


class Share:
    def __init__(self, sources, targets, scratch, sems):
        self.mix, self.out, self.gate_up, self.down, self.attention_gain, self.feed_gain = sources
        self.w_mix, self.w_gate, self.w_out, self.w_down, self.w_gains = targets
        self.mix_v, self.heads_v, self.gate_s, self.out_s, self.down_s, self.gains = scratch
        self.local, self.send, self.recv = sems
        self.s = lax.axis_index("section")
        self.c = lax.axis_index("ctx")
        self.f = lax.axis_index("fsdp")
        self.other = 1 - self.s
        self.depth = self.mix.shape[1]
        self.units = self.w_down.shape[1]
        self.peers = [lax.rem(self.f + k, 4) for k in range(1, 4)]
        self.rows = pl.ds(pl.multiple_of(self.f * self.depth, self.depth), self.depth)
        self.pending = []

    def greeted(self):
        return (
            [{"fsdp": peer} for peer in self.peers]
            + [{"section": self.other}, {"ctx": lax.rem(self.c + 2, 4)}]
            + [{"section": self.other, "fsdp": peer} for peer in self.peers]
        )

    def copy(self, src, dst, slot, arrival, peer):
        return pltpu.make_async_remote_copy(
            src, dst, self.send.at[slot], self.recv.at[arrival], device_id=peer, device_id_type=MESH
        )

    def go(self, src, dst, slot, arrival, peer):
        one = self.copy(src, dst, slot, arrival, peer)
        one.start()
        self.pending.append(one)

    def keep(self, src, dst, slot):
        one = pltpu.make_async_copy(src, dst, self.local.at[slot])
        one.start()
        return one

    def load(self):
        self.gains[...] = jnp.zeros_like(self.gains)
        self.gains[0:1, :] = self.attention_gain[...]
        self.gains[1:2, :] = self.feed_gain[...]
        self.loaded = self.keep(self.mix.at[0], self.mix_v, 0)
        out_rows = self.out.at[0, pl.ds(pl.multiple_of(self.c * HEAD, HEAD), HEAD)]
        down_rows = self.down.at[0, pl.ds(pl.multiple_of(self.c * self.units, self.units), self.units)]
        self.staged = [
            self.keep(self.gate_piece(self.f, part), self.gate_s.at[:, pl.ds(part * self.units, self.units)], 5 + part)
            for part in range(2)
        ]
        self.staged.append(self.keep(out_rows, self.out_s, 7))
        self.staged.append(self.keep(down_rows, self.down_s, 8))

    def head_rows(self, peer, part):
        head = peer * 4 + self.c
        start = head * HEAD if part == 0 else (16 + 8 * (part - 1) + head // 2) * HEAD
        return self.heads_v.at[pl.ds(pl.multiple_of(start, HEAD), HEAD)]

    def put(self, part):
        return self.w_mix.at[self.s, pl.ds(part * HEAD, HEAD), self.rows]

    def send_mix(self):
        self.loaded.wait()
        for g in range(8):
            here = slice(g * 4 * HEAD, (g + 1) * 4 * HEAD)
            self.heads_v[here, :] = self.mix_v[:, here].T
        for k, peer in enumerate(self.peers):
            for part in range(3):
                self.copy(self.head_rows(peer, part), self.put(part), k, self.f, {"fsdp": peer}).start()
        self.own_mix = [self.keep(self.head_rows(self.f, part), self.put(part), 2 + part) for part in range(3)]
        for one in self.staged:
            one.wait()
        self.own_gate = self.keep(self.gate_s, self.slab(self.w_gate, self.f), 5)
        self.own_out = self.keep(self.out_s, self.w_out.at[self.s], 7)
        self.own_down = self.keep(self.down_s, self.w_down.at[self.s], 8)
        mine = self.w_gains.at[self.s, :, pl.ds(pl.multiple_of(self.f * self.depth, self.depth), self.depth)]
        for k, peer in enumerate(self.peers):
            self.go(self.gains, mine, 20 + k, 16 + 4 * self.s + self.f, {"fsdp": peer})
            self.go(self.gains, mine, 23 + k, 16 + 4 * self.s + self.f, {"section": self.other, "fsdp": peer})
        self.go(self.gains, mine, 26, 16 + 4 * self.s + self.f, {"section": self.other})
        self.own_gains = self.keep(self.gains, mine, 1)

    def gate_piece(self, peer, part):
        hidden_units = self.gate_up.shape[2] // 2
        start = pl.multiple_of(part * hidden_units + (peer * 4 + self.c) * self.units, self.units)
        return self.gate_up.at[0, :, pl.ds(start, self.units)]

    def gate_put(self, part):
        return self.w_gate.at[self.s, self.rows, pl.ds(part * self.units, self.units)]

    def send_gate(self):
        for k, peer in enumerate(self.peers):
            for part in range(2):
                self.copy(self.gate_piece(peer, part), self.gate_put(part), 3 + k, 4 + self.f, {"fsdp": peer}).start()

    def slab(self, ref, origin):
        part = pl.ds(pl.multiple_of(origin * self.depth, self.depth), self.depth)
        return ref.at[self.s, :, part] if ref is self.w_mix else ref.at[self.s, part]

    def cross_slab(self, ref, k, slot, arrival, base):
        origin = lax.rem(self.f + 3 - k, 4)
        block = self.slab(ref, origin)
        self.copy(block, block, 0, arrival + origin, {"fsdp": origin}).wait_recv()
        self.go(block, block, slot + k, base + origin, {"section": self.other})

    def cross_mix(self, between):
        for one in self.own_mix:
            one.wait()
        self.go(self.slab(self.w_mix, self.f), self.slab(self.w_mix, self.f), 6, 8 + self.f, {"section": self.other})
        between()
        for k in range(3):
            self.cross_slab(self.w_mix, k, 7, 0, 8)
        self.send_gate()
        self.go(self.out_s, self.w_out.at[self.s], 10, 24, {"section": self.other})
        self.go(self.gate_s, self.slab(self.w_gate, self.f), 11, 12 + self.f, {"section": self.other})

    def cross_gate(self):
        for k in range(3):
            self.cross_slab(self.w_gate, k, 12, 4, 12)
        self.go(self.down_s, self.w_down.at[self.s], 15, 25, {"section": self.other})

    def there(self, ref, arrival):
        self.copy(ref, ref, 0, arrival, {"section": self.other}).wait_recv()

    def mix_there(self):
        for one in (self.own_gains, self.own_gate, self.own_out, self.own_down):
            one.wait()
        for origin in range(4):
            rows = pl.ds(origin * self.depth, self.depth)
            self.there(self.w_mix.at[self.other, :, rows], 8 + origin)
            self.there(self.w_gains.at[self.other, :, rows], 16 + 4 * self.other + origin)
        for k in range(3):
            origin = lax.rem(self.f + 3 - k, 4)
            columns = pl.ds(pl.multiple_of(origin * self.depth, self.depth), self.depth)
            self.there(self.w_gains.at[self.s, :, columns], 16 + 4 * self.s + origin)
        self.there(self.w_out.at[self.other], 24)

    def gate_there(self):
        for origin in range(4):
            self.there(self.w_gate.at[self.other, pl.ds(origin * self.depth, self.depth)], 12 + origin)

    def down_there(self):
        self.there(self.w_down.at[self.other], 25)

    def finish(self):
        for k, peer in enumerate(self.peers):
            block = self.slab(self.w_mix, self.f)
            self.copy(block, block, k, 0, {"fsdp": peer}).wait_send()
            block = self.slab(self.w_gate, self.f)
            self.copy(block, block, 3 + k, 0, {"fsdp": peer}).wait_send()
        for one in self.pending:
            one.wait_send()


class Loads:
    def __init__(self, sems):
        self.sems = sems
        self.copies = []

    def start(self, src, dst):
        one = pltpu.make_async_copy(src, dst, self.sems.at[len(self.copies)])
        one.start()
        self.copies.append(one)
        return one


def load_heads(loads, source, target):
    half = HEAD // 2
    target[...] = jnp.zeros_like(target)
    pieces = [(part * HEAD + h * half, part * LANES + h * SPAN, half) for part in range(2) for h in range(2)]
    pieces.append((2 * HEAD, 2 * LANES, HEAD))
    return [loads.start(source.at[pl.ds(a, count)], target.at[pl.ds(b, count)]) for a, b, count in pieces]


def plane_rows(d, rows):
    return pl.ds(pl.multiple_of(d * 4 * rows, 4 * rows), 4 * rows)


def make_tables(block_order, frequency, cosine, sine, place_col, place_row):
    s = lax.axis_index("section")
    blocks = block_order.shape[1]
    rows = place_col.shape[0] // blocks
    order = jnp.where(s == 0, block_order[0:1, :], block_order[1:2, :])
    inside_col = lax.broadcasted_iota(jnp.int32, (rows, 1), 0)
    inside_row = lax.broadcasted_iota(jnp.int32, (1, 2 * rows), 1)
    firsts = []
    for b in range(blocks):
        source = b - b % 4 + (b % 2) * 2 + (b % 4) // 2
        firsts.append(order[:, source : source + 1] * rows)
        place_col[b * rows : (b + 1) * rows, :] = firsts[b] + inside_col
    for b in range(0, blocks, 2):
        place_row[:, b * rows : (b + 2) * rows] = jnp.where(
            inside_row < rows, firsts[b] + inside_row, firsts[b + 1] + inside_row - rows
        )
    lane = lax.broadcasted_iota(jnp.int32, (4 * rows, LANES), 1)
    for part in range(blocks // 4):
        here = pl.ds(part * 4 * rows, 4 * rows)
        angles = place_col[here, :].astype(F32) * frequency[...]
        wave = jnp.sin(angles)
        cosine[here, :] = jnp.cos(angles)
        sine[here, :] = jnp.where(lane < SPAN, -wave, wave)


def forward_body(layer, share, x_own, weights, tables, kept, scratch, sems, prepare=None, before=None, ending=None, meet=None):
    w_mix, w_gate, w_out, w_down, w_gains = weights
    cosine, sine, place_col, place_row = tables
    normed_o, q_o, k_o, v_o, context_o, log_o, middle_o, normed_two_o, both_o, result_o = kept
    (x_v, normed_v, q_v, k_v, v_v, context_v, log_v, middle_v, two_v, both_v, hidden_v, result_v,
     mix_v, gate_v, out_v, down_v, gains_v, part_v, land_a, land_b, total_v) = scratch
    local, save, send_a, recv_a, send_b, recv_b, send_c, recv_c, send_d, recv_d = sems
    c = lax.axis_index("ctx")
    f = lax.axis_index("fsdp")
    rows = x_own.shape[0]
    units = down_v.shape[0]
    own_rows = pl.ds(pl.multiple_of(own_block(c, f) * rows, rows), rows)
    loads = Loads(local)
    saves = Loads(save)

    def save_to(src, dst):
        if dst is not None:
            saves.start(src, dst)

    load_x = loads.start(x_own, x_v.at[own_rows])
    out_v[...] = jnp.zeros_like(out_v)

    def load_first():
        return [
            loads.start(w_gains.at[layer], gains_v),
            loads.start(w_out.at[layer], out_v.at[pl.ds(0, HEAD)]),
        ] + load_heads(loads, w_mix.at[layer], mix_v)

    def project(d):
        here = plane_rows(d, rows)
        x = x_v[here, :].astype(F32)
        normed = (x * mean_square(x) * gains_v[0:1, :].astype(F32)).astype(BF)
        normed_v[here, :] = normed
        mixed = kernel_dot_nt(normed, mix_v[...])
        cos = cosine[here, :]
        sin = sine[here, :]
        q = mixed[:, :LANES]
        k = mixed[:, LANES : 2 * LANES]
        q_v[here, :] = (q * cos + turn(q) * sin).astype(BF)
        k_v[here, :] = (k * cos + turn(k) * sin).astype(BF)
        v_v[here, :] = mixed[:, 2 * LANES :].astype(BF)

    if share is None:
        first = load_first()
        load_gate = loads.start(w_gate.at[layer], gate_v)
        load_down = loads.start(w_down.at[layer], down_v)
        meet()
        load_x.wait()
        for one in first:
            one.wait()
        gather_rows(x_v, rows, send_a, recv_a, project)
    else:
        share.load()
        greet_more(share.greeted())
        load_x.wait()
        share.send_mix()
        gather_rows(x_v, rows, send_a, recv_a, started=lambda: share.cross_mix(prepare))
        share.mix_there()
        first = load_first()
        for one in first:
            one.wait()
        for d in range(4):
            project(d)
        share.cross_gate()
    for src, dst in ((normed_v, normed_o), (q_v, q_o), (k_v, k_o), (v_v, v_o)):
        save_to(src, dst)
    scale = HEAD ** (-0.5)

    def attention(d):
        here = plane_rows(d, rows)
        scores = kernel_dot_nt(q_v[here, :], k_v[...]) * scale
        allowed = place_row[...] <= place_col[here, :]
        scores = jnp.where(allowed, scores, masked_value)
        top = jnp.max(scores, axis=-1, keepdims=True)
        weights = jnp.exp(scores - top)
        amount = jnp.sum(weights, axis=-1, keepdims=True)
        context = (kernel_dot(weights.astype(BF), v_v[...]) / amount).astype(BF)
        context_v[here, :] = context
        log_v[here, :] = jnp.broadcast_to(top + jnp.log(amount), (4 * rows, LANES))
        part_v[here, :] = kernel_dot(context, out_v[...]).astype(BF)

    half = rows // 2

    def own_half(h):
        return pl.ds(pl.multiple_of(own_block(c, f) * rows + h * half, half), half)

    def middle_half(h):
        part = slice(h * half, (h + 1) * half)
        middle = x_v[own_half(h), :].astype(F32) + total_v[part, :]
        middle_v[part, :] = middle
        two_v[own_half(h), :] = (middle * mean_square(middle) * gains_v[1:2, :].astype(F32)).astype(BF)
        begin_rows(two_v, rows, send_c, recv_c, h)

    scatter_sum(part_v, total_v, land_a, send_b, recv_b, attention, done=middle_half)
    save_to(context_v, context_o)
    save_to(log_v, log_o)
    save_to(middle_v, middle_o)

    def gate_ready():
        if share is None:
            load_gate.wait()
        else:
            share.gate_there()
            loads.start(w_gate.at[layer], gate_v).wait()

    def feed(d):
        here = plane_rows(d, rows)
        both = kernel_dot(two_v[here, :], gate_v[...])
        both_v[here, :] = both
        gate = both[:, :units]
        hidden_v[here, :] = (gate * jax.nn.sigmoid(gate) * both[:, units:]).astype(BF)

    first = iter((True, False, False, False))

    def feed_when_ready(d):
        if next(first):
            gate_ready()
        feed(d)

    gather_rows(two_v, rows, send_c, recv_c, feed_when_ready, begun=True)
    save_to(two_v, normed_two_o)
    save_to(both_v, both_o)
    if share is None:
        load_down.wait()
    else:
        share.down_there()
        loads.start(w_down.at[layer], down_v).wait()

    def lower(d):
        here = plane_rows(d, rows)
        part_v[here, :] = kernel_dot(hidden_v[here, :], down_v[...]).astype(BF)

    if before is not None:
        before()
    scatter_sum(part_v, total_v, land_b, send_d, recv_d, lower, ending=ending)
    result_v[...] = (middle_v[...] + total_v[...]).astype(BF)
    saves.start(result_v, result_o)
    for one in saves.copies:
        one.wait()
    if share is not None:
        share.finish()


def forward_share_kernel(*refs):
    inputs, *refs = refs
    sources, refs = refs[:6], refs[6:]
    (block_order, frequency), refs = refs[:2], refs[2:]
    kept, refs = refs[:10], refs[10:]
    weights, refs = refs[:5], refs[5:]
    tables, refs = refs[:4], refs[4:]
    scratch, refs = refs[:21], refs[21:]
    packing, refs = refs[:6], refs[6:]
    sems, share_sems = refs[:10], refs[10:]
    share = Share(sources, weights, packing, share_sems)
    forward_body(
        0, share, inputs.at[lax.axis_index("section")], weights, tables, kept, scratch, sems,
        lambda: make_tables(block_order, frequency, *tables),
    )


def backward_body(layer, grad_own, weights, tables, saved, outs, scratch, sems, returning, forward=None, hand_on=None):
    w_mix, w_gate, w_out, w_down, w_gains = weights
    cosine, sine, place_col, place_row = tables
    (grad_v, x_v, normed_v, q_v, k_v, v_v, context_v, log_v, middle_v, two_v, both_v, both_grad_v, hidden_v,
     low_v, mixed_v, kv_land, kv_v, key_grad_v, value_grad_v, start_v,
     mix_grad_v, gate_grad_v, out_grad_v, down_grad_v, gain_grad_v,
     mix_v, gate_v, out_v, down_v, gains_v, part_v, land_a, land_b, total_v) = scratch
    local, save, pair_sems, send_a, recv_a, send_b, recv_b, send_c, recv_c, send_d, recv_d = sems
    c = lax.axis_index("ctx")
    f = lax.axis_index("fsdp")
    odd = lax.rem(c, 2)
    rows = x_v.shape[0]
    units = down_v.shape[0]
    own_rows = pl.ds(pl.multiple_of(own_block(c, f) * rows, rows), rows)
    loads = Loads(local)
    saves = Loads(save)
    key_grad_v[...] = jnp.zeros_like(key_grad_v)
    value_grad_v[...] = jnp.zeros_like(value_grad_v)
    gain_grad_v[...] = jnp.zeros_like(gain_grad_v)
    if forward is None:
        x_own, normed, q, k, v, context, log, middle, normed_two, both = saved
        load_down = loads.start(w_down.at[layer], down_v)
        load_both = loads.start(both, both_v)
        load_gate = loads.start(w_gate.at[layer], gate_v)
        out_v[...] = jnp.zeros_like(out_v)
        later = [
            loads.start(src, dst)
            for src, dst in (
                (normed_two, two_v), (middle, middle_v), (w_gains.at[layer], gains_v),
                (w_out.at[layer], out_v.at[pl.ds(0, HEAD)]), (q, q_v), (k, k_v), (v, v_v),
                (context, context_v), (log, log_v), (normed, normed_v), (x_own, x_v),
            )
        ] + load_heads(loads, w_mix.at[layer], mix_v)
        load_down.wait()
        load_both.wait()
    else:
        later = []
        load_grad = loads.start(grad_own, grad_v.at[own_rows])
    if returning is not None:
        begin_old, begin_feed, begin_mix, begin_return, finish = returning
        begin_old()

    def feed(d):
        here = plane_rows(d, rows)
        hidden_grad = kernel_dot_nt(grad_v[here, :], down_v[...])
        gate = both_v[here, :units]
        up = both_v[here, units:]
        sig = jax.nn.sigmoid(gate)
        silu = gate * sig
        hidden_v[here, :] = (silu * up).astype(BF)
        both_grad_v[here, :units] = (hidden_grad * up * sig * (1.0 + gate * (1.0 - sig))).astype(BF)
        both_grad_v[here, units:] = (hidden_grad * silu).astype(BF)

    if forward is None:
        gather_rows(grad_v, rows, send_a, recv_a, feed, begun=True)
        load_gate.wait()
    else:

        def before():
            load_grad.wait()
            for h in range(2):
                begin_rows(grad_v, rows, send_a, recv_a, h)

        forward(before, lambda: gather_rows(grad_v, rows, send_a, recv_a, feed, begun=True))

    def spread(d):
        here = plane_rows(d, rows)
        part_v[here, :] = kernel_dot_nt(both_grad_v[here, :], gate_v[...]).astype(BF)

    def feed_weights():
        for one in later[:1]:
            one.wait()
        down_grad_v[...] = kernel_dot_tn(hidden_v[...], grad_v[...]).astype(BF)
        for part in range(2):
            gate_grad_v[part] = kernel_dot_tn(
                two_v[...], both_grad_v[:, part * units : (part + 1) * units]
            ).astype(BF)
        if returning is None:
            saves.start(down_grad_v, outs[4])
            saves.start(gate_grad_v, outs[2])
        else:
            begin_feed()

    def norm_grads(error, value, gain, row):
        factor = mean_square(value)
        shaped = error * gain
        common = jnp.mean(shaped * value, axis=-1, keepdims=True)
        gain_grad_v[row : row + 1, :] += jnp.sum(error * value * factor, axis=0, keepdims=True)
        return factor * shaped - value * (factor * factor * factor) * common

    half = rows // 2

    def middle_half(h):
        part = slice(h * half, (h + 1) * half)
        own_half = pl.ds(pl.multiple_of(own_block(c, f) * rows + h * half, half), half)
        if h == 0:
            for one in later[1:]:
                one.wait()
        middle_grad = norm_grads(total_v[part, :], middle_v[part, :], gains_v[1:2, :].astype(F32), 1)
        middle_grad = middle_grad + grad_v[own_half, :].astype(F32)
        middle_v[part, :] = middle_grad
        low_v[own_half, :] = middle_grad.astype(BF)
        begin_rows(low_v, rows, send_c, recv_c, h)

    scatter_sum(part_v, total_v, land_a, send_b, recv_b, spread, feed_weights, done=middle_half)
    scale = HEAD ** (-0.5)

    def attention(d):
        here = plane_rows(d, rows)
        context_grad = kernel_dot_nt(low_v[here, :], out_v[...])
        common = jnp.sum(context_grad * context_v[here, :].astype(F32), axis=-1, keepdims=True)
        context_grad = context_grad.astype(BF)
        queries = q_v[here, :]
        scores = kernel_dot_nt(queries, k_v[...]) * scale
        allowed = place_row[...] <= place_col[here, :]
        weights = jnp.exp(jnp.where(allowed, scores, masked_value) - log_v[here, 0:1])
        weight_grad = kernel_dot_nt(context_grad, v_v[...])
        score_grad = (weights * (weight_grad - common)).astype(BF)
        value_grad_v[...] += kernel_dot_tn(weights.astype(BF), context_grad)
        key_grad_v[...] += kernel_dot_tn(score_grad, queries)
        query_grad = kernel_dot(score_grad, k_v[...]) * scale
        mixed_v[here, :LANES] = (query_grad * cosine[here, :] - turn(query_grad) * sine[here, :]).astype(BF)

    gather_rows(low_v, rows, send_c, recv_c, attention, begun=True)
    key_grad = key_grad_v[...] * scale
    mixed_v[:, LANES : 2 * LANES] = (key_grad * cosine[...] - turn(key_grad) * sine[...]).astype(BF)
    mixed_v[:, 2 * LANES :] = value_grad_v[...].astype(BF)
    pair = {"ctx": c + 1 - 2 * odd}

    def pair_copy(part):
        return pltpu.make_async_remote_copy(
            mixed_v.at[:, pl.ds(part * LANES, LANES)], kv_land, pair_sems.at[0], pair_sems.at[1],
            device_id=pair, device_id_type=MESH,
        )

    pl.when(odd == 0)(pair_copy(2).start)
    pl.when(odd == 1)(pair_copy(1).start)

    def spread_two(d):
        here = plane_rows(d, rows)
        part_v[here, :] = kernel_dot(mixed_v[here, :], mix_v[...]).astype(BF)

    def mix_weights():
        out_grad_v[...] = kernel_dot_tn(context_v[...], low_v[...])[:HEAD].astype(BF)
        short = HEAD // 2
        columns = kernel_dot_tn(mixed_v[:, :LANES], normed_v[...])
        mix_grad_v[:short, :] = columns[:short].astype(BF)
        mix_grad_v[short:HEAD, :] = columns[SPAN : SPAN + short].astype(BF)
        pair_copy(1).wait_recv()
        mine = jnp.where(odd == 0, mixed_v[:, LANES : 2 * LANES].astype(F32), mixed_v[:, 2 * LANES :].astype(F32))
        kv_v[...] = (mine + kv_land[...].astype(F32)).astype(BF)
        columns = kernel_dot_tn(kv_v[...], normed_v[...])
        mix_grad_v[HEAD : HEAD + short, :] = columns[:short].astype(BF)
        mix_grad_v[HEAD + short :, :] = jnp.where(
            odd == 0, columns[SPAN : SPAN + short], columns[short:HEAD]
        ).astype(BF)
        if returning is None:
            saves.start(out_grad_v, outs[3])
            saves.start(mix_grad_v, outs[1])
        else:
            begin_mix()

    def start_half(h):
        part = slice(h * half, (h + 1) * half)
        start_grad = norm_grads(total_v[part, :], x_v[part, :].astype(F32), gains_v[0:1, :].astype(F32), 0)
        start_grad = start_grad + middle_v[part, :]
        start_v[part, :] = start_grad
        if hand_on is not None:
            hand_on(h, start_grad)

    scatter_sum(part_v, total_v, land_b, send_d, recv_d, spread_two, mix_weights,
                None if returning is None else begin_return, start_half)
    if returning is None:
        saves.start(start_v, outs[0])
        saves.start(gain_grad_v, outs[5])
    else:
        finish(gain_grad_v)
    pair_copy(1).wait_send()
    for one in saves.copies:
        one.wait()


def turn_kernel(*refs):
    (x_own, cotangent, inputs), refs = refs[:3], refs[3:]
    weights, refs = refs[:5], refs[5:]
    tables, refs = refs[:4], refs[4:]
    saved, refs = refs[:9], refs[9:]
    (results_o, starts_o), refs = refs[:2], refs[2:]
    finals, refs = refs[:5], refs[5:]
    (result_old, start_old, mix_old, gate_old, out_old, down_old), refs = refs[:6], refs[6:]
    ahead, refs = refs[:21], refs[21:]
    more, refs = refs[:15], refs[15:]
    own, refs = refs[:10], refs[10:]
    gain_old, *refs = refs
    ahead_sems, first_sems, second_sems = refs[:10], refs[10:21], refs[21:32]
    return_sems, swap_sems = refs[32:37], refs[37]
    (x_v, normed_v, q_v, k_v, v_v, context_v, log_v, middle_v, two_v, both_v, hidden_v, result_v,
     mix_v, gate_v, out_v, down_v, gains_v, part_v, land_a, land_b, total_v) = ahead
    grad_v, own_v, both_grad_v, low_v = more[:4]
    scratch = [
        grad_v, own_v, normed_v, q_v, k_v, v_v, context_v, log_v, middle_v, two_v, both_v, both_grad_v, hidden_v,
        low_v, *more[4:], mix_v, gate_v, out_v, down_v, gains_v, part_v, land_a, land_b, total_v,
    ]
    start_new = more[9]
    mix_new, gate_new, out_new, down_new, gain_new = more[10:]
    gain_v = own[8]
    s = lax.axis_index("section")
    c = lax.axis_index("ctx")
    f = lax.axis_index("fsdp")
    rows = own_v.shape[0]
    half = rows // 2
    first_row = own_block(c, f) * rows

    def meet():
        peers = [{"fsdp": lax.rem(f + k, 4)} for k in range(1, 4)]
        greet_more(peers + [{"section": 1 - s}, {"ctx": lax.rem(c + 2, 4)}])

    def forward(before, ending):
        forward_body(
            1, None, x_own, weights, tables, [None] * 9 + [result_old], ahead, ahead_sems, None, before, ending, meet
        )
        own_v[...] = x_v[pl.ds(pl.multiple_of(first_row, rows), rows), :]

    def hand_on(h, start_grad):
        grad_v[pl.ds(pl.multiple_of(first_row + h * half, half), half), :] = start_grad.astype(BF)
        begin_rows(grad_v, rows, second_sems[3], second_sems[4], h)

    backward_body(
        1, cotangent.at[s], weights, tables, None, (start_old, mix_old, gate_old, out_old, down_old, gain_old),
        scratch, first_sems, None, forward, hand_on,
    )
    begin_old, begin_feed, begin_mix, begin_return, steps_after, wait_all = returner(
        tuple(finals) + tuple(own), return_sems,
        gate_new, down_new, mix_new, out_new, gate_old, down_old, mix_old, out_old,
    )

    def swap_copy(src, dst, slot):
        return pltpu.make_async_remote_copy(
            src, dst, swap_sems.at[slot], swap_sems.at[2 + slot], device_id={"section": 1 - s}, device_id_type=MESH
        )

    def swap_rows(away, home, out, slot):
        swap_copy(away, out.at[s], slot).start()
        pltpu.make_async_copy(home, out.at[s], swap_sems.at[4 + slot]).start()

    result_new = x_own

    def finish(gain_grad_v):
        @pl.when(s == 0)
        def _():
            swap_rows(result_old, result_new, results_o, 0)
            swap_rows(start_old, start_new, starts_o, 1)

        @pl.when(s == 1)
        def _():
            swap_rows(result_new, result_old, results_o, 0)
            swap_rows(start_new, start_old, starts_o, 1)

        gain_v[0] = jnp.zeros(gain_v.shape[1:], F32)
        gain_v[0, 0:2, :] = gain_grad_v[...]
        gain_v[0, 2:4, :] = gain_old[...]
        steps_after()
        wait_all()
        for slot, out in enumerate((results_o, starts_o)):
            pltpu.make_async_copy(out.at[s], out.at[s], swap_sems.at[4 + slot]).wait()
            swap_copy(out.at[s], out.at[1 - s], slot).wait()

    backward_body(
        0, None, weights, tables, [inputs.at[s], *saved], None, scratch, second_sems,
        (begin_old, begin_feed, begin_mix, begin_return, finish),
    )


def link_sems():
    dma = pltpu.SemaphoreType.DMA
    return [dma((GATHER_SENDS,)), dma((GATHER_RECVS,)), dma((SCATTER_SENDS,)), dma((SCATTER_RECVS,))] * 2


def low(*shape):
    return (shape, BF)


def full(*shape):
    return (shape, F32)


def shapes(specs):
    return [jax.ShapeDtypeStruct(*one) for one in specs]


def rooms(specs):
    return [pltpu.VMEM(*one) for one in specs]


def signals(*counts):
    return [pltpu.SemaphoreType.DMA((count,)) for count in counts]


def forward_scratch(rows, width, units):
    length = 16 * rows
    return [low(length, width), low(length, width)] + [low(length, LANES)] * 4 + [
        full(length, LANES), full(rows, width), low(length, width), full(length, 2 * units), low(length, units),
        low(rows, width), low(3 * LANES, width), low(width, 2 * units), low(LANES, width), low(units, width),
        low(16, width), low(length, width), low(19, rows, width), low(19, rows, width), full(rows, width)]


def forward_kept(rows, width, units):
    length = 16 * rows
    return [low(length, width)] + [low(length, LANES)] * 4 + [
        full(length, LANES), full(rows, width), low(length, width), full(length, 2 * units), low(rows, width)]


ANYWHERE = pl.BlockSpec(memory_space=pl.ANY)
INSIDE = pl.BlockSpec(memory_space=pltpu.VMEM)


def forward_share_call(inputs, shards, gains, block_order):
    rows, width = inputs.shape[1:]
    length = 16 * rows
    depth = shards[0].shape[1]
    units = shards[2].shape[2] // 32
    frequency = np.zeros((2, SPAN), np.float32)
    frequency[:, : HEAD // 2] = np.float32(rope_base) ** (-(np.arange(HEAD // 2, dtype=np.float32) * 2.0 / HEAD))
    packing = [low(depth, shards[0].shape[2]), low(shards[0].shape[2], depth), low(depth, 2 * units), low(HEAD, width),
               low(units, width), low(16, depth)]
    kept = forward_kept(rows, width, units)
    weights = [low(2, 3 * HEAD, width), low(2, width, 2 * units), low(2, HEAD, width), low(2, units, width), low(2, 16, width)]
    tables = [full(length, LANES), full(length, LANES), ((length, 1), jnp.int32), ((1, length), jnp.int32)]
    return pl.pallas_call(
        forward_share_kernel,
        out_shape=shapes(kept + weights + tables),
        in_specs=[ANYWHERE] * 5 + [INSIDE] * 4,
        out_specs=[ANYWHERE] * 15 + [INSIDE] * 4,
        scratch_shapes=rooms(forward_scratch(rows, width, units) + packing) + signals(10, 10) + link_sems()
        + signals(9, 27, 26),
        compiler_params=pltpu.CompilerParams(collective_id=0, has_side_effects=True, vmem_limit_bytes=60 << 20),
    )(inputs, *shards, *gains, block_order, jnp.asarray(frequency.reshape(1, LANES)))


def backward_grads(width, units):
    return [low(2 * HEAD, width), low(2, width, units), low(HEAD, width), low(units, width), full(2, width)]


def turn_call(x_own, cotangent, inputs, weights, tables, saved):
    rows, width = x_own.shape
    length = 16 * rows
    depth = width // 4
    units = weights[3].shape[1]
    grads = backward_grads(width, units)
    more = [low(length, width), low(rows, width), low(length, 2 * units), low(length, width), low(length, 3 * LANES),
            low(length, LANES), low(length, LANES), full(length, LANES), full(length, LANES), full(rows, width)] + grads
    own = grads[:4] + grads[:4] + [full(5, 8, width), full(5, 8, width)]
    finals = [low(2, rows, width), full(2, rows, width), low(16 * 2 * HEAD, depth), low(2, depth, 16 * units),
              low(4 * HEAD, width), low(4 * units, width), full(8, width)]
    old = [low(rows, width), full(rows, width)] + grads[:4]
    return pl.pallas_call(
        turn_kernel,
        out_shape=shapes(finals + old),
        in_specs=[ANYWHERE] * 8 + [INSIDE] * 4 + [ANYWHERE] * 9,
        out_specs=[ANYWHERE] * 6 + [INSIDE] + [ANYWHERE] * 6,
        scratch_shapes=rooms(forward_scratch(rows, width, units) + more + own + grads[4:]) + signals(10, 10) + link_sems()
        + signals(20, 7, 2) + link_sems() + signals(20, 7, 2) + link_sems() + signals(5, 23, 23, 50, 40, 6),
        compiler_params=pltpu.CompilerParams(collective_id=1, has_side_effects=True, vmem_limit_bytes=60 << 20),
    )(x_own, cotangent, inputs, *weights, *tables, *saved)


def returner(refs, sems, gate_new, down_new, mix_new, out_new, gate_old, down_old, mix_old, out_old):
    (mix_out, gate_out, out_out, down_out, gain_out,
     mix_v, gate_v, out_v, down_v, mix_x, gate_x, out_x, down_x, gain_v, gain_x) = refs
    local, send, recv, line_send, line_recv = sems
    s = lax.axis_index("section")
    c = lax.axis_index("ctx")
    f = lax.axis_index("fsdp")
    other = {"section": 1 - s}
    units = down_v.shape[0]
    depth = gate_out.shape[1]
    inner = jnp.logical_and(c > 0, c < 3)
    above = jnp.minimum(c + 1, 3)
    below = jnp.maximum(c - 1, 0)

    def copy(src, dst, slot, arrival, peer):
        return pltpu.make_async_remote_copy(
            src, dst, send.at[slot], recv.at[arrival], device_id=peer, device_id_type=MESH
        )

    def owner_part(owner):
        return pl.ds(pl.multiple_of(owner * depth, depth), depth)

    def cross_parts(away, theirs, first):
        for k in range(4):
            owner = lax.rem(f + k, 4)
            part = owner_part(owner)
            copy(away.at[:, part], theirs.at[:, part], first + k, first + owner, other).start()

    def cross_whole(away, theirs, slot):
        copy(away, theirs, slot, slot, other).start()

    def home(src, dst, k):
        pltpu.make_async_copy(src, dst, local.at[k]).start()

    def begin_old():
        @pl.when(s == 0)
        def _():
            cross_whole(down_old, down_x, 8)
            cross_parts(gate_old, gate_x, 0)
            cross_whole(out_old, out_x, 9)
            cross_parts(mix_old, mix_x, 4)

        @pl.when(s == 1)
        def _():
            home(down_old, down_v, 0)
            home(gate_old, gate_v, 1)
            home(out_old, out_v, 2)
            home(mix_old, mix_v, 3)

    def begin_feed():
        @pl.when(s == 0)
        def _():
            home(down_new, down_v, 0)
            home(gate_new, gate_v, 1)

        @pl.when(s == 1)
        def _():
            cross_whole(down_new, down_x, 8)
            cross_parts(gate_new, gate_x, 0)

    def begin_mix():
        @pl.when(s == 0)
        def _():
            home(out_new, out_v, 2)
            home(mix_new, mix_v, 3)

        @pl.when(s == 1)
        def _():
            cross_whole(out_new, out_x, 9)
            cross_parts(mix_new, mix_x, 4)

    def home_wait(k, dst):
        pltpu.make_async_copy(dst, dst, local.at[k]).wait()

    def arrived(ref, arrival):
        copy(ref, ref, 0, arrival, other).wait_recv()

    def gate_at(cc, ff):
        return gate_out.at[:, :, pl.ds(pl.multiple_of((ff * 4 + cc) * units, units), units)]

    def mix_at(cc, ff):
        return mix_out.at[pl.ds(pl.multiple_of((ff * 4 + cc) * 2 * HEAD, 2 * HEAD), 2 * HEAD)]

    def rows_at(ref, cc, count):
        return ref.at[pl.ds(pl.multiple_of(cc * count, count), count)]

    def out_at(cc, ff):
        return rows_at(out_out, cc, HEAD)

    def down_at(cc, ff):
        return rows_at(down_out, cc, units)

    origins = [lax.rem(f + k, 4) for k in (0, 3, 2, 1)]
    items = [(down_at, f)] + [(gate_at, one) for one in origins] + [(out_at, f)] + [(mix_at, one) for one in origins]

    def line(index, cc, slot, target):
        place, origin = items[index]
        return pltpu.make_async_remote_copy(
            place(cc, origin), place(cc, origin), line_send.at[slot], line_recv.at[cc * 10 + index],
            device_id={"ctx": target}, device_id_type=MESH,
        )

    def start_line(index):
        pl.when(c < 3)(line(index, c, index, above).start)
        pl.when(c > 0)(line(index, c, 10 + index, below).start)

    def fold(mine, theirs, arrival):
        arrived(theirs, arrival)
        mine[...] = (mine[...].astype(F32) + theirs[...].astype(F32)).astype(BF)

    def keep(src, dst):
        one = pltpu.make_async_copy(src, dst, local.at[4])
        one.start()
        one.wait()

    def whole_item(k, mine, theirs, arrival, place, index):
        home_wait(k, mine)
        fold(mine, theirs, arrival)
        keep(mine, place(c, f))
        start_line(index)

    def to_owner(k, mine, theirs, place, arrival_x, arrival_y, slot, index):
        owner = lax.rem(f + k, 4)
        rows = owner_part(owner)
        fold(mine.at[:, rows], theirs.at[:, rows], arrival_x + owner)
        if k:
            copy(mine.at[:, rows], place(c, f), slot + k, arrival_y + f, {"fsdp": owner}).start()
        else:
            keep(mine.at[:, rows], place(c, f))
            start_line(index)

    def from_owner(k, place, arrival, index):
        arrived(place(c, origins[k]), arrival + origins[k])
        start_line(index)

    gain_targets = [other, {"fsdp": f + 1 - 2 * lax.rem(f, 2)}, {"fsdp": f + 2 - 4 * (f // 2)},
                    {"ctx": c + 1 - 2 * lax.rem(c, 2)}, {"ctx": lax.rem(c + 2, 4)}]

    def gain_copy(k):
        return copy(gain_v.at[k], gain_x.at[k], 18 + k, 18 + k, gain_targets[k])

    def gain_sum(k):
        gain_copy(k).wait_recv()
        if k < 4:
            gain_v[k + 1] = gain_v[k] + gain_x[k]
            gain_copy(k + 1).start()
        else:
            gain_out[...] = gain_v[k] + gain_x[k]

    order = near_order(c)

    def onward(index, step):
        d = order[step]
        return line(index, d, 20 + (step - 1) * 10 + index, jnp.where(d < c, above, below))

    def pass_on(index, step):
        one = onward(index, step)
        one.wait_recv()
        pl.when(inner)(one.start)

    def near(index):
        pass_on(index, 1)
        pl.when(inner)(lambda: pass_on(index, 2))

    def far(index):
        pl.when(jnp.logical_not(inner))(lambda: pass_on(index, 2))
        pass_on(index, 3)

    def gate_first():
        home_wait(1, gate_v)
        to_owner(0, gate_v, gate_x, gate_at, 0, 10, 10, 1)

    def gate_rest(k):
        return lambda: to_owner(k, gate_v, gate_x, gate_at, 0, 10, 10, 1)

    def gate_from(k):
        return lambda: from_owner(k, gate_at, 10, 1 + k)

    def mix_first():
        home_wait(3, mix_v)
        to_owner(0, mix_v, mix_x, mix_at, 4, 14, 14, 6)

    def mix_rest(k):
        return lambda: to_owner(k, mix_v, mix_x, mix_at, 4, 14, 14, 6)

    def mix_from(k):
        return lambda: from_owner(k, mix_at, 14, 6 + k)

    def down_first():
        whole_item(0, down_v, down_x, 8, down_at, 0)

    def out_first():
        whole_item(2, out_v, out_x, 9, out_at, 5)

    def passing(*steps):
        return [functools.partial(near if sign > 0 else far, abs(sign) - 1) for sign in steps]

    after = [
        passing(1) + [gate_from(1), gate_from(2), gate_from(3), out_first, mix_first, mix_rest(1), mix_rest(2), mix_rest(3)],
        passing(2, -1, 3, -2, 4) + [mix_from(1), mix_from(2), mix_from(3)],
        passing(-3, 5, -4, 6, -5, 7),
        passing(-6, 8, -7, 9),
        passing(-8, 10, -9, -10),
    ]
    def begin_return():
        down_first()
        gate_first()
        for k in range(1, 4):
            gate_rest(k)()

    def steps_after():
        gain_copy(0).start()
        for k, steps in enumerate(after):
            for step in steps:
                step()
            gain_sum(k)

    def wait_all():
        for index in range(10):
            pl.when(c < 3)(line(index, c, index, above).wait_send)
            pl.when(c > 0)(line(index, c, 10 + index, below).wait_send)
            for step in range(1, 4):
                pl.when(inner)(onward(index, step).wait_send)
        for k in range(5):
            gain_copy(k).wait_send()
        for k in range(4):
            gate_part = gate_x.at[:, pl.ds(k * depth, depth)]
            mix_part = mix_x.at[:, pl.ds(k * depth, depth)]
            for slot in (k, 10 + k) if k else (k,):
                copy(gate_part, gate_part, slot, 0, other).wait_send()
                copy(mix_part, mix_part, 4 + slot, 0, other).wait_send()
        copy(down_x, down_x, 8, 0, other).wait_send()
        copy(out_x, out_x, 9, 0, other).wait_send()

    return begin_old, begin_feed, begin_mix, begin_return, steps_after, wait_all


def widen_kernel(mix, gate, out, down, gains, results, starts,
                 mix_f, gate_f, out_f, down_f, attention_f, feed_f, results_f, starts_f, places, turned, rest):
    step = pl.program_id(0)
    rows = gate.shape[1]
    four = 4 * HEAD
    width = 4 * four

    @pl.when(step == 0)
    def _():
        s = lax.axis_index("section")
        f = lax.axis_index("fsdp")
        depth = attention_f.shape[1]
        columns = pl.ds(pl.multiple_of(f * depth, depth), depth)
        attention_f[...] = gains[pl.ds(2 * s, 1), columns]
        feed_f[...] = gains[pl.ds(2 * s + 1, 1), columns]
        results_f[...] = results[...]
        starts_f[...] = starts[...]
        source = lax.broadcasted_iota(jnp.int32, (2 * four, 2 * four), 0)
        column = lax.broadcasted_iota(jnp.int32, (2 * four, 2 * four), 1)
        query = (column // HEAD) * 2 * HEAD + lax.rem(column, HEAD)
        beyond = column - four
        kind = beyond // (2 * HEAD)
        beyond = beyond - kind * 2 * HEAD
        other = (2 * (beyond // HEAD) + kind) * 2 * HEAD + HEAD + lax.rem(beyond, HEAD)
        places[...] = jnp.where(source == jnp.where(column < four, query, other), 1.0, 0.0).astype(BF)

    @pl.when(step < 4)
    def _():
        group = kernel_dot_tn(mix[...], places[...])
        turned[:, pl.ds(pl.multiple_of(step * four, four), four)] = group[:, :four]
        rest[step] = group[:, four:]

    @pl.when(step >= 4)
    def _():
        here = pl.ds(pl.multiple_of((step - 4) * 2 * rows, 2 * rows), 2 * rows)
        mix_f[:, :width] = turned[here, :]
        for g in range(2):
            for kind in range(2):
                at = width + kind * 2 * four + g * four
                part = slice(kind * 2 * HEAD, (kind + 1) * 2 * HEAD)
                mix_f[:, at : at + four] = jnp.concatenate([rest[2 * g + k, here, part] for k in range(2)], axis=1)

    half = gate.shape[2]
    gate_f[:, :half] = gate[0].astype(F32)
    gate_f[:, half:] = gate[1].astype(F32)
    out_f[...] = out[...].astype(F32)
    down_f[...] = down[...].astype(F32)


def widen_call(results, starts, mix, gate, out, down, gains):
    steps = 8
    depth = gate.shape[1]
    width = out.shape[1]
    rows = depth // steps

    def whole(array):
        return pl.BlockSpec(array.shape, lambda i: (0,) * array.ndim)

    down_rows = down.shape[0] // steps
    return pl.pallas_call(
        widen_kernel,
        grid=(steps,),
        out_shape=shapes([
            full(depth, 2 * width), full(depth, 2 * gate.shape[2]), full(*out.shape), full(*down.shape),
            full(1, depth), full(1, depth), low(*results.shape), full(*starts.shape),
        ]),
        in_specs=[
            pl.BlockSpec((8 * HEAD, depth), lambda i: (jnp.minimum(i, 3), 0)),
            pl.BlockSpec((2, rows, gate.shape[2]), lambda i: (0, i, 0)),
            pl.BlockSpec((rows, width), lambda i: (i, 0)),
            pl.BlockSpec((down_rows, width), lambda i: (i, 0)),
            whole(gains),
            whole(results),
            whole(starts),
        ],
        out_specs=[
            pl.BlockSpec((2 * rows, 2 * width), lambda i: (jnp.maximum(i - 4, 0), 0)),
            pl.BlockSpec((rows, 2 * gate.shape[2]), lambda i: (i, 0)),
            pl.BlockSpec((rows, width), lambda i: (i, 0)),
            pl.BlockSpec((down_rows, width), lambda i: (i, 0)),
            pl.BlockSpec((1, depth), lambda i: (0, 0)),
            pl.BlockSpec((1, depth), lambda i: (0, 0)),
            whole(results),
            whole(starts),
        ],
        scratch_shapes=rooms([low(8 * HEAD, 8 * HEAD), full(depth, width), full(4, depth, 4 * HEAD)]),
        compiler_params=pltpu.CompilerParams(vmem_limit_bytes=60 << 20),
    )(mix, gate, out, down, gains, results, starts)


def on_line():
    return lax.axis_size("ctx") == 4 and lax.axis_size("fsdp") == 4


def gather(own):
    return lax.all_gather(own, ("ctx", "fsdp"), axis=0, tiled=True)


def scatter(part):
    return lax.psum_scatter(part, ("ctx", "fsdp"), scatter_dimension=0, tiled=True)


def spread_halves(columns):
    halves = columns.reshape(columns.shape[:-1] + (2, HEAD // 2))
    halves = jnp.pad(halves, [(0, 0)] * (halves.ndim - 1) + [(0, SPAN - HEAD // 2)])
    return halves.reshape(columns.shape[:-1] + (LANES,))


def join_halves(columns):
    halves = columns.reshape(columns.shape[:-1] + (2, SPAN))[..., : HEAD // 2]
    return halves.reshape(columns.shape[:-1] + (HEAD,))


def angle_tables(positions):
    frequency = rope_base ** (-(jnp.arange(HEAD // 2, dtype=F32) * 2.0 / HEAD))
    frequency = jnp.pad(frequency, (0, SPAN - HEAD // 2))
    angles = positions.astype(F32)[:, None] * frequency[None, :]
    cosine = jnp.cos(angles)
    sine = jnp.sin(angles)
    return jnp.concatenate([cosine, cosine], axis=1), jnp.concatenate([-sine, sine], axis=1)


def rotate(values, cosine, sine):
    return values * cosine + jnp.roll(values, SPAN, axis=1) * sine


def rotate_back(grads, cosine, sine):
    return grads * cosine - jnp.roll(grads, SPAN, axis=1) * sine


def norm_rows(values):
    return lax.rsqrt(jnp.mean(values * values, axis=-1, keepdims=True) + norm_eps)


def norm_back(grad_out, values, factor, gain):
    shaped = grad_out * gain
    common = jnp.mean(shaped * values, axis=-1, keepdims=True)
    grad_in = factor * shaped - values * (factor * factor * factor) * common
    return grad_in, jnp.sum(grad_out * values * factor, axis=0)


def dot(left, right):
    return jnp.dot(left, right, preferred_element_type=F32)


def dot_nt(left, right):
    return lax.dot_general(left, right, (((1,), (1,)), ((), ())), preferred_element_type=F32)


def dot_tn(left, right):
    return lax.dot_general(left, right, (((0,), (0,)), ((), ())), preferred_element_type=F32)


class Plan:
    def __init__(self, width, hidden_units):
        self.c = lax.axis_index("ctx")
        self.f = lax.axis_index("fsdp")
        self.C = lax.axis_size("ctx")
        self.F = lax.axis_size("fsdp")
        self.heads = width // HEAD
        self.ratio = self.heads // KV_HEADS
        self.heads_f = self.heads // self.F
        self.groups_f = KV_HEADS // self.F
        self.share = self.C // self.heads_f
        self.units = hidden_units // (self.F * self.C)
        self.local_head = self.c // self.share
        self.part = self.c % self.share


def pick(array, index, axis):
    return lax.dynamic_index_in_dim(array, index, axis, keepdims=False)


def pack_weights(plan, mix, gate_up):
    depth = mix.shape[0]
    width = plan.heads * HEAD
    kv_width = KV_HEADS * HEAD
    F = plan.F
    queries = pick(mix[:, :width].reshape(depth, F, plan.heads_f, HEAD), plan.local_head, 2)
    group = plan.local_head // plan.ratio
    keys = pick(mix[:, width : width + kv_width].reshape(depth, F, plan.groups_f, HEAD), group, 2)
    values = pick(mix[:, width + kv_width :].reshape(depth, F, plan.groups_f, HEAD), group, 2)
    values = jnp.pad(values, ((0, 0), (0, 0), (0, LANES - HEAD)))
    half = gate_up.shape[1] // 2
    gate = pick(gate_up[:, :half].reshape(depth, F, plan.C, plan.units), plan.c, 2)
    up = pick(gate_up[:, half:].reshape(depth, F, plan.C, plan.units), plan.c, 2)
    packed = jnp.concatenate([spread_halves(queries), spread_halves(keys), values, gate, up], axis=2)
    return jnp.swapaxes(packed, 0, 1)


def attend(plan, q_part, k, v, positions, part_positions):
    scores = dot_nt(q_part, k) * HEAD ** (-0.5)
    allowed = positions[None, :] <= part_positions[:, None]
    scores = jnp.where(allowed, scores, masked_value)
    top = jnp.max(scores, axis=-1, keepdims=True)
    weights = jnp.exp(scores - top)
    total = jnp.sum(weights, axis=-1, keepdims=True)
    context = dot((weights / total).astype(BF), v)
    return context.astype(BF), top + jnp.log(total)


def attend_back(q_part, k, v, context_grad, context, log_total, positions, part_positions):
    scale = HEAD ** (-0.5)
    common = jnp.sum(context_grad.astype(F32) * context.astype(F32), axis=-1, keepdims=True)
    allowed = positions[None, :] <= part_positions[:, None]
    scores = dot_nt(q_part, k) * scale
    weights = jnp.exp(jnp.where(allowed, scores, masked_value) - log_total)
    weight_grad = dot_nt(context_grad, v)
    score_grad = (weights * (weight_grad - common)).astype(BF)
    value_grad = dot_tn(weights.astype(BF), context_grad)
    key_grad = dot_tn(score_grad, q_part) * scale
    query_grad = dot(score_grad, k) * scale
    return query_grad, key_grad, value_grad


def forward_layer(plan, x_own, weights, gains, positions, part_positions, tables):
    mix_cut, gate_cut, out, down = weights
    cosine, sine = tables
    length = positions.shape[0]
    x_all = gather(x_own)
    x32 = x_all.astype(F32)
    factor = norm_rows(x32)
    normed = (x32 * factor * gains[0]).astype(BF)
    mixed = dot(normed, mix_cut)
    q = rotate(mixed[:, :LANES], cosine, sine).astype(BF)
    k = rotate(mixed[:, LANES : 2 * LANES], cosine, sine).astype(BF)
    v = mixed[:, 2 * LANES :].astype(BF)
    rows = length // plan.share
    start = plan.part * rows
    q_part = lax.dynamic_slice_in_dim(q, start, rows, 0)
    context, log_total = attend(plan, q_part, k, v, positions, part_positions)
    partial = dot(context[:, :HEAD], out).astype(BF)
    if plan.share > 1:
        partial = lax.dynamic_update_slice_in_dim(
            jnp.zeros((length, partial.shape[1]), BF), partial, start, 0
        )
    middle = x_own.astype(F32) + scatter(partial)
    factor_two = norm_rows(middle)
    normed_two = gather((middle * factor_two * gains[1]).astype(BF))
    both = dot(normed_two, gate_cut)
    hidden = (jax.nn.silu(both[:, : plan.units]) * both[:, plan.units :]).astype(BF)
    result = middle + scatter(dot(hidden, down).astype(BF))
    kept = (x_own, normed, q_part, k, v, context, log_total, middle, normed_two, both, hidden)
    return result.astype(BF), kept


def backward_layer(plan, grad_own, weights, gains, kept, positions, part_positions, tables, part_tables):
    mix_cut, gate_cut, out, down = weights
    x_own, normed, q_part, k, v, context, log_total, middle, normed_two, both, hidden = kept
    length = positions.shape[0]
    rows = length // plan.share
    start = plan.part * rows
    grad_all = gather(grad_own)
    hidden_grad = dot_nt(grad_all, down)
    gate = both[:, : plan.units]
    up = both[:, plan.units :]
    sig = jax.nn.sigmoid(gate)
    gate_grad = hidden_grad * up * sig * (1.0 + gate * (1.0 - sig))
    up_grad = hidden_grad * gate * sig
    both_grad = jnp.concatenate([gate_grad, up_grad], axis=1).astype(BF)
    normed_two_grad = scatter(dot_nt(both_grad, gate_cut).astype(BF))
    middle_grad, feed_gain_grad = norm_back(normed_two_grad, middle, norm_rows(middle), gains[1])
    middle_grad = middle_grad + grad_own.astype(F32)
    middle_low = gather(middle_grad.astype(BF))
    middle_part = lax.dynamic_slice_in_dim(middle_low, start, rows, 0)
    context_grad = jnp.pad(dot_nt(middle_part, out), ((0, 0), (0, LANES - HEAD))).astype(BF)
    query_grad, key_grad, value_grad = attend_back(
        q_part, k, v, context_grad, context, log_total, positions, part_positions
    )
    query_grad = rotate_back(query_grad, *part_tables).astype(BF)
    if plan.share > 1:
        query_grad = lax.dynamic_update_slice_in_dim(
            jnp.zeros((length, LANES), BF), query_grad, start, 0
        )
    key_grad = rotate_back(key_grad, *tables).astype(BF)
    mixed_grad = jnp.concatenate([query_grad, key_grad, value_grad.astype(BF)], axis=1)
    normed_grad = scatter(dot_nt(mixed_grad, mix_cut).astype(BF))
    x32 = x_own.astype(F32)
    start_grad, attention_gain_grad = norm_back(normed_grad, x32, norm_rows(x32), gains[0])
    start_grad = start_grad + middle_grad
    mix_grad = jnp.stack(
        [dot_tn(normed, part).astype(BF) for part in (query_grad, key_grad, value_grad.astype(BF))]
    )
    gate_cut_grad = jnp.stack(
        [dot_tn(normed_two, part.astype(BF)).astype(BF) for part in (gate_grad, up_grad)]
    )
    out_grad = dot_tn(context, middle_part).astype(BF)[:HEAD]
    down_grad = dot_tn(hidden, grad_all).astype(BF)
    return start_grad, (mix_grad, gate_cut_grad, out_grad, down_grad), jnp.stack([attention_gain_grad, feed_gain_grad])


def swap_sections(array):
    return lax.ppermute(array, "section", [(0, 1), (1, 0)])


def by_layer_of(section, own, other):
    first = section == 0
    return jnp.where(first, own, other), jnp.where(first, other, own)


def shared_weights(plan, section, attention_gain, query_key_value, output_weight, feed_gain, gate_up, down_weight):
    depth = query_key_value.shape[1]
    width = depth * plan.F
    gains = lax.all_gather(
        jnp.stack([attention_gain[0], feed_gain[0]]), ("section", "fsdp"), axis=0, tiled=False
    )
    gains = gains.reshape(2, plan.F, 2, depth)
    gains = jnp.swapaxes(gains, 1, 2).reshape(2, 2, width).astype(F32)
    packed = pack_weights(plan, query_key_value[0], gate_up[0])
    own_cut = lax.all_to_all(packed, "fsdp", 0, 0).reshape(width, -1)
    own_out = lax.dynamic_slice_in_dim(output_weight[0], plan.local_head * HEAD, HEAD, 0)
    own_down = lax.dynamic_slice_in_dim(down_weight[0], plan.c * plan.units, plan.units, 0)
    cuts = by_layer_of(section, own_cut, swap_sections(own_cut))
    outs = by_layer_of(section, own_out, swap_sections(own_out))
    downs = by_layer_of(section, own_down, swap_sections(own_down))
    weights = [(cuts[s][:, : 3 * LANES], cuts[s][:, 3 * LANES :], outs[s], downs[s]) for s in range(2)]
    return weights, gains


def own_gain_sums(plan, section, gain_sum, depth):
    gain_sum = lax.dynamic_slice_in_dim(gain_sum, 2 * section, 2, 0)
    return lax.dynamic_slice_in_dim(gain_sum, plan.f * depth, depth, 1)


def returned_grads(plan, section, weight_grads, gain_grads, depth):
    C, F = plan.C, plan.F
    gain_sum = jnp.concatenate([gain_grads[0], gain_grads[1]])

    def collected(index):
        first, second = weight_grads[0][index], weight_grads[1][index]
        own = jnp.where(section == 0, first, second)
        away = jnp.where(section == 0, second, first)
        return (own.astype(F32) + swap_sections(away).astype(F32)).astype(BF)

    cut_grad = jnp.concatenate(list(collected(0)) + list(collected(1)), axis=1)
    cut_grad = lax.all_to_all(cut_grad.reshape(F, depth, -1), "fsdp", 0, 0)
    cut_grad = lax.all_gather(cut_grad, "ctx", axis=0, tiled=False)
    out_grad = lax.all_gather(collected(2), "ctx", axis=0, tiled=False)
    down_grad = lax.all_gather(collected(3), "ctx", axis=0, tiled=True).astype(F32)

    def heads_of(columns, count):
        folded = columns.astype(F32).reshape(count, C // count, F, depth, columns.shape[-1]).sum(axis=1)
        return jnp.transpose(folded, (2, 1, 0, 3))

    q_grad = join_halves(heads_of(cut_grad[..., :LANES], plan.heads_f)).reshape(depth, -1)
    k_grad = join_halves(heads_of(cut_grad[..., LANES : 2 * LANES], plan.groups_f)).reshape(depth, -1)
    v_grad = heads_of(cut_grad[..., 2 * LANES : 3 * LANES], plan.groups_f)[..., :HEAD].reshape(depth, -1)
    mix_grad = jnp.concatenate([q_grad, k_grad, v_grad], axis=1)
    both = jnp.transpose(cut_grad[..., 3 * LANES :], (2, 1, 0, 3)).astype(F32)
    gate_up_grad = jnp.concatenate(
        [both[..., : plan.units].reshape(depth, -1), both[..., plan.units :].reshape(depth, -1)], axis=1
    )
    out_grad = out_grad.astype(F32).reshape(plan.heads_f, plan.share, HEAD, depth * F).sum(axis=1).reshape(-1, depth * F)

    gain_sum = lax.psum(gain_sum, ("section", "ctx", "fsdp"))
    return mix_grad, gate_up_grad, out_grad, down_grad, own_gain_sums(plan, section, gain_sum, depth)


def on_device(
    inputs, cotangent, attention_gain, query_key_value, output_weight, feed_gain, gate_up, down_weight, block_order
):
    section = lax.axis_index("section")
    width = inputs.shape[2]
    hidden_units = down_weight.shape[1] * lax.axis_size("fsdp")
    plan = Plan(width, hidden_units)
    rows = inputs.shape[1]
    C, F = plan.C, plan.F
    length = rows * C * F
    depth = query_key_value.shape[1]

    def by_layer(own, other):
        first = section == 0
        return jnp.where(first, own, other), jnp.where(first, other, own)

    results = []
    input_grads = [None, None]
    weight_grads = [None, None]
    gain_grads = [None, None]
    kept = []
    if on_line():
        shards = (query_key_value, output_weight, gate_up, down_weight)
        first = forward_share_call(inputs, shards, (attention_gain, feed_gain), block_order)
        weights = first[10:15]
        common = first[15:]
        last = turn_call(first[9], cotangent, inputs, weights, common, first[:9])[:7]
        (mix_grad, gate_up_grad, out_grad, down_grad, attention_gain_grad, feed_gain_grad,
         section_outputs, section_input_grads) = widen_call(*last)
    else:
        order = pick(block_order, section, 0)
        positions = (order[:, None] * rows + jnp.arange(rows, dtype=jnp.int32)[None, :]).reshape(length)
        part_rows = length // plan.share
        part_positions = lax.dynamic_slice_in_dim(positions, plan.part * part_rows, part_rows, 0)
        tables = angle_tables(positions)
        part_tables = angle_tables(part_positions)

        x = pick(inputs, section, 0)
        grad = pick(cotangent, section, 0)
        weights, gains = shared_weights(
            plan, section, attention_gain, query_key_value, output_weight, feed_gain, gate_up, down_weight
        )
        for s in range(2):
            x, keep = forward_layer(plan, x, weights[s], gains[s], positions, part_positions, tables)
            kept.append(keep)
            results.append(x)
        for s in (1, 0):
            input_grads[s], weight_grads[s], gain_grads[s] = backward_layer(
                plan, grad, weights[s], gains[s], kept[s], positions, part_positions, tables, part_tables
            )
            grad = input_grads[s].astype(BF)
        def mine_and_theirs(first, second):
            return jnp.where(section == 0, first, second), jnp.where(section == 0, second, first)

        def by_batch(first, second):
            own, away = mine_and_theirs(first, second)
            return jnp.stack(by_layer(own, swap_sections(away)))

        section_outputs = by_batch(*results)
        section_input_grads = by_batch(*input_grads)

        shard_grads = returned_grads(plan, section, weight_grads, gain_grads, depth)
        mix_grad, gate_up_grad, out_grad, down_grad, gain_sum = shard_grads
        attention_gain_grad, feed_gain_grad = gain_sum[0][None], gain_sum[1][None]

    return (
        section_outputs[None],
        section_input_grads[None],
        attention_gain_grad,
        mix_grad[None],
        out_grad[None],
        feed_gain_grad,
        gate_up_grad[None],
        down_grad[None],
    )


def solution(mesh):
    placed = (
        P(None, ("ctx", "fsdp"), None),
        P(None, ("ctx", "fsdp"), None),
        P("section", "fsdp"),
        P("section", "fsdp", None),
        P("section", "fsdp", None),
        P("section", "fsdp"),
        P("section", "fsdp", None),
        P("section", "fsdp", None),
        P(),
    )
    return jax.shard_map(
        on_device,
        mesh=mesh,
        in_specs=placed,
        out_specs=(
            P("section", None, ("ctx", "fsdp"), None),
            P("section", None, ("ctx", "fsdp"), None),
            P("section", "fsdp"),
            P("section", "fsdp", None),
            P("section", "fsdp", None),
            P("section", "fsdp"),
            P("section", "fsdp", None),
            P("section", "fsdp", None),
        ),
        check_vma=False,
    )
```

```python
import functools

import jax
import jax.numpy as jnp
import numpy as np
from jax import lax
from jax.experimental import pallas as pl
from jax.experimental.pallas import tpu as pltpu
from jax.sharding import PartitionSpec as P

KV_HEADS = 8
HEAD = 96
LANES = 128
SPAN = 64
norm_eps = 1e-05
rope_base = 100000.0
masked_value = -1e30
BF = jnp.bfloat16
F32 = jnp.float32

MESH = pl.DeviceIdType.MESH


def greet():
    c = lax.axis_index("ctx")
    f = lax.axis_index("fsdp")
    barrier = pltpu.get_barrier_semaphore()
    inner = jnp.logical_and(c > 0, c < 3)
    for peer in (f + 2 - 4 * (f // 2), f + 1 - 2 * lax.rem(f, 2)):
        pl.semaphore_signal(barrier, inc=1, device_id={"fsdp": peer}, device_id_type=MESH)
    pl.semaphore_signal(barrier, inc=1, device_id={"ctx": lax.rem(c + 2, 4)}, device_id_type=MESH)

    @pl.when(c < 3)
    def _():
        pl.semaphore_signal(barrier, inc=1, device_id={"ctx": c + 1}, device_id_type=MESH)

    @pl.when(c > 0)
    def _():
        pl.semaphore_signal(barrier, inc=1, device_id={"ctx": c - 1}, device_id_type=MESH)

    @pl.when(inner)
    def _():
        pl.semaphore_wait(barrier, 5)

    @pl.when(jnp.logical_not(inner))
    def _():
        pl.semaphore_wait(barrier, 4)


def near_order(c):
    low = c < 2
    return [c, c + 1 - 2 * lax.rem(c, 2), jnp.where(low, 2, 1), jnp.where(low, 3, 0)]


def own_block(c, f):
    return c * 4 + lax.rem(f, 2) * 2 + f // 2


def begin_rows(whole, rows, send, recv, h):
    c = lax.axis_index("ctx")
    f = lax.axis_index("fsdp")
    half = rows // 2
    mine = whole.at[pl.ds(pl.multiple_of(own_block(c, f) * rows + h * half, half), half)]

    def copy(slot, arrival, peer):
        return pltpu.make_async_remote_copy(
            mine, mine, send.at[slot], recv.at[arrival], device_id=peer, device_id_type=MESH
        )

    pl.when(c < 3)(copy(0, 2 * c + h, {"ctx": jnp.minimum(c + 1, 3)}).start)
    pl.when(c > 0)(copy(1, 2 * c + h, {"ctx": jnp.maximum(c - 1, 0)}).start)
    copy(3, 8 + c, {"fsdp": f + 2 - 4 * (f // 2)}).start()


def gather_rows(whole, rows, send, recv, ready=None, started=None, begun=False):
    c = lax.axis_index("ctx")
    f = lax.axis_index("fsdp")
    y = f // 2
    lane = lax.rem(f, 2)
    inner = jnp.logical_and(c > 0, c < 3)
    outer = jnp.logical_not(inner)
    order = near_order(c)
    pair = order[1]
    half = rows // 2
    to_across = {"fsdp": f + 2 - 4 * y}
    to_twin = {"fsdp": f + 1 - 2 * lane}
    to_pair = {"ctx": pair}

    def at(d, k, yy, h):
        return whole.at[pl.ds(pl.multiple_of((d * 4 + k * 2 + yy) * rows + h * half, half), half)]

    def block(d, k, yy):
        return whole.at[pl.ds(pl.multiple_of((d * 4 + k * 2 + yy) * rows, rows), rows)]

    def two(d, k):
        return whole.at[pl.ds(pl.multiple_of((d * 4 + k * 2) * rows, rows), 2 * rows)]

    def copy(src, slot, arrival, peer):
        return pltpu.make_async_remote_copy(
            src, src, send.at[slot], recv.at[arrival], device_id=peer, device_id_type=MESH
        )

    def go(src, slot, arrival, peer, when=None):
        one = copy(src, slot, arrival, peer)
        if when is None:
            one.start()
        else:
            pl.when(when)(one.start)

    def arrived(ref, arrival):
        copy(ref, 0, arrival, to_twin).wait_recv()

    def gone(count, slot):
        copy(whole.at[pl.ds(0, count * half)], slot, 0, to_twin).wait_send()

    if not begun:
        for h in range(2):
            begin_rows(whole, rows, send, recv, h)
    if started is not None:
        started()

    events = [
        (pair, 0),
        (jnp.where(inner, order[2], pair), jnp.where(inner, 0, 1)),
        (jnp.where(inner, pair, order[2]), jnp.where(inner, 1, 0)),
        (order[2], 1),
        (order[3], 0),
        (order[3], 1),
    ]

    def along(index):
        d, h = events[index]
        piece = at(d, lane, y, h)
        arrived(piece, 2 * d + h)
        go(piece, 2, 2 * d + h, {"ctx": jnp.where(d < c, c + 1, c - 1)}, inner)
        go(piece, 3, 8 + d, to_across, jnp.logical_or(d != pair, h == 0) if index in (1, 2) else None)

    def complete(d):
        arrived(two(d, 1 - lane), 13 + d)
        if ready is not None:
            ready(d)

    def pair_half(when):
        go(at(c, lane, 1 - y, 1), 4, 12, to_pair, when)

    along(0)
    along(1)
    along(2)
    arrived(block(c, lane, 1 - y), 8 + c)
    pair_half(outer)
    go(two(c, lane), 5, 13 + c, to_twin)
    along(3)
    complete(c)
    along(4)
    along(5)
    pair_half(inner)
    arrived(block(order[2], lane, 1 - y), 8 + order[2])
    go(two(order[2], lane), 5, 13 + order[2], to_twin)
    go(block(order[3], lane, y), 5, 13 + order[3], to_twin)
    complete(order[2])
    arrived(at(pair, lane, 1 - y, 0), 8 + pair)
    arrived(at(pair, lane, 1 - y, 1), 12)
    go(two(pair, lane), 5, 13 + pair, to_twin)
    arrived(block(order[3], lane, 1 - y), 8 + order[3])
    go(block(order[3], lane, 1 - y), 5, 17, to_twin)
    complete(pair)
    arrived(block(order[3], 1 - lane, y), 13 + order[3])
    arrived(block(order[3], 1 - lane, 1 - y), 17)
    if ready is not None:
        ready(order[3])
    pl.when(c < 3)(lambda: gone(2, 0))
    pl.when(c > 0)(lambda: gone(2, 1))
    pl.when(inner)(lambda: gone(6, 2))
    gone(7, 3)
    gone(1, 4)
    gone(16, 5)


GATHER_SENDS = 6
GATHER_RECVS = 18


def scatter_sum(part, total, land, send, recv, produce=None, meanwhile=None, ending=None, done=None):
    c = lax.axis_index("ctx")
    f = lax.axis_index("fsdp")
    y = f // 2
    lane = lax.rem(f, 2)
    inner = jnp.logical_and(c > 0, c < 3)
    rows = total.shape[0]
    half = rows // 2
    order = near_order(c)[::-1]
    to_across = {"fsdp": f + 2 - 4 * y}
    to_twin = {"fsdp": f + 1 - 2 * lane}
    to_pair = {"ctx": order[2]}

    def rows_at(d, yy, h):
        return pl.ds(pl.multiple_of((d * 4 + lane * 2 + yy) * rows + h * half, half), half)

    def copy(src, dst, slot, arrival, peer):
        return pltpu.make_async_remote_copy(
            src, dst, send.at[slot], recv.at[arrival], device_id=peer, device_id_type=MESH
        )

    def go(src, dst, slot, arrival, peer):
        copy(src, dst, slot, arrival, peer).start()

    def gone(count, slot):
        ref = part.at[pl.ds(0, count * half)]
        copy(ref, ref, slot, 0, to_twin).wait_send()

    def piece(slot, h):
        return land.at[slot, pl.ds(h * half, half)]

    def landed(ref, arrival):
        copy(ref, ref, 0, arrival, to_twin).wait_recv()
        return ref[...].astype(F32)

    def begin(step):
        d = order[step]
        if produce is not None:
            produce(d)
        for yy, slot in ((1 - y, step), (y, 27 + step)):
            other = pl.ds(pl.multiple_of((d * 4 + 2 - lane * 2 + yy) * rows, rows), rows)
            go(part.at[other], land.at[2 * step + yy], 0, slot, to_twin)

    def twin_there(step, yy, slot):
        ref = land.at[2 * step + yy]
        copy(ref, ref, 0, slot, to_twin).wait_recv()

    def over(step, h, first=False):
        d = order[step]
        if first:
            twin_there(step, 1 - y, step)
        mine = rows_at(d, 1 - y, h)
        value = part[mine, :].astype(F32) + piece(2 * step + 1 - y, h)[...].astype(F32)
        if (step, h) == (3, 1):
            value = value + landed(piece(17, 0), 26)
        part[mine, :] = value.astype(BF)
        if (step, h) == (2, 1):
            go(part.at[mine], piece(17, 0), 3, 26, to_pair)
        else:
            go(part.at[mine], piece(8 + step, h), 1, 8 + 2 * step + h, to_across)

    def onward(step, h, first=False):
        d = order[step]
        mine = rows_at(d, y, h)
        if first:
            twin_there(step, y, 27 + step)
        value = part[mine, :].astype(F32) + piece(2 * step + y, h)[...].astype(F32)
        if (step, h) != (2, 1):
            value = value + landed(piece(8 + step, h), 8 + 2 * step + h)
        if step == 3:
            total[h * half : (h + 1) * half, :] = value
            return
        part[mine, :] = value.astype(BF)

        if step < 2:

            @pl.when(inner)
            def _():
                part[mine, :] = (part[mine, :].astype(F32) + landed(piece(12 + d, h), 16 + 2 * d + h)).astype(BF)

        here = jnp.logical_and(d < c, d == c - 1)
        target = jnp.where(d > c, c + 1, c - 1)
        slot = jnp.where(here, 16, 12 + d)
        arrival = jnp.where(here, 24, 16 + 2 * d) + h
        if step == 0:
            target = jnp.where(inner, d, target)
            slot = jnp.where(inner, 18, slot)
            arrival = jnp.where(inner, 31 + h, arrival)
        go(part.at[mine], piece(slot, h), 2, arrival, {"ctx": target})

    begin(0)
    over(0, 0, True)
    over(0, 1)
    begin(2)
    over(2, 1, True)
    begin(1)
    over(1, 0, True)
    onward(0, 0, True)
    over(1, 1)
    onward(0, 1)
    if meanwhile is not None:
        meanwhile()
    begin(3)
    over(2, 0)
    onward(1, 0, True)
    over(3, 0, True)
    onward(1, 1)
    over(3, 1)
    onward(2, 1, True)
    onward(2, 0)
    if ending is not None:
        ending()
    for h in range(2):
        onward(3, h, h == 0)

        @pl.when(c > 0)
        def _():
            total[h * half : (h + 1) * half, :] += landed(piece(12 + c, h), 16 + 2 * c + h)

        @pl.when(c < 3)
        def _():
            total[h * half : (h + 1) * half, :] += landed(piece(16, h), 24 + h)

        @pl.when(jnp.logical_not(inner))
        def _():
            total[h * half : (h + 1) * half, :] += landed(piece(18, h), 31 + h)

        if done is not None:
            done(h)

    gone(16, 0)
    gone(7, 1)
    gone(6, 2)
    gone(1, 3)


SCATTER_SENDS = 4
SCATTER_RECVS = 33


def kernel_dot(left, right):
    return jnp.dot(left, right, preferred_element_type=F32)


def kernel_dot_nt(left, right):
    return lax.dot_general(left, right, (((1,), (1,)), ((), ())), preferred_element_type=F32)


def kernel_dot_tn(left, right):
    return lax.dot_general(left, right, (((0,), (0,)), ((), ())), preferred_element_type=F32)


def turn(values):
    return pltpu.roll(values, SPAN, axis=1)


def mean_square(values):
    return lax.rsqrt(jnp.mean(values * values, axis=-1, keepdims=True) + norm_eps)


def greet_all(peers):
    barrier = pltpu.get_barrier_semaphore()
    for peer in peers:
        pl.semaphore_signal(barrier, inc=1, device_id=peer, device_id_type=MESH)
    return len(peers)


def greet_more(peers):
    c = lax.axis_index("ctx")
    barrier = pltpu.get_barrier_semaphore()
    count = greet_all(peers)
    inner = jnp.logical_and(c > 0, c < 3)

    @pl.when(c < 3)
    def _():
        pl.semaphore_signal(barrier, inc=1, device_id={"ctx": c + 1}, device_id_type=MESH)

    @pl.when(c > 0)
    def _():
        pl.semaphore_signal(barrier, inc=1, device_id={"ctx": c - 1}, device_id_type=MESH)

    @pl.when(inner)
    def _():
        pl.semaphore_wait(barrier, count + 2)

    @pl.when(jnp.logical_not(inner))
    def _():
        pl.semaphore_wait(barrier, count + 1)


class Share:
    def __init__(self, sources, targets, scratch, sems):
        self.mix, self.out, self.gate_up, self.down, self.attention_gain, self.feed_gain = sources
        self.w_mix, self.w_gate, self.w_out, self.w_down, self.w_gains = targets
        self.mix_v, self.heads_v, self.gate_s, self.out_s, self.down_s, self.gains = scratch
        self.local, self.send, self.recv = sems
        self.s = lax.axis_index("section")
        self.c = lax.axis_index("ctx")
        self.f = lax.axis_index("fsdp")
        self.other = 1 - self.s
        self.depth = self.mix.shape[1]
        self.units = self.w_down.shape[1]
        self.peers = [lax.rem(self.f + k, 4) for k in range(1, 4)]
        self.rows = pl.ds(pl.multiple_of(self.f * self.depth, self.depth), self.depth)
        self.pending = []

    def greeted(self):
        return (
            [{"fsdp": peer} for peer in self.peers]
            + [{"section": self.other}, {"ctx": lax.rem(self.c + 2, 4)}]
            + [{"section": self.other, "fsdp": peer} for peer in self.peers]
        )

    def copy(self, src, dst, slot, arrival, peer):
        return pltpu.make_async_remote_copy(
            src, dst, self.send.at[slot], self.recv.at[arrival], device_id=peer, device_id_type=MESH
        )

    def go(self, src, dst, slot, arrival, peer):
        one = self.copy(src, dst, slot, arrival, peer)
        one.start()
        self.pending.append(one)

    def keep(self, src, dst, slot):
        one = pltpu.make_async_copy(src, dst, self.local.at[slot])
        one.start()
        return one

    def load(self):
        self.gains[...] = jnp.zeros_like(self.gains)
        self.gains[0:1, :] = self.attention_gain[...]
        self.gains[1:2, :] = self.feed_gain[...]
        self.loaded = self.keep(self.mix.at[0], self.mix_v, 0)
        out_rows = self.out.at[0, pl.ds(pl.multiple_of(self.c * HEAD, HEAD), HEAD)]
        down_rows = self.down.at[0, pl.ds(pl.multiple_of(self.c * self.units, self.units), self.units)]
        self.staged = [
            self.keep(self.gate_piece(self.f, part), self.gate_s.at[:, pl.ds(part * self.units, self.units)], 5 + part)
            for part in range(2)
        ]
        self.staged.append(self.keep(out_rows, self.out_s, 7))
        self.staged.append(self.keep(down_rows, self.down_s, 8))

    def head_rows(self, peer, part):
        head = peer * 4 + self.c
        start = head * HEAD if part == 0 else (16 + 8 * (part - 1) + head // 2) * HEAD
        return self.heads_v.at[pl.ds(pl.multiple_of(start, HEAD), HEAD)]

    def put(self, part):
        return self.w_mix.at[self.s, pl.ds(part * HEAD, HEAD), self.rows]

    def send_mix(self):
        self.loaded.wait()
        for g in range(8):
            here = slice(g * 4 * HEAD, (g + 1) * 4 * HEAD)
            self.heads_v[here, :] = self.mix_v[:, here].T
        for k, peer in enumerate(self.peers):
            for part in range(3):
                self.copy(self.head_rows(peer, part), self.put(part), k, self.f, {"fsdp": peer}).start()
        self.own_mix = [self.keep(self.head_rows(self.f, part), self.put(part), 2 + part) for part in range(3)]
        for one in self.staged:
            one.wait()
        self.own_gate = self.keep(self.gate_s, self.slab(self.w_gate, self.f), 5)
        self.own_out = self.keep(self.out_s, self.w_out.at[self.s], 7)
        self.own_down = self.keep(self.down_s, self.w_down.at[self.s], 8)
        mine = self.w_gains.at[self.s, :, pl.ds(pl.multiple_of(self.f * self.depth, self.depth), self.depth)]
        for k, peer in enumerate(self.peers):
            self.go(self.gains, mine, 20 + k, 16 + 4 * self.s + self.f, {"fsdp": peer})
            self.go(self.gains, mine, 23 + k, 16 + 4 * self.s + self.f, {"section": self.other, "fsdp": peer})
        self.go(self.gains, mine, 26, 16 + 4 * self.s + self.f, {"section": self.other})
        self.own_gains = self.keep(self.gains, mine, 1)

    def gate_piece(self, peer, part):
        hidden_units = self.gate_up.shape[2] // 2
        start = pl.multiple_of(part * hidden_units + (peer * 4 + self.c) * self.units, self.units)
        return self.gate_up.at[0, :, pl.ds(start, self.units)]

    def gate_put(self, part):
        return self.w_gate.at[self.s, self.rows, pl.ds(part * self.units, self.units)]

    def send_gate(self):
        for k, peer in enumerate(self.peers):
            for part in range(2):
                self.copy(self.gate_piece(peer, part), self.gate_put(part), 3 + k, 4 + self.f, {"fsdp": peer}).start()

    def slab(self, ref, origin):
        part = pl.ds(pl.multiple_of(origin * self.depth, self.depth), self.depth)
        return ref.at[self.s, :, part] if ref is self.w_mix else ref.at[self.s, part]

    def cross_slab(self, ref, k, slot, arrival, base):
        origin = lax.rem(self.f + 3 - k, 4)
        block = self.slab(ref, origin)
        self.copy(block, block, 0, arrival + origin, {"fsdp": origin}).wait_recv()
        self.go(block, block, slot + k, base + origin, {"section": self.other})

    def cross_mix(self, between):
        for one in self.own_mix:
            one.wait()
        self.go(self.slab(self.w_mix, self.f), self.slab(self.w_mix, self.f), 6, 8 + self.f, {"section": self.other})
        between()
        for k in range(3):
            self.cross_slab(self.w_mix, k, 7, 0, 8)
        self.send_gate()
        self.go(self.out_s, self.w_out.at[self.s], 10, 24, {"section": self.other})
        self.go(self.gate_s, self.slab(self.w_gate, self.f), 11, 12 + self.f, {"section": self.other})

    def cross_gate(self):
        for k in range(3):
            self.cross_slab(self.w_gate, k, 12, 4, 12)
        self.go(self.down_s, self.w_down.at[self.s], 15, 25, {"section": self.other})

    def there(self, ref, arrival):
        self.copy(ref, ref, 0, arrival, {"section": self.other}).wait_recv()

    def gains_there(self):
        self.own_gains.wait()
        for origin in range(4):
            columns = pl.ds(origin * self.depth, self.depth)
            self.there(self.w_gains.at[self.other, :, columns], 16 + 4 * self.other + origin)
        for k in range(3):
            origin = lax.rem(self.f + 3 - k, 4)
            columns = pl.ds(pl.multiple_of(origin * self.depth, self.depth), self.depth)
            self.there(self.w_gains.at[self.s, :, columns], 16 + 4 * self.s + origin)

    def mix_there(self):
        for one in (self.own_gate, self.own_out, self.own_down):
            one.wait()
        for origin in range(4):
            rows = pl.ds(origin * self.depth, self.depth)
            self.there(self.w_mix.at[self.other, :, rows], 8 + origin)
        self.there(self.w_out.at[self.other], 24)

    def gate_there(self):
        for origin in range(4):
            self.there(self.w_gate.at[self.other, pl.ds(origin * self.depth, self.depth)], 12 + origin)

    def down_there(self):
        self.there(self.w_down.at[self.other], 25)

    def finish(self):
        for k, peer in enumerate(self.peers):
            block = self.slab(self.w_mix, self.f)
            self.copy(block, block, k, 0, {"fsdp": peer}).wait_send()
            block = self.slab(self.w_gate, self.f)
            self.copy(block, block, 3 + k, 0, {"fsdp": peer}).wait_send()
        for one in self.pending:
            one.wait_send()


class Loads:
    def __init__(self, sems):
        self.sems = sems
        self.copies = []

    def start(self, src, dst):
        one = pltpu.make_async_copy(src, dst, self.sems.at[len(self.copies)])
        one.start()
        self.copies.append(one)
        return one


def load_heads(loads, source, target):
    half = HEAD // 2
    target[...] = jnp.zeros_like(target)
    pieces = [(part * HEAD + h * half, part * LANES + h * SPAN, half) for part in range(2) for h in range(2)]
    pieces.append((2 * HEAD, 2 * LANES, HEAD))
    return [loads.start(source.at[pl.ds(a, count)], target.at[pl.ds(b, count)]) for a, b, count in pieces]


def plane_rows(d, rows):
    return pl.ds(pl.multiple_of(d * 4 * rows, 4 * rows), 4 * rows)


def make_tables(block_order, frequency, cosine, sine, place_col, place_row):
    s = lax.axis_index("section")
    blocks = block_order.shape[1]
    rows = place_col.shape[0] // blocks
    order = jnp.where(s == 0, block_order[0:1, :], block_order[1:2, :])
    inside_col = lax.broadcasted_iota(jnp.int32, (rows, 1), 0)
    inside_row = lax.broadcasted_iota(jnp.int32, (1, 2 * rows), 1)
    firsts = []
    for b in range(blocks):
        source = b - b % 4 + (b % 2) * 2 + (b % 4) // 2
        firsts.append(order[:, source : source + 1] * rows)
        place_col[b * rows : (b + 1) * rows, :] = firsts[b] + inside_col
    for b in range(0, blocks, 2):
        place_row[:, b * rows : (b + 2) * rows] = jnp.where(
            inside_row < rows, firsts[b] + inside_row, firsts[b + 1] + inside_row - rows
        )
    lane = lax.broadcasted_iota(jnp.int32, (4 * rows, LANES), 1)
    for part in range(blocks // 4):
        here = pl.ds(part * 4 * rows, 4 * rows)
        angles = place_col[here, :].astype(F32) * frequency[...]
        wave = jnp.sin(angles)
        cosine[here, :] = jnp.cos(angles)
        sine[here, :] = jnp.where(lane < SPAN, -wave, wave)


def forward_body(layer, share, x_own, weights, tables, kept, scratch, sems, prepare=None, before=None, ending=None, meet=None):
    w_mix, w_gate, w_out, w_down, w_gains = weights
    cosine, sine, place_col, place_row = tables
    normed_o, q_o, k_o, v_o, context_o, log_o, middle_o, normed_two_o, both_o, result_o = kept
    (x_v, normed_v, q_v, k_v, v_v, context_v, log_v, middle_v, two_v, both_v, hidden_v, result_v,
     mix_v, gate_v, out_v, down_v, gains_v, part_v, land_a, land_b, total_v) = scratch
    local, save, send_a, recv_a, send_b, recv_b, send_c, recv_c, send_d, recv_d = sems
    c = lax.axis_index("ctx")
    f = lax.axis_index("fsdp")
    rows = x_own.shape[0]
    units = down_v.shape[0]
    own_rows = pl.ds(pl.multiple_of(own_block(c, f) * rows, rows), rows)
    loads = Loads(local)
    saves = Loads(save)

    def save_to(src, dst):
        if dst is not None:
            saves.start(src, dst)

    load_x = loads.start(x_own, x_v.at[own_rows])
    out_v[...] = jnp.zeros_like(out_v)

    def load_first():
        return [
            loads.start(w_out.at[layer], out_v.at[pl.ds(0, HEAD)]),
        ] + load_heads(loads, w_mix.at[layer], mix_v)

    def normalize(d):
        here = plane_rows(d, rows)
        x = x_v[here, :].astype(F32)
        normed_v[here, :] = (x * mean_square(x) * gains_v[0:1, :].astype(F32)).astype(BF)

    def multiply(d):
        here = plane_rows(d, rows)
        mixed = kernel_dot_nt(normed_v[here, :], mix_v[...])
        cos = cosine[here, :]
        sin = sine[here, :]
        q = mixed[:, :LANES]
        k = mixed[:, LANES : 2 * LANES]
        q_v[here, :] = (q * cos + turn(q) * sin).astype(BF)
        k_v[here, :] = (k * cos + turn(k) * sin).astype(BF)
        v_v[here, :] = mixed[:, 2 * LANES :].astype(BF)

    if share is None:
        first = [loads.start(w_gains.at[layer], gains_v)] + load_first()
        load_gate = loads.start(w_gate.at[layer], gate_v)
        load_down = loads.start(w_down.at[layer], down_v)
        meet()
        load_x.wait()
        for one in first:
            one.wait()

        def project(d):
            normalize(d)
            multiply(d)

        gather_rows(x_v, rows, send_a, recv_a, project)
    else:
        share.load()
        greet_more(share.greeted())
        load_x.wait()
        share.send_mix()
        turns = iter((True, False, False, False))

        def normalize_when_ready(d):
            if next(turns):
                share.gains_there()
                loads.start(w_gains.at[layer], gains_v).wait()
            normalize(d)

        gather_rows(x_v, rows, send_a, recv_a, normalize_when_ready, started=lambda: share.cross_mix(prepare))
        share.mix_there()
        first = load_first()
        for one in first:
            one.wait()
        for d in range(4):
            multiply(d)
        share.cross_gate()
    for src, dst in ((normed_v, normed_o), (q_v, q_o), (k_v, k_o), (v_v, v_o)):
        save_to(src, dst)
    scale = HEAD ** (-0.5)

    def attention(d):
        here = plane_rows(d, rows)
        scores = kernel_dot_nt(q_v[here, :], k_v[...]) * scale
        allowed = place_row[...] <= place_col[here, :]
        scores = jnp.where(allowed, scores, masked_value)
        top = jnp.max(scores, axis=-1, keepdims=True)
        weights = jnp.exp(scores - top)
        amount = jnp.sum(weights, axis=-1, keepdims=True)
        context = (kernel_dot(weights.astype(BF), v_v[...]) / amount).astype(BF)
        context_v[here, :] = context
        log_v[here, :] = jnp.broadcast_to(top + jnp.log(amount), (4 * rows, LANES))
        part_v[here, :] = kernel_dot(context, out_v[...]).astype(BF)

    half = rows // 2

    def own_half(h):
        return pl.ds(pl.multiple_of(own_block(c, f) * rows + h * half, half), half)

    def middle_half(h):
        part = slice(h * half, (h + 1) * half)
        middle = x_v[own_half(h), :].astype(F32) + total_v[part, :]
        middle_v[part, :] = middle
        two_v[own_half(h), :] = (middle * mean_square(middle) * gains_v[1:2, :].astype(F32)).astype(BF)
        begin_rows(two_v, rows, send_c, recv_c, h)

    scatter_sum(part_v, total_v, land_a, send_b, recv_b, attention, done=middle_half)
    save_to(context_v, context_o)
    save_to(log_v, log_o)
    save_to(middle_v, middle_o)

    def gate_ready():
        if share is None:
            load_gate.wait()
        else:
            share.gate_there()
            loads.start(w_gate.at[layer], gate_v).wait()

    def feed(d):
        here = plane_rows(d, rows)
        both = kernel_dot(two_v[here, :], gate_v[...])
        both_v[here, :] = both
        gate = both[:, :units]
        hidden_v[here, :] = (gate * jax.nn.sigmoid(gate) * both[:, units:]).astype(BF)

    first = iter((True, False, False, False))

    def feed_when_ready(d):
        if next(first):
            gate_ready()
        feed(d)

    gather_rows(two_v, rows, send_c, recv_c, feed_when_ready, begun=True)
    save_to(two_v, normed_two_o)
    save_to(both_v, both_o)
    if share is None:
        load_down.wait()
    else:
        share.down_there()
        loads.start(w_down.at[layer], down_v).wait()

    def lower(d):
        here = plane_rows(d, rows)
        part_v[here, :] = kernel_dot(hidden_v[here, :], down_v[...]).astype(BF)

    if before is not None:
        before()
    scatter_sum(part_v, total_v, land_b, send_d, recv_d, lower, ending=ending)
    result_v[...] = (middle_v[...] + total_v[...]).astype(BF)
    saves.start(result_v, result_o)
    for one in saves.copies:
        one.wait()
    if share is not None:
        share.finish()


def forward_share_kernel(*refs):
    inputs, *refs = refs
    sources, refs = refs[:6], refs[6:]
    (block_order, frequency), refs = refs[:2], refs[2:]
    kept, refs = refs[:10], refs[10:]
    weights, refs = refs[:5], refs[5:]
    tables, refs = refs[:4], refs[4:]
    scratch, refs = refs[:21], refs[21:]
    packing, refs = refs[:6], refs[6:]
    sems, share_sems = refs[:10], refs[10:]
    share = Share(sources, weights, packing, share_sems)
    forward_body(
        0, share, inputs.at[lax.axis_index("section")], weights, tables, kept, scratch, sems,
        lambda: make_tables(block_order, frequency, *tables),
    )


def backward_body(layer, grad_own, weights, tables, saved, outs, scratch, sems, returning, forward=None, hand_on=None):
    w_mix, w_gate, w_out, w_down, w_gains = weights
    cosine, sine, place_col, place_row = tables
    (grad_v, x_v, normed_v, q_v, k_v, v_v, context_v, log_v, middle_v, two_v, both_v, both_grad_v, hidden_v,
     low_v, mixed_v, kv_land, kv_v, key_grad_v, value_grad_v, start_v,
     mix_grad_v, gate_grad_v, out_grad_v, down_grad_v, gain_grad_v,
     mix_v, gate_v, out_v, down_v, gains_v, part_v, land_a, land_b, total_v) = scratch
    local, save, pair_sems, send_a, recv_a, send_b, recv_b, send_c, recv_c, send_d, recv_d = sems
    c = lax.axis_index("ctx")
    f = lax.axis_index("fsdp")
    odd = lax.rem(c, 2)
    rows = x_v.shape[0]
    units = down_v.shape[0]
    own_rows = pl.ds(pl.multiple_of(own_block(c, f) * rows, rows), rows)
    loads = Loads(local)
    saves = Loads(save)
    key_grad_v[...] = jnp.zeros_like(key_grad_v)
    value_grad_v[...] = jnp.zeros_like(value_grad_v)
    gain_grad_v[...] = jnp.zeros_like(gain_grad_v)
    if forward is None:
        x_own, normed, q, k, v, context, log, middle, normed_two, both = saved
        load_down = loads.start(w_down.at[layer], down_v)
        load_both = loads.start(both, both_v)
        load_gate = loads.start(w_gate.at[layer], gate_v)
        out_v[...] = jnp.zeros_like(out_v)
        later = [
            loads.start(src, dst)
            for src, dst in (
                (normed_two, two_v), (middle, middle_v), (w_gains.at[layer], gains_v),
                (w_out.at[layer], out_v.at[pl.ds(0, HEAD)]), (q, q_v), (k, k_v), (v, v_v),
                (context, context_v), (log, log_v), (normed, normed_v), (x_own, x_v),
            )
        ] + load_heads(loads, w_mix.at[layer], mix_v)
        load_down.wait()
        load_both.wait()
    else:
        later = []
        load_grad = loads.start(grad_own, grad_v.at[own_rows])
    if returning is not None:
        begin_old, begin_feed, begin_mix, begin_return, finish = returning
        begin_old()

    def feed(d):
        here = plane_rows(d, rows)
        hidden_grad = kernel_dot_nt(grad_v[here, :], down_v[...])
        gate = both_v[here, :units]
        up = both_v[here, units:]
        sig = jax.nn.sigmoid(gate)
        silu = gate * sig
        hidden_v[here, :] = (silu * up).astype(BF)
        both_grad_v[here, :units] = (hidden_grad * up * sig * (1.0 + gate * (1.0 - sig))).astype(BF)
        both_grad_v[here, units:] = (hidden_grad * silu).astype(BF)

    if forward is None:
        gather_rows(grad_v, rows, send_a, recv_a, feed, begun=True)
        load_gate.wait()
    else:

        def before():
            load_grad.wait()
            for h in range(2):
                begin_rows(grad_v, rows, send_a, recv_a, h)

        forward(before, lambda: gather_rows(grad_v, rows, send_a, recv_a, feed, begun=True))

    def spread(d):
        here = plane_rows(d, rows)
        part_v[here, :] = kernel_dot_nt(both_grad_v[here, :], gate_v[...]).astype(BF)

    def feed_weights():
        for one in later[:1]:
            one.wait()
        down_grad_v[...] = kernel_dot_tn(hidden_v[...], grad_v[...]).astype(BF)
        for part in range(2):
            gate_grad_v[part] = kernel_dot_tn(
                two_v[...], both_grad_v[:, part * units : (part + 1) * units]
            ).astype(BF)
        if returning is None:
            saves.start(down_grad_v, outs[4])
            saves.start(gate_grad_v, outs[2])
        else:
            begin_feed()

    def norm_grads(error, value, gain, row):
        factor = mean_square(value)
        shaped = error * gain
        common = jnp.mean(shaped * value, axis=-1, keepdims=True)
        gain_grad_v[row : row + 1, :] += jnp.sum(error * value * factor, axis=0, keepdims=True)
        return factor * shaped - value * (factor * factor * factor) * common

    half = rows // 2

    def middle_half(h):
        part = slice(h * half, (h + 1) * half)
        own_half = pl.ds(pl.multiple_of(own_block(c, f) * rows + h * half, half), half)
        if h == 0:
            for one in later[1:]:
                one.wait()
        middle_grad = norm_grads(total_v[part, :], middle_v[part, :], gains_v[1:2, :].astype(F32), 1)
        middle_grad = middle_grad + grad_v[own_half, :].astype(F32)
        middle_v[part, :] = middle_grad
        low_v[own_half, :] = middle_grad.astype(BF)
        begin_rows(low_v, rows, send_c, recv_c, h)

    scatter_sum(part_v, total_v, land_a, send_b, recv_b, spread, feed_weights, done=middle_half)
    scale = HEAD ** (-0.5)

    def attention(d):
        here = plane_rows(d, rows)
        context_grad = kernel_dot_nt(low_v[here, :], out_v[...])
        common = jnp.sum(context_grad * context_v[here, :].astype(F32), axis=-1, keepdims=True)
        context_grad = context_grad.astype(BF)
        queries = q_v[here, :]
        scores = kernel_dot_nt(queries, k_v[...]) * scale
        allowed = place_row[...] <= place_col[here, :]
        weights = jnp.exp(jnp.where(allowed, scores, masked_value) - log_v[here, 0:1])
        weight_grad = kernel_dot_nt(context_grad, v_v[...])
        score_grad = (weights * (weight_grad - common)).astype(BF)
        value_grad_v[...] += kernel_dot_tn(weights.astype(BF), context_grad)
        key_grad_v[...] += kernel_dot_tn(score_grad, queries)
        query_grad = kernel_dot(score_grad, k_v[...]) * scale
        mixed_v[here, :LANES] = (query_grad * cosine[here, :] - turn(query_grad) * sine[here, :]).astype(BF)

    gather_rows(low_v, rows, send_c, recv_c, attention, begun=True)
    key_grad = key_grad_v[...] * scale
    mixed_v[:, LANES : 2 * LANES] = (key_grad * cosine[...] - turn(key_grad) * sine[...]).astype(BF)
    mixed_v[:, 2 * LANES :] = value_grad_v[...].astype(BF)
    pair = {"ctx": c + 1 - 2 * odd}

    def pair_copy(part):
        return pltpu.make_async_remote_copy(
            mixed_v.at[:, pl.ds(part * LANES, LANES)], kv_land, pair_sems.at[0], pair_sems.at[1],
            device_id=pair, device_id_type=MESH,
        )

    pl.when(odd == 0)(pair_copy(2).start)
    pl.when(odd == 1)(pair_copy(1).start)

    def spread_two(d):
        here = plane_rows(d, rows)
        part_v[here, :] = kernel_dot(mixed_v[here, :], mix_v[...]).astype(BF)

    def mix_weights():
        out_grad_v[...] = kernel_dot_tn(context_v[...], low_v[...])[:HEAD].astype(BF)
        short = HEAD // 2
        columns = kernel_dot_tn(mixed_v[:, :LANES], normed_v[...])
        mix_grad_v[:short, :] = columns[:short].astype(BF)
        mix_grad_v[short:HEAD, :] = columns[SPAN : SPAN + short].astype(BF)
        pair_copy(1).wait_recv()
        mine = jnp.where(odd == 0, mixed_v[:, LANES : 2 * LANES].astype(F32), mixed_v[:, 2 * LANES :].astype(F32))
        kv_v[...] = (mine + kv_land[...].astype(F32)).astype(BF)
        columns = kernel_dot_tn(kv_v[...], normed_v[...])
        mix_grad_v[HEAD : HEAD + short, :] = columns[:short].astype(BF)
        mix_grad_v[HEAD + short :, :] = jnp.where(
            odd == 0, columns[SPAN : SPAN + short], columns[short:HEAD]
        ).astype(BF)
        if returning is None:
            saves.start(out_grad_v, outs[3])
            saves.start(mix_grad_v, outs[1])
        else:
            begin_mix()

    def start_half(h):
        part = slice(h * half, (h + 1) * half)
        start_grad = norm_grads(total_v[part, :], x_v[part, :].astype(F32), gains_v[0:1, :].astype(F32), 0)
        start_grad = start_grad + middle_v[part, :]
        start_v[part, :] = start_grad
        if hand_on is not None:
            hand_on(h, start_grad)

    scatter_sum(part_v, total_v, land_b, send_d, recv_d, spread_two, mix_weights,
                None if returning is None else begin_return, start_half)
    if returning is None:
        saves.start(start_v, outs[0])
        saves.start(gain_grad_v, outs[5])
    else:
        finish(gain_grad_v)
    pair_copy(1).wait_send()
    for one in saves.copies:
        one.wait()


def turn_kernel(*refs):
    (x_own, cotangent, inputs), refs = refs[:3], refs[3:]
    weights, refs = refs[:5], refs[5:]
    tables, refs = refs[:4], refs[4:]
    saved, refs = refs[:9], refs[9:]
    (results_o, starts_o), refs = refs[:2], refs[2:]
    finals, refs = refs[:5], refs[5:]
    (result_old, start_old, mix_old, gate_old, out_old, down_old), refs = refs[:6], refs[6:]
    ahead, refs = refs[:21], refs[21:]
    more, refs = refs[:15], refs[15:]
    own, refs = refs[:10], refs[10:]
    gain_old, *refs = refs
    ahead_sems, first_sems, second_sems = refs[:10], refs[10:21], refs[21:32]
    return_sems, swap_sems = refs[32:37], refs[37]
    (x_v, normed_v, q_v, k_v, v_v, context_v, log_v, middle_v, two_v, both_v, hidden_v, result_v,
     mix_v, gate_v, out_v, down_v, gains_v, part_v, land_a, land_b, total_v) = ahead
    grad_v, own_v, both_grad_v, low_v = more[:4]
    scratch = [
        grad_v, own_v, normed_v, q_v, k_v, v_v, context_v, log_v, middle_v, two_v, both_v, both_grad_v, hidden_v,
        low_v, *more[4:], mix_v, gate_v, out_v, down_v, gains_v, part_v, land_a, land_b, total_v,
    ]
    start_new = more[9]
    mix_new, gate_new, out_new, down_new, gain_new = more[10:]
    gain_v = own[8]
    s = lax.axis_index("section")
    c = lax.axis_index("ctx")
    f = lax.axis_index("fsdp")
    rows = own_v.shape[0]
    half = rows // 2
    first_row = own_block(c, f) * rows

    def meet():
        peers = [{"fsdp": lax.rem(f + k, 4)} for k in range(1, 4)]
        greet_more(peers + [{"section": 1 - s}, {"ctx": lax.rem(c + 2, 4)}])

    def forward(before, ending):
        forward_body(
            1, None, x_own, weights, tables, [None] * 9 + [result_old], ahead, ahead_sems, None, before, ending, meet
        )
        own_v[...] = x_v[pl.ds(pl.multiple_of(first_row, rows), rows), :]

    def hand_on(h, start_grad):
        grad_v[pl.ds(pl.multiple_of(first_row + h * half, half), half), :] = start_grad.astype(BF)
        begin_rows(grad_v, rows, second_sems[3], second_sems[4], h)

    backward_body(
        1, cotangent.at[s], weights, tables, None, (start_old, mix_old, gate_old, out_old, down_old, gain_old),
        scratch, first_sems, None, forward, hand_on,
    )
    begin_old, begin_feed, begin_mix, begin_return, steps_after, wait_all = returner(
        tuple(finals) + tuple(own), return_sems,
        gate_new, down_new, mix_new, out_new, gate_old, down_old, mix_old, out_old,
    )

    def swap_copy(src, dst, slot):
        return pltpu.make_async_remote_copy(
            src, dst, swap_sems.at[slot], swap_sems.at[2 + slot], device_id={"section": 1 - s}, device_id_type=MESH
        )

    def swap_rows(away, home, out, slot):
        swap_copy(away, out.at[s], slot).start()
        pltpu.make_async_copy(home, out.at[s], swap_sems.at[4 + slot]).start()

    result_new = x_own

    def finish(gain_grad_v):
        @pl.when(s == 0)
        def _():
            swap_rows(result_old, result_new, results_o, 0)
            swap_rows(start_old, start_new, starts_o, 1)

        @pl.when(s == 1)
        def _():
            swap_rows(result_new, result_old, results_o, 0)
            swap_rows(start_new, start_old, starts_o, 1)

        gain_v[0] = jnp.zeros(gain_v.shape[1:], F32)
        gain_v[0, 0:2, :] = gain_grad_v[...]
        gain_v[0, 2:4, :] = gain_old[...]
        steps_after()
        wait_all()
        for slot, out in enumerate((results_o, starts_o)):
            pltpu.make_async_copy(out.at[s], out.at[s], swap_sems.at[4 + slot]).wait()
            swap_copy(out.at[s], out.at[1 - s], slot).wait()

    backward_body(
        0, None, weights, tables, [inputs.at[s], *saved], None, scratch, second_sems,
        (begin_old, begin_feed, begin_mix, begin_return, finish),
    )


def link_sems():
    dma = pltpu.SemaphoreType.DMA
    return [dma((GATHER_SENDS,)), dma((GATHER_RECVS,)), dma((SCATTER_SENDS,)), dma((SCATTER_RECVS,))] * 2


def low(*shape):
    return (shape, BF)


def full(*shape):
    return (shape, F32)


def shapes(specs):
    return [jax.ShapeDtypeStruct(*one) for one in specs]


def rooms(specs):
    return [pltpu.VMEM(*one) for one in specs]


def signals(*counts):
    return [pltpu.SemaphoreType.DMA((count,)) for count in counts]


def forward_scratch(rows, width, units):
    length = 16 * rows
    return [low(length, width), low(length, width)] + [low(length, LANES)] * 4 + [
        full(length, LANES), full(rows, width), low(length, width), full(length, 2 * units), low(length, units),
        low(rows, width), low(3 * LANES, width), low(width, 2 * units), low(LANES, width), low(units, width),
        low(16, width), low(length, width), low(19, rows, width), low(19, rows, width), full(rows, width)]


def forward_kept(rows, width, units):
    length = 16 * rows
    return [low(length, width)] + [low(length, LANES)] * 4 + [
        full(length, LANES), full(rows, width), low(length, width), full(length, 2 * units), low(rows, width)]


ANYWHERE = pl.BlockSpec(memory_space=pl.ANY)
INSIDE = pl.BlockSpec(memory_space=pltpu.VMEM)


def forward_share_call(inputs, shards, gains, block_order):
    rows, width = inputs.shape[1:]
    length = 16 * rows
    depth = shards[0].shape[1]
    units = shards[2].shape[2] // 32
    frequency = np.zeros((2, SPAN), np.float32)
    frequency[:, : HEAD // 2] = np.float32(rope_base) ** (-(np.arange(HEAD // 2, dtype=np.float32) * 2.0 / HEAD))
    packing = [low(depth, shards[0].shape[2]), low(shards[0].shape[2], depth), low(depth, 2 * units), low(HEAD, width),
               low(units, width), low(16, depth)]
    kept = forward_kept(rows, width, units)
    weights = [low(2, 3 * HEAD, width), low(2, width, 2 * units), low(2, HEAD, width), low(2, units, width), low(2, 16, width)]
    tables = [full(length, LANES), full(length, LANES), ((length, 1), jnp.int32), ((1, length), jnp.int32)]
    return pl.pallas_call(
        forward_share_kernel,
        out_shape=shapes(kept + weights + tables),
        in_specs=[ANYWHERE] * 5 + [INSIDE] * 4,
        out_specs=[ANYWHERE] * 15 + [INSIDE] * 4,
        scratch_shapes=rooms(forward_scratch(rows, width, units) + packing) + signals(10, 10) + link_sems()
        + signals(9, 27, 26),
        compiler_params=pltpu.CompilerParams(collective_id=0, has_side_effects=True, vmem_limit_bytes=60 << 20),
    )(inputs, *shards, *gains, block_order, jnp.asarray(frequency.reshape(1, LANES)))


def backward_grads(width, units):
    return [low(2 * HEAD, width), low(2, width, units), low(HEAD, width), low(units, width), full(2, width)]


def turn_call(x_own, cotangent, inputs, weights, tables, saved):
    rows, width = x_own.shape
    length = 16 * rows
    depth = width // 4
    units = weights[3].shape[1]
    grads = backward_grads(width, units)
    more = [low(length, width), low(rows, width), low(length, 2 * units), low(length, width), low(length, 3 * LANES),
            low(length, LANES), low(length, LANES), full(length, LANES), full(length, LANES), full(rows, width)] + grads
    own = grads[:4] + grads[:4] + [full(5, 8, width), full(5, 8, width)]
    finals = [low(2, rows, width), full(2, rows, width), low(16 * 2 * HEAD, depth), low(2, depth, 16 * units),
              low(4 * HEAD, width), low(4 * units, width), full(8, width)]
    old = [low(rows, width), full(rows, width)] + grads[:4]
    return pl.pallas_call(
        turn_kernel,
        out_shape=shapes(finals + old),
        in_specs=[ANYWHERE] * 8 + [INSIDE] * 4 + [ANYWHERE] * 9,
        out_specs=[ANYWHERE] * 6 + [INSIDE] + [ANYWHERE] * 6,
        scratch_shapes=rooms(forward_scratch(rows, width, units) + more + own + grads[4:]) + signals(10, 10) + link_sems()
        + signals(20, 7, 2) + link_sems() + signals(20, 7, 2) + link_sems() + signals(5, 23, 23, 50, 40, 6),
        compiler_params=pltpu.CompilerParams(collective_id=1, has_side_effects=True, vmem_limit_bytes=60 << 20),
    )(x_own, cotangent, inputs, *weights, *tables, *saved)


def returner(refs, sems, gate_new, down_new, mix_new, out_new, gate_old, down_old, mix_old, out_old):
    (mix_out, gate_out, out_out, down_out, gain_out,
     mix_v, gate_v, out_v, down_v, mix_x, gate_x, out_x, down_x, gain_v, gain_x) = refs
    local, send, recv, line_send, line_recv = sems
    s = lax.axis_index("section")
    c = lax.axis_index("ctx")
    f = lax.axis_index("fsdp")
    other = {"section": 1 - s}
    units = down_v.shape[0]
    depth = gate_out.shape[1]
    inner = jnp.logical_and(c > 0, c < 3)
    above = jnp.minimum(c + 1, 3)
    below = jnp.maximum(c - 1, 0)

    def copy(src, dst, slot, arrival, peer):
        return pltpu.make_async_remote_copy(
            src, dst, send.at[slot], recv.at[arrival], device_id=peer, device_id_type=MESH
        )

    def owner_part(owner):
        return pl.ds(pl.multiple_of(owner * depth, depth), depth)

    def cross_parts(away, theirs, first):
        for k in range(4):
            owner = lax.rem(f + k, 4)
            part = owner_part(owner)
            copy(away.at[:, part], theirs.at[:, part], first + k, first + owner, other).start()

    def cross_whole(away, theirs, slot):
        copy(away, theirs, slot, slot, other).start()

    def home(src, dst, k):
        pltpu.make_async_copy(src, dst, local.at[k]).start()

    def begin_old():
        @pl.when(s == 0)
        def _():
            cross_whole(down_old, down_x, 8)
            cross_parts(gate_old, gate_x, 0)
            cross_whole(out_old, out_x, 9)
            cross_parts(mix_old, mix_x, 4)

        @pl.when(s == 1)
        def _():
            home(down_old, down_v, 0)
            home(gate_old, gate_v, 1)
            home(out_old, out_v, 2)
            home(mix_old, mix_v, 3)

    def begin_feed():
        @pl.when(s == 0)
        def _():
            home(down_new, down_v, 0)
            home(gate_new, gate_v, 1)

        @pl.when(s == 1)
        def _():
            cross_whole(down_new, down_x, 8)
            cross_parts(gate_new, gate_x, 0)

    def begin_mix():
        @pl.when(s == 0)
        def _():
            home(out_new, out_v, 2)
            home(mix_new, mix_v, 3)

        @pl.when(s == 1)
        def _():
            cross_whole(out_new, out_x, 9)
            cross_parts(mix_new, mix_x, 4)

    def home_wait(k, dst):
        pltpu.make_async_copy(dst, dst, local.at[k]).wait()

    def arrived(ref, arrival):
        copy(ref, ref, 0, arrival, other).wait_recv()

    def gate_at(cc, ff):
        return gate_out.at[:, :, pl.ds(pl.multiple_of((ff * 4 + cc) * units, units), units)]

    def mix_at(cc, ff):
        return mix_out.at[pl.ds(pl.multiple_of((ff * 4 + cc) * 2 * HEAD, 2 * HEAD), 2 * HEAD)]

    def rows_at(ref, cc, count):
        return ref.at[pl.ds(pl.multiple_of(cc * count, count), count)]

    def out_at(cc, ff):
        return rows_at(out_out, cc, HEAD)

    def down_at(cc, ff):
        return rows_at(down_out, cc, units)

    origins = [lax.rem(f + k, 4) for k in (0, 3, 2, 1)]
    items = [(down_at, f)] + [(gate_at, one) for one in origins] + [(out_at, f)] + [(mix_at, one) for one in origins]

    def line(index, cc, slot, target):
        place, origin = items[index]
        return pltpu.make_async_remote_copy(
            place(cc, origin), place(cc, origin), line_send.at[slot], line_recv.at[cc * 10 + index],
            device_id={"ctx": target}, device_id_type=MESH,
        )

    def start_line(index):
        pl.when(c < 3)(line(index, c, index, above).start)
        pl.when(c > 0)(line(index, c, 10 + index, below).start)

    def fold(mine, theirs, arrival):
        arrived(theirs, arrival)
        mine[...] = (mine[...].astype(F32) + theirs[...].astype(F32)).astype(BF)

    def keep(src, dst):
        one = pltpu.make_async_copy(src, dst, local.at[4])
        one.start()
        one.wait()

    def whole_item(k, mine, theirs, arrival, place, index):
        home_wait(k, mine)
        fold(mine, theirs, arrival)
        keep(mine, place(c, f))
        start_line(index)

    def to_owner(k, mine, theirs, place, arrival_x, arrival_y, slot, index):
        owner = lax.rem(f + k, 4)
        rows = owner_part(owner)
        fold(mine.at[:, rows], theirs.at[:, rows], arrival_x + owner)
        if k:
            copy(mine.at[:, rows], place(c, f), slot + k, arrival_y + f, {"fsdp": owner}).start()
        else:
            keep(mine.at[:, rows], place(c, f))
            start_line(index)

    def from_owner(k, place, arrival, index):
        arrived(place(c, origins[k]), arrival + origins[k])
        start_line(index)

    gain_targets = [other, {"fsdp": f + 1 - 2 * lax.rem(f, 2)}, {"fsdp": f + 2 - 4 * (f // 2)},
                    {"ctx": c + 1 - 2 * lax.rem(c, 2)}, {"ctx": lax.rem(c + 2, 4)}]

    def gain_copy(k):
        return copy(gain_v.at[k], gain_x.at[k], 18 + k, 18 + k, gain_targets[k])

    def gain_sum(k):
        gain_copy(k).wait_recv()
        if k < 4:
            gain_v[k + 1] = gain_v[k] + gain_x[k]
            gain_copy(k + 1).start()
        else:
            gain_out[...] = gain_v[k] + gain_x[k]

    order = near_order(c)

    def onward(index, step):
        d = order[step]
        return line(index, d, 20 + (step - 1) * 10 + index, jnp.where(d < c, above, below))

    def pass_on(index, step):
        one = onward(index, step)
        one.wait_recv()
        pl.when(inner)(one.start)

    def near(index):
        pass_on(index, 1)
        pl.when(inner)(lambda: pass_on(index, 2))

    def far(index):
        pl.when(jnp.logical_not(inner))(lambda: pass_on(index, 2))
        pass_on(index, 3)

    def gate_first():
        home_wait(1, gate_v)
        to_owner(0, gate_v, gate_x, gate_at, 0, 10, 10, 1)

    def gate_rest(k):
        return lambda: to_owner(k, gate_v, gate_x, gate_at, 0, 10, 10, 1)

    def gate_from(k):
        return lambda: from_owner(k, gate_at, 10, 1 + k)

    def mix_first():
        home_wait(3, mix_v)
        to_owner(0, mix_v, mix_x, mix_at, 4, 14, 14, 6)

    def mix_rest(k):
        return lambda: to_owner(k, mix_v, mix_x, mix_at, 4, 14, 14, 6)

    def mix_from(k):
        return lambda: from_owner(k, mix_at, 14, 6 + k)

    def down_first():
        whole_item(0, down_v, down_x, 8, down_at, 0)

    def out_first():
        whole_item(2, out_v, out_x, 9, out_at, 5)

    def passing(*steps):
        return [functools.partial(near if sign > 0 else far, abs(sign) - 1) for sign in steps]

    after = [
        passing(1) + [gate_from(1), gate_from(2), gate_from(3), out_first, mix_first, mix_rest(1), mix_rest(2), mix_rest(3)],
        passing(2, -1, 3, -2, 4) + [mix_from(1), mix_from(2), mix_from(3)],
        passing(-3, 5, -4, 6, -5, 7),
        passing(-6, 8, -7, 9),
        passing(-8, 10, -9, -10),
    ]
    def begin_return():
        down_first()
        gate_first()
        for k in range(1, 4):
            gate_rest(k)()

    def steps_after():
        gain_copy(0).start()
        for k, steps in enumerate(after):
            for step in steps:
                step()
            gain_sum(k)

    def wait_all():
        for index in range(10):
            pl.when(c < 3)(line(index, c, index, above).wait_send)
            pl.when(c > 0)(line(index, c, 10 + index, below).wait_send)
            for step in range(1, 4):
                pl.when(inner)(onward(index, step).wait_send)
        for k in range(5):
            gain_copy(k).wait_send()
        for k in range(4):
            gate_part = gate_x.at[:, pl.ds(k * depth, depth)]
            mix_part = mix_x.at[:, pl.ds(k * depth, depth)]
            for slot in (k, 10 + k) if k else (k,):
                copy(gate_part, gate_part, slot, 0, other).wait_send()
                copy(mix_part, mix_part, 4 + slot, 0, other).wait_send()
        copy(down_x, down_x, 8, 0, other).wait_send()
        copy(out_x, out_x, 9, 0, other).wait_send()

    return begin_old, begin_feed, begin_mix, begin_return, steps_after, wait_all


def widen_kernel(mix, gate, out, down, gains, results, starts,
                 mix_f, gate_f, out_f, down_f, attention_f, feed_f, results_f, starts_f, places, turned, rest):
    step = pl.program_id(0)
    rows = gate.shape[1]
    four = 4 * HEAD
    width = 4 * four

    @pl.when(step == 0)
    def _():
        s = lax.axis_index("section")
        f = lax.axis_index("fsdp")
        depth = attention_f.shape[1]
        columns = pl.ds(pl.multiple_of(f * depth, depth), depth)
        attention_f[...] = gains[pl.ds(2 * s, 1), columns]
        feed_f[...] = gains[pl.ds(2 * s + 1, 1), columns]
        results_f[...] = results[...]
        starts_f[...] = starts[...]
        source = lax.broadcasted_iota(jnp.int32, (2 * four, 2 * four), 0)
        column = lax.broadcasted_iota(jnp.int32, (2 * four, 2 * four), 1)
        query = (column // HEAD) * 2 * HEAD + lax.rem(column, HEAD)
        beyond = column - four
        kind = beyond // (2 * HEAD)
        beyond = beyond - kind * 2 * HEAD
        other = (2 * (beyond // HEAD) + kind) * 2 * HEAD + HEAD + lax.rem(beyond, HEAD)
        places[...] = jnp.where(source == jnp.where(column < four, query, other), 1.0, 0.0).astype(BF)

    @pl.when(step < 4)
    def _():
        group = kernel_dot_tn(mix[...], places[...])
        turned[:, pl.ds(pl.multiple_of(step * four, four), four)] = group[:, :four]
        rest[step] = group[:, four:]

    @pl.when(step >= 4)
    def _():
        here = pl.ds(pl.multiple_of((step - 4) * 2 * rows, 2 * rows), 2 * rows)
        mix_f[:, :width] = turned[here, :]
        for g in range(2):
            for kind in range(2):
                at = width + kind * 2 * four + g * four
                part = slice(kind * 2 * HEAD, (kind + 1) * 2 * HEAD)
                mix_f[:, at : at + four] = jnp.concatenate([rest[2 * g + k, here, part] for k in range(2)], axis=1)

    half = gate.shape[2]
    gate_f[:, :half] = gate[0].astype(F32)
    gate_f[:, half:] = gate[1].astype(F32)
    out_f[...] = out[...].astype(F32)
    down_f[...] = down[...].astype(F32)


def widen_call(results, starts, mix, gate, out, down, gains):
    steps = 8
    depth = gate.shape[1]
    width = out.shape[1]
    rows = depth // steps

    def whole(array):
        return pl.BlockSpec(array.shape, lambda i: (0,) * array.ndim)

    down_rows = down.shape[0] // steps
    return pl.pallas_call(
        widen_kernel,
        grid=(steps,),
        out_shape=shapes([
            full(depth, 2 * width), full(depth, 2 * gate.shape[2]), full(*out.shape), full(*down.shape),
            full(1, depth), full(1, depth), low(*results.shape), full(*starts.shape),
        ]),
        in_specs=[
            pl.BlockSpec((8 * HEAD, depth), lambda i: (jnp.minimum(i, 3), 0)),
            pl.BlockSpec((2, rows, gate.shape[2]), lambda i: (0, i, 0)),
            pl.BlockSpec((rows, width), lambda i: (i, 0)),
            pl.BlockSpec((down_rows, width), lambda i: (i, 0)),
            whole(gains),
            whole(results),
            whole(starts),
        ],
        out_specs=[
            pl.BlockSpec((2 * rows, 2 * width), lambda i: (jnp.maximum(i - 4, 0), 0)),
            pl.BlockSpec((rows, 2 * gate.shape[2]), lambda i: (i, 0)),
            pl.BlockSpec((rows, width), lambda i: (i, 0)),
            pl.BlockSpec((down_rows, width), lambda i: (i, 0)),
            pl.BlockSpec((1, depth), lambda i: (0, 0)),
            pl.BlockSpec((1, depth), lambda i: (0, 0)),
            whole(results),
            whole(starts),
        ],
        scratch_shapes=rooms([low(8 * HEAD, 8 * HEAD), full(depth, width), full(4, depth, 4 * HEAD)]),
        compiler_params=pltpu.CompilerParams(vmem_limit_bytes=60 << 20),
    )(mix, gate, out, down, gains, results, starts)


def on_line():
    return lax.axis_size("ctx") == 4 and lax.axis_size("fsdp") == 4


def gather(own):
    return lax.all_gather(own, ("ctx", "fsdp"), axis=0, tiled=True)


def scatter(part):
    return lax.psum_scatter(part, ("ctx", "fsdp"), scatter_dimension=0, tiled=True)


def spread_halves(columns):
    halves = columns.reshape(columns.shape[:-1] + (2, HEAD // 2))
    halves = jnp.pad(halves, [(0, 0)] * (halves.ndim - 1) + [(0, SPAN - HEAD // 2)])
    return halves.reshape(columns.shape[:-1] + (LANES,))


def join_halves(columns):
    halves = columns.reshape(columns.shape[:-1] + (2, SPAN))[..., : HEAD // 2]
    return halves.reshape(columns.shape[:-1] + (HEAD,))


def angle_tables(positions):
    frequency = rope_base ** (-(jnp.arange(HEAD // 2, dtype=F32) * 2.0 / HEAD))
    frequency = jnp.pad(frequency, (0, SPAN - HEAD // 2))
    angles = positions.astype(F32)[:, None] * frequency[None, :]
    cosine = jnp.cos(angles)
    sine = jnp.sin(angles)
    return jnp.concatenate([cosine, cosine], axis=1), jnp.concatenate([-sine, sine], axis=1)


def rotate(values, cosine, sine):
    return values * cosine + jnp.roll(values, SPAN, axis=1) * sine


def rotate_back(grads, cosine, sine):
    return grads * cosine - jnp.roll(grads, SPAN, axis=1) * sine


def norm_rows(values):
    return lax.rsqrt(jnp.mean(values * values, axis=-1, keepdims=True) + norm_eps)


def norm_back(grad_out, values, factor, gain):
    shaped = grad_out * gain
    common = jnp.mean(shaped * values, axis=-1, keepdims=True)
    grad_in = factor * shaped - values * (factor * factor * factor) * common
    return grad_in, jnp.sum(grad_out * values * factor, axis=0)


def dot(left, right):
    return jnp.dot(left, right, preferred_element_type=F32)


def dot_nt(left, right):
    return lax.dot_general(left, right, (((1,), (1,)), ((), ())), preferred_element_type=F32)


def dot_tn(left, right):
    return lax.dot_general(left, right, (((0,), (0,)), ((), ())), preferred_element_type=F32)


class Plan:
    def __init__(self, width, hidden_units):
        self.c = lax.axis_index("ctx")
        self.f = lax.axis_index("fsdp")
        self.C = lax.axis_size("ctx")
        self.F = lax.axis_size("fsdp")
        self.heads = width // HEAD
        self.ratio = self.heads // KV_HEADS
        self.heads_f = self.heads // self.F
        self.groups_f = KV_HEADS // self.F
        self.share = self.C // self.heads_f
        self.units = hidden_units // (self.F * self.C)
        self.local_head = self.c // self.share
        self.part = self.c % self.share


def pick(array, index, axis):
    return lax.dynamic_index_in_dim(array, index, axis, keepdims=False)


def pack_weights(plan, mix, gate_up):
    depth = mix.shape[0]
    width = plan.heads * HEAD
    kv_width = KV_HEADS * HEAD
    F = plan.F
    queries = pick(mix[:, :width].reshape(depth, F, plan.heads_f, HEAD), plan.local_head, 2)
    group = plan.local_head // plan.ratio
    keys = pick(mix[:, width : width + kv_width].reshape(depth, F, plan.groups_f, HEAD), group, 2)
    values = pick(mix[:, width + kv_width :].reshape(depth, F, plan.groups_f, HEAD), group, 2)
    values = jnp.pad(values, ((0, 0), (0, 0), (0, LANES - HEAD)))
    half = gate_up.shape[1] // 2
    gate = pick(gate_up[:, :half].reshape(depth, F, plan.C, plan.units), plan.c, 2)
    up = pick(gate_up[:, half:].reshape(depth, F, plan.C, plan.units), plan.c, 2)
    packed = jnp.concatenate([spread_halves(queries), spread_halves(keys), values, gate, up], axis=2)
    return jnp.swapaxes(packed, 0, 1)


def attend(plan, q_part, k, v, positions, part_positions):
    scores = dot_nt(q_part, k) * HEAD ** (-0.5)
    allowed = positions[None, :] <= part_positions[:, None]
    scores = jnp.where(allowed, scores, masked_value)
    top = jnp.max(scores, axis=-1, keepdims=True)
    weights = jnp.exp(scores - top)
    total = jnp.sum(weights, axis=-1, keepdims=True)
    context = dot((weights / total).astype(BF), v)
    return context.astype(BF), top + jnp.log(total)


def attend_back(q_part, k, v, context_grad, context, log_total, positions, part_positions):
    scale = HEAD ** (-0.5)
    common = jnp.sum(context_grad.astype(F32) * context.astype(F32), axis=-1, keepdims=True)
    allowed = positions[None, :] <= part_positions[:, None]
    scores = dot_nt(q_part, k) * scale
    weights = jnp.exp(jnp.where(allowed, scores, masked_value) - log_total)
    weight_grad = dot_nt(context_grad, v)
    score_grad = (weights * (weight_grad - common)).astype(BF)
    value_grad = dot_tn(weights.astype(BF), context_grad)
    key_grad = dot_tn(score_grad, q_part) * scale
    query_grad = dot(score_grad, k) * scale
    return query_grad, key_grad, value_grad


def forward_layer(plan, x_own, weights, gains, positions, part_positions, tables):
    mix_cut, gate_cut, out, down = weights
    cosine, sine = tables
    length = positions.shape[0]
    x_all = gather(x_own)
    x32 = x_all.astype(F32)
    factor = norm_rows(x32)
    normed = (x32 * factor * gains[0]).astype(BF)
    mixed = dot(normed, mix_cut)
    q = rotate(mixed[:, :LANES], cosine, sine).astype(BF)
    k = rotate(mixed[:, LANES : 2 * LANES], cosine, sine).astype(BF)
    v = mixed[:, 2 * LANES :].astype(BF)
    rows = length // plan.share
    start = plan.part * rows
    q_part = lax.dynamic_slice_in_dim(q, start, rows, 0)
    context, log_total = attend(plan, q_part, k, v, positions, part_positions)
    partial = dot(context[:, :HEAD], out).astype(BF)
    if plan.share > 1:
        partial = lax.dynamic_update_slice_in_dim(
            jnp.zeros((length, partial.shape[1]), BF), partial, start, 0
        )
    middle = x_own.astype(F32) + scatter(partial)
    factor_two = norm_rows(middle)
    normed_two = gather((middle * factor_two * gains[1]).astype(BF))
    both = dot(normed_two, gate_cut)
    hidden = (jax.nn.silu(both[:, : plan.units]) * both[:, plan.units :]).astype(BF)
    result = middle + scatter(dot(hidden, down).astype(BF))
    kept = (x_own, normed, q_part, k, v, context, log_total, middle, normed_two, both, hidden)
    return result.astype(BF), kept


def backward_layer(plan, grad_own, weights, gains, kept, positions, part_positions, tables, part_tables):
    mix_cut, gate_cut, out, down = weights
    x_own, normed, q_part, k, v, context, log_total, middle, normed_two, both, hidden = kept
    length = positions.shape[0]
    rows = length // plan.share
    start = plan.part * rows
    grad_all = gather(grad_own)
    hidden_grad = dot_nt(grad_all, down)
    gate = both[:, : plan.units]
    up = both[:, plan.units :]
    sig = jax.nn.sigmoid(gate)
    gate_grad = hidden_grad * up * sig * (1.0 + gate * (1.0 - sig))
    up_grad = hidden_grad * gate * sig
    both_grad = jnp.concatenate([gate_grad, up_grad], axis=1).astype(BF)
    normed_two_grad = scatter(dot_nt(both_grad, gate_cut).astype(BF))
    middle_grad, feed_gain_grad = norm_back(normed_two_grad, middle, norm_rows(middle), gains[1])
    middle_grad = middle_grad + grad_own.astype(F32)
    middle_low = gather(middle_grad.astype(BF))
    middle_part = lax.dynamic_slice_in_dim(middle_low, start, rows, 0)
    context_grad = jnp.pad(dot_nt(middle_part, out), ((0, 0), (0, LANES - HEAD))).astype(BF)
    query_grad, key_grad, value_grad = attend_back(
        q_part, k, v, context_grad, context, log_total, positions, part_positions
    )
    query_grad = rotate_back(query_grad, *part_tables).astype(BF)
    if plan.share > 1:
        query_grad = lax.dynamic_update_slice_in_dim(
            jnp.zeros((length, LANES), BF), query_grad, start, 0
        )
    key_grad = rotate_back(key_grad, *tables).astype(BF)
    mixed_grad = jnp.concatenate([query_grad, key_grad, value_grad.astype(BF)], axis=1)
    normed_grad = scatter(dot_nt(mixed_grad, mix_cut).astype(BF))
    x32 = x_own.astype(F32)
    start_grad, attention_gain_grad = norm_back(normed_grad, x32, norm_rows(x32), gains[0])
    start_grad = start_grad + middle_grad
    mix_grad = jnp.stack(
        [dot_tn(normed, part).astype(BF) for part in (query_grad, key_grad, value_grad.astype(BF))]
    )
    gate_cut_grad = jnp.stack(
        [dot_tn(normed_two, part.astype(BF)).astype(BF) for part in (gate_grad, up_grad)]
    )
    out_grad = dot_tn(context, middle_part).astype(BF)[:HEAD]
    down_grad = dot_tn(hidden, grad_all).astype(BF)
    return start_grad, (mix_grad, gate_cut_grad, out_grad, down_grad), jnp.stack([attention_gain_grad, feed_gain_grad])


def swap_sections(array):
    return lax.ppermute(array, "section", [(0, 1), (1, 0)])


def by_layer_of(section, own, other):
    first = section == 0
    return jnp.where(first, own, other), jnp.where(first, other, own)


def shared_weights(plan, section, attention_gain, query_key_value, output_weight, feed_gain, gate_up, down_weight):
    depth = query_key_value.shape[1]
    width = depth * plan.F
    gains = lax.all_gather(
        jnp.stack([attention_gain[0], feed_gain[0]]), ("section", "fsdp"), axis=0, tiled=False
    )
    gains = gains.reshape(2, plan.F, 2, depth)
    gains = jnp.swapaxes(gains, 1, 2).reshape(2, 2, width).astype(F32)
    packed = pack_weights(plan, query_key_value[0], gate_up[0])
    own_cut = lax.all_to_all(packed, "fsdp", 0, 0).reshape(width, -1)
    own_out = lax.dynamic_slice_in_dim(output_weight[0], plan.local_head * HEAD, HEAD, 0)
    own_down = lax.dynamic_slice_in_dim(down_weight[0], plan.c * plan.units, plan.units, 0)
    cuts = by_layer_of(section, own_cut, swap_sections(own_cut))
    outs = by_layer_of(section, own_out, swap_sections(own_out))
    downs = by_layer_of(section, own_down, swap_sections(own_down))
    weights = [(cuts[s][:, : 3 * LANES], cuts[s][:, 3 * LANES :], outs[s], downs[s]) for s in range(2)]
    return weights, gains


def own_gain_sums(plan, section, gain_sum, depth):
    gain_sum = lax.dynamic_slice_in_dim(gain_sum, 2 * section, 2, 0)
    return lax.dynamic_slice_in_dim(gain_sum, plan.f * depth, depth, 1)


def returned_grads(plan, section, weight_grads, gain_grads, depth):
    C, F = plan.C, plan.F
    gain_sum = jnp.concatenate([gain_grads[0], gain_grads[1]])

    def collected(index):
        first, second = weight_grads[0][index], weight_grads[1][index]
        own = jnp.where(section == 0, first, second)
        away = jnp.where(section == 0, second, first)
        return (own.astype(F32) + swap_sections(away).astype(F32)).astype(BF)

    cut_grad = jnp.concatenate(list(collected(0)) + list(collected(1)), axis=1)
    cut_grad = lax.all_to_all(cut_grad.reshape(F, depth, -1), "fsdp", 0, 0)
    cut_grad = lax.all_gather(cut_grad, "ctx", axis=0, tiled=False)
    out_grad = lax.all_gather(collected(2), "ctx", axis=0, tiled=False)
    down_grad = lax.all_gather(collected(3), "ctx", axis=0, tiled=True).astype(F32)

    def heads_of(columns, count):
        folded = columns.astype(F32).reshape(count, C // count, F, depth, columns.shape[-1]).sum(axis=1)
        return jnp.transpose(folded, (2, 1, 0, 3))

    q_grad = join_halves(heads_of(cut_grad[..., :LANES], plan.heads_f)).reshape(depth, -1)
    k_grad = join_halves(heads_of(cut_grad[..., LANES : 2 * LANES], plan.groups_f)).reshape(depth, -1)
    v_grad = heads_of(cut_grad[..., 2 * LANES : 3 * LANES], plan.groups_f)[..., :HEAD].reshape(depth, -1)
    mix_grad = jnp.concatenate([q_grad, k_grad, v_grad], axis=1)
    both = jnp.transpose(cut_grad[..., 3 * LANES :], (2, 1, 0, 3)).astype(F32)
    gate_up_grad = jnp.concatenate(
        [both[..., : plan.units].reshape(depth, -1), both[..., plan.units :].reshape(depth, -1)], axis=1
    )
    out_grad = out_grad.astype(F32).reshape(plan.heads_f, plan.share, HEAD, depth * F).sum(axis=1).reshape(-1, depth * F)

    gain_sum = lax.psum(gain_sum, ("section", "ctx", "fsdp"))
    return mix_grad, gate_up_grad, out_grad, down_grad, own_gain_sums(plan, section, gain_sum, depth)


def on_device(
    inputs, cotangent, attention_gain, query_key_value, output_weight, feed_gain, gate_up, down_weight, block_order
):
    section = lax.axis_index("section")
    width = inputs.shape[2]
    hidden_units = down_weight.shape[1] * lax.axis_size("fsdp")
    plan = Plan(width, hidden_units)
    rows = inputs.shape[1]
    C, F = plan.C, plan.F
    length = rows * C * F
    depth = query_key_value.shape[1]

    def by_layer(own, other):
        first = section == 0
        return jnp.where(first, own, other), jnp.where(first, other, own)

    results = []
    input_grads = [None, None]
    weight_grads = [None, None]
    gain_grads = [None, None]
    kept = []
    if on_line():
        shards = (query_key_value, output_weight, gate_up, down_weight)
        first = forward_share_call(inputs, shards, (attention_gain, feed_gain), block_order)
        weights = first[10:15]
        common = first[15:]
        last = turn_call(first[9], cotangent, inputs, weights, common, first[:9])[:7]
        (mix_grad, gate_up_grad, out_grad, down_grad, attention_gain_grad, feed_gain_grad,
         section_outputs, section_input_grads) = widen_call(*last)
    else:
        order = pick(block_order, section, 0)
        positions = (order[:, None] * rows + jnp.arange(rows, dtype=jnp.int32)[None, :]).reshape(length)
        part_rows = length // plan.share
        part_positions = lax.dynamic_slice_in_dim(positions, plan.part * part_rows, part_rows, 0)
        tables = angle_tables(positions)
        part_tables = angle_tables(part_positions)

        x = pick(inputs, section, 0)
        grad = pick(cotangent, section, 0)
        weights, gains = shared_weights(
            plan, section, attention_gain, query_key_value, output_weight, feed_gain, gate_up, down_weight
        )
        for s in range(2):
            x, keep = forward_layer(plan, x, weights[s], gains[s], positions, part_positions, tables)
            kept.append(keep)
            results.append(x)
        for s in (1, 0):
            input_grads[s], weight_grads[s], gain_grads[s] = backward_layer(
                plan, grad, weights[s], gains[s], kept[s], positions, part_positions, tables, part_tables
            )
            grad = input_grads[s].astype(BF)
        def mine_and_theirs(first, second):
            return jnp.where(section == 0, first, second), jnp.where(section == 0, second, first)

        def by_batch(first, second):
            own, away = mine_and_theirs(first, second)
            return jnp.stack(by_layer(own, swap_sections(away)))

        section_outputs = by_batch(*results)
        section_input_grads = by_batch(*input_grads)

        shard_grads = returned_grads(plan, section, weight_grads, gain_grads, depth)
        mix_grad, gate_up_grad, out_grad, down_grad, gain_sum = shard_grads
        attention_gain_grad, feed_gain_grad = gain_sum[0][None], gain_sum[1][None]

    return (
        section_outputs[None],
        section_input_grads[None],
        attention_gain_grad,
        mix_grad[None],
        out_grad[None],
        feed_gain_grad,
        gate_up_grad[None],
        down_grad[None],
    )


def solution(mesh):
    placed = (
        P(None, ("ctx", "fsdp"), None),
        P(None, ("ctx", "fsdp"), None),
        P("section", "fsdp"),
        P("section", "fsdp", None),
        P("section", "fsdp", None),
        P("section", "fsdp"),
        P("section", "fsdp", None),
        P("section", "fsdp", None),
        P(),
    )
    return jax.shard_map(
        on_device,
        mesh=mesh,
        in_specs=placed,
        out_specs=(
            P("section", None, ("ctx", "fsdp"), None),
            P("section", None, ("ctx", "fsdp"), None),
            P("section", "fsdp"),
            P("section", "fsdp", None),
            P("section", "fsdp", None),
            P("section", "fsdp"),
            P("section", "fsdp", None),
            P("section", "fsdp", None),
        ),
        check_vma=False,
    )
```
